32 devices in a mesh: dp: 8 (over z, x), tensor: 4 (over y, core).
Axes of the slice: x: 2, y: 2, z: 4, core: 2. Of those that a mesh axis runs over, the one named last changes fastest.
Arguments:
- latents: float32 [24, 4096], P('dp', 'tensor'), may hold values from -6 to 6
- target_noise: float32 [24, 4096], P('dp', 'tensor'), may hold values from -6 to 6
- timesteps: int32 [24], P('dp'), may hold values from 1 to 999
- labels: int32 [24], P('dp'), may hold values from 0 to 1000
- step_count: int32 [], replicated, may hold values from 1 to 20
- embed_table: float32 [3640, 768], P(None, ('dp', 'tensor')), may hold values from -6 to 6
- layer_in: float32 [3, 768, 4, 1344], P(None, 'dp', 'tensor'), may hold values from -0.21875 to 0.21875
- layer_out: float32 [3, 4, 960, 768], P(None, 'tensor', 'dp'), may hold values from -0.21875 to 0.21875
- layer_ada: float32 [3, 768, 4608], P(None, 'dp', 'tensor'), may hold values from -0.21875 to 0.21875
- embed_first: float32 [3640, 768], P(None, ('dp', 'tensor')), may hold values from -0.00024 to 0.00024
- embed_second: float32 [3640, 768], P(None, ('dp', 'tensor')), may hold values from 3e-10 to 1e-08
- input_first: float32 [3, 768, 4, 1344], P(None, 'dp', 'tensor'), may hold values from -0.00024 to 0.00024
- input_second: float32 [3, 768, 4, 1344], P(None, 'dp', 'tensor'), may hold values from 3e-10 to 1e-08
- output_first: float32 [3, 4, 960, 768], P(None, 'tensor', 'dp'), may hold values from -0.00024 to 0.00024
- output_second: float32 [3, 4, 960, 768], P(None, 'tensor', 'dp'), may hold values from 3e-10 to 1e-08
- mod_first: float32 [3, 768, 4608], P(None, 'dp', 'tensor'), may hold values from -0.00024 to 0.00024
- mod_second: float32 [3, 768, 4608], P(None, 'dp', 'tensor'), may hold values from 3e-10 to 1e-08
Outputs:
- loss_value: float32 [], replicated
- grad_norm: float32 [], replicated
- embed_step: float32 [3640, 768], P(None, ('dp', 'tensor'))
- embed_first_new: float32 [3640, 768], P(None, ('dp', 'tensor'))
- embed_second_new: float32 [3640, 768], P(None, ('dp', 'tensor'))
- input_master: float32 [3, 768, 4, 1344], P(None, 'dp', 'tensor')
- input_first_new: float32 [3, 768, 4, 1344], P(None, 'dp', 'tensor')
- input_second_new: float32 [3, 768, 4, 1344], P(None, 'dp', 'tensor')
- input_copy: bfloat16 [3, 768, 4, 1344], P(None, 'dp', 'tensor')
- output_master: float32 [3, 4, 960, 768], P(None, 'tensor', 'dp')
- output_first_new: float32 [3, 4, 960, 768], P(None, 'tensor', 'dp')
- output_second_new: float32 [3, 4, 960, 768], P(None, 'tensor', 'dp')
- output_copy: bfloat16 [3, 4, 960, 768], P(None, 'tensor', 'dp')
- mod_master: float32 [3, 768, 4608], P(None, 'dp', 'tensor')
- mod_first_new: float32 [3, 768, 4608], P(None, 'dp', 'tensor')
- mod_second_new: float32 [3, 768, 4608], P(None, 'dp', 'tensor')
- mod_copy: bfloat16 [3, 768, 4608], P(None, 'dp', 'tensor')
The draws below stay inside these ranges and needn't reach their ends.
All inputs are finite; a program needn't handle non-finite values.
Results may differ from the reference program's by a relative error of at most 0.008.
The reference program's roundings to bfloat16 on the way count: a program that leaves them out, or rounds other values in their place, can miss the bound.
Values may be sent and summed in bfloat16 or wider, within the bound.
A program may use at most 256 MiB of HBM per device.

```python
import math
import jax
import jax.numpy as jnp
from jax import lax

D = 768
HEADS = 12
HEAD_DIM = 64
FF = 3072
CLASSES = 1001
FREQ = 256
CHANNELS = 4
PATCH = 2
SIDE = 32
LAYERS = 3
IMAGES = 24
TOKENS_IMG = 256
PIXELS = 4096
PATCH_IN = 16
HEADS_DEV = 3
IN_COLS = 1344
OUT_ROWS = 960
LAYER_ROWS = 14
ROWS = 3640
N_TENSOR = 4


def draw_embed_table(key, part):
    patch_in = PATCH * PATCH * CHANNELS
    patch_start = CLASSES
    time_start = patch_start + patch_in
    second_start = time_start + FREQ
    vector_start = second_start + 3 * D + patch_in
    row_index = jnp.arange(ROWS, dtype=jnp.int32)[:, None]
    row_scale = jnp.where(row_index < patch_start, 1.0, jnp.where(row_index < time_start, patch_in ** (-0.5), jnp.where(row_index < second_start, FREQ ** (-0.5), jnp.where(row_index < vector_start, D ** (-0.5), 0.5))))
    base_draw = jnp.clip(jax.random.normal(key, (ROWS, D), jnp.float32), -6.0, 6.0)
    return (base_draw * row_scale).astype(jnp.float32)


def set_ends(drawn, key, low, top_value):
    place = [jax.random.randint(jax.random.fold_in(key, axis), (), 0, length) for axis, length in enumerate(drawn.shape)]
    longest = drawn.shape.index(max(drawn.shape))
    next_to = place[:longest] + [(place[longest] + 1) % drawn.shape[longest]] + place[longest + 1:]
    return drawn.at[tuple(place)].set(low).at[tuple(next_to)].set(top_value)


def steps_of(stream_key, shape, split, least, high):
    def one(axis_at, blocks):
        draws = jax.random.uniform(jax.random.fold_in(jax.random.fold_in(stream_key, 6), axis_at), (blocks,), jnp.float32, least / len(split), high / len(split))
        return jnp.repeat(jnp.exp(draws), shape[axis_at] // blocks).reshape((-1,) + (1,) * (len(shape) - axis_at - 1))

    loudness = one(*split[0])
    for cut in split[1:]:
        loudness = loudness * one(*cut)
    return loudness


def normal_values(rng, extent, spread, most, shards=(), kind=jnp.bfloat16):
    values = jax.random.normal(rng, extent, jnp.float32) * spread
    if len(shards) > 0:
        values = steps_of(rng, extent, shards, -0.22, 0.18) * values
    return jnp.clip(values, min=-most, max=most).astype(kind)


def setup_inputs(seed: int = 0) -> dict:
    arg_keys = jax.random.split(jax.random.key(seed), 18)
    return {
        "latents": normal_values(arg_keys[0], (IMAGES, PIXELS), 1.0, 6.0, ((0, 8), (1, 4)), jnp.float32),
        "target_noise": normal_values(arg_keys[1], (IMAGES, PIXELS), 1.0, 6.0, ((0, 8), (1, 4)), jnp.float32),
        "timesteps": set_ends(jax.random.randint(arg_keys[2], (IMAGES,), 1, 1000), jax.random.fold_in(arg_keys[2], 1), 1, 999).astype(jnp.int32),
        "labels": set_ends(jax.random.randint(arg_keys[3], (IMAGES,), 0, CLASSES), jax.random.fold_in(arg_keys[3], 1), 0, CLASSES - 1).astype(jnp.int32),
        "step_count": jax.random.randint(arg_keys[4], (), 1, 21).astype(jnp.int32),
        "embed_table": draw_embed_table(jax.random.fold_in(arg_keys[17], 71), 0),
        "layer_in": normal_values(arg_keys[6], (LAYERS, D, N_TENSOR, IN_COLS), D ** -0.5, 0.21875, ((1, 8), (2, 4)), jnp.float32),
        "layer_out": normal_values(arg_keys[7], (LAYERS, N_TENSOR, OUT_ROWS, D), D ** -0.5, 0.21875, ((1, 4), (2, 8)), jnp.float32),
        "layer_ada": normal_values(arg_keys[8], (LAYERS, D, 6 * D), D ** -0.5, 0.21875, ((1, 8), (2, 4)), jnp.float32),
        "embed_first": normal_values(arg_keys[9], (ROWS, D), 0.00004, 0.00024, ((1, 32),), jnp.float32),
        "embed_second": jnp.clip(jnp.exp(math.log(9.99999993922529e-09) - 3.506558 * jax.random.uniform(arg_keys[10], (ROWS, D), jnp.float32) ** steps_of(arg_keys[10], (ROWS, D), ((1, 32),), -0.2, 0.2)), 2.999999970665357e-10, 9.99999993922529e-09),
        "input_first": normal_values(arg_keys[11], (LAYERS, D, N_TENSOR, IN_COLS), 0.00004, 0.00024, ((1, 8), (2, 4)), jnp.float32),
        "input_second": jnp.clip(jnp.exp(math.log(9.99999993922529e-09) - 3.506558 * jax.random.uniform(arg_keys[12], (LAYERS, D, N_TENSOR, IN_COLS), jnp.float32) ** steps_of(arg_keys[12], (LAYERS, D, N_TENSOR, IN_COLS), ((1, 8), (2, 4)), -0.2, 0.2)), 2.999999970665357e-10, 9.99999993922529e-09),
        "output_first": normal_values(arg_keys[13], (LAYERS, N_TENSOR, OUT_ROWS, D), 0.00004, 0.00024, ((1, 4), (2, 8)), jnp.float32),
        "output_second": jnp.clip(jnp.exp(math.log(9.99999993922529e-09) - 3.506558 * jax.random.uniform(arg_keys[14], (LAYERS, N_TENSOR, OUT_ROWS, D), jnp.float32) ** steps_of(arg_keys[14], (LAYERS, N_TENSOR, OUT_ROWS, D), ((1, 4), (2, 8)), -0.2, 0.2)), 2.999999970665357e-10, 9.99999993922529e-09),
        "mod_first": normal_values(arg_keys[15], (LAYERS, D, 6 * D), 0.00004, 0.00024, ((1, 8), (2, 4)), jnp.float32),
        "mod_second": jnp.clip(jnp.exp(math.log(9.99999993922529e-09) - 3.506558 * jax.random.uniform(arg_keys[16], (LAYERS, D, 6 * D), jnp.float32) ** steps_of(arg_keys[16], (LAYERS, D, 6 * D), ((1, 8), (2, 4)), -0.2, 0.2)), 2.999999970665357e-10, 9.99999993922529e-09),
    }


@jax.custom_vjp
def low(v):
    return lax.optimization_barrier(v.astype(jnp.bfloat16)).astype(jnp.float32)

@jax.custom_vjp
def low_back(v):
    return v

def low_keep(v):
    return (low(v), None)

def low_pass(kept, grad):
    return (grad,)

def back_keep(v):
    return (v, None)

def back_low(kept, grad):
    return (low(grad),)
low.defvjp(low_keep, low_pass)
low_back.defvjp(back_keep, back_low)
EPS_NORM = 1e-06
LEARN_RATE = 0.01
DECAY = 0.01
BETA_ONE = 0.5
BETA_TWO = 0.5
ADAM_EPS = 1e-08
CLIP_NORM = 0.25
PRECISE = lax.Precision.HIGHEST

def dense(left_op, right_op):
    return jnp.dot(left_op, right_op, precision=PRECISE, preferred_element_type=jnp.float32)

def layer_norm(values):
    center = values - lax.optimization_barrier(jnp.mean(values, axis=-1, keepdims=True))
    return center * lax.rsqrt(lax.optimization_barrier(jnp.mean(center * center, axis=-1, keepdims=True)) + EPS_NORM)

def modulate(values, shift_vec, scale_vec):
    return layer_norm(values) * (1.0 + scale_vec[:, None, :]) + shift_vec[:, None, :]

def time_features(step_ints):
    half_width = FREQ // 2
    frequency = jnp.exp(-math.log(10000.0) * jnp.arange(half_width, dtype=jnp.float32) / half_width)
    angles = step_ints.astype(jnp.float32)[:, None] * frequency[None, :]
    return jnp.concatenate([jnp.cos(angles), jnp.sin(angles)], axis=1)

def noise_levels(step_ints):
    base_cos = math.cos(0.008 / 1.008 * math.pi / 2)
    angles = (step_ints.astype(jnp.float32) / 1000.0 + 0.008) / 1.008 * (math.pi / 2)
    signal_level = jnp.cos(angles) ** 2 / base_cos ** 2
    return (jnp.sqrt(signal_level), jnp.sqrt(1.0 - signal_level))

def position_table(first_row, row_count):
    grid_side = SIDE // PATCH
    quarter = D // 4
    omegas = jnp.exp(-math.log(10000.0) * jnp.arange(quarter, dtype=jnp.float32) / quarter)
    token_index = jnp.arange(row_count * grid_side, dtype=jnp.int32)
    row_angle = (first_row + token_index // grid_side).astype(jnp.float32)[:, None] * omegas[None, :]
    col_angle = (token_index % grid_side).astype(jnp.float32)[:, None] * omegas[None, :]
    return jnp.concatenate([jnp.sin(row_angle), jnp.cos(row_angle), jnp.sin(col_angle), jnp.cos(col_angle)], axis=1)

def patchify(flat_pixels, row_count):
    grid_side = SIDE // PATCH
    shaped = flat_pixels.reshape(flat_pixels.shape[0], row_count, PATCH, grid_side, PATCH, CHANNELS)
    return shaped.transpose(0, 1, 3, 2, 4, 5).reshape(flat_pixels.shape[0], row_count * grid_side, PATCH * PATCH * CHANNELS)

def table_starts():
    patch_in = PATCH * PATCH * CHANNELS
    patch_start = CLASSES
    time_start = patch_start + patch_in
    second_start = time_start + FREQ
    final_start = second_start + D
    head_start = final_start + 2 * D
    vector_start = head_start + patch_in
    layer_start = vector_start + 5
    return (patch_start, time_start, second_start, final_start, head_start, vector_start, layer_start)

def attend(triple):
    queries, keys_in, values_in = triple
    scores = low_back(jnp.einsum('qhd,khd->hqk', queries, keys_in, precision=PRECISE) * HEAD_DIM ** (-0.5))
    exponent = jnp.exp(scores - lax.optimization_barrier(jnp.max(scores, axis=-1, keepdims=True)))
    probs_row = exponent / lax.optimization_barrier(jnp.sum(exponent, axis=-1, keepdims=True))
    return low(low_back(jnp.einsum('hqk,khd->qhd', low(probs_row), values_in, precision=PRECISE)))

def group_loss(params, latents, target_noise, timesteps, labels):
    table, weight_in, weight_out, weight_ada = params
    copies = low(table)
    patch_start, time_start, second_start, final_start, head_start, vector_start, layer_start = table_starts()
    images = latents.shape[0]
    grid_side = SIDE // PATCH
    group_width = HEADS_DEV * HEAD_DIM
    patch_in = PATCH * PATCH * CHANNELS
    pixels = patchify(latents, grid_side)
    targets = patchify(target_noise, grid_side)
    keep_coef, drop_coef = noise_levels(timesteps)
    noisy = keep_coef[:, None, None] * pixels + drop_coef[:, None, None] * targets
    vectors = copies[vector_start:vector_start + 5]
    residual = jnp.einsum('btp,pd->btd', noisy, copies[patch_start:patch_start + patch_in], precision=PRECISE) + vectors[0] + position_table(0, grid_side)[None]
    onehot = (labels[:, None] == jnp.arange(CLASSES, dtype=jnp.int32)[None, :]).astype(jnp.float32)
    hidden = jax.nn.silu(dense(time_features(timesteps), copies[time_start:time_start + FREQ]) + vectors[1])
    signal = jax.nn.silu(dense(hidden, copies[second_start:second_start + D]) + vectors[2] + dense(onehot, copies[0:CLASSES]))
    signal_low = low(signal)
    head_shape = (images, TOKENS_IMG, HEADS, HEAD_DIM)
    for layer_idx in range(LAYERS):
        bias_start = layer_start + layer_idx * LAYER_ROWS
        bias_rows = copies[bias_start:bias_start + LAYER_ROWS]
        modulation = low_back(dense(signal_low, low(weight_ada[layer_idx]))) + bias_rows[0:6].reshape(6 * D)
        pieces = [modulation[:, piece_idx * D:(piece_idx + 1) * D] for piece_idx in range(6)]
        group_in = low(weight_in[layer_idx])
        group_out = low(weight_out[layer_idx])
        w_query = group_in[:, :, 0:group_width].reshape(D, D)
        w_key = group_in[:, :, group_width:2 * group_width].reshape(D, D)
        w_value = group_in[:, :, 2 * group_width:3 * group_width].reshape(D, D)
        w_up = group_in[:, :, 3 * group_width:].reshape(D, FF)
        w_attn = group_out[:, 0:group_width, :].reshape(D, D)
        w_down = group_out[:, group_width:, :].reshape(FF, D)
        normed = low(modulate(residual, pieces[0], pieces[1]))
        queries = low(low_back(jnp.einsum('btd,de->bte', normed, w_query, precision=PRECISE)) + bias_rows[8])
        keys_low = low(low_back(jnp.einsum('btd,de->bte', normed, w_key, precision=PRECISE)))
        values_low = low(low_back(jnp.einsum('btd,de->bte', normed, w_value, precision=PRECISE)) + bias_rows[9])
        mixed_out = lax.map(jax.checkpoint(attend), (queries.reshape(head_shape), keys_low.reshape(head_shape), values_low.reshape(head_shape)))
        mixed_out = mixed_out.reshape(images, TOKENS_IMG, D)
        branch = low_back(jnp.einsum('bte,ed->btd', mixed_out, w_attn, precision=PRECISE)) + bias_rows[6]
        residual = residual + pieces[2][:, None, :] * branch
        normed_m = low(modulate(residual, pieces[3], pieces[4]))
        upper_pre = low_back(jnp.einsum('btd,df->btf', normed_m, w_up, precision=PRECISE)) + bias_rows[10:].reshape(FF)
        act_low = low(jax.nn.gelu(upper_pre, approximate=True))
        down_out = low_back(jnp.einsum('btf,fd->btd', act_low, w_down, precision=PRECISE)) + bias_rows[7]
        residual = residual + pieces[5][:, None, :] * down_out
    final_shift = dense(signal, copies[final_start:final_start + D]) + vectors[3]
    final_scale = dense(signal, copies[final_start + D:final_start + 2 * D]) + vectors[4]
    final_in = modulate(residual, final_shift, final_scale)
    predicted = jnp.einsum('btd,pd->btp', final_in, copies[head_start:head_start + patch_in], precision=PRECISE)
    error_all = predicted - targets
    return jnp.sum(error_all * error_all) / (IMAGES * TOKENS_IMG * PATCH_IN)

def adam_update(weight, first, second, grad, factor, first_fix, second_fix):
    clipped = grad * factor
    first_new = BETA_ONE * first + (1.0 - BETA_ONE) * clipped
    second_new = BETA_TWO * second + (1.0 - BETA_TWO) * clipped * clipped
    step_size = first_new / first_fix / (jnp.sqrt(second_new / second_fix) + ADAM_EPS)
    change = -LEARN_RATE * (step_size + DECAY * weight)
    master = weight + change
    return (master, first_new, second_new, master.astype(jnp.bfloat16), change)

def reference(latents, target_noise, timesteps, labels, step_count, embed_table, layer_in, layer_out, layer_ada, embed_first, embed_second, input_first, input_second, output_first, output_second, mod_first, mod_second):
    params = (embed_table, layer_in, layer_out, layer_ada)
    group_size = math.gcd(IMAGES, 16)
    group_count = IMAGES // group_size

    def one_group(carry, group_idx):
        row_start = group_idx * group_size

        def pick(array):
            return lax.dynamic_slice_in_dim(array, row_start, group_size, 0)

        def loss_of(weights):
            return group_loss(weights, pick(latents), pick(target_noise), pick(timesteps), pick(labels))
        loss_part, pullback = jax.vjp(loss_of, params)
        gradients = pullback(jnp.ones((), jnp.float32))[0]
        return ((carry[0] + loss_part, jax.tree.map(jnp.add, carry[1], gradients)), None)
    zeros = jax.tree.map(jnp.zeros_like, params)
    (loss_value, gradients), _ = lax.scan(one_group, (jnp.zeros((), jnp.float32), zeros), jnp.arange(group_count, dtype=jnp.int32))
    squares = jnp.sum(gradients[0] * gradients[0]) + jnp.sum(gradients[1] * gradients[1]) + jnp.sum(gradients[2] * gradients[2]) + jnp.sum(gradients[3] * gradients[3])
    grad_norm = jnp.sqrt(squares)
    factor = jnp.minimum(1.0, CLIP_NORM / grad_norm)
    first_fix = 1.0 - BETA_ONE ** step_count.astype(jnp.float32)
    second_fix = 1.0 - BETA_TWO ** step_count.astype(jnp.float32)
    embed_out = adam_update(embed_table, embed_first, embed_second, gradients[0], factor, first_fix, second_fix)
    input_out = adam_update(layer_in, input_first, input_second, gradients[1], factor, first_fix, second_fix)
    output_out = adam_update(layer_out, output_first, output_second, gradients[2], factor, first_fix, second_fix)
    mod_out = adam_update(layer_ada, mod_first, mod_second, gradients[3], factor, first_fix, second_fix)
    return (loss_value, grad_norm, embed_out[4], embed_out[1], embed_out[2], input_out[0], input_out[1], input_out[2], input_out[3], output_out[0], output_out[1], output_out[2], output_out[3], mod_out[0], mod_out[1], mod_out[2], mod_out[3])
```

```python
import functools
import math

import jax
import jax.numpy as jnp
from jax import lax
from jax.experimental import pallas as pl
from jax.experimental.pallas import tpu as pltpu
from jax.sharding import PartitionSpec as P

D = 768
HEADS = 12
HEAD_DIM = 64
FF = 3072
CLASSES = 1001
FREQ = 256
CHANNELS = 4
PATCH = 2
SIDE = 32
LAYERS = 3


EPS_NORM = 1e-06
LEARN_RATE = 0.01
DECAY = 0.01
BETA_ONE = 0.5
BETA_TWO = 0.5
ADAM_EPS = 1e-08
CLIP_NORM = 0.25
PRECISE = lax.Precision.HIGHEST


def dense(left_op, right_op):
    return jnp.dot(left_op, right_op, precision=PRECISE, preferred_element_type=jnp.float32)


def layer_norm(values):
    center = values - jnp.mean(values, axis=-1, keepdims=True)
    return center * lax.rsqrt(jnp.mean(center * center, axis=-1, keepdims=True) + EPS_NORM)


def modulate(values, shift_vec, scale_vec):
    return layer_norm(values) * (1.0 + scale_vec[:, None, :]) + shift_vec[:, None, :]


def gelu_tanh(values):
    return jax.nn.gelu(values, approximate=True)


def silu_slope(values):
    sigmoid_val = jax.nn.sigmoid(values)
    return sigmoid_val * (1.0 + values * (1.0 - sigmoid_val))


def time_features(step_ints):
    half_width = FREQ // 2
    frequency = jnp.exp(-math.log(10000.0) * jnp.arange(half_width, dtype=jnp.float32) / half_width)
    angles = step_ints.astype(jnp.float32)[:, None] * frequency[None, :]
    return jnp.concatenate([jnp.cos(angles), jnp.sin(angles)], axis=1)


def noise_levels(step_ints):
    base_cos = math.cos(0.008 / 1.008 * math.pi / 2)
    angles = (step_ints.astype(jnp.float32) / 1000.0 + 0.008) / 1.008 * (math.pi / 2)
    signal_level = jnp.cos(angles) ** 2 / base_cos**2
    return (jnp.sqrt(signal_level), jnp.sqrt(1.0 - signal_level))


def position_table(first_row, row_count):
    grid_side = SIDE // PATCH
    quarter = D // 4
    omegas = jnp.exp(-math.log(10000.0) * jnp.arange(quarter, dtype=jnp.float32) / quarter)
    token_index = jnp.arange(row_count * grid_side, dtype=jnp.int32)
    row_angle = (first_row + token_index // grid_side).astype(jnp.float32)[:, None] * omegas[
        None, :
    ]
    col_angle = (token_index % grid_side).astype(jnp.float32)[:, None] * omegas[None, :]
    return jnp.concatenate(
        [jnp.sin(row_angle), jnp.cos(row_angle), jnp.sin(col_angle), jnp.cos(col_angle)], axis=1
    )


def patchify(flat_pixels, row_count):
    grid_side = SIDE // PATCH
    shaped = flat_pixels.reshape(flat_pixels.shape[0], row_count, PATCH, grid_side, PATCH, CHANNELS)
    return shaped.transpose(0, 1, 3, 2, 4, 5).reshape(
        flat_pixels.shape[0], row_count * grid_side, PATCH * PATCH * CHANNELS
    )


def table_starts():
    patch_in = PATCH * PATCH * CHANNELS
    patch_start = CLASSES
    time_start = patch_start + patch_in
    second_start = time_start + FREQ
    final_start = second_start + D
    head_start = final_start + 2 * D
    vector_start = head_start + patch_in
    layer_start = vector_start + 5
    return (
        patch_start,
        time_start,
        second_start,
        final_start,
        head_start,
        vector_start,
        layer_start,
    )


def group_place(group):
    if group == "all":
        width = lax.axis_size("tensor")
        place = lax.axis_index("dp") * width + lax.axis_index("tensor")
        size = lax.axis_size("dp") * width
        return place, size, lambda at: {"dp": at // width, "tensor": lax.rem(at, width)}
    return lax.axis_index(group), lax.axis_size(group), lambda at: {group: at}


def exchange_kernel(group, spread, source, target, send_sems, recv_sems, local_sem):
    place, size, coords = group_place(group)
    barrier = pltpu.get_barrier_semaphore()

    def greet(step, carry):
        peer = coords(lax.rem(place + step, size))
        pl.semaphore_signal(barrier, inc=1, device_id=peer, device_id_type=pl.DeviceIdType.MESH)
        return carry

    def copy_to(step):
        there = lax.rem(place + step, size)
        return pltpu.make_async_remote_copy(
            src_ref=source.at[there] if spread else source,
            dst_ref=target.at[place],
            send_sem=send_sems.at[step],
            recv_sem=recv_sems.at[step],
            device_id=coords(there),
            device_id_type=pl.DeviceIdType.MESH,
        )

    def begin(step, carry):
        copy_to(step).start()
        return carry

    def finish(step, carry):
        copy_to(step).wait()
        return carry

    lax.fori_loop(1, size, greet, 0)
    mine = pltpu.make_async_copy(
        source.at[place] if spread else source, target.at[place], local_sem
    )
    mine.start()
    pl.semaphore_wait(barrier, size - 1)
    lax.fori_loop(1, size, begin, 0)
    mine.wait()
    lax.fori_loop(1, size, finish, 0)


def exchange(values, group, spread, call_id):
    if group == "all":
        size = lax.axis_size("dp") * lax.axis_size("tensor")
    else:
        size = lax.axis_size(group)
    block = values.shape[1:] if spread else values.shape
    return pl.pallas_call(
        functools.partial(exchange_kernel, group, spread),
        out_shape=jax.ShapeDtypeStruct((size,) + block, values.dtype),
        in_specs=[pl.BlockSpec(memory_space=pltpu.VMEM)],
        out_specs=pl.BlockSpec(memory_space=pltpu.VMEM),
        scratch_shapes=[
            pltpu.SemaphoreType.DMA((size,)),
            pltpu.SemaphoreType.DMA((size,)),
            pltpu.SemaphoreType.DMA,
        ],
        compiler_params=pltpu.CompilerParams(
            collective_id=call_id, has_side_effects=True, vmem_limit_bytes=32 * 2**20
        ),
        name="exchange_" + group,
    )(values)


def gather_tokens(values):
    return lax.all_gather(values, "tensor", axis=1, tiled=True)


def sum_tokens(values):
    return lax.psum_scatter(
        values.astype(jnp.bfloat16), "tensor", scatter_dimension=1, tiled=True
    ).astype(jnp.float32)


def adam_update(weight, first, second, grad, factor, first_fix, second_fix):
    clipped = grad * factor
    first_new = BETA_ONE * first + (1.0 - BETA_ONE) * clipped
    second_new = BETA_TWO * second + (1.0 - BETA_TWO) * clipped * clipped
    step_size = first_new / first_fix / (jnp.sqrt(second_new / second_fix) + ADAM_EPS)
    change = -LEARN_RATE * (step_size + DECAY * weight)
    master = weight + change
    return (master, first_new, second_new, master.astype(jnp.bfloat16), change)


def local(
    latents,
    target_noise,
    timesteps,
    labels,
    step_count,
    embed_table,
    layer_in,
    layer_out,
    layer_ada,
    embed_first,
    embed_second,
    input_first,
    input_second,
    output_first,
    output_second,
    mod_first,
    mod_second,
):
    tensor_size = lax.axis_size("tensor")
    tensor_rank = lax.axis_index("tensor")
    images = latents.shape[0]
    grid_side = SIDE // PATCH
    local_rows = grid_side // tensor_size
    tokens_all = grid_side * grid_side
    heads_local = HEADS // tensor_size
    group_width = heads_local * HEAD_DIM
    unit_count = FF // tensor_size
    patch_in = PATCH * PATCH * CHANNELS
    count_all = images * lax.axis_size("dp") * tokens_all * patch_in
    scale_dot = HEAD_DIM ** (-0.5)
    patch_start, time_start, second_start, final_start, head_start, vector_start, layer_start = (
        table_starts()
    )
    layer_rows = 10 + FF // D
    head_shape = (images, tokens_all, heads_local, HEAD_DIM)
    flat_shape = (images, tokens_all, group_width)
    dp_rank = lax.axis_index("dp")
    dp_size = lax.axis_size("dp")
    place_count = dp_size * tensor_size
    images_all = images * dp_size
    table_cols = embed_table.T.astype(jnp.bfloat16).astype(jnp.float32)
    cols = table_cols.shape[0]
    mod_rows = layer_ada.shape[1]
    mod_cols = layer_ada.shape[2]
    mod_low = layer_ada.astype(jnp.bfloat16)

    def col_block(row_start, row_count):
        return table_cols[:, row_start : row_start + row_count]

    vector_count = 5 + LAYERS * layer_rows
    small_count = 2 * patch_in + vector_count
    lanes = -(-(small_count + 2 * images) // 128) * 128
    scalar_lanes = jnp.concatenate([timesteps, labels]).astype(jnp.float32)
    small_send = jnp.concatenate(
        [
            col_block(patch_start, patch_in),
            col_block(head_start, patch_in + vector_count),
            jnp.broadcast_to(scalar_lanes[None, :], (cols, 2 * images)),
            jnp.zeros((cols, lanes - small_count - 2 * images), jnp.float32),
        ],
        axis=1,
    )
    small_all = exchange(small_send, "all", False, 1)
    small_rows = small_all.reshape(D, lanes).T
    patch_w = small_rows[0:patch_in]
    head_w = small_rows[patch_in : 2 * patch_in]
    vectors = small_rows[2 * patch_in : 2 * patch_in + 5]
    bias_all = small_rows[2 * patch_in + 5 : small_count]
    scalars_all = small_all[::tensor_size, 0, small_count : small_count + 2 * images].astype(
        jnp.int32
    )
    timesteps_all = scalars_all[:, :images].reshape(images_all)
    labels_all = scalars_all[:, images:].reshape(images_all)
    time_feats = time_features(timesteps_all)
    onehot = (labels_all[:, None] == jnp.arange(CLASSES, dtype=jnp.int32)[None, :]).astype(
        jnp.float32
    )
    pre_time = dense(col_block(time_start, FREQ), time_feats.T) + col_block(vector_start + 1, 1)
    hidden = exchange(jax.nn.silu(pre_time), "all", False, 2).reshape(D, images_all)
    second_cols = col_block(second_start, D)
    shift_cols = col_block(final_start, D)
    scale_cols = col_block(final_start + D, D)
    pre_signal = (
        dense(second_cols, hidden)
        + col_block(vector_start + 2, 1)
        + dense(col_block(0, CLASSES), onehot.T)
    )
    signal = exchange(jax.nn.silu(pre_signal), "all", False, 3).reshape(D, images_all)
    final_send = jnp.concatenate(
        [
            dense(shift_cols, signal) + col_block(vector_start + 3, 1),
            dense(scale_cols, signal) + col_block(vector_start + 4, 1),
        ],
        axis=0,
    )
    final_all = exchange(final_send, "all", False, 4).reshape(place_count, 2, cols, images_all)
    final_own = lax.dynamic_slice_in_dim(final_all, dp_rank * images, images, 3)
    final_own = final_own.transpose(1, 3, 0, 2).reshape(2, images, D)
    final_shift, final_scale = final_own[0], final_own[1]
    signal_low = lax.dynamic_slice_in_dim(
        signal.astype(jnp.bfloat16), dp_rank * mod_rows, mod_rows, 0
    )
    mod_part = jnp.einsum("db,lde->ble", signal_low, mod_low, preferred_element_type=jnp.float32)
    mod_part = mod_part.reshape(dp_size, images * LAYERS, mod_cols)
    mod_local = jnp.sum(exchange(mod_part, "dp", True, 5), axis=0)
    mod_full = exchange(mod_local, "tensor", False, 6)
    mod_full = mod_full.reshape(tensor_size, images, LAYERS, mod_cols)
    mod_full = mod_full.transpose(2, 1, 0, 3).reshape(LAYERS, images, tensor_size * mod_cols)
    pixels = patchify(latents, local_rows)
    targets = patchify(target_noise, local_rows)
    keep_coef, drop_coef = noise_levels(timesteps)
    noisy = keep_coef[:, None, None] * pixels + drop_coef[:, None, None] * targets
    residual = (
        jnp.einsum("btp,pd->btd", noisy, patch_w, precision=PRECISE)
        + vectors[0]
        + position_table(tensor_rank * local_rows, local_rows)[None]
    )
    saved_acts = []
    for layer_idx in range(LAYERS):
        weight_in, weight_out = (
            lax.all_gather(
                layer_in[layer_idx]
                .astype(jnp.bfloat16)
                .reshape(layer_in.shape[1], layer_in.shape[3]),
                "dp",
                axis=0,
                tiled=True,
            ),
            lax.all_gather(
                layer_out[layer_idx].astype(jnp.bfloat16).reshape(layer_out.shape[2], D),
                "dp",
                axis=0,
                tiled=True,
            ),
        )
        bias_rows = bias_all[layer_idx * layer_rows : (layer_idx + 1) * layer_rows]
        up_all = bias_rows[10:].reshape(FF)
        ada_bias = bias_rows[0:6].reshape(6 * D)
        out_bias = bias_rows[6]
        down_bias = bias_rows[7]
        query_bias = lax.dynamic_slice_in_dim(bias_rows[8], tensor_rank * group_width, group_width)
        value_bias = lax.dynamic_slice_in_dim(bias_rows[9], tensor_rank * group_width, group_width)
        up_bias = lax.dynamic_slice_in_dim(up_all, tensor_rank * unit_count, unit_count)
        modulation = mod_full[layer_idx] + ada_bias
        shift_a, scale_a, gate_a, shift_m, scale_m, gate_m = [
            modulation[:, piece_idx * D : (piece_idx + 1) * D] for piece_idx in range(6)
        ]
        w_qkv = weight_in[:, : 3 * group_width]
        w_up = weight_in[:, 3 * group_width :]
        w_attn = weight_out[:group_width]
        w_down = weight_out[group_width:]
        normed_a, norm_pull_a = jax.vjp(modulate, residual, shift_a, scale_a)
        rows_a = gather_tokens(normed_a.astype(jnp.bfloat16))
        projected = jnp.einsum("btd,de->bte", rows_a, w_qkv, preferred_element_type=jnp.float32)
        queries = (
            (projected[..., :group_width] + query_bias).astype(jnp.bfloat16).reshape(head_shape)
        )
        keys_low = (
            projected[..., group_width : 2 * group_width].astype(jnp.bfloat16).reshape(head_shape)
        )
        values_low = (
            (projected[..., 2 * group_width :] + value_bias)
            .astype(jnp.bfloat16)
            .reshape(head_shape)
        )
        scores = (
            jnp.einsum("bqhd,bkhd->bhqk", queries, keys_low, preferred_element_type=jnp.float32)
            * scale_dot
        )
        row_max = jnp.max(scores, axis=-1, keepdims=True)
        exponent = jnp.exp(scores - row_max)
        row_total = jnp.sum(exponent, axis=-1, keepdims=True)
        log_total = row_max + jnp.log(row_total)
        probs_low = (exponent / row_total).astype(jnp.bfloat16)
        mixed_out = (
            jnp.einsum("bhqk,bkhd->bqhd", probs_low, values_low, preferred_element_type=jnp.float32)
            .astype(jnp.bfloat16)
            .reshape(flat_shape)
        )
        branch = (
            sum_tokens(
                jnp.einsum("bte,ed->btd", mixed_out, w_attn, preferred_element_type=jnp.float32)
            )
            + out_bias
        )
        residual_mid = residual + gate_a[:, None, :] * branch
        normed_m, norm_pull_m = jax.vjp(modulate, residual_mid, shift_m, scale_m)
        rows_m = gather_tokens(normed_m.astype(jnp.bfloat16))
        upper_pre = (
            jnp.einsum("btd,df->btf", rows_m, w_up, preferred_element_type=jnp.float32) + up_bias
        )
        activated, gelu_pull = jax.vjp(gelu_tanh, upper_pre)
        act_low = activated.astype(jnp.bfloat16)
        down_out = (
            sum_tokens(
                jnp.einsum("btf,fd->btd", act_low, w_down, preferred_element_type=jnp.float32)
            )
            + down_bias
        )
        residual = residual_mid + gate_m[:, None, :] * down_out
        saved_acts.append(
            (
                norm_pull_a,
                rows_a,
                queries,
                keys_low,
                values_low,
                log_total,
                mixed_out,
                branch,
                gate_a,
                norm_pull_m,
                rows_m,
                gelu_pull,
                act_low,
                down_out,
                gate_m,
                w_qkv,
                w_up,
                w_attn,
                w_down,
            )
        )
    final_in, final_norm_pull = jax.vjp(modulate, residual, final_shift, final_scale)
    predicted = jnp.einsum("btd,pd->btp", final_in, head_w, precision=PRECISE)
    error_all = predicted - targets
    loss_part = jnp.sum(error_all * error_all) / count_all
    d_pred = 2.0 * error_all / count_all
    d_head = jnp.einsum("btp,btd->pd", d_pred, final_in, precision=PRECISE)
    d_final = jnp.einsum("btp,pd->btd", d_pred, head_w, precision=PRECISE)
    d_residual, d_final_shift, d_final_scale = final_norm_pull(d_final)
    grads_in = []
    grads_out = []
    mod_parts = []
    bias_blocks = []
    for layer_idx in reversed(range(LAYERS)):
        (
            norm_pull_a,
            rows_a,
            queries,
            keys_low,
            values_low,
            log_total,
            mixed_out,
            branch,
            gate_a,
            norm_pull_m,
            rows_m,
            gelu_pull,
            act_low,
            down_out,
            gate_m,
            w_qkv,
            w_up,
            w_attn,
            w_down,
        ) = saved_acts[layer_idx]
        d_gate_m = jnp.sum(d_residual * down_out, axis=1)
        d_down = d_residual * gate_m[:, None, :]
        d_down_bias = jnp.sum(d_down, axis=(0, 1))
        d_down_rows = gather_tokens(d_down.astype(jnp.bfloat16))
        d_w_down = jnp.einsum(
            "btf,btd->fd", act_low, d_down_rows, preferred_element_type=jnp.float32
        )
        d_act = jnp.einsum("btd,fd->btf", d_down_rows, w_down, preferred_element_type=jnp.float32)
        d_upper = gelu_pull(d_act)[0]
        d_up_bias = jnp.sum(d_upper, axis=(0, 1))
        d_upper_low = d_upper.astype(jnp.bfloat16)
        d_w_up = jnp.einsum("btd,btf->df", rows_m, d_upper_low, preferred_element_type=jnp.float32)
        d_normed_m = sum_tokens(
            jnp.einsum("btf,df->btd", d_upper_low, w_up, preferred_element_type=jnp.float32)
        )
        d_mid, d_shift_m, d_scale_m = norm_pull_m(d_normed_m)
        d_residual = d_residual + d_mid
        d_gate_a = jnp.sum(d_residual * branch, axis=1)
        d_branch = d_residual * gate_a[:, None, :]
        d_out_bias = jnp.sum(d_branch, axis=(0, 1))
        d_branch_rows = gather_tokens(d_branch.astype(jnp.bfloat16))
        d_w_attn = jnp.einsum(
            "bte,btd->ed", mixed_out, d_branch_rows, preferred_element_type=jnp.float32
        )
        d_mixed = (
            jnp.einsum("btd,ed->bte", d_branch_rows, w_attn, preferred_element_type=jnp.float32)
            .astype(jnp.bfloat16)
            .reshape(head_shape)
        )
        scores = (
            jnp.einsum("bqhd,bkhd->bhqk", queries, keys_low, preferred_element_type=jnp.float32)
            * scale_dot
        )
        probs_row = jnp.exp(scores - log_total)
        d_probs = jnp.einsum(
            "bqhd,bkhd->bhqk", d_mixed, values_low, preferred_element_type=jnp.float32
        )
        d_values = jnp.einsum(
            "bhqk,bqhd->bkhd",
            probs_row.astype(jnp.bfloat16),
            d_mixed,
            preferred_element_type=jnp.float32,
        )
        d_scores = (
            probs_row * (d_probs - jnp.sum(probs_row * d_probs, axis=-1, keepdims=True))
        ).astype(jnp.bfloat16)
        d_queries = (
            jnp.einsum("bhqk,bkhd->bqhd", d_scores, keys_low, preferred_element_type=jnp.float32)
            * scale_dot
        )
        d_keys = (
            jnp.einsum("bhqk,bqhd->bkhd", d_scores, queries, preferred_element_type=jnp.float32)
            * scale_dot
        )
        d_query_bias = jnp.sum(d_queries.reshape(flat_shape), axis=(0, 1))
        d_value_bias = jnp.sum(d_values.reshape(flat_shape), axis=(0, 1))
        d_projected = jnp.concatenate(
            [
                d_queries.reshape(flat_shape),
                d_keys.reshape(flat_shape),
                d_values.reshape(flat_shape),
            ],
            axis=2,
        ).astype(jnp.bfloat16)
        d_w_qkv = jnp.einsum("btd,bte->de", rows_a, d_projected, preferred_element_type=jnp.float32)
        d_normed_a = sum_tokens(
            jnp.einsum("bte,de->btd", d_projected, w_qkv, preferred_element_type=jnp.float32)
        )
        d_before, d_shift_a, d_scale_a = norm_pull_a(d_normed_a)
        d_residual = d_residual + d_before
        d_modulation = jnp.concatenate(
            [d_shift_a, d_scale_a, d_gate_a, d_shift_m, d_scale_m, d_gate_m], axis=1
        )
        mod_parts.insert(0, d_modulation)
        grad_in, grad_out = (
            lax.psum_scatter(
                jnp.concatenate([d_w_qkv, d_w_up], axis=1).astype(jnp.bfloat16),
                "dp",
                scatter_dimension=0,
                tiled=True,
            ).astype(jnp.float32),
            lax.psum_scatter(
                jnp.concatenate([d_w_attn, d_w_down], axis=0).astype(jnp.bfloat16),
                "dp",
                scatter_dimension=0,
                tiled=True,
            ).astype(jnp.float32),
        )
        grads_in.insert(0, grad_in)
        grads_out.insert(0, grad_out)
        query_row = lax.dynamic_update_slice_in_dim(
            jnp.zeros((D,), jnp.float32), d_query_bias, tensor_rank * group_width, 0
        )
        value_row = lax.dynamic_update_slice_in_dim(
            jnp.zeros((D,), jnp.float32), d_value_bias, tensor_rank * group_width, 0
        )
        up_rows = lax.dynamic_update_slice_in_dim(
            jnp.zeros((FF,), jnp.float32), d_up_bias, tensor_rank * unit_count, 0
        ).reshape(FF // D, D)
        bias_blocks.insert(
            0,
            jnp.concatenate(
                [
                    jnp.sum(d_modulation, axis=0).reshape(6, D),
                    d_out_bias[None],
                    d_down_bias[None],
                    query_row[None],
                    value_row[None],
                    up_rows,
                ],
                axis=0,
            ),
        )
    d_patch_w = jnp.einsum("btp,btd->pd", noisy, d_residual, precision=PRECISE)
    d_patch_b = jnp.sum(d_residual, axis=(0, 1))
    row_parts = jnp.concatenate(
        [d_patch_w, d_head, d_patch_b[None]] + bias_blocks + [d_final_shift, d_final_scale],
        axis=0,
    )
    row_count = row_parts.shape[0]
    row_lanes = -(-row_count // 128) * 128
    row_parts = jnp.pad(row_parts, ((0, row_lanes - row_count), (0, 0)))
    row_all = exchange(row_parts.T.reshape(place_count, cols, row_lanes), "all", True, 7)
    row_sums = jnp.sum(row_all, axis=0)
    final_at = row_count - 2 * images
    final_sums = jnp.sum(
        row_all[:, :, final_at:row_count].reshape(dp_size, tensor_size, cols, 2, images), axis=1
    )
    final_sums = final_sums.transpose(2, 1, 0, 3).reshape(2, cols, images_all)
    d_shift_cols, d_scale_cols = final_sums[0], final_sums[1]
    mod_parts = jnp.stack(mod_parts).reshape(LAYERS * images, tensor_size, mod_cols)
    d_mod_own = jnp.sum(exchange(mod_parts.transpose(1, 0, 2), "tensor", True, 8), axis=0)
    d_mod_low = exchange(d_mod_own.astype(jnp.bfloat16), "dp", False, 9)
    d_mod_low = d_mod_low.reshape(dp_size, LAYERS, images, mod_cols)
    d_mod_low = d_mod_low.transpose(1, 0, 2, 3).reshape(LAYERS, images_all, mod_cols)
    mod_grad = jnp.einsum(
        "db,lbe->lde", signal_low, d_mod_low, preferred_element_type=jnp.float32
    )
    d_signal_rows = jnp.einsum(
        "lbe,lde->db", d_mod_low, mod_low, preferred_element_type=jnp.float32
    )
    d_signal_part = dense(shift_cols.T, d_shift_cols) + dense(scale_cols.T, d_scale_cols)
    d_signal_part = d_signal_part + lax.dynamic_update_slice_in_dim(
        jnp.zeros((D, images_all), jnp.float32), d_signal_rows, dp_rank * mod_rows, 0
    )
    d_signal_cols = jnp.sum(
        exchange(d_signal_part.reshape(place_count, cols, images_all), "all", True, 10), axis=0
    )
    d_pre_signal = d_signal_cols * silu_slope(pre_signal)
    d_hidden_part = dense(second_cols.T, d_pre_signal)
    d_hidden_cols = jnp.sum(
        exchange(d_hidden_part.reshape(place_count, cols, images_all), "all", True, 11), axis=0
    )
    d_hidden = d_hidden_cols * silu_slope(pre_time)
    table_grad = jnp.concatenate(
        [
            dense(d_pre_signal, onehot),
            row_sums[:, 0:patch_in],
            dense(d_hidden, time_feats),
            dense(d_pre_signal, hidden.T),
            dense(d_shift_cols, signal.T),
            dense(d_scale_cols, signal.T),
            row_sums[:, patch_in : 2 * patch_in + 1],
            jnp.sum(d_hidden, axis=1, keepdims=True),
            jnp.sum(d_pre_signal, axis=1, keepdims=True),
            jnp.sum(d_shift_cols, axis=1, keepdims=True),
            jnp.sum(d_scale_cols, axis=1, keepdims=True),
            row_sums[:, 2 * patch_in + 1 : final_at],
        ],
        axis=1,
    )
    input_grad = jnp.stack(grads_in).reshape(layer_in.shape)
    output_grad = jnp.stack(grads_out).reshape(layer_out.shape)
    local_squares = (
        jnp.sum(table_grad * table_grad)
        + jnp.sum(input_grad * input_grad)
        + jnp.sum(output_grad * output_grad)
        + jnp.sum(mod_grad * mod_grad)
    )
    scalar_send = jnp.where(
        lax.broadcasted_iota(jnp.int32, (8, 128), 1) == 0, loss_part, local_squares
    )
    scalar_sums = jnp.sum(exchange(scalar_send, "all", False, 12)[:, 0, 0:2], axis=0)
    loss_value = scalar_sums[0]
    square_total = scalar_sums[1]
    grad_norm = jnp.sqrt(square_total)
    factor = jnp.minimum(1.0, CLIP_NORM / grad_norm)
    first_fix = 1.0 - BETA_ONE ** step_count.astype(jnp.float32)
    second_fix = 1.0 - BETA_TWO ** step_count.astype(jnp.float32)
    embed_out = adam_update(
        embed_table.T, embed_first.T, embed_second.T, table_grad, factor, first_fix, second_fix
    )
    input_out = adam_update(
        layer_in, input_first, input_second, input_grad, factor, first_fix, second_fix
    )
    output_out = adam_update(
        layer_out, output_first, output_second, output_grad, factor, first_fix, second_fix
    )
    mod_out = adam_update(layer_ada, mod_first, mod_second, mod_grad, factor, first_fix, second_fix)
    return (
        (loss_value, grad_norm, embed_out[4].T, embed_out[1].T, embed_out[2].T)
        + input_out[0:4]
        + output_out[0:4]
        + mod_out[0:4]
    )


def solution(mesh):
    placed = (
        P("dp", "tensor"),
        P("dp", "tensor"),
        P("dp"),
        P("dp"),
        P(),
        P(None, ("dp", "tensor")),
        P(None, "dp", "tensor", None),
        P(None, "tensor", "dp", None),
        P(None, "dp", "tensor"),
        P(None, ("dp", "tensor")),
        P(None, ("dp", "tensor")),
        P(None, "dp", "tensor", None),
        P(None, "dp", "tensor", None),
        P(None, "tensor", "dp", None),
        P(None, "tensor", "dp", None),
        P(None, "dp", "tensor"),
        P(None, "dp", "tensor"),
    )
    return jax.shard_map(
        local,
        mesh=mesh,
        in_specs=placed,
        out_specs=(
            P(),
            P(),
            P(None, ("dp", "tensor")),
            P(None, ("dp", "tensor")),
            P(None, ("dp", "tensor")),
            P(None, "dp", "tensor", None),
            P(None, "dp", "tensor", None),
            P(None, "dp", "tensor", None),
            P(None, "dp", "tensor", None),
            P(None, "tensor", "dp", None),
            P(None, "tensor", "dp", None),
            P(None, "tensor", "dp", None),
            P(None, "tensor", "dp", None),
            P(None, "dp", "tensor"),
            P(None, "dp", "tensor"),
            P(None, "dp", "tensor"),
            P(None, "dp", "tensor"),
        ),
        check_vma=False,
    )
```

```python
import functools
import math

import jax
import jax.numpy as jnp
from jax import lax
from jax.experimental import pallas as pl
from jax.experimental.pallas import tpu as pltpu
from jax.sharding import PartitionSpec as P

D = 768
HEADS = 12
HEAD_DIM = 64
FF = 3072
CLASSES = 1001
FREQ = 256
CHANNELS = 4
PATCH = 2
SIDE = 32
LAYERS = 3


EPS_NORM = 1e-06
LEARN_RATE = 0.01
DECAY = 0.01
BETA_ONE = 0.5
BETA_TWO = 0.5
ADAM_EPS = 1e-08
CLIP_NORM = 0.25
PRECISE = lax.Precision.HIGHEST


def dense(left_op, right_op):
    return jnp.dot(left_op, right_op, precision=PRECISE, preferred_element_type=jnp.float32)


def layer_norm(values):
    center = values - jnp.mean(values, axis=-1, keepdims=True)
    return center * lax.rsqrt(jnp.mean(center * center, axis=-1, keepdims=True) + EPS_NORM)


def modulate(values, shift_vec, scale_vec):
    return layer_norm(values) * (1.0 + scale_vec[:, None, :]) + shift_vec[:, None, :]


def gelu_tanh(values):
    return jax.nn.gelu(values, approximate=True)


def silu_slope(values):
    sigmoid_val = jax.nn.sigmoid(values)
    return sigmoid_val * (1.0 + values * (1.0 - sigmoid_val))


def time_features(step_ints):
    half_width = FREQ // 2
    frequency = jnp.exp(-math.log(10000.0) * jnp.arange(half_width, dtype=jnp.float32) / half_width)
    angles = step_ints.astype(jnp.float32)[:, None] * frequency[None, :]
    return jnp.concatenate([jnp.cos(angles), jnp.sin(angles)], axis=1)


def noise_levels(step_ints):
    base_cos = math.cos(0.008 / 1.008 * math.pi / 2)
    angles = (step_ints.astype(jnp.float32) / 1000.0 + 0.008) / 1.008 * (math.pi / 2)
    signal_level = jnp.cos(angles) ** 2 / base_cos**2
    return (jnp.sqrt(signal_level), jnp.sqrt(1.0 - signal_level))


def position_table(first_row, row_count):
    grid_side = SIDE // PATCH
    quarter = D // 4
    omegas = jnp.exp(-math.log(10000.0) * jnp.arange(quarter, dtype=jnp.float32) / quarter)
    token_index = jnp.arange(row_count * grid_side, dtype=jnp.int32)
    row_angle = (first_row + token_index // grid_side).astype(jnp.float32)[:, None] * omegas[
        None, :
    ]
    col_angle = (token_index % grid_side).astype(jnp.float32)[:, None] * omegas[None, :]
    return jnp.concatenate(
        [jnp.sin(row_angle), jnp.cos(row_angle), jnp.sin(col_angle), jnp.cos(col_angle)], axis=1
    )


def patchify(flat_pixels, row_count):
    grid_side = SIDE // PATCH
    shaped = flat_pixels.reshape(flat_pixels.shape[0], row_count, PATCH, grid_side, PATCH, CHANNELS)
    return shaped.transpose(0, 1, 3, 2, 4, 5).reshape(
        flat_pixels.shape[0], row_count * grid_side, PATCH * PATCH * CHANNELS
    )


def table_starts():
    patch_in = PATCH * PATCH * CHANNELS
    patch_start = CLASSES
    time_start = patch_start + patch_in
    second_start = time_start + FREQ
    final_start = second_start + D
    head_start = final_start + 2 * D
    vector_start = head_start + patch_in
    layer_start = vector_start + 5
    return (
        patch_start,
        time_start,
        second_start,
        final_start,
        head_start,
        vector_start,
        layer_start,
    )


def group_place(group):
    if group == "all":
        width = lax.axis_size("tensor")
        place = lax.axis_index("dp") * width + lax.axis_index("tensor")
        size = lax.axis_size("dp") * width
        return place, size, lambda at: {"dp": at // width, "tensor": lax.rem(at, width)}
    return lax.axis_index(group), lax.axis_size(group), lambda at: {group: at}


def exchange_kernel(group, spread, source, target, send_sems, recv_sems, local_sem):
    place, size, coords = group_place(group)
    barrier = pltpu.get_barrier_semaphore()

    def greet(step, carry):
        peer = coords(lax.rem(place + step, size))
        pl.semaphore_signal(barrier, inc=1, device_id=peer, device_id_type=pl.DeviceIdType.MESH)
        return carry

    def copy_to(step):
        there = lax.rem(place + step, size)
        return pltpu.make_async_remote_copy(
            src_ref=source.at[there] if spread else source,
            dst_ref=target.at[place],
            send_sem=send_sems.at[step],
            recv_sem=recv_sems.at[step],
            device_id=coords(there),
            device_id_type=pl.DeviceIdType.MESH,
        )

    def begin(step, carry):
        copy_to(step).start()
        return carry

    def finish(step, carry):
        copy_to(step).wait()
        return carry

    lax.fori_loop(1, size, greet, 0)
    mine = pltpu.make_async_copy(
        source.at[place] if spread else source, target.at[place], local_sem
    )
    mine.start()
    pl.semaphore_wait(barrier, size - 1)
    lax.fori_loop(1, size, begin, 0)
    mine.wait()
    lax.fori_loop(1, size, finish, 0)


def exchange(values, group, spread, call_id):
    if group == "all":
        size = lax.axis_size("dp") * lax.axis_size("tensor")
    else:
        size = lax.axis_size(group)
    block = values.shape[1:] if spread else values.shape
    return pl.pallas_call(
        functools.partial(exchange_kernel, group, spread),
        out_shape=jax.ShapeDtypeStruct((size,) + block, values.dtype),
        in_specs=[pl.BlockSpec(memory_space=pltpu.VMEM)],
        out_specs=pl.BlockSpec(memory_space=pltpu.VMEM),
        scratch_shapes=[
            pltpu.SemaphoreType.DMA((size,)),
            pltpu.SemaphoreType.DMA((size,)),
            pltpu.SemaphoreType.DMA,
        ],
        compiler_params=pltpu.CompilerParams(
            collective_id=call_id, has_side_effects=True, vmem_limit_bytes=32 * 2**20
        ),
        name="exchange_" + group,
    )(values)


MESH = pl.DeviceIdType.MESH
ACT_VMEM = 60 * 2**20


def dot_nn(left_op, right_op):
    return jnp.dot(left_op, right_op, preferred_element_type=jnp.float32)


def dot_nt(left_op, right_op):
    return lax.dot_general(
        left_op, right_op, (((1,), (1,)), ((), ())), preferred_element_type=jnp.float32
    )


def dot_tn(left_op, right_op):
    return lax.dot_general(
        left_op, right_op, (((0,), (0,)), ((), ())), preferred_element_type=jnp.float32
    )


def norm_parts(values):
    center = values - jnp.mean(values, axis=-1, keepdims=True)
    rstd = lax.rsqrt(jnp.mean(center * center, axis=-1, keepdims=True) + EPS_NORM)
    return center * rstd, rstd


def greet_tensor():
    rank = lax.axis_index("tensor")
    half = lax.axis_size("tensor") // 2
    core_peer = {"tensor": rank + 1 - 2 * lax.rem(rank, 2)}
    chip_peer = {"tensor": lax.rem(rank + half, 2 * half)}
    barrier = pltpu.get_barrier_semaphore()
    for peer in (core_peer, chip_peer):
        pl.semaphore_signal(barrier, inc=1, device_id=peer, device_id_type=MESH)
    pl.semaphore_wait(barrier, 2)


class Spread:
    def __init__(self, rows_ref, send_sems, recv_sems):
        self.rows, self.send, self.recv = rows_ref, send_sems, recv_sems
        self.rank = lax.axis_index("tensor")
        self.own_core = lax.rem(self.rank, 2)
        self.core_peer = self.rank + 1 - 2 * self.own_core
        self.chip_peer = lax.rem(self.rank + 2, 4)
        self.count = rows_ref.shape[1] // 4

    def block(self, image, owner):
        return self.rows.at[image, pl.ds(pl.multiple_of(owner * self.count, 16), self.count), :]

    def copy(self, image, owner, peer, which):
        return pltpu.make_async_remote_copy(
            src_ref=self.block(image, owner),
            dst_ref=self.block(image, owner),
            send_sem=self.send.at[image, which],
            recv_sem=self.recv.at[image, which],
            device_id={"tensor": peer},
            device_id_type=MESH,
        )

    def put(self, image, values):
        self.rows[image, pl.ds(pl.multiple_of(self.rank * self.count, 16), self.count), :] = values
        self.copy(image, self.rank, self.chip_peer, 0).start()
        self.copy(image, self.rank, self.core_peer, 1).start()

    def forward(self, image):
        self.copy(image, self.rank, self.chip_peer, 0).wait_recv()
        self.copy(image, self.chip_peer, self.core_peer, 2).start()

    def wait(self, image):
        self.copy(image, self.rank, self.core_peer, 1).wait_recv()
        self.copy(image, self.chip_peer, self.core_peer, 2).wait_recv()

    def close(self, image):
        self.copy(image, self.rank, self.chip_peer, 0).wait_send()
        self.copy(image, self.rank, self.core_peer, 1).wait_send()
        self.copy(image, self.chip_peer, self.core_peer, 2).wait_send()


class Collect:
    def __init__(self, part, near, far_out, far_in, send_sems, recv_sems):
        self.part, self.near, self.far_out, self.far_in = part, near, far_out, far_in
        self.send, self.recv = send_sems, recv_sems
        self.rank = lax.axis_index("tensor")
        self.own_core = lax.rem(self.rank, 2)
        self.own_chip = self.rank // 2
        self.core_peer = self.rank + 1 - 2 * self.own_core
        self.chip_peer = lax.rem(self.rank + 2, 4)
        self.count = part.shape[1] // 4

    def block(self, image, owner):
        return self.part.at[image, pl.ds(pl.multiple_of(owner * self.count, 16), self.count), :]

    def near_copy(self, image, far):
        chip = 1 - self.own_chip if far else self.own_chip
        return pltpu.make_async_remote_copy(
            src_ref=self.block(image, 2 * chip + 1 - self.own_core),
            dst_ref=self.near.at[image, far],
            send_sem=self.send.at[image, far],
            recv_sem=self.recv.at[image, far],
            device_id={"tensor": self.core_peer},
            device_id_type=MESH,
        )

    def far_copy(self, image):
        return pltpu.make_async_remote_copy(
            src_ref=self.far_out.at[image],
            dst_ref=self.far_in.at[image],
            send_sem=self.send.at[image, 2],
            recv_sem=self.recv.at[image, 2],
            device_id={"tensor": self.chip_peer},
            device_id_type=MESH,
        )

    def put(self, image, values):
        self.part[image] = values.astype(jnp.bfloat16)
        self.near_copy(image, 1).start()
        self.near_copy(image, 0).start()

    def load(self, image, owner):
        at = pl.ds(pl.multiple_of(owner * self.count, 16), self.count)
        return self.part[image, at, :].astype(jnp.float32)

    def forward(self, image):
        self.near_copy(image, 1).wait_recv()
        total = self.load(image, self.chip_peer) + self.near[image, 1].astype(jnp.float32)
        self.far_out[image] = total.astype(jnp.bfloat16)
        self.far_copy(image).start()

    def take(self, image):
        self.near_copy(image, 0).wait_recv()
        total = self.load(image, self.rank) + self.near[image, 0].astype(jnp.float32)
        self.far_copy(image).wait_recv()
        return total + self.far_in[image].astype(jnp.float32)

    def close(self, image):
        self.near_copy(image, 1).wait_send()
        self.near_copy(image, 0).wait_send()
        self.far_copy(image).wait_send()


def collect_scratch(images, tokens):
    count = tokens // 4
    return [
        pltpu.VMEM((images, tokens, D), jnp.bfloat16),
        pltpu.VMEM((images, 2, count, D), jnp.bfloat16),
        pltpu.VMEM((images, count, D), jnp.bfloat16),
        pltpu.VMEM((images, count, D), jnp.bfloat16),
    ]


def each(count, body):
    def step(index, carry):
        body(index)
        return carry

    lax.fori_loop(0, count, step, 0)


def head_slice(matrix, head):
    return matrix[:, head * HEAD_DIM : (head + 1) * HEAD_DIM]


def soft_rows(queries, keys_in):
    scores = dot_nt(queries, keys_in) * (HEAD_DIM ** (-0.5))
    exponent = jnp.exp(scores - jnp.max(scores, axis=-1, keepdims=True))
    return exponent / jnp.sum(exponent, axis=-1, keepdims=True)


def forward_kernel(
    res_ref,
    mod_ref,
    vec_ref,
    qkv_bias_ref,
    up_bias_ref,
    w_qkv_ref,
    w_up_ref,
    w_attn_ref,
    w_down_ref,
    res_out,
    rows_a,
    qkv_out,
    mixed_out,
    branch_out,
    mid_out,
    rows_m,
    upper_out,
    down_out,
    part_a,
    near_a,
    far_out_a,
    far_in_a,
    part_m,
    near_m,
    far_out_m,
    far_in_m,
    sends,
    recvs,
):
    images = res_ref.shape[0]
    group_width = w_attn_ref.shape[0]
    greet_tensor()
    spread_a = Spread(rows_a, sends.at[0], recvs.at[0])
    spread_m = Spread(rows_m, sends.at[1], recvs.at[1])
    collect_a = Collect(part_a, near_a, far_out_a, far_in_a, sends.at[2], recvs.at[2])
    collect_m = Collect(part_m, near_m, far_out_m, far_in_m, sends.at[3], recvs.at[3])

    def mod_row(image, piece):
        return mod_ref[image, pl.ds(piece, 1), :]

    def start_norm(image):
        normed, _ = norm_parts(res_ref[image])
        normed = normed * (1.0 + mod_row(image, 1)) + mod_row(image, 0)
        spread_a.put(image, normed.astype(jnp.bfloat16))

    def attend(image):
        spread_a.wait(image)
        rows = rows_a[image]
        projected = dot_nn(rows, w_qkv_ref[...]) + qkv_bias_ref[...]
        qkv = projected.astype(jnp.bfloat16)
        qkv_out[image] = qkv
        heads = []
        for head in range(group_width // HEAD_DIM):
            probs = soft_rows(
                head_slice(qkv[:, :group_width], head),
                head_slice(qkv[:, group_width : 2 * group_width], head),
            )
            heads.append(
                dot_nn(probs.astype(jnp.bfloat16), head_slice(qkv[:, 2 * group_width :], head))
            )
        mixed = jnp.concatenate(heads, axis=1).astype(jnp.bfloat16)
        mixed_out[image] = mixed
        collect_a.put(image, dot_nn(mixed, w_attn_ref[...]))

    def middle(image):
        branch = collect_a.take(image) + vec_ref[0:1, :]
        branch_out[image] = branch
        mid = res_ref[image] + mod_row(image, 2) * branch
        mid_out[image] = mid
        normed, _ = norm_parts(mid)
        normed = normed * (1.0 + mod_row(image, 4)) + mod_row(image, 3)
        spread_m.put(image, normed.astype(jnp.bfloat16))

    def feed(image):
        spread_m.wait(image)
        upper = dot_nn(rows_m[image], w_up_ref[...]) + up_bias_ref[...]
        upper_out[image] = upper
        collect_m.put(image, dot_nn(gelu_tanh(upper).astype(jnp.bfloat16), w_down_ref[...]))

    def finish(image):
        down = collect_m.take(image) + vec_ref[1:2, :]
        down_out[image] = down
        res_out[image] = mid_out[image] + mod_row(image, 5) * down

    def close(image):
        spread_a.close(image)
        spread_m.close(image)
        collect_a.close(image)
        collect_m.close(image)

    each(images, start_norm)
    each(images, spread_a.forward)
    each(images, attend)
    each(images, collect_a.forward)
    each(images, middle)
    each(images, spread_m.forward)
    each(images, feed)
    each(images, collect_m.forward)
    each(images, finish)
    each(images, close)


def forward_layer(residual, mod_vec, vec_bias, qkv_bias, up_bias, w_qkv, w_up, w_attn, w_down):
    images, count, _ = residual.shape
    tokens = 4 * count
    low, full = jnp.bfloat16, jnp.float32
    shapes = [
        ((images, count, D), full),
        ((images, tokens, D), low),
        ((images, tokens, w_qkv.shape[1]), low),
        ((images, tokens, w_attn.shape[0]), low),
        ((images, count, D), full),
        ((images, count, D), full),
        ((images, tokens, D), low),
        ((images, tokens, w_up.shape[1]), full),
        ((images, count, D), full),
    ]
    return pl.pallas_call(
        forward_kernel,
        out_shape=[jax.ShapeDtypeStruct(*shape) for shape in shapes],
        in_specs=[pl.BlockSpec(memory_space=pltpu.VMEM)] * 9,
        out_specs=[pl.BlockSpec(memory_space=pltpu.VMEM)] * 9,
        scratch_shapes=collect_scratch(images, tokens)
        + collect_scratch(images, tokens)
        + [
            pltpu.SemaphoreType.DMA((4, images, 3)),
            pltpu.SemaphoreType.DMA((4, images, 3)),
        ],
        compiler_params=pltpu.CompilerParams(
            collective_id=20, has_side_effects=True, vmem_limit_bytes=ACT_VMEM
        ),
        cost_estimate=pl.CostEstimate(
            flops=30 * 10**9, bytes_accessed=15 * 2**20, transcendentals=0
        ),
        name="block_forward",
    )(residual, mod_vec, vec_bias, qkv_bias, up_bias, w_qkv, w_up, w_attn, w_down)


def gelu_slope(values):
    root = math.sqrt(2.0 / math.pi)
    square = values * values
    tanh = jnp.tanh(root * (values + 0.044715 * values * square))
    half = 0.5 * (1.0 + tanh)
    slope = half + 0.5 * values * (1.0 - tanh * tanh) * root * (1.0 + 3.0 * 0.044715 * square)
    return values * half, slope


def norm_pull(values, scale_row, d_normed):
    normed, rstd = norm_parts(values)
    d_shift = jnp.sum(d_normed, axis=0, keepdims=True)
    d_scale = jnp.sum(d_normed * normed, axis=0, keepdims=True)
    inner = d_normed * (1.0 + scale_row)
    mean_one = jnp.mean(inner, axis=-1, keepdims=True)
    mean_two = jnp.mean(inner * normed, axis=-1, keepdims=True)
    return (inner - mean_one - normed * mean_two) * rstd, d_shift, d_scale


def backward_kernel(
    d_res_ref,
    mod_ref,
    res_ref,
    rows_a,
    qkv_ref,
    mixed_ref,
    branch_ref,
    mid_ref,
    rows_m,
    upper_ref,
    down_ref,
    w_qkv_ref,
    w_up_ref,
    w_attn_ref,
    w_down_ref,
    d_res_out,
    d_in,
    d_out,
    d_mod,
    d_vec,
    d_qkv_bias,
    d_up_bias,
    d_mid,
    d_rows_m,
    d_rows_a,
    act_low,
    d_upper,
    d_qkv,
    part_a,
    near_a,
    far_out_a,
    far_in_a,
    part_m,
    near_m,
    far_out_m,
    far_in_m,
    sends,
    recvs,
):
    images = res_ref.shape[0]
    tokens = rows_a.shape[1]
    group_width = w_attn_ref.shape[0]
    qkv_width = 3 * group_width
    units = w_up_ref.shape[1]
    greet_tensor()
    spread_m = Spread(d_rows_m, sends.at[0], recvs.at[0])
    spread_a = Spread(d_rows_a, sends.at[1], recvs.at[1])
    collect_m = Collect(part_m, near_m, far_out_m, far_in_m, sends.at[2], recvs.at[2])
    collect_a = Collect(part_a, near_a, far_out_a, far_in_a, sends.at[3], recvs.at[3])
    d_vec[...] = jnp.zeros_like(d_vec)
    d_qkv_bias[...] = jnp.zeros_like(d_qkv_bias)
    d_up_bias[...] = jnp.zeros_like(d_up_bias)

    def mod_row(image, piece):
        return mod_ref[image, pl.ds(piece, 1), :]

    def start_down(image):
        d_res = d_res_ref[image]
        d_mod[image, pl.ds(5, 1), :] = jnp.sum(d_res * down_ref[image], axis=0, keepdims=True)
        d_down = d_res * mod_row(image, 5)
        d_vec[1:2, :] += jnp.sum(d_down, axis=0, keepdims=True)
        spread_m.put(image, d_down.astype(jnp.bfloat16))

    def feed(image):
        spread_m.wait(image)
        d_act = dot_nt(d_rows_m[image], w_down_ref[...])
        act, slope = gelu_slope(upper_ref[image])
        act_low[image] = act.astype(jnp.bfloat16)
        d_up = d_act * slope
        d_up_bias[...] += jnp.sum(d_up, axis=0, keepdims=True)
        d_up_low = d_up.astype(jnp.bfloat16)
        d_upper[image] = d_up_low
        collect_m.put(image, dot_nt(d_up_low, w_up_ref[...]))

    def rows_of(ref, width):
        return ref[...].reshape(images * tokens, width)

    def feed_weights():
        tile = 256

        def step(index, carry):
            at = pl.ds(pl.multiple_of(index * tile, tile), tile)
            grad = dot_tn(
                act_low[:, :, at].reshape(images * tokens, tile), rows_of(d_rows_m, D)
            )
            d_out[pl.ds(pl.multiple_of(group_width + index * tile, 64), tile), :] = grad.astype(
                jnp.bfloat16
            )
            grad = dot_tn(
                rows_m[:, :, at].reshape(images * tokens, tile), rows_of(d_upper, units)
            )
            d_in[pl.ds(pl.multiple_of(index * tile, tile), tile), qkv_width:] = grad.astype(
                jnp.bfloat16
            )
            return carry

        lax.fori_loop(0, units // tile, step, 0)

    def middle(image):
        d_value, d_shift, d_scale = norm_pull(
            mid_ref[image], mod_row(image, 4), collect_m.take(image)
        )
        d_mod[image, pl.ds(3, 1), :] = d_shift
        d_mod[image, pl.ds(4, 1), :] = d_scale
        d_value = d_res_ref[image] + d_value
        d_mid[image] = d_value
        d_mod[image, pl.ds(2, 1), :] = jnp.sum(d_value * branch_ref[image], axis=0, keepdims=True)
        d_branch = d_value * mod_row(image, 2)
        d_vec[0:1, :] += jnp.sum(d_branch, axis=0, keepdims=True)
        spread_a.put(image, d_branch.astype(jnp.bfloat16))

    def attend(image):
        spread_a.wait(image)
        d_mixed = dot_nt(d_rows_a[image], w_attn_ref[...]).astype(jnp.bfloat16)
        qkv = qkv_ref[image]
        d_queries, d_keys, d_values = [], [], []
        scale_dot = HEAD_DIM ** (-0.5)
        for head in range(group_width // HEAD_DIM):
            queries = head_slice(qkv[:, :group_width], head)
            keys_in = head_slice(qkv[:, group_width : 2 * group_width], head)
            values_in = head_slice(qkv[:, 2 * group_width :], head)
            d_head = head_slice(d_mixed, head)
            probs = soft_rows(queries, keys_in)
            d_probs = dot_nt(d_head, values_in)
            d_values.append(dot_tn(probs.astype(jnp.bfloat16), d_head))
            inner = jnp.sum(probs * d_probs, axis=-1, keepdims=True)
            d_scores = (probs * (d_probs - inner)).astype(jnp.bfloat16)
            d_queries.append(dot_nn(d_scores, keys_in) * scale_dot)
            d_keys.append(dot_tn(d_scores, queries) * scale_dot)
        joined = jnp.concatenate(d_queries + d_keys + d_values, axis=1)
        d_qkv_bias[...] += jnp.sum(joined, axis=0, keepdims=True)
        joined = joined.astype(jnp.bfloat16)
        d_qkv[image] = joined
        collect_a.put(image, dot_nt(joined, w_qkv_ref[...]))

    def attend_weights():
        d_out[0:group_width, :] = dot_tn(
            rows_of(mixed_ref, group_width), rows_of(d_rows_a, D)
        ).astype(jnp.bfloat16)
        tile = 256

        def step(index, carry):
            at = pl.ds(pl.multiple_of(index * tile, tile), tile)
            grad = dot_tn(
                rows_a[:, :, at].reshape(images * tokens, tile), rows_of(d_qkv, qkv_width)
            )
            d_in[at, 0:qkv_width] = grad.astype(jnp.bfloat16)
            return carry

        lax.fori_loop(0, D // tile, step, 0)

    def finish(image):
        d_value, d_shift, d_scale = norm_pull(
            res_ref[image], mod_row(image, 1), collect_a.take(image)
        )
        d_mod[image, pl.ds(0, 1), :] = d_shift
        d_mod[image, pl.ds(1, 1), :] = d_scale
        d_res_out[image] = d_mid[image] + d_value

    def close(image):
        spread_a.close(image)
        spread_m.close(image)
        collect_a.close(image)
        collect_m.close(image)

    each(images, start_down)
    each(images, spread_m.forward)
    each(images, feed)
    each(images, collect_m.forward)
    feed_weights()
    each(images, middle)
    each(images, spread_a.forward)
    each(images, attend)
    each(images, collect_a.forward)
    attend_weights()
    each(images, finish)
    each(images, close)


def backward_layer(d_residual, mod_vec, saved, weights):
    images, count, _ = d_residual.shape
    tokens = 4 * count
    low, full = jnp.bfloat16, jnp.float32
    w_qkv, w_up, w_attn, w_down = weights
    group_width, units = w_attn.shape[0], w_up.shape[1]
    shapes = [
        ((images, count, D), full),
        ((D, 3 * group_width + units), low),
        ((group_width + units, D), low),
        ((images, 6, D), full),
        ((2, D), full),
        ((1, 3 * group_width), full),
        ((1, units), full),
    ]
    return pl.pallas_call(
        backward_kernel,
        out_shape=[jax.ShapeDtypeStruct(*shape) for shape in shapes],
        in_specs=[pl.BlockSpec(memory_space=pltpu.VMEM)] * 15,
        out_specs=[pl.BlockSpec(memory_space=pltpu.VMEM)] * 7,
        scratch_shapes=[
            pltpu.VMEM((images, count, D), full),
            pltpu.VMEM((images, tokens, D), low),
            pltpu.VMEM((images, tokens, D), low),
            pltpu.VMEM((images, tokens, units), low),
            pltpu.VMEM((images, tokens, units), low),
            pltpu.VMEM((images, tokens, 3 * group_width), low),
        ]
        + collect_scratch(images, tokens)
        + collect_scratch(images, tokens)
        + [
            pltpu.SemaphoreType.DMA((4, images, 3)),
            pltpu.SemaphoreType.DMA((4, images, 3)),
        ],
        compiler_params=pltpu.CompilerParams(
            collective_id=21, has_side_effects=True, vmem_limit_bytes=ACT_VMEM
        ),
        cost_estimate=pl.CostEstimate(
            flops=60 * 10**9, bytes_accessed=25 * 2**20, transcendentals=0
        ),
        name="block_backward",
    )(d_residual, mod_vec, *saved, *weights)


def adam_update(weight, first, second, grad, factor, first_fix, second_fix):
    clipped = grad * factor
    first_new = BETA_ONE * first + (1.0 - BETA_ONE) * clipped
    second_new = BETA_TWO * second + (1.0 - BETA_TWO) * clipped * clipped
    step_size = first_new / first_fix / (jnp.sqrt(second_new / second_fix) + ADAM_EPS)
    change = -LEARN_RATE * (step_size + DECAY * weight)
    master = weight + change
    return (master, first_new, second_new, master.astype(jnp.bfloat16), change)


def local(
    latents,
    target_noise,
    timesteps,
    labels,
    step_count,
    embed_table,
    layer_in,
    layer_out,
    layer_ada,
    embed_first,
    embed_second,
    input_first,
    input_second,
    output_first,
    output_second,
    mod_first,
    mod_second,
):
    tensor_size = lax.axis_size("tensor")
    tensor_rank = lax.axis_index("tensor")
    images = latents.shape[0]
    grid_side = SIDE // PATCH
    local_rows = grid_side // tensor_size
    tokens_all = grid_side * grid_side
    heads_local = HEADS // tensor_size
    group_width = heads_local * HEAD_DIM
    unit_count = FF // tensor_size
    patch_in = PATCH * PATCH * CHANNELS
    count_all = images * lax.axis_size("dp") * tokens_all * patch_in
    patch_start, time_start, second_start, final_start, head_start, vector_start, layer_start = (
        table_starts()
    )
    layer_rows = 10 + FF // D
    dp_rank = lax.axis_index("dp")
    dp_size = lax.axis_size("dp")
    place_count = dp_size * tensor_size
    images_all = images * dp_size
    table_cols = embed_table.T.astype(jnp.bfloat16).astype(jnp.float32)
    cols = table_cols.shape[0]
    mod_rows = layer_ada.shape[1]
    mod_cols = layer_ada.shape[2]
    mod_low = layer_ada.astype(jnp.bfloat16)

    def col_block(row_start, row_count):
        return table_cols[:, row_start : row_start + row_count]

    vector_count = 5 + LAYERS * layer_rows
    small_count = 2 * patch_in + vector_count
    lanes = -(-(small_count + 2 * images) // 128) * 128
    scalar_lanes = jnp.concatenate([timesteps, labels]).astype(jnp.float32)
    small_send = jnp.concatenate(
        [
            col_block(patch_start, patch_in),
            col_block(head_start, patch_in + vector_count),
            jnp.broadcast_to(scalar_lanes[None, :], (cols, 2 * images)),
            jnp.zeros((cols, lanes - small_count - 2 * images), jnp.float32),
        ],
        axis=1,
    )
    small_all = exchange(small_send, "all", False, 1)
    small_rows = small_all.reshape(D, lanes).T
    patch_w = small_rows[0:patch_in]
    head_w = small_rows[patch_in : 2 * patch_in]
    vectors = small_rows[2 * patch_in : 2 * patch_in + 5]
    bias_all = small_rows[2 * patch_in + 5 : small_count]
    scalars_all = small_all[::tensor_size, 0, small_count : small_count + 2 * images].astype(
        jnp.int32
    )
    timesteps_all = scalars_all[:, :images].reshape(images_all)
    labels_all = scalars_all[:, images:].reshape(images_all)
    time_feats = time_features(timesteps_all)
    onehot = (labels_all[:, None] == jnp.arange(CLASSES, dtype=jnp.int32)[None, :]).astype(
        jnp.float32
    )
    pre_time = dense(col_block(time_start, FREQ), time_feats.T) + col_block(vector_start + 1, 1)
    hidden = exchange(jax.nn.silu(pre_time), "all", False, 2).reshape(D, images_all)
    second_cols = col_block(second_start, D)
    shift_cols = col_block(final_start, D)
    scale_cols = col_block(final_start + D, D)
    pre_signal = (
        dense(second_cols, hidden)
        + col_block(vector_start + 2, 1)
        + dense(col_block(0, CLASSES), onehot.T)
    )
    signal = exchange(jax.nn.silu(pre_signal), "all", False, 3).reshape(D, images_all)
    final_send = jnp.concatenate(
        [
            dense(shift_cols, signal) + col_block(vector_start + 3, 1),
            dense(scale_cols, signal) + col_block(vector_start + 4, 1),
        ],
        axis=0,
    )
    final_all = exchange(final_send, "all", False, 4).reshape(place_count, 2, cols, images_all)
    final_own = lax.dynamic_slice_in_dim(final_all, dp_rank * images, images, 3)
    final_own = final_own.transpose(1, 3, 0, 2).reshape(2, images, D)
    final_shift, final_scale = final_own[0], final_own[1]
    signal_low = lax.dynamic_slice_in_dim(
        signal.astype(jnp.bfloat16), dp_rank * mod_rows, mod_rows, 0
    )
    mod_part = jnp.einsum("db,lde->ble", signal_low, mod_low, preferred_element_type=jnp.float32)
    mod_part = mod_part.reshape(dp_size, images * LAYERS, mod_cols)
    mod_local = jnp.sum(exchange(mod_part, "dp", True, 5), axis=0)
    mod_full = exchange(mod_local, "tensor", False, 6)
    mod_full = mod_full.reshape(tensor_size, images, LAYERS, mod_cols)
    mod_full = mod_full.transpose(2, 1, 0, 3).reshape(LAYERS, images, tensor_size * mod_cols)
    pixels = patchify(latents, local_rows)
    targets = patchify(target_noise, local_rows)
    keep_coef, drop_coef = noise_levels(timesteps)
    noisy = keep_coef[:, None, None] * pixels + drop_coef[:, None, None] * targets
    residual = (
        jnp.einsum("btp,pd->btd", noisy, patch_w, precision=PRECISE)
        + vectors[0]
        + position_table(tensor_rank * local_rows, local_rows)[None]
    )
    saved_acts = []
    for layer_idx in range(LAYERS):
        weight_in, weight_out = (
            lax.all_gather(
                layer_in[layer_idx]
                .astype(jnp.bfloat16)
                .reshape(layer_in.shape[1], layer_in.shape[3]),
                "dp",
                axis=0,
                tiled=True,
            ),
            lax.all_gather(
                layer_out[layer_idx].astype(jnp.bfloat16).reshape(layer_out.shape[2], D),
                "dp",
                axis=0,
                tiled=True,
            ),
        )
        bias_rows = bias_all[layer_idx * layer_rows : (layer_idx + 1) * layer_rows]
        up_all = bias_rows[10:].reshape(FF)
        ada_bias = bias_rows[0:6].reshape(6 * D)
        out_bias = bias_rows[6]
        down_bias = bias_rows[7]
        query_bias = lax.dynamic_slice_in_dim(bias_rows[8], tensor_rank * group_width, group_width)
        value_bias = lax.dynamic_slice_in_dim(bias_rows[9], tensor_rank * group_width, group_width)
        up_bias = lax.dynamic_slice_in_dim(up_all, tensor_rank * unit_count, unit_count)
        mod_vec = (mod_full[layer_idx] + ada_bias).reshape(images, 6, D)
        weights = (
            weight_in[:, : 3 * group_width],
            weight_in[:, 3 * group_width :],
            weight_out[:group_width],
            weight_out[group_width:],
        )
        qkv_bias = jnp.concatenate(
            [query_bias, jnp.zeros((group_width,), jnp.float32), value_bias]
        )[None]
        outs = forward_layer(
            residual,
            mod_vec,
            jnp.stack([out_bias, down_bias]),
            qkv_bias,
            up_bias[None],
            *weights,
        )
        saved_acts.append((mod_vec, (residual,) + tuple(outs[1:]), weights))
        residual = outs[0]
    final_in, final_norm_pull = jax.vjp(modulate, residual, final_shift, final_scale)
    predicted = jnp.einsum("btd,pd->btp", final_in, head_w, precision=PRECISE)
    error_all = predicted - targets
    loss_part = jnp.sum(error_all * error_all) / count_all
    d_pred = 2.0 * error_all / count_all
    d_head = jnp.einsum("btp,btd->pd", d_pred, final_in, precision=PRECISE)
    d_final = jnp.einsum("btp,pd->btd", d_pred, head_w, precision=PRECISE)
    d_residual, d_final_shift, d_final_scale = final_norm_pull(d_final)
    grads_in = []
    grads_out = []
    mod_parts = []
    bias_blocks = []
    for layer_idx in reversed(range(LAYERS)):
        mod_vec, saved, weights = saved_acts[layer_idx]
        d_residual, d_w_in, d_w_out, d_mod_vec, d_vec, d_qkv_bias, d_up_bias = backward_layer(
            d_residual, mod_vec, saved, weights
        )
        d_modulation = d_mod_vec.reshape(images, 6 * D)
        d_out_bias, d_down_bias = d_vec[0], d_vec[1]
        d_query_bias = d_qkv_bias[0, :group_width]
        d_value_bias = d_qkv_bias[0, 2 * group_width :]
        d_up_bias = d_up_bias[0]
        mod_parts.insert(0, d_modulation)
        grad_in, grad_out = (
            lax.psum_scatter(
                d_w_in,
                "dp",
                scatter_dimension=0,
                tiled=True,
            ).astype(jnp.float32),
            lax.psum_scatter(
                d_w_out,
                "dp",
                scatter_dimension=0,
                tiled=True,
            ).astype(jnp.float32),
        )
        grads_in.insert(0, grad_in)
        grads_out.insert(0, grad_out)
        query_row = lax.dynamic_update_slice_in_dim(
            jnp.zeros((D,), jnp.float32), d_query_bias, tensor_rank * group_width, 0
        )
        value_row = lax.dynamic_update_slice_in_dim(
            jnp.zeros((D,), jnp.float32), d_value_bias, tensor_rank * group_width, 0
        )
        up_rows = lax.dynamic_update_slice_in_dim(
            jnp.zeros((FF,), jnp.float32), d_up_bias, tensor_rank * unit_count, 0
        ).reshape(FF // D, D)
        bias_blocks.insert(
            0,
            jnp.concatenate(
                [
                    jnp.sum(d_modulation, axis=0).reshape(6, D),
                    d_out_bias[None],
                    d_down_bias[None],
                    query_row[None],
                    value_row[None],
                    up_rows,
                ],
                axis=0,
            ),
        )
    d_patch_w = jnp.einsum("btp,btd->pd", noisy, d_residual, precision=PRECISE)
    d_patch_b = jnp.sum(d_residual, axis=(0, 1))
    row_parts = jnp.concatenate(
        [d_patch_w, d_head, d_patch_b[None]] + bias_blocks + [d_final_shift, d_final_scale],
        axis=0,
    )
    row_count = row_parts.shape[0]
    row_lanes = -(-row_count // 128) * 128
    row_parts = jnp.pad(row_parts, ((0, row_lanes - row_count), (0, 0)))
    row_all = exchange(row_parts.T.reshape(place_count, cols, row_lanes), "all", True, 7)
    row_sums = jnp.sum(row_all, axis=0)
    final_at = row_count - 2 * images
    final_sums = jnp.sum(
        row_all[:, :, final_at:row_count].reshape(dp_size, tensor_size, cols, 2, images), axis=1
    )
    final_sums = final_sums.transpose(2, 1, 0, 3).reshape(2, cols, images_all)
    d_shift_cols, d_scale_cols = final_sums[0], final_sums[1]
    mod_parts = jnp.stack(mod_parts).reshape(LAYERS * images, tensor_size, mod_cols)
    d_mod_own = jnp.sum(exchange(mod_parts.transpose(1, 0, 2), "tensor", True, 8), axis=0)
    d_mod_low = exchange(d_mod_own.astype(jnp.bfloat16), "dp", False, 9)
    d_mod_low = d_mod_low.reshape(dp_size, LAYERS, images, mod_cols)
    d_mod_low = d_mod_low.transpose(1, 0, 2, 3).reshape(LAYERS, images_all, mod_cols)
    mod_grad = jnp.einsum(
        "db,lbe->lde", signal_low, d_mod_low, preferred_element_type=jnp.float32
    )
    d_signal_rows = jnp.einsum(
        "lbe,lde->db", d_mod_low, mod_low, preferred_element_type=jnp.float32
    )
    d_signal_part = dense(shift_cols.T, d_shift_cols) + dense(scale_cols.T, d_scale_cols)
    d_signal_part = d_signal_part + lax.dynamic_update_slice_in_dim(
        jnp.zeros((D, images_all), jnp.float32), d_signal_rows, dp_rank * mod_rows, 0
    )
    d_signal_cols = jnp.sum(
        exchange(d_signal_part.reshape(place_count, cols, images_all), "all", True, 10), axis=0
    )
    d_pre_signal = d_signal_cols * silu_slope(pre_signal)
    d_hidden_part = dense(second_cols.T, d_pre_signal)
    d_hidden_cols = jnp.sum(
        exchange(d_hidden_part.reshape(place_count, cols, images_all), "all", True, 11), axis=0
    )
    d_hidden = d_hidden_cols * silu_slope(pre_time)
    table_grad = jnp.concatenate(
        [
            dense(d_pre_signal, onehot),
            row_sums[:, 0:patch_in],
            dense(d_hidden, time_feats),
            dense(d_pre_signal, hidden.T),
            dense(d_shift_cols, signal.T),
            dense(d_scale_cols, signal.T),
            row_sums[:, patch_in : 2 * patch_in + 1],
            jnp.sum(d_hidden, axis=1, keepdims=True),
            jnp.sum(d_pre_signal, axis=1, keepdims=True),
            jnp.sum(d_shift_cols, axis=1, keepdims=True),
            jnp.sum(d_scale_cols, axis=1, keepdims=True),
            row_sums[:, 2 * patch_in + 1 : final_at],
        ],
        axis=1,
    )
    input_grad = jnp.stack(grads_in).reshape(layer_in.shape)
    output_grad = jnp.stack(grads_out).reshape(layer_out.shape)
    local_squares = (
        jnp.sum(table_grad * table_grad)
        + jnp.sum(input_grad * input_grad)
        + jnp.sum(output_grad * output_grad)
        + jnp.sum(mod_grad * mod_grad)
    )
    scalar_send = jnp.where(
        lax.broadcasted_iota(jnp.int32, (8, 128), 1) == 0, loss_part, local_squares
    )
    scalar_sums = jnp.sum(exchange(scalar_send, "all", False, 12)[:, 0, 0:2], axis=0)
    loss_value = scalar_sums[0]
    square_total = scalar_sums[1]
    grad_norm = jnp.sqrt(square_total)
    factor = jnp.minimum(1.0, CLIP_NORM / grad_norm)
    first_fix = 1.0 - BETA_ONE ** step_count.astype(jnp.float32)
    second_fix = 1.0 - BETA_TWO ** step_count.astype(jnp.float32)
    embed_out = adam_update(
        embed_table.T, embed_first.T, embed_second.T, table_grad, factor, first_fix, second_fix
    )
    input_out = adam_update(
        layer_in, input_first, input_second, input_grad, factor, first_fix, second_fix
    )
    output_out = adam_update(
        layer_out, output_first, output_second, output_grad, factor, first_fix, second_fix
    )
    mod_out = adam_update(layer_ada, mod_first, mod_second, mod_grad, factor, first_fix, second_fix)
    return (
        (loss_value, grad_norm, embed_out[4].T, embed_out[1].T, embed_out[2].T)
        + input_out[0:4]
        + output_out[0:4]
        + mod_out[0:4]
    )


def solution(mesh):
    placed = (
        P("dp", "tensor"),
        P("dp", "tensor"),
        P("dp"),
        P("dp"),
        P(),
        P(None, ("dp", "tensor")),
        P(None, "dp", "tensor", None),
        P(None, "tensor", "dp", None),
        P(None, "dp", "tensor"),
        P(None, ("dp", "tensor")),
        P(None, ("dp", "tensor")),
        P(None, "dp", "tensor", None),
        P(None, "dp", "tensor", None),
        P(None, "tensor", "dp", None),
        P(None, "tensor", "dp", None),
        P(None, "dp", "tensor"),
        P(None, "dp", "tensor"),
    )
    return jax.shard_map(
        local,
        mesh=mesh,
        in_specs=placed,
        out_specs=(
            P(),
            P(),
            P(None, ("dp", "tensor")),
            P(None, ("dp", "tensor")),
            P(None, ("dp", "tensor")),
            P(None, "dp", "tensor", None),
            P(None, "dp", "tensor", None),
            P(None, "dp", "tensor", None),
            P(None, "dp", "tensor", None),
            P(None, "tensor", "dp", None),
            P(None, "tensor", "dp", None),
            P(None, "tensor", "dp", None),
            P(None, "tensor", "dp", None),
            P(None, "dp", "tensor"),
            P(None, "dp", "tensor"),
            P(None, "dp", "tensor"),
            P(None, "dp", "tensor"),
        ),
        check_vma=False,
    )
```

```python
import functools
import math

import jax
import jax.numpy as jnp
from jax import lax
from jax.experimental import pallas as pl
from jax.experimental.pallas import tpu as pltpu
from jax.sharding import PartitionSpec as P

D = 768
HEADS = 12
HEAD_DIM = 64
FF = 3072
CLASSES = 1001
FREQ = 256
CHANNELS = 4
PATCH = 2
SIDE = 32
LAYERS = 3


EPS_NORM = 1e-06
LEARN_RATE = 0.01
DECAY = 0.01
BETA_ONE = 0.5
BETA_TWO = 0.5
ADAM_EPS = 1e-08
CLIP_NORM = 0.25
PRECISE = lax.Precision.HIGHEST


def dense(left_op, right_op):
    return jnp.dot(left_op, right_op, precision=PRECISE, preferred_element_type=jnp.float32)


def layer_norm(values):
    center = values - jnp.mean(values, axis=-1, keepdims=True)
    return center * lax.rsqrt(jnp.mean(center * center, axis=-1, keepdims=True) + EPS_NORM)


def modulate(values, shift_vec, scale_vec):
    return layer_norm(values) * (1.0 + scale_vec[:, None, :]) + shift_vec[:, None, :]


def gelu_tanh(values):
    return jax.nn.gelu(values, approximate=True)


def silu_slope(values):
    sigmoid_val = jax.nn.sigmoid(values)
    return sigmoid_val * (1.0 + values * (1.0 - sigmoid_val))


def time_features(step_ints):
    half_width = FREQ // 2
    frequency = jnp.exp(-math.log(10000.0) * jnp.arange(half_width, dtype=jnp.float32) / half_width)
    angles = step_ints.astype(jnp.float32)[:, None] * frequency[None, :]
    return jnp.concatenate([jnp.cos(angles), jnp.sin(angles)], axis=1)


def noise_levels(step_ints):
    base_cos = math.cos(0.008 / 1.008 * math.pi / 2)
    angles = (step_ints.astype(jnp.float32) / 1000.0 + 0.008) / 1.008 * (math.pi / 2)
    signal_level = jnp.cos(angles) ** 2 / base_cos**2
    return (jnp.sqrt(signal_level), jnp.sqrt(1.0 - signal_level))


def position_table(first_row, row_count):
    grid_side = SIDE // PATCH
    quarter = D // 4
    omegas = jnp.exp(-math.log(10000.0) * jnp.arange(quarter, dtype=jnp.float32) / quarter)
    token_index = jnp.arange(row_count * grid_side, dtype=jnp.int32)
    row_angle = (first_row + token_index // grid_side).astype(jnp.float32)[:, None] * omegas[
        None, :
    ]
    col_angle = (token_index % grid_side).astype(jnp.float32)[:, None] * omegas[None, :]
    return jnp.concatenate(
        [jnp.sin(row_angle), jnp.cos(row_angle), jnp.sin(col_angle), jnp.cos(col_angle)], axis=1
    )


def patchify(flat_pixels, row_count):
    grid_side = SIDE // PATCH
    shaped = flat_pixels.reshape(flat_pixels.shape[0], row_count, PATCH, grid_side, PATCH, CHANNELS)
    return shaped.transpose(0, 1, 3, 2, 4, 5).reshape(
        flat_pixels.shape[0], row_count * grid_side, PATCH * PATCH * CHANNELS
    )


def table_starts():
    patch_in = PATCH * PATCH * CHANNELS
    patch_start = CLASSES
    time_start = patch_start + patch_in
    second_start = time_start + FREQ
    final_start = second_start + D
    head_start = final_start + 2 * D
    vector_start = head_start + patch_in
    layer_start = vector_start + 5
    return (
        patch_start,
        time_start,
        second_start,
        final_start,
        head_start,
        vector_start,
        layer_start,
    )


def group_place(group):
    if group == "all":
        width = lax.axis_size("tensor")
        place = lax.axis_index("dp") * width + lax.axis_index("tensor")
        size = lax.axis_size("dp") * width
        return place, size, lambda at: {"dp": at // width, "tensor": lax.rem(at, width)}
    return lax.axis_index(group), lax.axis_size(group), lambda at: {group: at}


def exchange_kernel(group, spread, source, target, send_sems, recv_sems, local_sem):
    place, size, coords = group_place(group)
    barrier = pltpu.get_barrier_semaphore()

    def greet(step, carry):
        peer = coords(lax.rem(place + step, size))
        pl.semaphore_signal(barrier, inc=1, device_id=peer, device_id_type=pl.DeviceIdType.MESH)
        return carry

    def copy_to(step):
        there = lax.rem(place + step, size)
        return pltpu.make_async_remote_copy(
            src_ref=source.at[there] if spread else source,
            dst_ref=target.at[place],
            send_sem=send_sems.at[step],
            recv_sem=recv_sems.at[step],
            device_id=coords(there),
            device_id_type=pl.DeviceIdType.MESH,
        )

    def begin(step, carry):
        copy_to(step).start()
        return carry

    def finish(step, carry):
        copy_to(step).wait()
        return carry

    lax.fori_loop(1, size, greet, 0)
    mine = pltpu.make_async_copy(
        source.at[place] if spread else source, target.at[place], local_sem
    )
    mine.start()
    pl.semaphore_wait(barrier, size - 1)
    lax.fori_loop(1, size, begin, 0)
    mine.wait()
    lax.fori_loop(1, size, finish, 0)


def exchange(values, group, spread, call_id):
    if group == "all":
        size = lax.axis_size("dp") * lax.axis_size("tensor")
    else:
        size = lax.axis_size(group)
    block = values.shape[1:] if spread else values.shape
    return pl.pallas_call(
        functools.partial(exchange_kernel, group, spread),
        out_shape=jax.ShapeDtypeStruct((size,) + block, values.dtype),
        in_specs=[pl.BlockSpec(memory_space=pltpu.VMEM)],
        out_specs=pl.BlockSpec(memory_space=pltpu.VMEM),
        scratch_shapes=[
            pltpu.SemaphoreType.DMA((size,)),
            pltpu.SemaphoreType.DMA((size,)),
            pltpu.SemaphoreType.DMA,
        ],
        compiler_params=pltpu.CompilerParams(
            collective_id=call_id, has_side_effects=True, vmem_limit_bytes=32 * 2**20
        ),
        name="exchange_" + group,
    )(values)


MESH = pl.DeviceIdType.MESH
ACT_VMEM = 60 * 2**20


def dot_nn(left_op, right_op):
    return jnp.dot(left_op, right_op, preferred_element_type=jnp.float32)


def dot_nt(left_op, right_op):
    return lax.dot_general(
        left_op, right_op, (((1,), (1,)), ((), ())), preferred_element_type=jnp.float32
    )


def dot_tn(left_op, right_op):
    return lax.dot_general(
        left_op, right_op, (((0,), (0,)), ((), ())), preferred_element_type=jnp.float32
    )


def norm_parts(values):
    center = values - jnp.mean(values, axis=-1, keepdims=True)
    rstd = lax.rsqrt(jnp.mean(center * center, axis=-1, keepdims=True) + EPS_NORM)
    return center * rstd, rstd


def greet(line):
    rank = lax.axis_index("tensor")
    half = lax.axis_size("tensor") // 2
    core_peer = {"tensor": rank + 1 - 2 * lax.rem(rank, 2)}
    chip_peer = {"tensor": lax.rem(rank + half, 2 * half)}
    barrier = pltpu.get_barrier_semaphore()
    for peer in (core_peer, chip_peer):
        pl.semaphore_signal(barrier, inc=1, device_id=peer, device_id_type=MESH)
    count = 2
    if line is not None:
        line.greet()
        count = count + line.answers()
    pl.semaphore_wait(barrier, count)


class Spread:
    def __init__(self, rows_ref, send_sems, recv_sems):
        self.rows, self.send, self.recv = rows_ref, send_sems, recv_sems
        self.rank = lax.axis_index("tensor")
        self.own_core = lax.rem(self.rank, 2)
        self.core_peer = self.rank + 1 - 2 * self.own_core
        self.chip_peer = lax.rem(self.rank + 2, 4)
        self.count = rows_ref.shape[1] // 4

    def block(self, image, owner):
        return self.rows.at[image, pl.ds(pl.multiple_of(owner * self.count, 16), self.count), :]

    def copy(self, image, owner, peer, which):
        return pltpu.make_async_remote_copy(
            src_ref=self.block(image, owner),
            dst_ref=self.block(image, owner),
            send_sem=self.send.at[image, which],
            recv_sem=self.recv.at[image, which],
            device_id={"tensor": peer},
            device_id_type=MESH,
        )

    def put(self, image, values):
        self.rows[image, pl.ds(pl.multiple_of(self.rank * self.count, 16), self.count), :] = values
        self.copy(image, self.rank, self.chip_peer, 0).start()
        self.copy(image, self.rank, self.core_peer, 1).start()

    def forward(self, image):
        self.copy(image, self.rank, self.chip_peer, 0).wait_recv()
        self.copy(image, self.chip_peer, self.core_peer, 2).start()

    def wait(self, image):
        self.copy(image, self.rank, self.core_peer, 1).wait_recv()
        self.copy(image, self.chip_peer, self.core_peer, 2).wait_recv()

    def close(self, image):
        self.copy(image, self.rank, self.chip_peer, 0).wait_send()
        self.copy(image, self.rank, self.core_peer, 1).wait_send()
        self.copy(image, self.chip_peer, self.core_peer, 2).wait_send()


class Collect:
    def __init__(self, part, near, far_out, far_in, send_sems, recv_sems):
        self.part, self.near, self.far_out, self.far_in = part, near, far_out, far_in
        self.send, self.recv = send_sems, recv_sems
        self.rank = lax.axis_index("tensor")
        self.own_core = lax.rem(self.rank, 2)
        self.own_chip = self.rank // 2
        self.core_peer = self.rank + 1 - 2 * self.own_core
        self.chip_peer = lax.rem(self.rank + 2, 4)
        self.count = part.shape[1] // 4

    def block(self, image, owner):
        return self.part.at[image, pl.ds(pl.multiple_of(owner * self.count, 16), self.count), :]

    def near_copy(self, image, far):
        chip = 1 - self.own_chip if far else self.own_chip
        return pltpu.make_async_remote_copy(
            src_ref=self.block(image, 2 * chip + 1 - self.own_core),
            dst_ref=self.near.at[image, far],
            send_sem=self.send.at[image, far],
            recv_sem=self.recv.at[image, far],
            device_id={"tensor": self.core_peer},
            device_id_type=MESH,
        )

    def far_copy(self, image):
        return pltpu.make_async_remote_copy(
            src_ref=self.far_out.at[image],
            dst_ref=self.far_in.at[image],
            send_sem=self.send.at[image, 2],
            recv_sem=self.recv.at[image, 2],
            device_id={"tensor": self.chip_peer},
            device_id_type=MESH,
        )

    def put(self, image, values):
        self.part[image] = values.astype(jnp.bfloat16)
        self.near_copy(image, 1).start()
        self.near_copy(image, 0).start()

    def load(self, image, owner):
        at = pl.ds(pl.multiple_of(owner * self.count, 16), self.count)
        return self.part[image, at, :].astype(jnp.float32)

    def forward(self, image):
        self.near_copy(image, 1).wait_recv()
        total = self.load(image, self.chip_peer) + self.near[image, 1].astype(jnp.float32)
        self.far_out[image] = total.astype(jnp.bfloat16)
        self.far_copy(image).start()

    def take(self, image):
        self.near_copy(image, 0).wait_recv()
        total = self.load(image, self.rank) + self.near[image, 0].astype(jnp.float32)
        self.far_copy(image).wait_recv()
        return total + self.far_in[image].astype(jnp.float32)

    def close(self, image):
        self.near_copy(image, 1).wait_send()
        self.near_copy(image, 0).wait_send()
        self.far_copy(image).wait_send()


def collect_scratch(images, tokens):
    count = tokens // 4
    return [
        pltpu.VMEM((images, tokens, D), jnp.bfloat16),
        pltpu.VMEM((images, 2, count, D), jnp.bfloat16),
        pltpu.VMEM((images, count, D), jnp.bfloat16),
        pltpu.VMEM((images, count, D), jnp.bfloat16),
    ]


def each(count, body):
    def step(index, carry):
        body(index)
        return carry

    lax.fori_loop(0, count, step, 0)


class Line:
    def __init__(self):
        self.size = lax.axis_size("dp") // 2
        self.place = lax.axis_index("dp")
        self.at = self.place // 2
        self.side = lax.rem(self.place, 2)
        self.pair = self.place + 1 - 2 * self.side
        self.has_up = self.at + 1 < self.size
        self.has_down = self.at > 0

    def greet(self):
        barrier = pltpu.get_barrier_semaphore()
        pl.semaphore_signal(barrier, inc=1, device_id={"dp": self.pair}, device_id_type=MESH)

        @pl.when(self.has_up)
        def _():
            up = {"dp": self.place + 2}
            pl.semaphore_signal(barrier, inc=1, device_id=up, device_id_type=MESH)

        @pl.when(self.has_down)
        def _():
            down = {"dp": self.place - 2}
            pl.semaphore_signal(barrier, inc=1, device_id=down, device_id_type=MESH)

    def answers(self):
        return 1 + self.has_up.astype(jnp.int32) + self.has_down.astype(jnp.int32)


UP, DOWN, PAIR = 0, 1, 2


class Gather:
    def __init__(self, line, shards, wholes, sends, recvs, local_sems):
        self.line, self.shards, self.wholes = line, shards, wholes
        self.sends, self.recvs, self.local_sems = sends, recvs, local_sems

    def copy(self, part, way, step, owner, fresh=False):
        line = self.line
        there = {UP: line.place + 2, DOWN: line.place - 2, PAIR: line.pair}[way]
        return pltpu.make_async_remote_copy(
            src_ref=self.shards[part] if fresh else self.wholes[part].at[owner],
            dst_ref=self.wholes[part].at[owner],
            send_sem=self.sends.at[way, step, part],
            recv_sem=self.recvs.at[way, step, part],
            device_id={"dp": there},
            device_id_type=MESH,
        )

    def local_copy(self, part):
        return pltpu.make_async_copy(
            self.shards[part], self.wholes[part].at[self.line.place], self.local_sems.at[part]
        )

    def start(self):
        line = self.line
        parts = range(len(self.shards))

        @pl.when(line.has_up)
        def _():
            for part in parts:
                self.copy(part, UP, 0, line.place, True).start()

        @pl.when(line.has_down)
        def _():
            for part in parts:
                self.copy(part, DOWN, 0, line.place, True).start()

        for part in parts:
            self.copy(part, PAIR, line.at, line.place, True).start()
            self.local_copy(part).start()

    def tick(self, step):
        line = self.line
        parts = range(len(self.shards))
        for way, there, can in ((UP, -step, line.has_up), (DOWN, step, line.has_down)):
            owner = line.place + 2 * there
            spot = line.at + there

            @pl.when((spot >= 0) & (spot < line.size))
            def _(way=way, can=can, owner=owner, spot=spot):
                for part in parts:
                    self.copy(part, way, step - 1, owner).wait_recv()

                @pl.when(can)
                def _():
                    for part in parts:
                        self.copy(part, way, step, owner).start()

                for part in parts:
                    self.copy(part, PAIR, spot, owner).start()

    def finish(self):
        line = self.line
        parts = range(len(self.shards))
        for part in parts:
            self.local_copy(part).wait()

        def side(spot):
            for part in parts:
                self.copy(part, PAIR, spot, 2 * spot + line.side).wait()

        each(line.size, side)

        def along(step):
            for way, there, can in ((UP, -step, line.has_up), (DOWN, step, line.has_down)):
                spot = line.at + there

                @pl.when((spot >= 0) & (spot < line.size) & can)
                def _(way=way, there=there):
                    for part in parts:
                        self.copy(part, way, step, line.place + 2 * there).wait_send()

        each(line.size, along)


class Reduce:
    def __init__(self, line, terms, totals, pair_in, way_in, way_out, sends, recvs):
        self.line, self.terms, self.totals = line, terms, totals
        self.pair_in, self.way_in, self.way_out = pair_in, way_in, way_out
        self.sends, self.recvs = sends, recvs

    def pair_copy(self, part, spot):
        return pltpu.make_async_remote_copy(
            src_ref=self.terms[part].at[2 * spot + 1 - self.line.side],
            dst_ref=self.pair_in[part].at[spot],
            send_sem=self.sends.at[PAIR, spot, part],
            recv_sem=self.recvs.at[PAIR, spot, part],
            device_id={"dp": self.line.pair},
            device_id_type=MESH,
        )

    def way_copy(self, part, way, spot):
        there = self.line.place + 2 if way == UP else self.line.place - 2
        return pltpu.make_async_remote_copy(
            src_ref=self.way_out[part].at[way, spot],
            dst_ref=self.way_in[part].at[way, spot],
            send_sem=self.sends.at[way, spot, part],
            recv_sem=self.recvs.at[way, spot, part],
            device_id={"dp": there},
            device_id_type=MESH,
        )

    def start(self):
        last = self.line.size - 1

        def outer(step):
            for part in range(len(self.terms)):
                self.pair_copy(part, last - step).start()

            @pl.when(last - step > step)
            def _():
                for part in range(len(self.terms)):
                    self.pair_copy(part, step).start()

        each((self.line.size + 1) // 2, outer)

    def pair_sum(self, part, spot):
        own = self.terms[part][2 * spot + self.line.side].astype(jnp.float32)
        return own + self.pair_in[part][spot].astype(jnp.float32)

    def pass_on(self, way, spot, more):
        for part in range(len(self.terms)):
            self.pair_copy(part, spot).wait_recv()
            self.way_out[part][way, spot] = self.pair_sum(part, spot).astype(jnp.bfloat16)

            @pl.when(more)
            def _(part=part):
                self.way_copy(part, way, spot).wait_recv()
                self.way_out[part][way, spot] = (
                    self.pair_sum(part, spot) + self.way_in[part][way, spot].astype(jnp.float32)
                ).astype(jnp.bfloat16)

            self.way_copy(part, way, spot).start()

    def tick(self, step):
        line = self.line
        last = line.size - 1

        @pl.when(last - step > line.at)
        def _():
            self.pass_on(UP, last - step, line.has_down)

        @pl.when(line.at > step)
        def _():
            self.pass_on(DOWN, step, line.has_up)

    def finish(self):
        line = self.line
        spot = line.at
        for part in range(len(self.terms)):
            self.pair_copy(part, spot).wait_recv()
            self.totals[part][...] = self.pair_sum(part, spot)
        for way, can in ((UP, line.has_down), (DOWN, line.has_up)):

            @pl.when(can)
            def _(way=way):
                for part in range(len(self.terms)):
                    self.way_copy(part, way, spot).wait_recv()
                    self.totals[part][...] += self.way_in[part][way, spot].astype(jnp.float32)

        def close(spot):
            for part in range(len(self.terms)):
                self.pair_copy(part, spot).wait_send()
            for way, passed in ((UP, spot > line.at), (DOWN, spot < line.at)):

                @pl.when(passed)
                def _(way=way):
                    for part in range(len(self.terms)):
                        self.way_copy(part, way, spot).wait_send()

        each(line.size, close)


def run_ticks(task, first, last):
    if task is not None:
        for step in range(first, last):
            task.tick(step)


def head_slice(matrix, head):
    return matrix[:, head * HEAD_DIM : (head + 1) * HEAD_DIM]


def soft_rows(queries, keys_in):
    scores = dot_nt(queries, keys_in) * (HEAD_DIM ** (-0.5))
    exponent = jnp.exp(scores - jnp.max(scores, axis=-1, keepdims=True))
    return exponent / jnp.sum(exponent, axis=-1, keepdims=True)


def forward_kernel(
    res_ref,
    mod_ref,
    vec_ref,
    qkv_bias_ref,
    up_bias_ref,
    w_qkv_ref,
    w_up_ref,
    w_attn_ref,
    w_down_ref,
    *rest,
):
    with_gather = len(rest) > 19
    shards, rest = (rest[:3], rest[3:]) if with_gather else ((), rest)
    (
        res_out,
        rows_a,
        qkv_out,
        mixed_out,
        branch_out,
        mid_out,
        rows_m,
        upper_out,
        down_out,
    ) = rest[:9]
    wholes, rest = (rest[9:12], rest[12:]) if with_gather else ((), rest[9:])
    (
    part_a,
    near_a,
    far_out_a,
    far_in_a,
    part_m,
    near_m,
    far_out_m,
    far_in_m,
    sends,
    recvs,
    ) = rest[:10]
    images = res_ref.shape[0]
    group_width = w_attn_ref.shape[0]
    gather, last_step = None, 0
    if with_gather:
        line = Line()
        greet(line)
        gather = Gather(line, shards, wholes, *rest[10:])
        last_step = line.size
    else:
        greet(None)
    spread_a = Spread(rows_a, sends.at[0], recvs.at[0])
    spread_m = Spread(rows_m, sends.at[1], recvs.at[1])
    collect_a = Collect(part_a, near_a, far_out_a, far_in_a, sends.at[2], recvs.at[2])
    collect_m = Collect(part_m, near_m, far_out_m, far_in_m, sends.at[3], recvs.at[3])

    def mod_row(image, piece):
        return mod_ref[image, pl.ds(piece, 1), :]

    def start_norm(image):
        normed, _ = norm_parts(res_ref[image])
        normed = normed * (1.0 + mod_row(image, 1)) + mod_row(image, 0)
        spread_a.put(image, normed.astype(jnp.bfloat16))

    def attend(image):
        spread_a.wait(image)
        rows = rows_a[image]
        projected = dot_nn(rows, w_qkv_ref[...]) + qkv_bias_ref[...]
        qkv = projected.astype(jnp.bfloat16)
        qkv_out[image] = qkv
        heads = []
        for head in range(group_width // HEAD_DIM):
            probs = soft_rows(
                head_slice(qkv[:, :group_width], head),
                head_slice(qkv[:, group_width : 2 * group_width], head),
            )
            heads.append(
                dot_nn(probs.astype(jnp.bfloat16), head_slice(qkv[:, 2 * group_width :], head))
            )
        mixed = jnp.concatenate(heads, axis=1).astype(jnp.bfloat16)
        mixed_out[image] = mixed
        collect_a.put(image, dot_nn(mixed, w_attn_ref[...]))

    def middle(image):
        branch = collect_a.take(image) + vec_ref[0:1, :]
        branch_out[image] = branch
        mid = res_ref[image] + mod_row(image, 2) * branch
        mid_out[image] = mid
        normed, _ = norm_parts(mid)
        normed = normed * (1.0 + mod_row(image, 4)) + mod_row(image, 3)
        spread_m.put(image, normed.astype(jnp.bfloat16))

    def feed(image):
        spread_m.wait(image)
        upper = dot_nn(rows_m[image], w_up_ref[...]) + up_bias_ref[...]
        upper_out[image] = upper
        collect_m.put(image, dot_nn(gelu_tanh(upper).astype(jnp.bfloat16), w_down_ref[...]))

    def finish(image):
        down = collect_m.take(image) + vec_ref[1:2, :]
        down_out[image] = down
        res_out[image] = mid_out[image] + mod_row(image, 5) * down

    def close(image):
        spread_a.close(image)
        spread_m.close(image)
        collect_a.close(image)
        collect_m.close(image)

    each(images, start_norm)
    if with_gather:
        gather.start()
    each(images, spread_a.forward)
    each(images, attend)
    run_ticks(gather, 1, min(2, last_step))
    each(images, collect_a.forward)
    each(images, middle)
    each(images, spread_m.forward)
    run_ticks(gather, 2, min(3, last_step))
    each(images, feed)
    run_ticks(gather, 3, min(4, last_step))
    each(images, collect_m.forward)
    each(images, finish)
    each(images, close)
    if with_gather:
        each(max(last_step - 4, 0), lambda step: gather.tick(step + 4))
        gather.finish()


def forward_layer(
    residual, mod_vec, vec_bias, qkv_bias, up_bias, w_qkv, w_up, w_attn, w_down, shards
):
    images, count, _ = residual.shape
    tokens = 4 * count
    low, full = jnp.bfloat16, jnp.float32
    shapes = [
        ((images, count, D), full),
        ((images, tokens, D), low),
        ((images, tokens, w_qkv.shape[1]), low),
        ((images, tokens, w_attn.shape[0]), low),
        ((images, count, D), full),
        ((images, count, D), full),
        ((images, tokens, D), low),
        ((images, tokens, w_up.shape[1]), full),
        ((images, count, D), full),
    ]
    scratch = [
        pltpu.SemaphoreType.DMA((4, images, 3)),
        pltpu.SemaphoreType.DMA((4, images, 3)),
    ]
    if shards:
        dp_size = lax.axis_size("dp")
        shapes += [((dp_size,) + shard.shape, low) for shard in shards]
        scratch += [
            pltpu.SemaphoreType.DMA((3, dp_size // 2, 3)),
            pltpu.SemaphoreType.DMA((3, dp_size // 2, 3)),
            pltpu.SemaphoreType.DMA((3,)),
        ]
    return pl.pallas_call(
        forward_kernel,
        out_shape=[jax.ShapeDtypeStruct(*shape) for shape in shapes],
        in_specs=[pl.BlockSpec(memory_space=pltpu.VMEM)] * (9 + len(shards)),
        out_specs=[pl.BlockSpec(memory_space=pltpu.VMEM)] * len(shapes),
        scratch_shapes=collect_scratch(images, tokens) + collect_scratch(images, tokens) + scratch,
        compiler_params=pltpu.CompilerParams(
            collective_id=20 if shards else 22, has_side_effects=True, vmem_limit_bytes=ACT_VMEM
        ),
        cost_estimate=pl.CostEstimate(
            flops=30 * 10**9, bytes_accessed=15 * 2**20, transcendentals=0
        ),
        name="block_forward",
    )(residual, mod_vec, vec_bias, qkv_bias, up_bias, w_qkv, w_up, w_attn, w_down, *shards)


def gelu_slope(values):
    root = math.sqrt(2.0 / math.pi)
    square = values * values
    tanh = jnp.tanh(root * (values + 0.044715 * values * square))
    half = 0.5 * (1.0 + tanh)
    slope = half + 0.5 * values * (1.0 - tanh * tanh) * root * (1.0 + 3.0 * 0.044715 * square)
    return values * half, slope


def norm_pull(values, scale_row, d_normed):
    normed, rstd = norm_parts(values)
    d_shift = jnp.sum(d_normed, axis=0, keepdims=True)
    d_scale = jnp.sum(d_normed * normed, axis=0, keepdims=True)
    inner = d_normed * (1.0 + scale_row)
    mean_one = jnp.mean(inner, axis=-1, keepdims=True)
    mean_two = jnp.mean(inner * normed, axis=-1, keepdims=True)
    return (inner - mean_one - normed * mean_two) * rstd, d_shift, d_scale


def backward_kernel(
    d_res_ref,
    mod_ref,
    res_ref,
    rows_a,
    qkv_ref,
    mixed_ref,
    branch_ref,
    mid_ref,
    rows_m,
    upper_ref,
    down_ref,
    w_qkv_ref,
    w_up_ref,
    w_attn_ref,
    w_down_ref,
    *rest,
):
    with_reduce = len(rest) > 24
    terms, rest = (rest[:3], rest[3:]) if with_reduce else ((), rest)
    (
        d_res_out,
        d_w_qkv,
        d_w_up,
        d_out,
        d_mod,
        d_vec,
        d_qkv_bias,
        d_up_bias,
    ) = rest[:8]
    totals, rest = (rest[8:11], rest[11:]) if with_reduce else ((), rest[8:])
    (
    d_mid,
    d_rows_m,
    d_rows_a,
    act_low,
    d_upper,
    d_qkv,
    part_a,
    near_a,
    far_out_a,
    far_in_a,
    part_m,
    near_m,
    far_out_m,
    far_in_m,
    sends,
    recvs,
    ) = rest[:16]
    images = res_ref.shape[0]
    tokens = rows_a.shape[1]
    group_width = w_attn_ref.shape[0]
    qkv_width = 3 * group_width
    units = w_up_ref.shape[1]
    reduce, last_step = None, 0
    if with_reduce:
        line = Line()
        greet(line)
        pair_in, way_in, way_out = rest[16:19], rest[19:22], rest[22:25]
        reduce = Reduce(line, terms, totals, pair_in, way_in, way_out, *rest[25:])
        last_step = line.size
    else:
        greet(None)
    spread_m = Spread(d_rows_m, sends.at[0], recvs.at[0])
    spread_a = Spread(d_rows_a, sends.at[1], recvs.at[1])
    collect_m = Collect(part_m, near_m, far_out_m, far_in_m, sends.at[2], recvs.at[2])
    collect_a = Collect(part_a, near_a, far_out_a, far_in_a, sends.at[3], recvs.at[3])
    d_vec[...] = jnp.zeros_like(d_vec)
    d_qkv_bias[...] = jnp.zeros_like(d_qkv_bias)
    d_up_bias[...] = jnp.zeros_like(d_up_bias)

    def mod_row(image, piece):
        return mod_ref[image, pl.ds(piece, 1), :]

    def start_down(image):
        d_res = d_res_ref[image]
        d_mod[image, pl.ds(5, 1), :] = jnp.sum(d_res * down_ref[image], axis=0, keepdims=True)
        d_down = d_res * mod_row(image, 5)
        d_vec[1:2, :] += jnp.sum(d_down, axis=0, keepdims=True)
        spread_m.put(image, d_down.astype(jnp.bfloat16))

    def feed(image):
        spread_m.wait(image)
        d_act = dot_nt(d_rows_m[image], w_down_ref[...])
        act, slope = gelu_slope(upper_ref[image])
        act_low[image] = act.astype(jnp.bfloat16)
        d_up = d_act * slope
        d_up_bias[...] += jnp.sum(d_up, axis=0, keepdims=True)
        d_up_low = d_up.astype(jnp.bfloat16)
        d_upper[image] = d_up_low
        collect_m.put(image, dot_nt(d_up_low, w_up_ref[...]))

    def rows_of(ref, width):
        return ref[...].reshape(images * tokens, width)

    def feed_weights():
        tile = 256

        def step(index, carry):
            at = pl.ds(pl.multiple_of(index * tile, tile), tile)
            grad = dot_tn(
                act_low[:, :, at].reshape(images * tokens, tile), rows_of(d_rows_m, D)
            )
            d_out[pl.ds(pl.multiple_of(group_width + index * tile, 64), tile), :] = grad.astype(
                jnp.bfloat16
            )
            grad = dot_tn(
                rows_m[:, :, at].reshape(images * tokens, tile), rows_of(d_upper, units)
            )
            d_w_up[pl.ds(pl.multiple_of(index * tile, tile), tile), :] = grad.astype(jnp.bfloat16)
            return carry

        lax.fori_loop(0, units // tile, step, 0)

    def middle(image):
        d_value, d_shift, d_scale = norm_pull(
            mid_ref[image], mod_row(image, 4), collect_m.take(image)
        )
        d_mod[image, pl.ds(3, 1), :] = d_shift
        d_mod[image, pl.ds(4, 1), :] = d_scale
        d_value = d_res_ref[image] + d_value
        d_mid[image] = d_value
        d_mod[image, pl.ds(2, 1), :] = jnp.sum(d_value * branch_ref[image], axis=0, keepdims=True)
        d_branch = d_value * mod_row(image, 2)
        d_vec[0:1, :] += jnp.sum(d_branch, axis=0, keepdims=True)
        spread_a.put(image, d_branch.astype(jnp.bfloat16))

    def attend(image):
        spread_a.wait(image)
        d_mixed = dot_nt(d_rows_a[image], w_attn_ref[...]).astype(jnp.bfloat16)
        qkv = qkv_ref[image]
        d_queries, d_keys, d_values = [], [], []
        scale_dot = HEAD_DIM ** (-0.5)
        for head in range(group_width // HEAD_DIM):
            queries = head_slice(qkv[:, :group_width], head)
            keys_in = head_slice(qkv[:, group_width : 2 * group_width], head)
            values_in = head_slice(qkv[:, 2 * group_width :], head)
            d_head = head_slice(d_mixed, head)
            probs = soft_rows(queries, keys_in)
            d_probs = dot_nt(d_head, values_in)
            d_values.append(dot_tn(probs.astype(jnp.bfloat16), d_head))
            inner = jnp.sum(probs * d_probs, axis=-1, keepdims=True)
            d_scores = (probs * (d_probs - inner)).astype(jnp.bfloat16)
            d_queries.append(dot_nn(d_scores, keys_in) * scale_dot)
            d_keys.append(dot_tn(d_scores, queries) * scale_dot)
        joined = jnp.concatenate(d_queries + d_keys + d_values, axis=1)
        d_qkv_bias[...] += jnp.sum(joined, axis=0, keepdims=True)
        joined = joined.astype(jnp.bfloat16)
        d_qkv[image] = joined
        collect_a.put(image, dot_nt(joined, w_qkv_ref[...]))

    def attend_weights():
        d_out[0:group_width, :] = dot_tn(
            rows_of(mixed_ref, group_width), rows_of(d_rows_a, D)
        ).astype(jnp.bfloat16)
        tile = 256

        def step(index, carry):
            at = pl.ds(pl.multiple_of(index * tile, tile), tile)
            grad = dot_tn(
                rows_a[:, :, at].reshape(images * tokens, tile), rows_of(d_qkv, qkv_width)
            )
            d_w_qkv[at, :] = grad.astype(jnp.bfloat16)
            return carry

        lax.fori_loop(0, D // tile, step, 0)

    def finish(image):
        d_value, d_shift, d_scale = norm_pull(
            res_ref[image], mod_row(image, 1), collect_a.take(image)
        )
        d_mod[image, pl.ds(0, 1), :] = d_shift
        d_mod[image, pl.ds(1, 1), :] = d_scale
        d_res_out[image] = d_mid[image] + d_value

    def close(image):
        spread_a.close(image)
        spread_m.close(image)
        collect_a.close(image)
        collect_m.close(image)

    each(images, start_down)
    if with_reduce:
        reduce.start()
    each(images, spread_m.forward)
    each(images, feed)
    each(images, collect_m.forward)
    feed_weights()
    run_ticks(reduce, 0, min(1, last_step))
    each(images, middle)
    each(images, spread_a.forward)
    run_ticks(reduce, 1, min(2, last_step))
    each(images, attend)
    run_ticks(reduce, 2, min(3, last_step))
    each(images, collect_a.forward)
    attend_weights()
    run_ticks(reduce, 3, min(4, last_step))
    each(images, finish)
    each(images, close)
    if with_reduce:
        each(max(last_step - 4, 0), lambda step: reduce.tick(step + 4))
        reduce.finish()


def backward_layer(d_residual, mod_vec, saved, weights, terms):
    images, count, _ = d_residual.shape
    tokens = 4 * count
    low, full = jnp.bfloat16, jnp.float32
    w_qkv, w_up, w_attn, w_down = weights
    group_width, units = w_attn.shape[0], w_up.shape[1]
    shapes = [
        ((images, count, D), full),
        ((D, 3 * group_width), low),
        ((D, units), low),
        ((group_width + units, D), low),
        ((images, 6, D), full),
        ((2, D), full),
        ((1, 3 * group_width), full),
        ((1, units), full),
    ]
    scratch = [
        pltpu.SemaphoreType.DMA((4, images, 3)),
        pltpu.SemaphoreType.DMA((4, images, 3)),
    ]
    if terms:
        spots = lax.axis_size("dp") // 2
        blocks = [term.shape[1:] for term in terms]
        shapes += [(block, full) for block in blocks]
        scratch += [pltpu.VMEM((spots,) + block, low) for block in blocks]
        scratch += [pltpu.VMEM((2, spots) + block, low) for block in blocks]
        scratch += [pltpu.VMEM((2, spots) + block, low) for block in blocks]
        scratch += [
            pltpu.SemaphoreType.DMA((3, spots, 3)),
            pltpu.SemaphoreType.DMA((3, spots, 3)),
        ]
    return pl.pallas_call(
        backward_kernel,
        out_shape=[jax.ShapeDtypeStruct(*shape) for shape in shapes],
        in_specs=[pl.BlockSpec(memory_space=pltpu.VMEM)] * (15 + len(terms)),
        out_specs=[pl.BlockSpec(memory_space=pltpu.VMEM)] * len(shapes),
        scratch_shapes=[
            pltpu.VMEM((images, count, D), full),
            pltpu.VMEM((images, tokens, D), low),
            pltpu.VMEM((images, tokens, D), low),
            pltpu.VMEM((images, tokens, units), low),
            pltpu.VMEM((images, tokens, units), low),
            pltpu.VMEM((images, tokens, 3 * group_width), low),
        ]
        + collect_scratch(images, tokens)
        + collect_scratch(images, tokens)
        + scratch,
        compiler_params=pltpu.CompilerParams(
            collective_id=21 if terms else 23, has_side_effects=True, vmem_limit_bytes=ACT_VMEM
        ),
        cost_estimate=pl.CostEstimate(
            flops=60 * 10**9, bytes_accessed=25 * 2**20, transcendentals=0
        ),
        name="block_backward",
    )(d_residual, mod_vec, *saved, *weights, *terms)


def adam_update(weight, first, second, grad, factor, first_fix, second_fix):
    clipped = grad * factor
    first_new = BETA_ONE * first + (1.0 - BETA_ONE) * clipped
    second_new = BETA_TWO * second + (1.0 - BETA_TWO) * clipped * clipped
    step_size = first_new / first_fix / (jnp.sqrt(second_new / second_fix) + ADAM_EPS)
    change = -LEARN_RATE * (step_size + DECAY * weight)
    master = weight + change
    return (master, first_new, second_new, master.astype(jnp.bfloat16), change)


def local(
    latents,
    target_noise,
    timesteps,
    labels,
    step_count,
    embed_table,
    layer_in,
    layer_out,
    layer_ada,
    embed_first,
    embed_second,
    input_first,
    input_second,
    output_first,
    output_second,
    mod_first,
    mod_second,
):
    tensor_size = lax.axis_size("tensor")
    tensor_rank = lax.axis_index("tensor")
    images = latents.shape[0]
    grid_side = SIDE // PATCH
    local_rows = grid_side // tensor_size
    tokens_all = grid_side * grid_side
    heads_local = HEADS // tensor_size
    group_width = heads_local * HEAD_DIM
    unit_count = FF // tensor_size
    patch_in = PATCH * PATCH * CHANNELS
    count_all = images * lax.axis_size("dp") * tokens_all * patch_in
    patch_start, time_start, second_start, final_start, head_start, vector_start, layer_start = (
        table_starts()
    )
    layer_rows = 10 + FF // D
    dp_rank = lax.axis_index("dp")
    dp_size = lax.axis_size("dp")
    place_count = dp_size * tensor_size
    images_all = images * dp_size
    table_cols = embed_table.T.astype(jnp.bfloat16).astype(jnp.float32)
    cols = table_cols.shape[0]
    mod_rows = layer_ada.shape[1]
    mod_cols = layer_ada.shape[2]
    mod_low = layer_ada.astype(jnp.bfloat16)

    def col_block(row_start, row_count):
        return table_cols[:, row_start : row_start + row_count]

    vector_count = 5 + LAYERS * layer_rows
    small_count = 2 * patch_in + vector_count
    lanes = -(-(small_count + 2 * images) // 128) * 128
    scalar_lanes = jnp.concatenate([timesteps, labels]).astype(jnp.float32)
    small_send = jnp.concatenate(
        [
            col_block(patch_start, patch_in),
            col_block(head_start, patch_in + vector_count),
            jnp.broadcast_to(scalar_lanes[None, :], (cols, 2 * images)),
            jnp.zeros((cols, lanes - small_count - 2 * images), jnp.float32),
        ],
        axis=1,
    )
    small_all = exchange(small_send, "all", False, 1)
    small_rows = small_all.reshape(D, lanes).T
    patch_w = small_rows[0:patch_in]
    head_w = small_rows[patch_in : 2 * patch_in]
    vectors = small_rows[2 * patch_in : 2 * patch_in + 5]
    bias_all = small_rows[2 * patch_in + 5 : small_count]
    scalars_all = small_all[::tensor_size, 0, small_count : small_count + 2 * images].astype(
        jnp.int32
    )
    timesteps_all = scalars_all[:, :images].reshape(images_all)
    labels_all = scalars_all[:, images:].reshape(images_all)
    time_feats = time_features(timesteps_all)
    onehot = (labels_all[:, None] == jnp.arange(CLASSES, dtype=jnp.int32)[None, :]).astype(
        jnp.float32
    )
    pre_time = dense(col_block(time_start, FREQ), time_feats.T) + col_block(vector_start + 1, 1)
    hidden = exchange(jax.nn.silu(pre_time), "all", False, 2).reshape(D, images_all)
    second_cols = col_block(second_start, D)
    shift_cols = col_block(final_start, D)
    scale_cols = col_block(final_start + D, D)
    pre_signal = (
        dense(second_cols, hidden)
        + col_block(vector_start + 2, 1)
        + dense(col_block(0, CLASSES), onehot.T)
    )
    signal = exchange(jax.nn.silu(pre_signal), "all", False, 3).reshape(D, images_all)
    final_send = jnp.concatenate(
        [
            dense(shift_cols, signal) + col_block(vector_start + 3, 1),
            dense(scale_cols, signal) + col_block(vector_start + 4, 1),
        ],
        axis=0,
    )
    final_all = exchange(final_send, "all", False, 4).reshape(place_count, 2, cols, images_all)
    final_own = lax.dynamic_slice_in_dim(final_all, dp_rank * images, images, 3)
    final_own = final_own.transpose(1, 3, 0, 2).reshape(2, images, D)
    final_shift, final_scale = final_own[0], final_own[1]
    signal_low = lax.dynamic_slice_in_dim(
        signal.astype(jnp.bfloat16), dp_rank * mod_rows, mod_rows, 0
    )
    mod_part = jnp.einsum("db,lde->ble", signal_low, mod_low, preferred_element_type=jnp.float32)
    mod_part = mod_part.reshape(dp_size, images * LAYERS, mod_cols)
    mod_local = jnp.sum(exchange(mod_part, "dp", True, 5), axis=0)
    mod_full = exchange(mod_local, "tensor", False, 6)
    mod_full = mod_full.reshape(tensor_size, images, LAYERS, mod_cols)
    mod_full = mod_full.transpose(2, 1, 0, 3).reshape(LAYERS, images, tensor_size * mod_cols)
    pixels = patchify(latents, local_rows)
    targets = patchify(target_noise, local_rows)
    keep_coef, drop_coef = noise_levels(timesteps)
    noisy = keep_coef[:, None, None] * pixels + drop_coef[:, None, None] * targets
    residual = (
        jnp.einsum("btp,pd->btd", noisy, patch_w, precision=PRECISE)
        + vectors[0]
        + position_table(tensor_rank * local_rows, local_rows)[None]
    )
    saved_acts = []
    shards_all = []
    for layer_idx in range(LAYERS):
        shard_in = layer_in[layer_idx, :, 0].astype(jnp.bfloat16)
        shard_out = layer_out[layer_idx, 0].astype(jnp.bfloat16)
        shards_all.append(
            (shard_in[:, : 3 * group_width], shard_in[:, 3 * group_width :], shard_out)
        )
    wholes = [lax.all_gather(shard, "dp") for shard in shards_all[0]]
    for layer_idx in range(LAYERS):
        bias_rows = bias_all[layer_idx * layer_rows : (layer_idx + 1) * layer_rows]
        up_all = bias_rows[10:].reshape(FF)
        ada_bias = bias_rows[0:6].reshape(6 * D)
        out_bias = bias_rows[6]
        down_bias = bias_rows[7]
        query_bias = lax.dynamic_slice_in_dim(bias_rows[8], tensor_rank * group_width, group_width)
        value_bias = lax.dynamic_slice_in_dim(bias_rows[9], tensor_rank * group_width, group_width)
        up_bias = lax.dynamic_slice_in_dim(up_all, tensor_rank * unit_count, unit_count)
        mod_vec = (mod_full[layer_idx] + ada_bias).reshape(images, 6, D)
        weight_out = wholes[2].reshape(group_width + unit_count, D)
        weights = (
            wholes[0].reshape(D, 3 * group_width),
            wholes[1].reshape(D, unit_count),
            weight_out[:group_width],
            weight_out[group_width:],
        )
        qkv_bias = jnp.concatenate(
            [query_bias, jnp.zeros((group_width,), jnp.float32), value_bias]
        )[None]
        outs = forward_layer(
            residual,
            mod_vec,
            jnp.stack([out_bias, down_bias]),
            qkv_bias,
            up_bias[None],
            *weights,
            shards_all[layer_idx + 1] if layer_idx + 1 < LAYERS else (),
        )
        wholes = outs[9:]
        saved_acts.append((mod_vec, (residual,) + tuple(outs[1:9]), weights))
        residual = outs[0]
    final_in, final_norm_pull = jax.vjp(modulate, residual, final_shift, final_scale)
    predicted = jnp.einsum("btd,pd->btp", final_in, head_w, precision=PRECISE)
    error_all = predicted - targets
    loss_part = jnp.sum(error_all * error_all) / count_all
    d_pred = 2.0 * error_all / count_all
    d_head = jnp.einsum("btp,btd->pd", d_pred, final_in, precision=PRECISE)
    d_final = jnp.einsum("btp,pd->btd", d_pred, head_w, precision=PRECISE)
    d_residual, d_final_shift, d_final_scale = final_norm_pull(d_final)
    totals = []
    terms = ()
    mod_parts = []
    bias_blocks = []
    for layer_idx in reversed(range(LAYERS)):
        mod_vec, saved, weights = saved_acts[layer_idx]
        outs = backward_layer(d_residual, mod_vec, saved, weights, terms)
        d_residual, d_w_qkv, d_w_up, d_w_out, d_mod_vec, d_vec, d_qkv_bias, d_up_bias = outs[:8]
        if terms:
            totals.insert(0, outs[8:])
        terms = [
            term.reshape((dp_size, -1) + term.shape[1:]) for term in (d_w_qkv, d_w_up, d_w_out)
        ]
        d_modulation = d_mod_vec.reshape(images, 6 * D)
        d_out_bias, d_down_bias = d_vec[0], d_vec[1]
        d_query_bias = d_qkv_bias[0, :group_width]
        d_value_bias = d_qkv_bias[0, 2 * group_width :]
        d_up_bias = d_up_bias[0]
        mod_parts.insert(0, d_modulation)
        query_row = lax.dynamic_update_slice_in_dim(
            jnp.zeros((D,), jnp.float32), d_query_bias, tensor_rank * group_width, 0
        )
        value_row = lax.dynamic_update_slice_in_dim(
            jnp.zeros((D,), jnp.float32), d_value_bias, tensor_rank * group_width, 0
        )
        up_rows = lax.dynamic_update_slice_in_dim(
            jnp.zeros((FF,), jnp.float32), d_up_bias, tensor_rank * unit_count, 0
        ).reshape(FF // D, D)
        bias_blocks.insert(
            0,
            jnp.concatenate(
                [
                    jnp.sum(d_modulation, axis=0).reshape(6, D),
                    d_out_bias[None],
                    d_down_bias[None],
                    query_row[None],
                    value_row[None],
                    up_rows,
                ],
                axis=0,
            ),
        )
    totals.insert(
        0,
        [
            lax.psum_scatter(term, "dp", scatter_dimension=0).astype(jnp.float32)
            for term in terms
        ],
    )
    d_patch_w = jnp.einsum("btp,btd->pd", noisy, d_residual, precision=PRECISE)
    d_patch_b = jnp.sum(d_residual, axis=(0, 1))
    row_parts = jnp.concatenate(
        [d_patch_w, d_head, d_patch_b[None]] + bias_blocks + [d_final_shift, d_final_scale],
        axis=0,
    )
    row_count = row_parts.shape[0]
    row_lanes = -(-row_count // 128) * 128
    row_parts = jnp.pad(row_parts, ((0, row_lanes - row_count), (0, 0)))
    row_all = exchange(row_parts.T.reshape(place_count, cols, row_lanes), "all", True, 7)
    row_sums = jnp.sum(row_all, axis=0)
    final_at = row_count - 2 * images
    final_sums = jnp.sum(
        row_all[:, :, final_at:row_count].reshape(dp_size, tensor_size, cols, 2, images), axis=1
    )
    final_sums = final_sums.transpose(2, 1, 0, 3).reshape(2, cols, images_all)
    d_shift_cols, d_scale_cols = final_sums[0], final_sums[1]
    mod_parts = jnp.stack(mod_parts).reshape(LAYERS * images, tensor_size, mod_cols)
    d_mod_own = jnp.sum(exchange(mod_parts.transpose(1, 0, 2), "tensor", True, 8), axis=0)
    d_mod_low = exchange(d_mod_own.astype(jnp.bfloat16), "dp", False, 9)
    d_mod_low = d_mod_low.reshape(dp_size, LAYERS, images, mod_cols)
    d_mod_low = d_mod_low.transpose(1, 0, 2, 3).reshape(LAYERS, images_all, mod_cols)
    mod_grad = jnp.einsum(
        "db,lbe->lde", signal_low, d_mod_low, preferred_element_type=jnp.float32
    )
    d_signal_rows = jnp.einsum(
        "lbe,lde->db", d_mod_low, mod_low, preferred_element_type=jnp.float32
    )
    d_signal_part = dense(shift_cols.T, d_shift_cols) + dense(scale_cols.T, d_scale_cols)
    d_signal_part = d_signal_part + lax.dynamic_update_slice_in_dim(
        jnp.zeros((D, images_all), jnp.float32), d_signal_rows, dp_rank * mod_rows, 0
    )
    d_signal_cols = jnp.sum(
        exchange(d_signal_part.reshape(place_count, cols, images_all), "all", True, 10), axis=0
    )
    d_pre_signal = d_signal_cols * silu_slope(pre_signal)
    d_hidden_part = dense(second_cols.T, d_pre_signal)
    d_hidden_cols = jnp.sum(
        exchange(d_hidden_part.reshape(place_count, cols, images_all), "all", True, 11), axis=0
    )
    d_hidden = d_hidden_cols * silu_slope(pre_time)
    table_grad = jnp.concatenate(
        [
            dense(d_pre_signal, onehot),
            row_sums[:, 0:patch_in],
            dense(d_hidden, time_feats),
            dense(d_pre_signal, hidden.T),
            dense(d_shift_cols, signal.T),
            dense(d_scale_cols, signal.T),
            row_sums[:, patch_in : 2 * patch_in + 1],
            jnp.sum(d_hidden, axis=1, keepdims=True),
            jnp.sum(d_pre_signal, axis=1, keepdims=True),
            jnp.sum(d_shift_cols, axis=1, keepdims=True),
            jnp.sum(d_scale_cols, axis=1, keepdims=True),
            row_sums[:, 2 * patch_in + 1 : final_at],
        ],
        axis=1,
    )
    input_grad = jnp.stack([jnp.concatenate(total[0:2], axis=1) for total in totals])
    input_grad = input_grad.reshape(layer_in.shape)
    output_grad = jnp.stack([total[2] for total in totals]).reshape(layer_out.shape)
    local_squares = (
        jnp.sum(table_grad * table_grad)
        + jnp.sum(input_grad * input_grad)
        + jnp.sum(output_grad * output_grad)
        + jnp.sum(mod_grad * mod_grad)
    )
    scalar_send = jnp.where(
        lax.broadcasted_iota(jnp.int32, (8, 128), 1) == 0, loss_part, local_squares
    )
    scalar_sums = jnp.sum(exchange(scalar_send, "all", False, 12)[:, 0, 0:2], axis=0)
    loss_value = scalar_sums[0]
    square_total = scalar_sums[1]
    grad_norm = jnp.sqrt(square_total)
    factor = jnp.minimum(1.0, CLIP_NORM / grad_norm)
    first_fix = 1.0 - BETA_ONE ** step_count.astype(jnp.float32)
    second_fix = 1.0 - BETA_TWO ** step_count.astype(jnp.float32)
    embed_out = adam_update(
        embed_table.T, embed_first.T, embed_second.T, table_grad, factor, first_fix, second_fix
    )
    input_out = adam_update(
        layer_in, input_first, input_second, input_grad, factor, first_fix, second_fix
    )
    output_out = adam_update(
        layer_out, output_first, output_second, output_grad, factor, first_fix, second_fix
    )
    mod_out = adam_update(layer_ada, mod_first, mod_second, mod_grad, factor, first_fix, second_fix)
    return (
        (loss_value, grad_norm, embed_out[4].T, embed_out[1].T, embed_out[2].T)
        + input_out[0:4]
        + output_out[0:4]
        + mod_out[0:4]
    )


def solution(mesh):
    placed = (
        P("dp", "tensor"),
        P("dp", "tensor"),
        P("dp"),
        P("dp"),
        P(),
        P(None, ("dp", "tensor")),
        P(None, "dp", "tensor", None),
        P(None, "tensor", "dp", None),
        P(None, "dp", "tensor"),
        P(None, ("dp", "tensor")),
        P(None, ("dp", "tensor")),
        P(None, "dp", "tensor", None),
        P(None, "dp", "tensor", None),
        P(None, "tensor", "dp", None),
        P(None, "tensor", "dp", None),
        P(None, "dp", "tensor"),
        P(None, "dp", "tensor"),
    )
    return jax.shard_map(
        local,
        mesh=mesh,
        in_specs=placed,
        out_specs=(
            P(),
            P(),
            P(None, ("dp", "tensor")),
            P(None, ("dp", "tensor")),
            P(None, ("dp", "tensor")),
            P(None, "dp", "tensor", None),
            P(None, "dp", "tensor", None),
            P(None, "dp", "tensor", None),
            P(None, "dp", "tensor", None),
            P(None, "tensor", "dp", None),
            P(None, "tensor", "dp", None),
            P(None, "tensor", "dp", None),
            P(None, "tensor", "dp", None),
            P(None, "dp", "tensor"),
            P(None, "dp", "tensor"),
            P(None, "dp", "tensor"),
            P(None, "dp", "tensor"),
        ),
        check_vma=False,
    )
```

```python
import functools
import math

import jax
import jax.numpy as jnp
from jax import lax
from jax.experimental import pallas as pl
from jax.experimental.pallas import tpu as pltpu
from jax.sharding import PartitionSpec as P

D = 768
HEADS = 12
HEAD_DIM = 64
FF = 3072
CLASSES = 1001
FREQ = 256
CHANNELS = 4
PATCH = 2
SIDE = 32
LAYERS = 3


EPS_NORM = 1e-06
LEARN_RATE = 0.01
DECAY = 0.01
BETA_ONE = 0.5
BETA_TWO = 0.5
ADAM_EPS = 1e-08
CLIP_NORM = 0.25
PRECISE = lax.Precision.HIGHEST


def dense(left_op, right_op):
    return jnp.dot(left_op, right_op, precision=PRECISE, preferred_element_type=jnp.float32)


def layer_norm(values):
    center = values - jnp.mean(values, axis=-1, keepdims=True)
    return center * lax.rsqrt(jnp.mean(center * center, axis=-1, keepdims=True) + EPS_NORM)


def modulate(values, shift_vec, scale_vec):
    return layer_norm(values) * (1.0 + scale_vec[:, None, :]) + shift_vec[:, None, :]


def gelu_tanh(values):
    return jax.nn.gelu(values, approximate=True)


def silu_slope(values):
    sigmoid_val = jax.nn.sigmoid(values)
    return sigmoid_val * (1.0 + values * (1.0 - sigmoid_val))


def time_features(step_ints):
    half_width = FREQ // 2
    frequency = jnp.exp(-math.log(10000.0) * jnp.arange(half_width, dtype=jnp.float32) / half_width)
    angles = step_ints.astype(jnp.float32)[:, None] * frequency[None, :]
    return jnp.concatenate([jnp.cos(angles), jnp.sin(angles)], axis=1)


def noise_levels(step_ints):
    base_cos = math.cos(0.008 / 1.008 * math.pi / 2)
    angles = (step_ints.astype(jnp.float32) / 1000.0 + 0.008) / 1.008 * (math.pi / 2)
    signal_level = jnp.cos(angles) ** 2 / base_cos**2
    return (jnp.sqrt(signal_level), jnp.sqrt(1.0 - signal_level))


def position_table(first_row, row_count):
    grid_side = SIDE // PATCH
    quarter = D // 4
    omegas = jnp.exp(-math.log(10000.0) * jnp.arange(quarter, dtype=jnp.float32) / quarter)
    token_index = jnp.arange(row_count * grid_side, dtype=jnp.int32)
    row_angle = (first_row + token_index // grid_side).astype(jnp.float32)[:, None] * omegas[
        None, :
    ]
    col_angle = (token_index % grid_side).astype(jnp.float32)[:, None] * omegas[None, :]
    return jnp.concatenate(
        [jnp.sin(row_angle), jnp.cos(row_angle), jnp.sin(col_angle), jnp.cos(col_angle)], axis=1
    )


def patchify(flat_pixels, row_count):
    grid_side = SIDE // PATCH
    shaped = flat_pixels.reshape(flat_pixels.shape[0], row_count, PATCH, grid_side, PATCH, CHANNELS)
    return shaped.transpose(0, 1, 3, 2, 4, 5).reshape(
        flat_pixels.shape[0], row_count * grid_side, PATCH * PATCH * CHANNELS
    )


def table_starts():
    patch_in = PATCH * PATCH * CHANNELS
    patch_start = CLASSES
    time_start = patch_start + patch_in
    second_start = time_start + FREQ
    final_start = second_start + D
    head_start = final_start + 2 * D
    vector_start = head_start + patch_in
    layer_start = vector_start + 5
    return (
        patch_start,
        time_start,
        second_start,
        final_start,
        head_start,
        vector_start,
        layer_start,
    )


def group_place(group):
    if group == "all":
        width = lax.axis_size("tensor")
        place = lax.axis_index("dp") * width + lax.axis_index("tensor")
        size = lax.axis_size("dp") * width
        return place, size, lambda at: {"dp": at // width, "tensor": lax.rem(at, width)}
    return lax.axis_index(group), lax.axis_size(group), lambda at: {group: at}


def greet_group(group):
    place, size, coords = group_place(group)
    barrier = pltpu.get_barrier_semaphore()

    def greet_one(step, carry):
        peer = coords(lax.rem(place + step, size))
        pl.semaphore_signal(barrier, inc=1, device_id=peer, device_id_type=pl.DeviceIdType.MESH)
        return carry

    lax.fori_loop(1, size, greet_one, 0)
    pl.semaphore_wait(barrier, size - 1)


class Crowd:
    def __init__(self, group, source_at, target, send_sems, recv_sems, local_sem):
        self.place, self.size, self.coords = group_place(group)
        self.source_at, self.target = source_at, target
        self.sends, self.recvs, self.local_sem = send_sems, recv_sems, local_sem

    def copy_to(self, step):
        there = lax.rem(self.place + step, self.size)
        return pltpu.make_async_remote_copy(
            src_ref=self.source_at(there),
            dst_ref=self.target.at[self.place],
            send_sem=self.sends.at[step],
            recv_sem=self.recvs.at[step],
            device_id=self.coords(there),
            device_id_type=pl.DeviceIdType.MESH,
        )

    def own_copy(self):
        return pltpu.make_async_copy(
            self.source_at(self.place), self.target.at[self.place], self.local_sem
        )

    def start(self):
        def begin(step, carry):
            self.copy_to(step).start()
            return carry

        lax.fori_loop(1, self.size, begin, 0)
        self.own_copy().start()

    def wait(self):
        def finish(step, carry):
            self.copy_to(step).wait()
            return carry

        self.own_copy().wait()
        lax.fori_loop(1, self.size, finish, 0)


def crowd_scratch(size):
    return [
        pltpu.SemaphoreType.DMA((size,)),
        pltpu.SemaphoreType.DMA((size,)),
        pltpu.SemaphoreType.DMA,
    ]


def exchange_kernel(group, spread, source, target, send_sems, recv_sems, local_sem):
    greet_group(group)
    crowd = Crowd(
        group,
        lambda place: source.at[place] if spread else source,
        target,
        send_sems,
        recv_sems,
        local_sem,
    )
    crowd.start()
    crowd.wait()


def exchange(values, group, spread, call_id):
    if group == "all":
        size = lax.axis_size("dp") * lax.axis_size("tensor")
    else:
        size = lax.axis_size(group)
    block = values.shape[1:] if spread else values.shape
    return pl.pallas_call(
        functools.partial(exchange_kernel, group, spread),
        out_shape=jax.ShapeDtypeStruct((size,) + block, values.dtype),
        in_specs=[pl.BlockSpec(memory_space=pltpu.VMEM)],
        out_specs=pl.BlockSpec(memory_space=pltpu.VMEM),
        scratch_shapes=crowd_scratch(size),
        compiler_params=pltpu.CompilerParams(
            collective_id=call_id, has_side_effects=True, vmem_limit_bytes=32 * 2**20
        ),
        name="exchange_" + group,
    )(values)


MESH = pl.DeviceIdType.MESH
ACT_VMEM = 60 * 2**20


def dot_nn(left_op, right_op):
    return jnp.dot(left_op, right_op, preferred_element_type=jnp.float32)


def dot_nt(left_op, right_op):
    return lax.dot_general(
        left_op, right_op, (((1,), (1,)), ((), ())), preferred_element_type=jnp.float32
    )


def dot_tn(left_op, right_op):
    return lax.dot_general(
        left_op, right_op, (((0,), (0,)), ((), ())), preferred_element_type=jnp.float32
    )


def norm_parts(values):
    center = values - jnp.mean(values, axis=-1, keepdims=True)
    rstd = lax.rsqrt(jnp.mean(center * center, axis=-1, keepdims=True) + EPS_NORM)
    return center * rstd, rstd


def greet(line):
    rank = lax.axis_index("tensor")
    half = lax.axis_size("tensor") // 2
    core_peer = {"tensor": rank + 1 - 2 * lax.rem(rank, 2)}
    chip_peer = {"tensor": lax.rem(rank + half, 2 * half)}
    barrier = pltpu.get_barrier_semaphore()
    for peer in (core_peer, chip_peer):
        pl.semaphore_signal(barrier, inc=1, device_id=peer, device_id_type=MESH)
    count = 2
    if line is not None:
        line.greet()
        count = count + line.answers()
    pl.semaphore_wait(barrier, count)


class Spread:
    def __init__(self, rows_ref, send_sems, recv_sems):
        self.rows, self.send, self.recv = rows_ref, send_sems, recv_sems
        self.rank = lax.axis_index("tensor")
        self.own_core = lax.rem(self.rank, 2)
        self.core_peer = self.rank + 1 - 2 * self.own_core
        self.chip_peer = lax.rem(self.rank + 2, 4)
        self.count = rows_ref.shape[1] // 4

    def block(self, image, owner):
        return self.rows.at[image, pl.ds(pl.multiple_of(owner * self.count, 16), self.count), :]

    def copy(self, image, owner, peer, which):
        return pltpu.make_async_remote_copy(
            src_ref=self.block(image, owner),
            dst_ref=self.block(image, owner),
            send_sem=self.send.at[image, which],
            recv_sem=self.recv.at[image, which],
            device_id={"tensor": peer},
            device_id_type=MESH,
        )

    def put(self, image, values):
        self.rows[image, pl.ds(pl.multiple_of(self.rank * self.count, 16), self.count), :] = values
        self.copy(image, self.rank, self.chip_peer, 0).start()
        self.copy(image, self.rank, self.core_peer, 1).start()

    def forward(self, image):
        self.copy(image, self.rank, self.chip_peer, 0).wait_recv()
        self.copy(image, self.chip_peer, self.core_peer, 2).start()

    def wait(self, image):
        self.copy(image, self.rank, self.core_peer, 1).wait_recv()
        self.copy(image, self.chip_peer, self.core_peer, 2).wait_recv()

    def close(self, image):
        self.copy(image, self.rank, self.chip_peer, 0).wait_send()
        self.copy(image, self.rank, self.core_peer, 1).wait_send()
        self.copy(image, self.chip_peer, self.core_peer, 2).wait_send()


class Collect:
    def __init__(self, part, near, far_out, far_in, send_sems, recv_sems):
        self.part, self.near, self.far_out, self.far_in = part, near, far_out, far_in
        self.send, self.recv = send_sems, recv_sems
        self.rank = lax.axis_index("tensor")
        self.own_core = lax.rem(self.rank, 2)
        self.own_chip = self.rank // 2
        self.core_peer = self.rank + 1 - 2 * self.own_core
        self.chip_peer = lax.rem(self.rank + 2, 4)
        self.count = part.shape[1] // 4

    def block(self, image, owner):
        return self.part.at[image, pl.ds(pl.multiple_of(owner * self.count, 16), self.count), :]

    def near_copy(self, image, far):
        chip = 1 - self.own_chip if far else self.own_chip
        return pltpu.make_async_remote_copy(
            src_ref=self.block(image, 2 * chip + 1 - self.own_core),
            dst_ref=self.near.at[image, far],
            send_sem=self.send.at[image, far],
            recv_sem=self.recv.at[image, far],
            device_id={"tensor": self.core_peer},
            device_id_type=MESH,
        )

    def far_copy(self, image):
        return pltpu.make_async_remote_copy(
            src_ref=self.far_out.at[image],
            dst_ref=self.far_in.at[image],
            send_sem=self.send.at[image, 2],
            recv_sem=self.recv.at[image, 2],
            device_id={"tensor": self.chip_peer},
            device_id_type=MESH,
        )

    def put(self, image, values):
        self.part[image] = values.astype(jnp.bfloat16)
        self.near_copy(image, 1).start()
        self.near_copy(image, 0).start()

    def load(self, image, owner):
        at = pl.ds(pl.multiple_of(owner * self.count, 16), self.count)
        return self.part[image, at, :].astype(jnp.float32)

    def forward(self, image):
        self.near_copy(image, 1).wait_recv()
        total = self.load(image, self.chip_peer) + self.near[image, 1].astype(jnp.float32)
        self.far_out[image] = total.astype(jnp.bfloat16)
        self.far_copy(image).start()

    def take(self, image):
        self.near_copy(image, 0).wait_recv()
        total = self.load(image, self.rank) + self.near[image, 0].astype(jnp.float32)
        self.far_copy(image).wait_recv()
        return total + self.far_in[image].astype(jnp.float32)

    def close(self, image):
        self.near_copy(image, 1).wait_send()
        self.near_copy(image, 0).wait_send()
        self.far_copy(image).wait_send()


def collect_scratch(images, tokens):
    count = tokens // 4
    return [
        pltpu.VMEM((images, tokens, D), jnp.bfloat16),
        pltpu.VMEM((images, 2, count, D), jnp.bfloat16),
        pltpu.VMEM((images, count, D), jnp.bfloat16),
        pltpu.VMEM((images, count, D), jnp.bfloat16),
    ]


def each(count, body):
    def step(index, carry):
        body(index)
        return carry

    lax.fori_loop(0, count, step, 0)


class Line:
    def __init__(self):
        self.size = lax.axis_size("dp") // 2
        self.place = lax.axis_index("dp")
        self.at = self.place // 2
        self.side = lax.rem(self.place, 2)
        self.pair = self.place + 1 - 2 * self.side
        self.has_up = self.at + 1 < self.size
        self.has_down = self.at > 0

    def greet(self):
        barrier = pltpu.get_barrier_semaphore()
        pl.semaphore_signal(barrier, inc=1, device_id={"dp": self.pair}, device_id_type=MESH)

        @pl.when(self.has_up)
        def _():
            up = {"dp": self.place + 2}
            pl.semaphore_signal(barrier, inc=1, device_id=up, device_id_type=MESH)

        @pl.when(self.has_down)
        def _():
            down = {"dp": self.place - 2}
            pl.semaphore_signal(barrier, inc=1, device_id=down, device_id_type=MESH)

    def answers(self):
        return 1 + self.has_up.astype(jnp.int32) + self.has_down.astype(jnp.int32)


UP, DOWN, PAIR = 0, 1, 2


class Gather:
    def __init__(self, line, shards, wholes, sends, recvs, local_sems):
        self.line, self.shards, self.wholes = line, shards, wholes
        self.sends, self.recvs, self.local_sems = sends, recvs, local_sems

    def copy(self, part, way, step, owner, fresh=False):
        line = self.line
        there = {UP: line.place + 2, DOWN: line.place - 2, PAIR: line.pair}[way]
        return pltpu.make_async_remote_copy(
            src_ref=self.shards[part] if fresh else self.wholes[part].at[owner],
            dst_ref=self.wholes[part].at[owner],
            send_sem=self.sends.at[way, step, part],
            recv_sem=self.recvs.at[way, step, part],
            device_id={"dp": there},
            device_id_type=MESH,
        )

    def local_copy(self, part):
        return pltpu.make_async_copy(
            self.shards[part], self.wholes[part].at[self.line.place], self.local_sems.at[part]
        )

    def start(self):
        line = self.line
        parts = range(len(self.shards))

        @pl.when(line.has_up)
        def _():
            for part in parts:
                self.copy(part, UP, 0, line.place, True).start()

        @pl.when(line.has_down)
        def _():
            for part in parts:
                self.copy(part, DOWN, 0, line.place, True).start()

        for part in parts:
            self.copy(part, PAIR, line.at, line.place, True).start()
            self.local_copy(part).start()

    def tick(self, step):
        line = self.line
        parts = range(len(self.shards))
        for way, there, can in ((UP, -step, line.has_up), (DOWN, step, line.has_down)):
            owner = line.place + 2 * there
            spot = line.at + there

            @pl.when((spot >= 0) & (spot < line.size))
            def _(way=way, can=can, owner=owner, spot=spot):
                for part in parts:
                    self.copy(part, way, step - 1, owner).wait_recv()

                @pl.when(can)
                def _():
                    for part in parts:
                        self.copy(part, way, step, owner).start()

                for part in parts:
                    self.copy(part, PAIR, spot, owner).start()

    def finish(self):
        line = self.line
        parts = range(len(self.shards))
        for part in parts:
            self.local_copy(part).wait()

        def side(spot):
            for part in parts:
                self.copy(part, PAIR, spot, 2 * spot + line.side).wait()

        each(line.size, side)

        def along(step):
            for way, there, can in ((UP, -step, line.has_up), (DOWN, step, line.has_down)):
                spot = line.at + there

                @pl.when((spot >= 0) & (spot < line.size) & can)
                def _(way=way, there=there):
                    for part in parts:
                        self.copy(part, way, step, line.place + 2 * there).wait_send()

        each(line.size, along)


class Reduce:
    def __init__(self, line, terms, totals, pair_in, way_in, way_out, sends, recvs):
        self.line, self.terms, self.totals = line, terms, totals
        self.pair_in, self.way_in, self.way_out = pair_in, way_in, way_out
        self.sends, self.recvs = sends, recvs

    def pair_copy(self, part, spot):
        return pltpu.make_async_remote_copy(
            src_ref=self.terms[part].at[2 * spot + 1 - self.line.side],
            dst_ref=self.pair_in[part].at[spot],
            send_sem=self.sends.at[PAIR, spot, part],
            recv_sem=self.recvs.at[PAIR, spot, part],
            device_id={"dp": self.line.pair},
            device_id_type=MESH,
        )

    def way_copy(self, part, way, spot):
        there = self.line.place + 2 if way == UP else self.line.place - 2
        return pltpu.make_async_remote_copy(
            src_ref=self.way_out[part].at[way, spot],
            dst_ref=self.way_in[part].at[way, spot],
            send_sem=self.sends.at[way, spot, part],
            recv_sem=self.recvs.at[way, spot, part],
            device_id={"dp": there},
            device_id_type=MESH,
        )

    def start(self):
        last = self.line.size - 1

        def outer(step):
            for part in range(len(self.terms)):
                self.pair_copy(part, last - step).start()

            @pl.when(last - step > step)
            def _():
                for part in range(len(self.terms)):
                    self.pair_copy(part, step).start()

        each((self.line.size + 1) // 2, outer)

    def pair_sum(self, part, spot):
        own = self.terms[part][2 * spot + self.line.side].astype(jnp.float32)
        return own + self.pair_in[part][spot].astype(jnp.float32)

    def pass_on(self, way, spot, more):
        for part in range(len(self.terms)):
            self.pair_copy(part, spot).wait_recv()
            self.way_out[part][way, spot] = self.pair_sum(part, spot).astype(jnp.bfloat16)

            @pl.when(more)
            def _(part=part):
                self.way_copy(part, way, spot).wait_recv()
                self.way_out[part][way, spot] = (
                    self.pair_sum(part, spot) + self.way_in[part][way, spot].astype(jnp.float32)
                ).astype(jnp.bfloat16)

            self.way_copy(part, way, spot).start()

    def tick(self, step):
        line = self.line
        last = line.size - 1

        @pl.when(last - step > line.at)
        def _():
            self.pass_on(UP, last - step, line.has_down)

        @pl.when(line.at > step)
        def _():
            self.pass_on(DOWN, step, line.has_up)

    def finish(self):
        line = self.line
        spot = line.at
        for part in range(len(self.terms)):
            self.pair_copy(part, spot).wait_recv()
            self.totals[part][...] = self.pair_sum(part, spot)
        for way, can in ((UP, line.has_down), (DOWN, line.has_up)):

            @pl.when(can)
            def _(way=way):
                for part in range(len(self.terms)):
                    self.way_copy(part, way, spot).wait_recv()
                    self.totals[part][...] += self.way_in[part][way, spot].astype(jnp.float32)

        def close(spot):
            for part in range(len(self.terms)):
                self.pair_copy(part, spot).wait_send()
            for way, passed in ((UP, spot > line.at), (DOWN, spot < line.at)):

                @pl.when(passed)
                def _(way=way):
                    for part in range(len(self.terms)):
                        self.way_copy(part, way, spot).wait_send()

        each(line.size, close)


def run_ticks(task, first, last):
    if task is not None:
        for step in range(first, last):
            task.tick(step)


def head_slice(matrix, head):
    return matrix[:, head * HEAD_DIM : (head + 1) * HEAD_DIM]


def soft_rows(queries, keys_in):
    scores = dot_nt(queries, keys_in) * (HEAD_DIM ** (-0.5))
    exponent = jnp.exp(scores - jnp.max(scores, axis=-1, keepdims=True))
    return exponent / jnp.sum(exponent, axis=-1, keepdims=True)


def forward_kernel(
    res_ref,
    mod_ref,
    vec_ref,
    qkv_bias_ref,
    up_bias_ref,
    w_qkv_ref,
    w_up_ref,
    w_attn_ref,
    w_down_ref,
    *rest,
):
    with_gather = len(rest) > 19
    shards, rest = (rest[:3], rest[3:]) if with_gather else ((), rest)
    (
        res_out,
        rows_a,
        qkv_out,
        mixed_out,
        branch_out,
        mid_out,
        rows_m,
        upper_out,
        down_out,
    ) = rest[:9]
    wholes, rest = (rest[9:12], rest[12:]) if with_gather else ((), rest[9:])
    (
    part_a,
    near_a,
    far_out_a,
    far_in_a,
    part_m,
    near_m,
    far_out_m,
    far_in_m,
    sends,
    recvs,
    ) = rest[:10]
    images = res_ref.shape[0]
    group_width = w_attn_ref.shape[0]
    gather, last_step = None, 0
    if with_gather:
        line = Line()
        greet(line)
        gather = Gather(line, shards, wholes, *rest[10:])
        last_step = line.size
    else:
        greet(None)
    spread_a = Spread(rows_a, sends.at[0], recvs.at[0])
    spread_m = Spread(rows_m, sends.at[1], recvs.at[1])
    collect_a = Collect(part_a, near_a, far_out_a, far_in_a, sends.at[2], recvs.at[2])
    collect_m = Collect(part_m, near_m, far_out_m, far_in_m, sends.at[3], recvs.at[3])

    def mod_row(image, piece):
        return mod_ref[image, pl.ds(piece, 1), :]

    def start_norm(image):
        normed, _ = norm_parts(res_ref[image])
        normed = normed * (1.0 + mod_row(image, 1)) + mod_row(image, 0)
        spread_a.put(image, normed.astype(jnp.bfloat16))

    def attend(image):
        spread_a.wait(image)
        rows = rows_a[image]
        projected = dot_nn(rows, w_qkv_ref[...]) + qkv_bias_ref[...]
        qkv = projected.astype(jnp.bfloat16)
        qkv_out[image] = qkv
        heads = []
        for head in range(group_width // HEAD_DIM):
            probs = soft_rows(
                head_slice(qkv[:, :group_width], head),
                head_slice(qkv[:, group_width : 2 * group_width], head),
            )
            heads.append(
                dot_nn(probs.astype(jnp.bfloat16), head_slice(qkv[:, 2 * group_width :], head))
            )
        mixed = jnp.concatenate(heads, axis=1).astype(jnp.bfloat16)
        mixed_out[image] = mixed
        collect_a.put(image, dot_nn(mixed, w_attn_ref[...]))

    def middle(image):
        branch = collect_a.take(image) + vec_ref[0:1, :]
        branch_out[image] = branch
        mid = res_ref[image] + mod_row(image, 2) * branch
        mid_out[image] = mid
        normed, _ = norm_parts(mid)
        normed = normed * (1.0 + mod_row(image, 4)) + mod_row(image, 3)
        spread_m.put(image, normed.astype(jnp.bfloat16))

    def feed(image):
        spread_m.wait(image)
        upper = dot_nn(rows_m[image], w_up_ref[...]) + up_bias_ref[...]
        upper_out[image] = upper
        collect_m.put(image, dot_nn(gelu_tanh(upper).astype(jnp.bfloat16), w_down_ref[...]))

    def finish(image):
        down = collect_m.take(image) + vec_ref[1:2, :]
        down_out[image] = down
        res_out[image] = mid_out[image] + mod_row(image, 5) * down

    def close(image):
        spread_a.close(image)
        spread_m.close(image)
        collect_a.close(image)
        collect_m.close(image)

    each(images, start_norm)
    if with_gather:
        gather.start()
    each(images, spread_a.forward)
    each(images, attend)
    run_ticks(gather, 1, min(2, last_step))
    each(images, collect_a.forward)
    each(images, middle)
    each(images, spread_m.forward)
    run_ticks(gather, 2, min(3, last_step))
    each(images, feed)
    run_ticks(gather, 3, min(4, last_step))
    each(images, collect_m.forward)
    each(images, finish)
    each(images, close)
    if with_gather:
        each(max(last_step - 4, 0), lambda step: gather.tick(step + 4))
        gather.finish()


def forward_layer(
    residual, mod_vec, vec_bias, qkv_bias, up_bias, w_qkv, w_up, w_attn, w_down, shards
):
    images, count, _ = residual.shape
    tokens = 4 * count
    low, full = jnp.bfloat16, jnp.float32
    shapes = [
        ((images, count, D), full),
        ((images, tokens, D), low),
        ((images, tokens, w_qkv.shape[1]), low),
        ((images, tokens, w_attn.shape[0]), low),
        ((images, count, D), full),
        ((images, count, D), full),
        ((images, tokens, D), low),
        ((images, tokens, w_up.shape[1]), full),
        ((images, count, D), full),
    ]
    scratch = [
        pltpu.SemaphoreType.DMA((4, images, 3)),
        pltpu.SemaphoreType.DMA((4, images, 3)),
    ]
    if shards:
        dp_size = lax.axis_size("dp")
        shapes += [((dp_size,) + shard.shape, low) for shard in shards]
        scratch += [
            pltpu.SemaphoreType.DMA((3, dp_size // 2, 3)),
            pltpu.SemaphoreType.DMA((3, dp_size // 2, 3)),
            pltpu.SemaphoreType.DMA((3,)),
        ]
    return pl.pallas_call(
        forward_kernel,
        out_shape=[jax.ShapeDtypeStruct(*shape) for shape in shapes],
        in_specs=[pl.BlockSpec(memory_space=pltpu.VMEM)] * (9 + len(shards)),
        out_specs=[pl.BlockSpec(memory_space=pltpu.VMEM)] * len(shapes),
        scratch_shapes=collect_scratch(images, tokens) + collect_scratch(images, tokens) + scratch,
        compiler_params=pltpu.CompilerParams(
            collective_id=20 if shards else 22, has_side_effects=True, vmem_limit_bytes=ACT_VMEM
        ),
        cost_estimate=pl.CostEstimate(
            flops=30 * 10**9, bytes_accessed=15 * 2**20, transcendentals=0
        ),
        name="block_forward",
    )(residual, mod_vec, vec_bias, qkv_bias, up_bias, w_qkv, w_up, w_attn, w_down, *shards)


def gelu_slope(values):
    root = math.sqrt(2.0 / math.pi)
    square = values * values
    tanh = jnp.tanh(root * (values + 0.044715 * values * square))
    half = 0.5 * (1.0 + tanh)
    slope = half + 0.5 * values * (1.0 - tanh * tanh) * root * (1.0 + 3.0 * 0.044715 * square)
    return values * half, slope


def norm_pull(values, scale_row, d_normed):
    normed, rstd = norm_parts(values)
    d_shift = jnp.sum(d_normed, axis=0, keepdims=True)
    d_scale = jnp.sum(d_normed * normed, axis=0, keepdims=True)
    inner = d_normed * (1.0 + scale_row)
    mean_one = jnp.mean(inner, axis=-1, keepdims=True)
    mean_two = jnp.mean(inner * normed, axis=-1, keepdims=True)
    return (inner - mean_one - normed * mean_two) * rstd, d_shift, d_scale


def backward_kernel(
    d_res_ref,
    mod_ref,
    res_ref,
    rows_a,
    qkv_ref,
    mixed_ref,
    branch_ref,
    mid_ref,
    rows_m,
    upper_ref,
    down_ref,
    w_qkv_ref,
    w_up_ref,
    w_attn_ref,
    w_down_ref,
    *rest,
):
    with_reduce = len(rest) > 24
    terms, rest = (rest[:3], rest[3:]) if with_reduce else ((), rest)
    (
        d_res_out,
        d_w_qkv,
        d_w_up,
        d_out,
        d_mod,
        d_vec,
        d_qkv_bias,
        d_up_bias,
    ) = rest[:8]
    totals, rest = (rest[8:11], rest[11:]) if with_reduce else ((), rest[8:])
    (
    d_mid,
    d_rows_m,
    d_rows_a,
    act_low,
    d_upper,
    d_qkv,
    part_a,
    near_a,
    far_out_a,
    far_in_a,
    part_m,
    near_m,
    far_out_m,
    far_in_m,
    sends,
    recvs,
    ) = rest[:16]
    images = res_ref.shape[0]
    tokens = rows_a.shape[1]
    group_width = w_attn_ref.shape[0]
    qkv_width = 3 * group_width
    units = w_up_ref.shape[1]
    reduce, last_step = None, 0
    if with_reduce:
        line = Line()
        greet(line)
        pair_in, way_in, way_out = rest[16:19], rest[19:22], rest[22:25]
        reduce = Reduce(line, terms, totals, pair_in, way_in, way_out, *rest[25:])
        last_step = line.size
    else:
        greet(None)
    spread_m = Spread(d_rows_m, sends.at[0], recvs.at[0])
    spread_a = Spread(d_rows_a, sends.at[1], recvs.at[1])
    collect_m = Collect(part_m, near_m, far_out_m, far_in_m, sends.at[2], recvs.at[2])
    collect_a = Collect(part_a, near_a, far_out_a, far_in_a, sends.at[3], recvs.at[3])
    d_vec[...] = jnp.zeros_like(d_vec)
    d_qkv_bias[...] = jnp.zeros_like(d_qkv_bias)
    d_up_bias[...] = jnp.zeros_like(d_up_bias)

    def mod_row(image, piece):
        return mod_ref[image, pl.ds(piece, 1), :]

    def start_down(image):
        d_res = d_res_ref[image]
        d_mod[image, pl.ds(5, 1), :] = jnp.sum(d_res * down_ref[image], axis=0, keepdims=True)
        d_down = d_res * mod_row(image, 5)
        d_vec[1:2, :] += jnp.sum(d_down, axis=0, keepdims=True)
        spread_m.put(image, d_down.astype(jnp.bfloat16))

    def feed(image):
        spread_m.wait(image)
        d_act = dot_nt(d_rows_m[image], w_down_ref[...])
        act, slope = gelu_slope(upper_ref[image])
        act_low[image] = act.astype(jnp.bfloat16)
        d_up = d_act * slope
        d_up_bias[...] += jnp.sum(d_up, axis=0, keepdims=True)
        d_up_low = d_up.astype(jnp.bfloat16)
        d_upper[image] = d_up_low
        collect_m.put(image, dot_nt(d_up_low, w_up_ref[...]))

    def rows_of(ref, width):
        return ref[...].reshape(images * tokens, width)

    def feed_weights():
        tile = 256

        def step(index, carry):
            at = pl.ds(pl.multiple_of(index * tile, tile), tile)
            grad = dot_tn(
                act_low[:, :, at].reshape(images * tokens, tile), rows_of(d_rows_m, D)
            )
            d_out[pl.ds(pl.multiple_of(group_width + index * tile, 64), tile), :] = grad.astype(
                jnp.bfloat16
            )
            grad = dot_tn(
                rows_m[:, :, at].reshape(images * tokens, tile), rows_of(d_upper, units)
            )
            d_w_up[pl.ds(pl.multiple_of(index * tile, tile), tile), :] = grad.astype(jnp.bfloat16)
            return carry

        lax.fori_loop(0, units // tile, step, 0)

    def middle(image):
        d_value, d_shift, d_scale = norm_pull(
            mid_ref[image], mod_row(image, 4), collect_m.take(image)
        )
        d_mod[image, pl.ds(3, 1), :] = d_shift
        d_mod[image, pl.ds(4, 1), :] = d_scale
        d_value = d_res_ref[image] + d_value
        d_mid[image] = d_value
        d_mod[image, pl.ds(2, 1), :] = jnp.sum(d_value * branch_ref[image], axis=0, keepdims=True)
        d_branch = d_value * mod_row(image, 2)
        d_vec[0:1, :] += jnp.sum(d_branch, axis=0, keepdims=True)
        spread_a.put(image, d_branch.astype(jnp.bfloat16))

    def attend(image):
        spread_a.wait(image)
        d_mixed = dot_nt(d_rows_a[image], w_attn_ref[...]).astype(jnp.bfloat16)
        qkv = qkv_ref[image]
        d_queries, d_keys, d_values = [], [], []
        scale_dot = HEAD_DIM ** (-0.5)
        for head in range(group_width // HEAD_DIM):
            queries = head_slice(qkv[:, :group_width], head)
            keys_in = head_slice(qkv[:, group_width : 2 * group_width], head)
            values_in = head_slice(qkv[:, 2 * group_width :], head)
            d_head = head_slice(d_mixed, head)
            probs = soft_rows(queries, keys_in)
            d_probs = dot_nt(d_head, values_in)
            d_values.append(dot_tn(probs.astype(jnp.bfloat16), d_head))
            inner = jnp.sum(probs * d_probs, axis=-1, keepdims=True)
            d_scores = (probs * (d_probs - inner)).astype(jnp.bfloat16)
            d_queries.append(dot_nn(d_scores, keys_in) * scale_dot)
            d_keys.append(dot_tn(d_scores, queries) * scale_dot)
        joined = jnp.concatenate(d_queries + d_keys + d_values, axis=1)
        d_qkv_bias[...] += jnp.sum(joined, axis=0, keepdims=True)
        joined = joined.astype(jnp.bfloat16)
        d_qkv[image] = joined
        collect_a.put(image, dot_nt(joined, w_qkv_ref[...]))

    def attend_weights():
        d_out[0:group_width, :] = dot_tn(
            rows_of(mixed_ref, group_width), rows_of(d_rows_a, D)
        ).astype(jnp.bfloat16)
        tile = 256

        def step(index, carry):
            at = pl.ds(pl.multiple_of(index * tile, tile), tile)
            grad = dot_tn(
                rows_a[:, :, at].reshape(images * tokens, tile), rows_of(d_qkv, qkv_width)
            )
            d_w_qkv[at, :] = grad.astype(jnp.bfloat16)
            return carry

        lax.fori_loop(0, D // tile, step, 0)

    def finish(image):
        d_value, d_shift, d_scale = norm_pull(
            res_ref[image], mod_row(image, 1), collect_a.take(image)
        )
        d_mod[image, pl.ds(0, 1), :] = d_shift
        d_mod[image, pl.ds(1, 1), :] = d_scale
        d_res_out[image] = d_mid[image] + d_value

    def close(image):
        spread_a.close(image)
        spread_m.close(image)
        collect_a.close(image)
        collect_m.close(image)

    each(images, start_down)
    if with_reduce:
        reduce.start()
    each(images, spread_m.forward)
    each(images, feed)
    each(images, collect_m.forward)
    feed_weights()
    run_ticks(reduce, 0, min(1, last_step))
    each(images, middle)
    each(images, spread_a.forward)
    run_ticks(reduce, 1, min(2, last_step))
    each(images, attend)
    run_ticks(reduce, 2, min(3, last_step))
    each(images, collect_a.forward)
    attend_weights()
    run_ticks(reduce, 3, min(4, last_step))
    each(images, finish)
    each(images, close)
    if with_reduce:
        each(max(last_step - 4, 0), lambda step: reduce.tick(step + 4))
        reduce.finish()


def backward_layer(d_residual, mod_vec, saved, weights, terms):
    images, count, _ = d_residual.shape
    tokens = 4 * count
    low, full = jnp.bfloat16, jnp.float32
    w_qkv, w_up, w_attn, w_down = weights
    group_width, units = w_attn.shape[0], w_up.shape[1]
    shapes = [
        ((images, count, D), full),
        ((D, 3 * group_width), low),
        ((D, units), low),
        ((group_width + units, D), low),
        ((images, 6, D), full),
        ((2, D), full),
        ((1, 3 * group_width), full),
        ((1, units), full),
    ]
    scratch = [
        pltpu.SemaphoreType.DMA((4, images, 3)),
        pltpu.SemaphoreType.DMA((4, images, 3)),
    ]
    if terms:
        spots = lax.axis_size("dp") // 2
        blocks = [term.shape[1:] for term in terms]
        shapes += [(block, full) for block in blocks]
        scratch += [pltpu.VMEM((spots,) + block, low) for block in blocks]
        scratch += [pltpu.VMEM((2, spots) + block, low) for block in blocks]
        scratch += [pltpu.VMEM((2, spots) + block, low) for block in blocks]
        scratch += [
            pltpu.SemaphoreType.DMA((3, spots, 3)),
            pltpu.SemaphoreType.DMA((3, spots, 3)),
        ]
    return pl.pallas_call(
        backward_kernel,
        out_shape=[jax.ShapeDtypeStruct(*shape) for shape in shapes],
        in_specs=[pl.BlockSpec(memory_space=pltpu.VMEM)] * (15 + len(terms)),
        out_specs=[pl.BlockSpec(memory_space=pltpu.VMEM)] * len(shapes),
        scratch_shapes=[
            pltpu.VMEM((images, count, D), full),
            pltpu.VMEM((images, tokens, D), low),
            pltpu.VMEM((images, tokens, D), low),
            pltpu.VMEM((images, tokens, units), low),
            pltpu.VMEM((images, tokens, units), low),
            pltpu.VMEM((images, tokens, 3 * group_width), low),
        ]
        + collect_scratch(images, tokens)
        + collect_scratch(images, tokens)
        + scratch,
        compiler_params=pltpu.CompilerParams(
            collective_id=21 if terms else 23, has_side_effects=True, vmem_limit_bytes=ACT_VMEM
        ),
        cost_estimate=pl.CostEstimate(
            flops=60 * 10**9, bytes_accessed=25 * 2**20, transcendentals=0
        ),
        name="block_backward",
    )(d_residual, mod_vec, *saved, *weights, *terms)


def dense_nt(left_op, right_op):
    return lax.dot_general(
        left_op,
        right_op,
        (((1,), (1,)), ((), ())),
        precision=PRECISE,
        preferred_element_type=jnp.float32,
    )


def dense_tn(left_op, right_op):
    return lax.dot_general(
        left_op,
        right_op,
        (((0,), (0,)), ((), ())),
        precision=PRECISE,
        preferred_element_type=jnp.float32,
    )


def chosen(shape, rule, kind):
    row = lax.broadcasted_iota(jnp.int32, shape, 0)
    col = lax.broadcasted_iota(jnp.int32, shape, 1)
    return jnp.where(rule(row, col), 1.0, 0.0).astype(kind)


def fold(values):
    groups = values.shape[-2] // 8
    pieces = [values[..., 8 * at : 8 * at + 8, :] for at in range(groups)]
    used = groups * values.shape[-1]
    if used % 128:
        pieces.append(jnp.zeros(values.shape[:-2] + (8, 128 - used % 128), values.dtype))
    return jnp.concatenate(pieces, axis=-1)


def folded_lanes(cols, count):
    return -(-(cols // 8 * count) // 128) * 128


def unfold(values, cols, count):
    pieces = [values[..., at * count : (at + 1) * count] for at in range(cols // 8)]
    return jnp.concatenate(pieces, axis=-2)


def slots_of(images):
    return -(-LAYERS * images // 16) * 16


def head_kernel(
    images,
    small_ref,
    feats_ref,
    table_ref,
    time_ref,
    second_ref,
    shift_ref,
    scale_ref,
    bias_ref,
    mod_ref,
    *rest,
):
    shards = rest[0:3]
    (
        small_all,
        feats_out,
        pre_time_out,
        hidden_out,
        pre_signal_out,
        signal_out,
        final_all,
        mod_all,
    ) = rest[3:11]
    wholes = rest[11:14]
    (
        feats_all,
        hidden_own,
        hidden_all,
        signal_own,
        signal_all,
        final_own,
        mod_part,
        mod_in,
        mod_own,
        small_dp,
    ) = rest[14:24]
    crowds = [rest[24 + 3 * index : 27 + 3 * index] for index in range(8)]
    gather_sems = rest[48:]
    dp_size = lax.axis_size("dp")
    tensor_size = lax.axis_size("tensor")
    dp_rank = lax.axis_index("dp")
    images_all = images * dp_size
    slots = mod_own.shape[0]
    greet_group("all")
    gather = Gather(Line(), shards, wholes, *gather_sems)
    feats = Crowd("dp", lambda place: feats_ref, feats_all, *crowds[0])
    small = Crowd("dp", lambda place: small_ref, small_dp, *crowds[1])
    small_spread = Crowd("tensor", lambda place: small_dp, small_all, *crowds[7])
    hidden = Crowd("all", lambda place: hidden_own, hidden_all, *crowds[2])
    signal = Crowd("all", lambda place: signal_own, signal_all, *crowds[3])
    final = Crowd("all", lambda place: final_own.at[place // tensor_size], final_all, *crowds[4])
    mod_sum = Crowd("dp", lambda place: mod_part.at[place], mod_in, *crowds[5])
    feats.start()
    small.start()
    gather.start()
    feats.wait()
    pick = chosen(
        (images_all, 8 * dp_size),
        lambda row, col: (row // images == col // 8) & (lax.rem(row, images) == lax.rem(col, 8)),
        jnp.float32,
    )
    feats_sum = dense(pick, feats_all[...].reshape(8 * dp_size, feats_all.shape[2]))
    feats_out[...] = feats_sum
    pre_time = dense_nt(time_ref[...], feats_sum[:, 0:FREQ]) + bias_ref[:, 1:2]
    pre_time_out[...] = pre_time
    hidden_own[...] = fold(jax.nn.silu(pre_time))
    hidden.start()
    class_lanes = -(-CLASSES // 128) * 128
    labels = jnp.round(feats_sum[:, FREQ : FREQ + 1]).astype(jnp.int32)
    lane = lax.broadcasted_iota(jnp.int32, (images_all, class_lanes), 1)
    onehot = jnp.where(lane == labels, 1.0, 0.0)
    class_part = dense_nt(table_ref[:, 0:class_lanes], onehot) + bias_ref[:, 2:3]
    gather.tick(1)
    hidden.wait()
    cols = second_ref.shape[0]
    hidden_full = unfold(hidden_all[...], cols, images_all).reshape(D, images_all)
    hidden_out[...] = hidden_full
    pre_signal = dense(second_ref[...], hidden_full) + class_part
    pre_signal_out[...] = pre_signal
    signal_own[...] = fold(jax.nn.silu(pre_signal))
    signal.start()
    gather.tick(2)
    signal.wait()
    signal_full = unfold(signal_all[...], cols, images_all).reshape(D, images_all)
    signal_out[...] = signal_full
    mod_rows = mod_ref.shape[1]
    own_rows = pl.ds(pl.multiple_of(dp_rank * mod_rows, 8), mod_rows)
    signal_low = signal_out[own_rows, :].astype(jnp.bfloat16)
    total = None
    for layer_idx in range(LAYERS):
        pick = chosen(
            (images_all, dp_size * slots),
            lambda row, col: (
                (row // images == col // slots)
                & (lax.rem(row, images) + layer_idx * images == lax.rem(col, slots))
            ),
            jnp.bfloat16,
        )
        placed = dot_nn(signal_low, pick).astype(jnp.bfloat16)
        term = dot_tn(placed, mod_ref[layer_idx])
        total = term if total is None else total + term
    mod_part[...] = total.reshape(mod_part.shape)
    mod_sum.start()
    small.wait()
    small_spread.start()
    finals = jnp.concatenate(
        [
            dense(shift_ref[...], signal_full) + bias_ref[:, 3:4],
            dense(scale_ref[...], signal_full) + bias_ref[:, 4:5],
            jnp.zeros((128 - 2 * shift_ref.shape[0], images_all), jnp.float32),
        ],
        axis=0,
    )
    pick = chosen(
        (8 * dp_size, images_all),
        lambda row, col: (row // 8 == col // images) & (lax.rem(row, 8) == lax.rem(col, images)),
        jnp.float32,
    )
    final_own[...] = dense_nt(pick, finals).reshape(final_own.shape)
    final.start()
    run_ticks(gather, 3, min(4, dp_size // 2))
    mod_sum.wait()
    mod_own[...] = jnp.sum(mod_in[...], axis=0)
    mod_spread = Crowd("tensor", lambda place: mod_own, mod_all, *crowds[6])
    mod_spread.start()
    each(max(dp_size // 2 - 4, 0), lambda step: gather.tick(step + 4))
    small_spread.wait()
    final.wait()
    mod_spread.wait()
    gather.finish()


def head_call(small, feats, table, times, second, shift, scale, bias, mod_low, shards, images):
    dp_size, tensor_size = lax.axis_size("dp"), lax.axis_size("tensor")
    size = dp_size * tensor_size
    images_all = images * dp_size
    cols = table.shape[0]
    slots = slots_of(images)
    folded = folded_lanes(cols, images_all)
    full, low = jnp.float32, jnp.bfloat16
    shapes = [
        ((tensor_size, dp_size) + small.shape, full),
        ((images_all, feats.shape[1]), full),
        ((cols, images_all), full),
        ((D, images_all), full),
        ((cols, images_all), full),
        ((D, images_all), full),
        ((size, 8, 128), full),
        ((tensor_size, slots, mod_low.shape[2]), full),
    ] + [((dp_size,) + shard.shape, low) for shard in shards]
    scratch = [
        pltpu.VMEM((dp_size,) + feats.shape, full),
        pltpu.VMEM((8, folded), full),
        pltpu.VMEM((size, 8, folded), full),
        pltpu.VMEM((8, folded), full),
        pltpu.VMEM((size, 8, folded), full),
        pltpu.VMEM((dp_size, 8, 128), full),
        pltpu.VMEM((dp_size, slots, mod_low.shape[2]), full),
        pltpu.VMEM((dp_size, slots, mod_low.shape[2]), full),
        pltpu.VMEM((slots, mod_low.shape[2]), full),
        pltpu.VMEM((dp_size,) + small.shape, full),
    ]
    for count in (dp_size, dp_size, size, size, size, dp_size, tensor_size, tensor_size):
        scratch += crowd_scratch(count)
    scratch += [
        pltpu.SemaphoreType.DMA((3, dp_size // 2, 3)),
        pltpu.SemaphoreType.DMA((3, dp_size // 2, 3)),
        pltpu.SemaphoreType.DMA((3,)),
    ]
    return pl.pallas_call(
        functools.partial(head_kernel, images),
        out_shape=[jax.ShapeDtypeStruct(*shape) for shape in shapes],
        in_specs=[pl.BlockSpec(memory_space=pltpu.VMEM)] * (9 + len(shards)),
        out_specs=[pl.BlockSpec(memory_space=pltpu.VMEM)] * len(shapes),
        scratch_shapes=scratch,
        compiler_params=pltpu.CompilerParams(
            collective_id=30, has_side_effects=True, vmem_limit_bytes=ACT_VMEM
        ),
        name="head",
    )(small, feats, table, times, second, shift, scale, bias, mod_low, *shards)


def tail_kernel(
    images,
    final_at,
    row_ref,
    mod_ref,
    weight_ref,
    second_ref,
    shift_ref,
    scale_ref,
    pre_signal_ref,
    pre_time_ref,
    *rest,
):
    terms = rest[0:3]
    row_sums, d_final, d_mod_all, d_signal_own, d_hidden_own = rest[3:8]
    totals = rest[8:11]
    row_in, mod_in, mod_low, signal_part, signal_out, signal_in, hidden_out, hidden_in = rest[11:19]
    pair_in, way_in, way_out = rest[19:22], rest[22:25], rest[25:28]
    crowds = [rest[28 + 3 * index : 31 + 3 * index] for index in range(5)]
    reduce_sems = rest[43:]
    dp_size = lax.axis_size("dp")
    tensor_size = lax.axis_size("tensor")
    dp_rank = lax.axis_index("dp")
    images_all = images * dp_size
    cols, lanes = row_ref.shape[1:]
    mod_rows = weight_ref.shape[1]
    slots = mod_low.shape[0]
    last_step = dp_size // 2
    greet_group("all")
    reduce = Reduce(Line(), terms, totals, pair_in, way_in, way_out, *reduce_sems)

    mod_sum = Crowd("tensor", lambda place: mod_ref.at[place], mod_in, *crowds[0])
    rows = Crowd("all", lambda place: row_ref.at[place], row_in, *crowds[1])
    mod_spread = Crowd("dp", lambda place: mod_low, d_mod_all, *crowds[2])
    signal = Crowd("all", lambda place: signal_out.at[place], signal_in, *crowds[3])
    hidden = Crowd("all", lambda place: hidden_out.at[place], hidden_in, *crowds[4])
    mod_sum.start()
    rows.start()
    reduce.start()
    mod_sum.wait()
    mod_low[...] = jnp.sum(mod_in[...], axis=0).astype(jnp.bfloat16)
    mod_spread.start()
    rows.wait()
    row_sums[...] = jnp.sum(row_in[...], axis=0)
    group_sums = [
        jnp.sum(row_in[at * tensor_size : (at + 1) * tensor_size], axis=0)
        for at in range(dp_size)
    ]
    joined = jnp.concatenate(group_sums, axis=1)

    def final_of(piece):
        return dense(
            joined,
            chosen(
                (dp_size * lanes, images_all),
                lambda row, col: (
                    (row // lanes == col // images)
                    & (lax.rem(row, lanes) == final_at + piece * images + lax.rem(col, images))
                ),
                jnp.float32,
            ),
        )

    d_shift, d_scale = final_of(0), final_of(1)
    d_final[0] = d_shift
    d_final[1] = d_scale
    signal_part[...] = dense_tn(shift_ref[...], d_shift) + dense_tn(scale_ref[...], d_scale)
    run_ticks(reduce, 0, min(1, last_step))
    mod_spread.wait()
    d_mod = d_mod_all[...].reshape(dp_size * slots, mod_low.shape[1])
    own_rows = pl.ds(pl.multiple_of(dp_rank * mod_rows, 8), mod_rows)
    for layer_idx in range(LAYERS):
        pick = chosen(
            (dp_size * slots, images_all),
            lambda row, col: (
                (row // slots == col // images)
                & (lax.rem(row, slots) == layer_idx * images + lax.rem(col, images))
            ),
            jnp.float32,
        )
        signal_part[own_rows, :] += dense(dot_nt(weight_ref[layer_idx], d_mod), pick)
    places = dp_size * tensor_size
    signal_out[...] = fold(signal_part[...].reshape(places, cols, images_all))
    signal.start()
    run_ticks(reduce, 1, min(2, last_step))
    signal.wait()
    d_signal = unfold(jnp.sum(signal_in[...], axis=0), cols, images_all)
    d_signal = d_signal * silu_slope(pre_signal_ref[...])
    d_signal_own[...] = d_signal
    d_hidden = dense_tn(second_ref[...], d_signal)
    hidden_out[...] = fold(d_hidden.reshape(places, cols, images_all))
    hidden.start()
    run_ticks(reduce, 2, min(3, last_step))
    hidden.wait()
    d_hidden = unfold(jnp.sum(hidden_in[...], axis=0), cols, images_all)
    d_hidden_own[...] = d_hidden * silu_slope(pre_time_ref[...])
    run_ticks(reduce, 3, min(4, last_step))
    each(max(last_step - 4, 0), lambda step: reduce.tick(step + 4))
    reduce.finish()


def tail_call(rows, mods, mod_low, second, shift, scale, pre_signal, pre_time, terms, images, at):
    dp_size, tensor_size = lax.axis_size("dp"), lax.axis_size("tensor")
    size = dp_size * tensor_size
    images_all = images * dp_size
    cols, lanes = rows.shape[1:]
    folded = folded_lanes(cols, images_all)
    full, low = jnp.float32, jnp.bfloat16
    spots = dp_size // 2
    blocks = [term.shape[1:] for term in terms]
    shapes = [
        ((cols, lanes), full),
        ((2, cols, images_all), full),
        ((dp_size,) + mods.shape[1:], low),
        ((cols, images_all), full),
        ((cols, images_all), full),
    ] + [(block, full) for block in blocks]
    scratch = [
        pltpu.VMEM(rows.shape, full),
        pltpu.VMEM(mods.shape, full),
        pltpu.VMEM(mods.shape[1:], low),
        pltpu.VMEM((D, images_all), full),
        pltpu.VMEM((size, 8, folded), full),
        pltpu.VMEM((size, 8, folded), full),
        pltpu.VMEM((size, 8, folded), full),
        pltpu.VMEM((size, 8, folded), full),
    ]
    scratch += [pltpu.VMEM((spots,) + block, low) for block in blocks]
    scratch += [pltpu.VMEM((2, spots) + block, low) for block in blocks]
    scratch += [pltpu.VMEM((2, spots) + block, low) for block in blocks]
    for count in (tensor_size, size, dp_size, size, size):
        scratch += crowd_scratch(count)
    scratch += [
        pltpu.SemaphoreType.DMA((3, spots, 3)),
        pltpu.SemaphoreType.DMA((3, spots, 3)),
    ]
    return pl.pallas_call(
        functools.partial(tail_kernel, images, at),
        out_shape=[jax.ShapeDtypeStruct(*shape) for shape in shapes],
        in_specs=[pl.BlockSpec(memory_space=pltpu.VMEM)] * (8 + len(terms)),
        out_specs=[pl.BlockSpec(memory_space=pltpu.VMEM)] * len(shapes),
        scratch_shapes=scratch,
        compiler_params=pltpu.CompilerParams(
            collective_id=31, has_side_effects=True, vmem_limit_bytes=ACT_VMEM
        ),
        name="tail",
    )(rows, mods, mod_low, second, shift, scale, pre_signal, pre_time, *terms)


def adam_update(weight, first, second, grad, factor, first_fix, second_fix):
    clipped = grad * factor
    first_new = BETA_ONE * first + (1.0 - BETA_ONE) * clipped
    second_new = BETA_TWO * second + (1.0 - BETA_TWO) * clipped * clipped
    step_size = first_new / first_fix / (jnp.sqrt(second_new / second_fix) + ADAM_EPS)
    change = -LEARN_RATE * (step_size + DECAY * weight)
    master = weight + change
    return (master, first_new, second_new, master.astype(jnp.bfloat16), change)


def local(
    latents,
    target_noise,
    timesteps,
    labels,
    step_count,
    embed_table,
    layer_in,
    layer_out,
    layer_ada,
    embed_first,
    embed_second,
    input_first,
    input_second,
    output_first,
    output_second,
    mod_first,
    mod_second,
):
    tensor_size = lax.axis_size("tensor")
    tensor_rank = lax.axis_index("tensor")
    images = latents.shape[0]
    grid_side = SIDE // PATCH
    local_rows = grid_side // tensor_size
    tokens_all = grid_side * grid_side
    heads_local = HEADS // tensor_size
    group_width = heads_local * HEAD_DIM
    unit_count = FF // tensor_size
    patch_in = PATCH * PATCH * CHANNELS
    count_all = images * lax.axis_size("dp") * tokens_all * patch_in
    patch_start, time_start, second_start, final_start, head_start, vector_start, layer_start = (
        table_starts()
    )
    layer_rows = 10 + FF // D
    dp_rank = lax.axis_index("dp")
    dp_size = lax.axis_size("dp")
    place_count = dp_size * tensor_size
    images_all = images * dp_size
    table_cols = lax.reduce_precision(embed_table.T, 8, 7)
    cols = table_cols.shape[0]
    mod_rows = layer_ada.shape[1]
    mod_cols = layer_ada.shape[2]
    mod_low = layer_ada.astype(jnp.bfloat16)

    def col_block(row_start, row_count):
        return table_cols[:, row_start : row_start + row_count]

    vector_count = 5 + LAYERS * layer_rows
    small_count = 2 * patch_in + vector_count
    lanes = -(-(small_count + 2 * images) // 128) * 128
    shards_all = []
    for layer_idx in range(LAYERS):
        shard_in = layer_in[layer_idx, :, 0].astype(jnp.bfloat16)
        shard_out = layer_out[layer_idx, 0].astype(jnp.bfloat16)
        shards_all.append(
            (shard_in[:, : 3 * group_width], shard_in[:, 3 * group_width :], shard_out)
        )
    second_cols = col_block(second_start, D)
    shift_cols = col_block(final_start, D)
    scale_cols = col_block(final_start + D, D)
    fused = cols % 8 == 0 and images <= 8
    if fused:
        small_send = jnp.concatenate(
            [
                col_block(patch_start, patch_in),
                col_block(head_start, patch_in + vector_count),
                jnp.zeros((cols, lanes - small_count), jnp.float32),
            ],
            axis=1,
        )
        feats_send = jnp.concatenate(
            [
                time_features(timesteps),
                jnp.broadcast_to(labels.astype(jnp.float32)[:, None], (images, 128)),
            ],
            axis=1,
        )
        feats_send = jnp.pad(feats_send, ((0, 8 - images), (0, 0)))
        outs = head_call(
            small_send,
            feats_send,
            table_cols,
            col_block(time_start, FREQ),
            second_cols,
            shift_cols,
            scale_cols,
            col_block(vector_start, 5),
            mod_low,
            shards_all[0],
            images,
        )
        small_all, feats_all, pre_time, hidden, pre_signal, signal, final_all, mod_full = outs[:8]
        wholes = outs[8:]
        small_all = small_all.transpose(1, 0, 2, 3)
        time_feats = feats_all[:, :FREQ]
        labels_all = jnp.round(feats_all[:, FREQ]).astype(jnp.int32)
        signal_low = lax.dynamic_slice_in_dim(
            signal.astype(jnp.bfloat16), dp_rank * mod_rows, mod_rows, 0
        )
        final_own = final_all[:, :images, : 2 * cols].reshape(place_count, images, 2, cols)
        final_own = final_own.transpose(2, 1, 0, 3).reshape(2, images, D)
        mod_full = mod_full[:, : LAYERS * images].reshape(tensor_size, LAYERS, images, mod_cols)
        mod_full = mod_full.transpose(1, 2, 0, 3).reshape(LAYERS, images, tensor_size * mod_cols)
    else:
        scalar_lanes = jnp.concatenate([timesteps, labels]).astype(jnp.float32)
        small_send = jnp.concatenate(
            [
                col_block(patch_start, patch_in),
                col_block(head_start, patch_in + vector_count),
                jnp.broadcast_to(scalar_lanes[None, :], (cols, 2 * images)),
                jnp.zeros((cols, lanes - small_count - 2 * images), jnp.float32),
            ],
            axis=1,
        )
        small_all = exchange(small_send, "all", False, 1)
        scalars_all = small_all[::tensor_size, 0, small_count : small_count + 2 * images].astype(
            jnp.int32
        )
        timesteps_all = scalars_all[:, :images].reshape(images_all)
        labels_all = scalars_all[:, images:].reshape(images_all)
        time_feats = time_features(timesteps_all)
        onehot = (labels_all[:, None] == jnp.arange(CLASSES, dtype=jnp.int32)[None, :]).astype(
            jnp.float32
        )
        pre_time = dense(col_block(time_start, FREQ), time_feats.T) + col_block(vector_start + 1, 1)
        hidden = exchange(jax.nn.silu(pre_time), "all", False, 2).reshape(D, images_all)
        pre_signal = (
            dense(second_cols, hidden)
            + col_block(vector_start + 2, 1)
            + dense(col_block(0, CLASSES), onehot.T)
        )
        signal = exchange(jax.nn.silu(pre_signal), "all", False, 3).reshape(D, images_all)
        final_send = jnp.concatenate(
            [
                dense(shift_cols, signal) + col_block(vector_start + 3, 1),
                dense(scale_cols, signal) + col_block(vector_start + 4, 1),
            ],
            axis=0,
        )
        final_all = exchange(final_send, "all", False, 4).reshape(place_count, 2, cols, images_all)
        final_own = lax.dynamic_slice_in_dim(final_all, dp_rank * images, images, 3)
        final_own = final_own.transpose(1, 3, 0, 2).reshape(2, images, D)
        signal_low = lax.dynamic_slice_in_dim(
            signal.astype(jnp.bfloat16), dp_rank * mod_rows, mod_rows, 0
        )
        mod_part = jnp.einsum("db,lde->ble", signal_low, mod_low, preferred_element_type=jnp.float32)
        mod_part = mod_part.reshape(dp_size, images * LAYERS, mod_cols)
        mod_local = jnp.sum(exchange(mod_part, "dp", True, 5), axis=0)
        mod_full = exchange(mod_local, "tensor", False, 6)
        mod_full = mod_full.reshape(tensor_size, images, LAYERS, mod_cols)
        mod_full = mod_full.transpose(2, 1, 0, 3).reshape(LAYERS, images, tensor_size * mod_cols)
        wholes = [lax.all_gather(shard, "dp") for shard in shards_all[0]]
    small_rows = small_all.reshape(D, lanes).T
    patch_w = small_rows[0:patch_in]
    head_w = small_rows[patch_in : 2 * patch_in]
    vectors = small_rows[2 * patch_in : 2 * patch_in + 5]
    bias_all = small_rows[2 * patch_in + 5 : small_count]
    onehot = (labels_all[:, None] == jnp.arange(CLASSES, dtype=jnp.int32)[None, :]).astype(
        jnp.float32
    )
    final_shift, final_scale = final_own[0], final_own[1]
    pixels = patchify(latents, local_rows)
    targets = patchify(target_noise, local_rows)
    keep_coef, drop_coef = noise_levels(timesteps)
    noisy = keep_coef[:, None, None] * pixels + drop_coef[:, None, None] * targets
    residual = (
        jnp.einsum("btp,pd->btd", noisy, patch_w, precision=PRECISE)
        + vectors[0]
        + position_table(tensor_rank * local_rows, local_rows)[None]
    )
    saved_acts = []
    for layer_idx in range(LAYERS):
        bias_rows = bias_all[layer_idx * layer_rows : (layer_idx + 1) * layer_rows]
        up_all = bias_rows[10:].reshape(FF)
        ada_bias = bias_rows[0:6].reshape(6 * D)
        out_bias = bias_rows[6]
        down_bias = bias_rows[7]
        query_bias = lax.dynamic_slice_in_dim(bias_rows[8], tensor_rank * group_width, group_width)
        value_bias = lax.dynamic_slice_in_dim(bias_rows[9], tensor_rank * group_width, group_width)
        up_bias = lax.dynamic_slice_in_dim(up_all, tensor_rank * unit_count, unit_count)
        mod_vec = (mod_full[layer_idx] + ada_bias).reshape(images, 6, D)
        weight_out = wholes[2].reshape(group_width + unit_count, D)
        weights = (
            wholes[0].reshape(D, 3 * group_width),
            wholes[1].reshape(D, unit_count),
            weight_out[:group_width],
            weight_out[group_width:],
        )
        qkv_bias = jnp.concatenate(
            [query_bias, jnp.zeros((group_width,), jnp.float32), value_bias]
        )[None]
        outs = forward_layer(
            residual,
            mod_vec,
            jnp.stack([out_bias, down_bias]),
            qkv_bias,
            up_bias[None],
            *weights,
            shards_all[layer_idx + 1] if layer_idx + 1 < LAYERS else (),
        )
        wholes = outs[9:]
        saved_acts.append((mod_vec, (residual,) + tuple(outs[1:9]), weights))
        residual = outs[0]
    final_in, final_norm_pull = jax.vjp(modulate, residual, final_shift, final_scale)
    predicted = jnp.einsum("btd,pd->btp", final_in, head_w, precision=PRECISE)
    error_all = predicted - targets
    loss_part = jnp.sum(error_all * error_all) / count_all
    d_pred = 2.0 * error_all / count_all
    d_head = jnp.einsum("btp,btd->pd", d_pred, final_in, precision=PRECISE)
    d_final = jnp.einsum("btp,pd->btd", d_pred, head_w, precision=PRECISE)
    d_residual, d_final_shift, d_final_scale = final_norm_pull(d_final)
    totals = []
    terms = ()
    mod_parts = []
    bias_blocks = []
    for layer_idx in reversed(range(LAYERS)):
        mod_vec, saved, weights = saved_acts[layer_idx]
        outs = backward_layer(d_residual, mod_vec, saved, weights, terms)
        d_residual, d_w_qkv, d_w_up, d_w_out, d_mod_vec, d_vec, d_qkv_bias, d_up_bias = outs[:8]
        if terms:
            totals.insert(0, outs[8:])
        terms = [
            term.reshape((dp_size, -1) + term.shape[1:]) for term in (d_w_qkv, d_w_up, d_w_out)
        ]
        d_modulation = d_mod_vec.reshape(images, 6 * D)
        d_out_bias, d_down_bias = d_vec[0], d_vec[1]
        d_query_bias = d_qkv_bias[0, :group_width]
        d_value_bias = d_qkv_bias[0, 2 * group_width :]
        d_up_bias = d_up_bias[0]
        mod_parts.insert(0, d_modulation)
        query_row = lax.dynamic_update_slice_in_dim(
            jnp.zeros((D,), jnp.float32), d_query_bias, tensor_rank * group_width, 0
        )
        value_row = lax.dynamic_update_slice_in_dim(
            jnp.zeros((D,), jnp.float32), d_value_bias, tensor_rank * group_width, 0
        )
        up_rows = lax.dynamic_update_slice_in_dim(
            jnp.zeros((FF,), jnp.float32), d_up_bias, tensor_rank * unit_count, 0
        ).reshape(FF // D, D)
        bias_blocks.insert(
            0,
            jnp.concatenate(
                [
                    jnp.sum(d_modulation, axis=0).reshape(6, D),
                    d_out_bias[None],
                    d_down_bias[None],
                    query_row[None],
                    value_row[None],
                    up_rows,
                ],
                axis=0,
            ),
        )
    d_patch_w = jnp.einsum("btp,btd->pd", noisy, d_residual, precision=PRECISE)
    d_patch_b = jnp.sum(d_residual, axis=(0, 1))
    row_parts = jnp.concatenate(
        [d_patch_w, d_head, d_patch_b[None]] + bias_blocks + [d_final_shift, d_final_scale],
        axis=0,
    )
    row_count = row_parts.shape[0]
    row_lanes = -(-row_count // 128) * 128
    row_parts = jnp.pad(row_parts, ((0, row_lanes - row_count), (0, 0)))
    final_at = row_count - 2 * images
    row_send = row_parts.T.reshape(place_count, cols, row_lanes)
    mod_send = jnp.stack(mod_parts).reshape(LAYERS * images, tensor_size, mod_cols)
    mod_send = mod_send.transpose(1, 0, 2)
    if fused:
        slots = slots_of(images)
        outs = tail_call(
            row_send,
            jnp.pad(mod_send, ((0, 0), (0, slots - LAYERS * images), (0, 0))),
            mod_low,
            second_cols,
            shift_cols,
            scale_cols,
            pre_signal,
            pre_time,
            terms,
            images,
            final_at,
        )
        row_sums, final_sums, d_mod_low, d_pre_signal, d_hidden = outs[:5]
        totals.insert(0, outs[5:])
        d_shift_cols, d_scale_cols = final_sums[0], final_sums[1]
        d_mod_low = d_mod_low[:, : LAYERS * images]
        d_mod_low = d_mod_low.reshape(dp_size, LAYERS, images, mod_cols)
        d_mod_low = d_mod_low.transpose(1, 0, 2, 3).reshape(LAYERS, images_all, mod_cols)
    else:
        totals.insert(
            0,
            [
                lax.psum_scatter(term, "dp", scatter_dimension=0).astype(jnp.float32)
                for term in terms
            ],
        )
        row_all = exchange(row_send, "all", True, 7)
        row_sums = jnp.sum(row_all, axis=0)
        final_sums = jnp.sum(
            row_all[:, :, final_at:row_count].reshape(dp_size, tensor_size, cols, 2, images), axis=1
        )
        final_sums = final_sums.transpose(2, 1, 0, 3).reshape(2, cols, images_all)
        d_shift_cols, d_scale_cols = final_sums[0], final_sums[1]
        d_mod_own = jnp.sum(exchange(mod_send, "tensor", True, 8), axis=0)
        d_mod_low = exchange(d_mod_own.astype(jnp.bfloat16), "dp", False, 9)
        d_mod_low = d_mod_low.reshape(dp_size, LAYERS, images, mod_cols)
        d_mod_low = d_mod_low.transpose(1, 0, 2, 3).reshape(LAYERS, images_all, mod_cols)
        d_signal_rows = jnp.einsum(
            "lbe,lde->db", d_mod_low, mod_low, preferred_element_type=jnp.float32
        )
        d_signal_part = dense(shift_cols.T, d_shift_cols) + dense(scale_cols.T, d_scale_cols)
        d_signal_part = d_signal_part + lax.dynamic_update_slice_in_dim(
            jnp.zeros((D, images_all), jnp.float32), d_signal_rows, dp_rank * mod_rows, 0
        )
        d_signal_cols = jnp.sum(
            exchange(d_signal_part.reshape(place_count, cols, images_all), "all", True, 10), axis=0
        )
        d_pre_signal = d_signal_cols * silu_slope(pre_signal)
        d_hidden_part = dense(second_cols.T, d_pre_signal)
        d_hidden_cols = jnp.sum(
            exchange(d_hidden_part.reshape(place_count, cols, images_all), "all", True, 11), axis=0
        )
        d_hidden = d_hidden_cols * silu_slope(pre_time)
    mod_grad = jnp.einsum(
        "db,lbe->lde", signal_low, d_mod_low, preferred_element_type=jnp.float32
    )
    table_grad = jnp.concatenate(
        [
            dense(d_pre_signal, onehot),
            row_sums[:, 0:patch_in],
            dense(d_hidden, time_feats),
            dense(d_pre_signal, hidden.T),
            dense(d_shift_cols, signal.T),
            dense(d_scale_cols, signal.T),
            row_sums[:, patch_in : 2 * patch_in + 1],
            jnp.sum(d_hidden, axis=1, keepdims=True),
            jnp.sum(d_pre_signal, axis=1, keepdims=True),
            jnp.sum(d_shift_cols, axis=1, keepdims=True),
            jnp.sum(d_scale_cols, axis=1, keepdims=True),
            row_sums[:, 2 * patch_in + 1 : final_at],
        ],
        axis=1,
    )
    input_grad = jnp.stack([jnp.concatenate(total[0:2], axis=1) for total in totals])
    input_grad = input_grad.reshape(layer_in.shape)
    output_grad = jnp.stack([total[2] for total in totals]).reshape(layer_out.shape)
    local_squares = (
        jnp.sum(table_grad * table_grad)
        + jnp.sum(input_grad * input_grad)
        + jnp.sum(output_grad * output_grad)
        + jnp.sum(mod_grad * mod_grad)
    )
    scalar_send = jnp.where(
        lax.broadcasted_iota(jnp.int32, (8, 128), 1) == 0, loss_part, local_squares
    )
    scalar_sums = jnp.sum(exchange(scalar_send, "all", False, 12)[:, 0, 0:2], axis=0)
    loss_value = scalar_sums[0]
    square_total = scalar_sums[1]
    grad_norm = jnp.sqrt(square_total)
    factor = jnp.minimum(1.0, CLIP_NORM / grad_norm)
    first_fix = 1.0 - BETA_ONE ** step_count.astype(jnp.float32)
    second_fix = 1.0 - BETA_TWO ** step_count.astype(jnp.float32)
    embed_out = adam_update(
        embed_table.T, embed_first.T, embed_second.T, table_grad, factor, first_fix, second_fix
    )
    input_out = adam_update(
        layer_in, input_first, input_second, input_grad, factor, first_fix, second_fix
    )
    output_out = adam_update(
        layer_out, output_first, output_second, output_grad, factor, first_fix, second_fix
    )
    mod_out = adam_update(layer_ada, mod_first, mod_second, mod_grad, factor, first_fix, second_fix)
    return (
        (loss_value, grad_norm, embed_out[4].T, embed_out[1].T, embed_out[2].T)
        + input_out[0:4]
        + output_out[0:4]
        + mod_out[0:4]
    )


def solution(mesh):
    placed = (
        P("dp", "tensor"),
        P("dp", "tensor"),
        P("dp"),
        P("dp"),
        P(),
        P(None, ("dp", "tensor")),
        P(None, "dp", "tensor", None),
        P(None, "tensor", "dp", None),
        P(None, "dp", "tensor"),
        P(None, ("dp", "tensor")),
        P(None, ("dp", "tensor")),
        P(None, "dp", "tensor", None),
        P(None, "dp", "tensor", None),
        P(None, "tensor", "dp", None),
        P(None, "tensor", "dp", None),
        P(None, "dp", "tensor"),
        P(None, "dp", "tensor"),
    )
    return jax.shard_map(
        local,
        mesh=mesh,
        in_specs=placed,
        out_specs=(
            P(),
            P(),
            P(None, ("dp", "tensor")),
            P(None, ("dp", "tensor")),
            P(None, ("dp", "tensor")),
            P(None, "dp", "tensor", None),
            P(None, "dp", "tensor", None),
            P(None, "dp", "tensor", None),
            P(None, "dp", "tensor", None),
            P(None, "tensor", "dp", None),
            P(None, "tensor", "dp", None),
            P(None, "tensor", "dp", None),
            P(None, "tensor", "dp", None),
            P(None, "dp", "tensor"),
            P(None, "dp", "tensor"),
            P(None, "dp", "tensor"),
            P(None, "dp", "tensor"),
        ),
        check_vma=False,
    )
```

```python
import functools
import math

import jax
import jax.numpy as jnp
from jax import lax
from jax.experimental import pallas as pl
from jax.experimental.pallas import tpu as pltpu
from jax.sharding import PartitionSpec as P

D = 768
HEADS = 12
HEAD_DIM = 64
FF = 3072
CLASSES = 1001
FREQ = 256
CHANNELS = 4
PATCH = 2
SIDE = 32
LAYERS = 3


EPS_NORM = 1e-06
LEARN_RATE = 0.01
DECAY = 0.01
BETA_ONE = 0.5
BETA_TWO = 0.5
ADAM_EPS = 1e-08
CLIP_NORM = 0.25
PRECISE = lax.Precision.HIGHEST


def dense(left_op, right_op):
    return jnp.dot(left_op, right_op, precision=PRECISE, preferred_element_type=jnp.float32)


def layer_norm(values):
    center = values - jnp.mean(values, axis=-1, keepdims=True)
    return center * lax.rsqrt(jnp.mean(center * center, axis=-1, keepdims=True) + EPS_NORM)


def modulate(values, shift_vec, scale_vec):
    return layer_norm(values) * (1.0 + scale_vec[:, None, :]) + shift_vec[:, None, :]


def gelu_tanh(values):
    return jax.nn.gelu(values, approximate=True)


def silu_slope(values):
    sigmoid_val = jax.nn.sigmoid(values)
    return sigmoid_val * (1.0 + values * (1.0 - sigmoid_val))


def time_features(step_ints):
    half_width = FREQ // 2
    frequency = jnp.exp(-math.log(10000.0) * jnp.arange(half_width, dtype=jnp.float32) / half_width)
    angles = step_ints.astype(jnp.float32)[:, None] * frequency[None, :]
    return jnp.concatenate([jnp.cos(angles), jnp.sin(angles)], axis=1)


def noise_levels(step_ints):
    base_cos = math.cos(0.008 / 1.008 * math.pi / 2)
    angles = (step_ints.astype(jnp.float32) / 1000.0 + 0.008) / 1.008 * (math.pi / 2)
    signal_level = jnp.cos(angles) ** 2 / base_cos**2
    return (jnp.sqrt(signal_level), jnp.sqrt(1.0 - signal_level))


def position_table(first_row, row_count):
    grid_side = SIDE // PATCH
    quarter = D // 4
    omegas = jnp.exp(-math.log(10000.0) * jnp.arange(quarter, dtype=jnp.float32) / quarter)
    token_index = jnp.arange(row_count * grid_side, dtype=jnp.int32)
    row_angle = (first_row + token_index // grid_side).astype(jnp.float32)[:, None] * omegas[
        None, :
    ]
    col_angle = (token_index % grid_side).astype(jnp.float32)[:, None] * omegas[None, :]
    return jnp.concatenate(
        [jnp.sin(row_angle), jnp.cos(row_angle), jnp.sin(col_angle), jnp.cos(col_angle)], axis=1
    )


def patchify(flat_pixels, row_count):
    grid_side = SIDE // PATCH
    shaped = flat_pixels.reshape(flat_pixels.shape[0], row_count, PATCH, grid_side, PATCH, CHANNELS)
    return shaped.transpose(0, 1, 3, 2, 4, 5).reshape(
        flat_pixels.shape[0], row_count * grid_side, PATCH * PATCH * CHANNELS
    )


def table_starts():
    patch_in = PATCH * PATCH * CHANNELS
    patch_start = CLASSES
    time_start = patch_start + patch_in
    second_start = time_start + FREQ
    final_start = second_start + D
    head_start = final_start + 2 * D
    vector_start = head_start + patch_in
    layer_start = vector_start + 5
    return (
        patch_start,
        time_start,
        second_start,
        final_start,
        head_start,
        vector_start,
        layer_start,
    )


def group_place(group):
    if group == "all":
        width = lax.axis_size("tensor")
        place = lax.axis_index("dp") * width + lax.axis_index("tensor")
        size = lax.axis_size("dp") * width
        return place, size, lambda at: {"dp": at // width, "tensor": lax.rem(at, width)}
    return lax.axis_index(group), lax.axis_size(group), lambda at: {group: at}


def greet_group(group):
    place, size, coords = group_place(group)
    barrier = pltpu.get_barrier_semaphore()

    def greet_one(step, carry):
        peer = coords(lax.rem(place + step, size))
        pl.semaphore_signal(barrier, inc=1, device_id=peer, device_id_type=pl.DeviceIdType.MESH)
        return carry

    lax.fori_loop(1, size, greet_one, 0)
    pl.semaphore_wait(barrier, size - 1)


class Crowd:
    def __init__(self, group, source_at, target, send_sems, recv_sems, local_sem):
        self.place, self.size, self.coords = group_place(group)
        self.source_at, self.target = source_at, target
        self.sends, self.recvs, self.local_sem = send_sems, recv_sems, local_sem

    def copy_to(self, step):
        there = lax.rem(self.place + step, self.size)
        return pltpu.make_async_remote_copy(
            src_ref=self.source_at(there),
            dst_ref=self.target.at[self.place],
            send_sem=self.sends.at[step],
            recv_sem=self.recvs.at[step],
            device_id=self.coords(there),
            device_id_type=pl.DeviceIdType.MESH,
        )

    def own_copy(self):
        return pltpu.make_async_copy(
            self.source_at(self.place), self.target.at[self.place], self.local_sem
        )

    def start(self):
        def begin(step, carry):
            self.copy_to(step).start()
            return carry

        lax.fori_loop(1, self.size, begin, 0)
        self.own_copy().start()

    def wait(self):
        def finish(step, carry):
            self.copy_to(step).wait()
            return carry

        self.own_copy().wait()
        lax.fori_loop(1, self.size, finish, 0)


def crowd_scratch(size):
    return [
        pltpu.SemaphoreType.DMA((size,)),
        pltpu.SemaphoreType.DMA((size,)),
        pltpu.SemaphoreType.DMA,
    ]


def exchange_kernel(group, spread, source, target, send_sems, recv_sems, local_sem):
    greet_group(group)
    crowd = Crowd(
        group,
        lambda place: source.at[place] if spread else source,
        target,
        send_sems,
        recv_sems,
        local_sem,
    )
    crowd.start()
    crowd.wait()


def exchange(values, group, spread, call_id):
    if group == "all":
        size = lax.axis_size("dp") * lax.axis_size("tensor")
    else:
        size = lax.axis_size(group)
    block = values.shape[1:] if spread else values.shape
    return pl.pallas_call(
        functools.partial(exchange_kernel, group, spread),
        out_shape=jax.ShapeDtypeStruct((size,) + block, values.dtype),
        in_specs=[pl.BlockSpec(memory_space=pltpu.VMEM)],
        out_specs=pl.BlockSpec(memory_space=pltpu.VMEM),
        scratch_shapes=crowd_scratch(size),
        compiler_params=pltpu.CompilerParams(
            collective_id=call_id, has_side_effects=True, vmem_limit_bytes=32 * 2**20
        ),
        name="exchange_" + group,
    )(values)


MESH = pl.DeviceIdType.MESH
ACT_VMEM = 60 * 2**20


def dot_nn(left_op, right_op):
    return jnp.dot(left_op, right_op, preferred_element_type=jnp.float32)


def dot_nt(left_op, right_op):
    return lax.dot_general(
        left_op, right_op, (((1,), (1,)), ((), ())), preferred_element_type=jnp.float32
    )


def dot_tn(left_op, right_op):
    return lax.dot_general(
        left_op, right_op, (((0,), (0,)), ((), ())), preferred_element_type=jnp.float32
    )


def norm_parts(values):
    center = values - jnp.mean(values, axis=-1, keepdims=True)
    rstd = lax.rsqrt(jnp.mean(center * center, axis=-1, keepdims=True) + EPS_NORM)
    return center * rstd, rstd


def greet(line):
    rank = lax.axis_index("tensor")
    half = lax.axis_size("tensor") // 2
    core_peer = {"tensor": rank + 1 - 2 * lax.rem(rank, 2)}
    chip_peer = {"tensor": lax.rem(rank + half, 2 * half)}
    barrier = pltpu.get_barrier_semaphore()
    for peer in (core_peer, chip_peer):
        pl.semaphore_signal(barrier, inc=1, device_id=peer, device_id_type=MESH)
    count = 2
    if line is not None:
        line.greet()
        count = count + line.answers()
    pl.semaphore_wait(barrier, count)


class Spread:
    def __init__(self, rows_ref, send_sems, recv_sems):
        self.rows, self.send, self.recv = rows_ref, send_sems, recv_sems
        self.rank = lax.axis_index("tensor")
        self.own_core = lax.rem(self.rank, 2)
        self.core_peer = self.rank + 1 - 2 * self.own_core
        self.chip_peer = lax.rem(self.rank + 2, 4)
        self.count = rows_ref.shape[1] // 4

    def block(self, image, owner):
        return self.rows.at[image, pl.ds(pl.multiple_of(owner * self.count, 16), self.count), :]

    def copy(self, image, owner, peer, which):
        return pltpu.make_async_remote_copy(
            src_ref=self.block(image, owner),
            dst_ref=self.block(image, owner),
            send_sem=self.send.at[image, which],
            recv_sem=self.recv.at[image, which],
            device_id={"tensor": peer},
            device_id_type=MESH,
        )

    def put(self, image, values):
        self.rows[image, pl.ds(pl.multiple_of(self.rank * self.count, 16), self.count), :] = values
        self.copy(image, self.rank, self.chip_peer, 0).start()
        self.copy(image, self.rank, self.core_peer, 1).start()

    def forward(self, image):
        self.copy(image, self.rank, self.chip_peer, 0).wait_recv()
        self.copy(image, self.chip_peer, self.core_peer, 2).start()

    def wait(self, image):
        self.copy(image, self.rank, self.core_peer, 1).wait_recv()
        self.copy(image, self.chip_peer, self.core_peer, 2).wait_recv()

    def close(self, image):
        self.copy(image, self.rank, self.chip_peer, 0).wait_send()
        self.copy(image, self.rank, self.core_peer, 1).wait_send()
        self.copy(image, self.chip_peer, self.core_peer, 2).wait_send()


class Collect:
    def __init__(self, part, near, far_out, far_in, send_sems, recv_sems):
        self.part, self.near, self.far_out, self.far_in = part, near, far_out, far_in
        self.send, self.recv = send_sems, recv_sems
        self.rank = lax.axis_index("tensor")
        self.own_core = lax.rem(self.rank, 2)
        self.own_chip = self.rank // 2
        self.core_peer = self.rank + 1 - 2 * self.own_core
        self.chip_peer = lax.rem(self.rank + 2, 4)
        self.count = part.shape[1] // 4

    def block(self, image, owner):
        return self.part.at[image, pl.ds(pl.multiple_of(owner * self.count, 16), self.count), :]

    def near_copy(self, image, far):
        chip = 1 - self.own_chip if far else self.own_chip
        return pltpu.make_async_remote_copy(
            src_ref=self.block(image, 2 * chip + 1 - self.own_core),
            dst_ref=self.near.at[image, far],
            send_sem=self.send.at[image, far],
            recv_sem=self.recv.at[image, far],
            device_id={"tensor": self.core_peer},
            device_id_type=MESH,
        )

    def far_copy(self, image):
        return pltpu.make_async_remote_copy(
            src_ref=self.far_out.at[image],
            dst_ref=self.far_in.at[image],
            send_sem=self.send.at[image, 2],
            recv_sem=self.recv.at[image, 2],
            device_id={"tensor": self.chip_peer},
            device_id_type=MESH,
        )

    def put(self, image, values):
        self.part[image] = values.astype(jnp.bfloat16)
        self.near_copy(image, 1).start()
        self.near_copy(image, 0).start()

    def load(self, image, owner):
        at = pl.ds(pl.multiple_of(owner * self.count, 16), self.count)
        return self.part[image, at, :].astype(jnp.float32)

    def forward(self, image):
        self.near_copy(image, 1).wait_recv()
        total = self.load(image, self.chip_peer) + self.near[image, 1].astype(jnp.float32)
        self.far_out[image] = total.astype(jnp.bfloat16)
        self.far_copy(image).start()

    def take(self, image):
        self.near_copy(image, 0).wait_recv()
        total = self.load(image, self.rank) + self.near[image, 0].astype(jnp.float32)
        self.far_copy(image).wait_recv()
        return total + self.far_in[image].astype(jnp.float32)

    def close(self, image):
        self.near_copy(image, 1).wait_send()
        self.near_copy(image, 0).wait_send()
        self.far_copy(image).wait_send()


def collect_scratch(images, tokens):
    count = tokens // 4
    return [
        pltpu.VMEM((images, tokens, D), jnp.bfloat16),
        pltpu.VMEM((images, 2, count, D), jnp.bfloat16),
        pltpu.VMEM((images, count, D), jnp.bfloat16),
        pltpu.VMEM((images, count, D), jnp.bfloat16),
    ]


def each(count, body):
    def step(index, carry):
        body(index)
        return carry

    lax.fori_loop(0, count, step, 0)


class Line:
    def __init__(self):
        self.size = lax.axis_size("dp") // 2
        self.place = lax.axis_index("dp")
        self.at = self.place // 2
        self.side = lax.rem(self.place, 2)
        self.pair = self.place + 1 - 2 * self.side
        self.has_up = self.at + 1 < self.size
        self.has_down = self.at > 0

    def greet(self):
        barrier = pltpu.get_barrier_semaphore()
        pl.semaphore_signal(barrier, inc=1, device_id={"dp": self.pair}, device_id_type=MESH)

        @pl.when(self.has_up)
        def _():
            up = {"dp": self.place + 2}
            pl.semaphore_signal(barrier, inc=1, device_id=up, device_id_type=MESH)

        @pl.when(self.has_down)
        def _():
            down = {"dp": self.place - 2}
            pl.semaphore_signal(barrier, inc=1, device_id=down, device_id_type=MESH)

    def answers(self):
        return 1 + self.has_up.astype(jnp.int32) + self.has_down.astype(jnp.int32)


UP, DOWN, PAIR = 0, 1, 2


class Gather:
    def __init__(self, line, shards, wholes, sends, recvs, local_sems):
        self.line, self.shards, self.wholes = line, shards, wholes
        self.sends, self.recvs, self.local_sems = sends, recvs, local_sems

    def copy(self, part, way, step, owner, fresh=False):
        line = self.line
        there = {UP: line.place + 2, DOWN: line.place - 2, PAIR: line.pair}[way]
        return pltpu.make_async_remote_copy(
            src_ref=self.shards[part] if fresh else self.wholes[part].at[owner],
            dst_ref=self.wholes[part].at[owner],
            send_sem=self.sends.at[way, step, part],
            recv_sem=self.recvs.at[way, step, part],
            device_id={"dp": there},
            device_id_type=MESH,
        )

    def local_copy(self, part):
        return pltpu.make_async_copy(
            self.shards[part], self.wholes[part].at[self.line.place], self.local_sems.at[part]
        )

    def start(self):
        line = self.line
        parts = range(len(self.shards))

        @pl.when(line.has_up)
        def _():
            for part in parts:
                self.copy(part, UP, 0, line.place, True).start()

        @pl.when(line.has_down)
        def _():
            for part in parts:
                self.copy(part, DOWN, 0, line.place, True).start()

        for part in parts:
            self.copy(part, PAIR, line.at, line.place, True).start()
            self.local_copy(part).start()

    def came(self, way, step):
        there = -step if way == UP else step
        spot = self.line.at + there
        return self.line.place + 2 * there, spot, (spot >= 0) & (spot < self.line.size)

    def hand_on(self, step, way):
        line = self.line
        owner, _, real = self.came(way, step)
        can = line.has_up if way == UP else line.has_down

        @pl.when(real)
        def _():
            for part in range(len(self.shards)):
                self.copy(part, way, step - 1, owner).wait_recv()

            @pl.when(can)
            def _():
                for part in range(len(self.shards)):
                    self.copy(part, way, step, owner).start()

    def hand_over(self, step, way, when=True):
        owner, spot, real = self.came(way, step)

        @pl.when(real & when)
        def _():
            for part in range(len(self.shards)):
                self.copy(part, PAIR, spot, owner).start()

    def tick(self, step):
        for way in (UP, DOWN):
            self.hand_on(step, way)
            self.hand_over(step, way)

    def finish(self):
        line = self.line
        parts = range(len(self.shards))
        for part in parts:
            self.local_copy(part).wait()

        def side(spot):
            for part in parts:
                self.copy(part, PAIR, spot, 2 * spot + line.side).wait()

        each(line.size, side)

        def along(step):
            for way, there, can in ((UP, -step, line.has_up), (DOWN, step, line.has_down)):
                spot = line.at + there

                @pl.when((spot >= 0) & (spot < line.size) & can)
                def _(way=way, there=there):
                    for part in parts:
                        self.copy(part, way, step, line.place + 2 * there).wait_send()

        each(line.size, along)


class Reduce:
    def __init__(self, line, terms, totals, pair_in, way_in, way_out, sends, recvs):
        self.line, self.terms, self.totals = line, terms, totals
        self.pair_in, self.way_in, self.way_out = pair_in, way_in, way_out
        self.sends, self.recvs = sends, recvs

    def pair_copy(self, part, spot):
        return pltpu.make_async_remote_copy(
            src_ref=self.terms[part].at[2 * spot + 1 - self.line.side],
            dst_ref=self.pair_in[part].at[spot],
            send_sem=self.sends.at[PAIR, spot, part],
            recv_sem=self.recvs.at[PAIR, spot, part],
            device_id={"dp": self.line.pair},
            device_id_type=MESH,
        )

    def way_copy(self, part, way, spot):
        there = self.line.place + 2 if way == UP else self.line.place - 2
        return pltpu.make_async_remote_copy(
            src_ref=self.way_out[part].at[way, spot],
            dst_ref=self.way_in[part].at[way, spot],
            send_sem=self.sends.at[way, spot, part],
            recv_sem=self.recvs.at[way, spot, part],
            device_id={"dp": there},
            device_id_type=MESH,
        )

    def start(self):
        each(self.line.size, self.send_pair)

    def send_pair(self, step):
        line = self.line
        far = line.size - 1 - step

        @pl.when(line.at + far < line.size)
        def _():
            for part in range(len(self.terms)):
                self.pair_copy(part, line.at + far).start()

        @pl.when((line.at - far >= 0) & (far > 0))
        def _():
            for part in range(len(self.terms)):
                self.pair_copy(part, line.at - far).start()

    def pair_sum(self, part, spot):
        own = self.terms[part][2 * spot + self.line.side].astype(jnp.float32)
        return own + self.pair_in[part][spot].astype(jnp.float32)

    def pass_on(self, way, spot, more):
        for part in range(len(self.terms)):
            self.pair_copy(part, spot).wait_recv()
            self.way_out[part][way, spot] = self.pair_sum(part, spot).astype(jnp.bfloat16)

            @pl.when(more)
            def _(part=part):
                self.way_copy(part, way, spot).wait_recv()
                self.way_out[part][way, spot] = (
                    self.pair_sum(part, spot) + self.way_in[part][way, spot].astype(jnp.float32)
                ).astype(jnp.bfloat16)

            self.way_copy(part, way, spot).start()

    def tick(self, step):
        line = self.line
        far = line.size - 1 - step

        @pl.when(line.at + far < line.size)
        def _():
            self.pass_on(UP, line.at + far, line.has_down)

        @pl.when(line.at - far >= 0)
        def _():
            self.pass_on(DOWN, line.at - far, line.has_up)

    def finish(self):
        line = self.line
        spot = line.at
        for part in range(len(self.terms)):
            self.pair_copy(part, spot).wait_recv()
            self.totals[part][...] = self.pair_sum(part, spot)
        for way, can in ((UP, line.has_down), (DOWN, line.has_up)):

            @pl.when(can)
            def _(way=way):
                for part in range(len(self.terms)):
                    self.way_copy(part, way, spot).wait_recv()
                    self.totals[part][...] += self.way_in[part][way, spot].astype(jnp.float32)

        def close(spot):
            for part in range(len(self.terms)):
                self.pair_copy(part, spot).wait_send()
            for way, passed in ((UP, spot > line.at), (DOWN, spot < line.at)):

                @pl.when(passed)
                def _(way=way):
                    for part in range(len(self.terms)):
                        self.way_copy(part, way, spot).wait_send()

        each(line.size, close)


def run_ticks(task, first, last):
    if task is not None:
        for step in range(first, last):
            task.tick(step)


def head_slice(matrix, head):
    return matrix[:, head * HEAD_DIM : (head + 1) * HEAD_DIM]


def soft_rows(queries, keys_in):
    scores = dot_nt(queries, keys_in) * (HEAD_DIM ** (-0.5))
    exponent = jnp.exp(scores - jnp.max(scores, axis=-1, keepdims=True))
    return exponent / jnp.sum(exponent, axis=-1, keepdims=True)


def forward_kernel(
    layer_idx,
    res_ref,
    mod_ref,
    vec_ref,
    qkv_bias_ref,
    up_bias_ref,
    w_qkv_ref,
    w_up_ref,
    w_out_ref,
    *rest,
):
    with_gather = len(rest) > 19
    shards, rest = (rest[:3], rest[3:]) if with_gather else ((), rest)
    group_width = w_qkv_ref.shape[1] // 3
    w_attn_ref, w_down_ref = w_out_ref.at[0:group_width, :], w_out_ref.at[group_width:, :]
    (
        res_out,
        rows_a,
        qkv_out,
        mixed_out,
        branch_out,
        mid_out,
        rows_m,
        upper_out,
        down_out,
    ) = rest[:9]
    wholes, rest = (rest[9:12], rest[12:]) if with_gather else ((), rest[9:])
    (
    part_a,
    near_a,
    far_out_a,
    far_in_a,
    part_m,
    near_m,
    far_out_m,
    far_in_m,
    sends,
    recvs,
    ) = rest[:10]
    images = res_ref.shape[0]
    gather, last_step = None, 0
    if with_gather:
        line = Line()
        greet(line)
        own = [shard.at[layer_idx + 1] for shard in shards]
        gather = Gather(line, own, wholes, *rest[10:])
        last_step = line.size
    else:
        greet(None)
    spread_a = Spread(rows_a, sends.at[0], recvs.at[0])
    spread_m = Spread(rows_m, sends.at[1], recvs.at[1])
    collect_a = Collect(part_a, near_a, far_out_a, far_in_a, sends.at[2], recvs.at[2])
    collect_m = Collect(part_m, near_m, far_out_m, far_in_m, sends.at[3], recvs.at[3])

    def mod_row(image, piece):
        return mod_ref[image, pl.ds(piece, 1), :]

    def start_norm(image):
        normed, _ = norm_parts(res_ref[image])
        normed = normed * (1.0 + mod_row(image, 1)) + mod_row(image, 0)
        spread_a.put(image, normed.astype(jnp.bfloat16))

    def attend(image):
        spread_a.wait(image)
        rows = rows_a[image]
        projected = dot_nn(rows, w_qkv_ref[...]) + qkv_bias_ref[...]
        qkv = projected.astype(jnp.bfloat16)
        qkv_out[image] = qkv
        heads = []
        for head in range(group_width // HEAD_DIM):
            probs = soft_rows(
                head_slice(qkv[:, :group_width], head),
                head_slice(qkv[:, group_width : 2 * group_width], head),
            )
            heads.append(
                dot_nn(probs.astype(jnp.bfloat16), head_slice(qkv[:, 2 * group_width :], head))
            )
        mixed = jnp.concatenate(heads, axis=1).astype(jnp.bfloat16)
        mixed_out[image] = mixed
        collect_a.put(image, dot_nn(mixed, w_attn_ref[...]))

    def middle(image):
        branch = collect_a.take(image) + vec_ref[0:1, :]
        branch_out[image] = branch
        mid = res_ref[image] + mod_row(image, 2) * branch
        mid_out[image] = mid
        normed, _ = norm_parts(mid)
        normed = normed * (1.0 + mod_row(image, 4)) + mod_row(image, 3)
        spread_m.put(image, normed.astype(jnp.bfloat16))

    def feed(image):
        spread_m.wait(image)
        upper = dot_nn(rows_m[image], w_up_ref[...]) + up_bias_ref[...]
        upper_out[image] = upper
        collect_m.put(image, dot_nn(gelu_tanh(upper).astype(jnp.bfloat16), w_down_ref[...]))

    def finish(image):
        down = collect_m.take(image) + vec_ref[1:2, :]
        down_out[image] = down
        res_out[image] = mid_out[image] + mod_row(image, 5) * down

    def close(image):
        spread_a.close(image)
        spread_m.close(image)
        collect_a.close(image)
        collect_m.close(image)

    if with_gather:
        gather.start()
    each(images, start_norm)
    each(images, spread_a.forward)
    each(images, attend)
    run_ticks(gather, 1, min(2, last_step))
    each(images, collect_a.forward)
    each(images, middle)
    each(images, spread_m.forward)
    run_ticks(gather, 2, min(3, last_step))
    each(images, feed)
    run_ticks(gather, 3, min(4, last_step))
    each(images, collect_m.forward)
    each(images, finish)
    each(images, close)
    if with_gather:
        each(max(last_step - 4, 0), lambda step: gather.tick(step + 4))
        gather.finish()


def forward_layer(
    residual, mod_vec, vec_bias, qkv_bias, up_bias, w_qkv, w_up, w_out, shards, layer_idx
):
    images, count, _ = residual.shape
    tokens = 4 * count
    low, full = jnp.bfloat16, jnp.float32
    shapes = [
        ((images, count, D), full),
        ((images, tokens, D), low),
        ((images, tokens, w_qkv.shape[1]), low),
        ((images, tokens, w_qkv.shape[1] // 3), low),
        ((images, count, D), full),
        ((images, count, D), full),
        ((images, tokens, D), low),
        ((images, tokens, w_up.shape[1]), full),
        ((images, count, D), full),
    ]
    scratch = [
        pltpu.SemaphoreType.DMA((4, images, 3)),
        pltpu.SemaphoreType.DMA((4, images, 3)),
    ]
    if shards:
        dp_size = lax.axis_size("dp")
        shapes += [((dp_size,) + shard.shape[1:], low) for shard in shards]
        scratch += [
            pltpu.SemaphoreType.DMA((3, dp_size // 2, 3)),
            pltpu.SemaphoreType.DMA((3, dp_size // 2, 3)),
            pltpu.SemaphoreType.DMA((3,)),
        ]
    return pl.pallas_call(
        functools.partial(forward_kernel, layer_idx),
        out_shape=[jax.ShapeDtypeStruct(*shape) for shape in shapes],
        in_specs=[pl.BlockSpec(memory_space=pltpu.VMEM)] * 8
        + [pl.BlockSpec(memory_space=pl.ANY)] * len(shards),
        out_specs=[pl.BlockSpec(memory_space=pltpu.VMEM)] * len(shapes),
        scratch_shapes=collect_scratch(images, tokens) + collect_scratch(images, tokens) + scratch,
        compiler_params=pltpu.CompilerParams(
            collective_id=16 + layer_idx, has_side_effects=True, vmem_limit_bytes=ACT_VMEM
        ),
        cost_estimate=pl.CostEstimate(
            flops=30 * 10**9, bytes_accessed=15 * 2**20, transcendentals=0
        ),
        name="block_forward",
    )(residual, mod_vec, vec_bias, qkv_bias, up_bias, w_qkv, w_up, w_out, *shards)


def gelu_slope(values):
    root = math.sqrt(2.0 / math.pi)
    square = values * values
    tanh = jnp.tanh(root * (values + 0.044715 * values * square))
    half = 0.5 * (1.0 + tanh)
    slope = half + 0.5 * values * (1.0 - tanh * tanh) * root * (1.0 + 3.0 * 0.044715 * square)
    return values * half, slope


def norm_pull(values, scale_row, d_normed):
    normed, rstd = norm_parts(values)
    d_shift = jnp.sum(d_normed, axis=0, keepdims=True)
    d_scale = jnp.sum(d_normed * normed, axis=0, keepdims=True)
    inner = d_normed * (1.0 + scale_row)
    mean_one = jnp.mean(inner, axis=-1, keepdims=True)
    mean_two = jnp.mean(inner * normed, axis=-1, keepdims=True)
    return (inner - mean_one - normed * mean_two) * rstd, d_shift, d_scale


def backward_kernel(
    d_res_ref,
    mod_ref,
    res_ref,
    rows_a,
    qkv_ref,
    mixed_ref,
    branch_ref,
    mid_ref,
    rows_m,
    upper_ref,
    down_ref,
    w_qkv_ref,
    w_up_ref,
    w_out_ref,
    *rest,
):
    with_reduce = len(rest) > 24
    group_width = w_qkv_ref.shape[1] // 3
    w_attn_ref, w_down_ref = w_out_ref.at[0:group_width, :], w_out_ref.at[group_width:, :]
    terms, rest = (rest[:3], rest[3:]) if with_reduce else ((), rest)
    (
        d_res_out,
        d_w_qkv,
        d_w_up,
        d_out,
        d_mod,
        d_vec,
        d_qkv_bias,
        d_up_bias,
    ) = rest[:8]
    totals, rest = (rest[8:11], rest[11:]) if with_reduce else ((), rest[8:])
    (
    d_mid,
    d_rows_m,
    d_rows_a,
    act_low,
    d_upper,
    d_qkv,
    part_a,
    near_a,
    far_out_a,
    far_in_a,
    part_m,
    near_m,
    far_out_m,
    far_in_m,
    sends,
    recvs,
    ) = rest[:16]
    images = res_ref.shape[0]
    tokens = rows_a.shape[1]
    qkv_width = 3 * group_width
    units = w_up_ref.shape[1]
    reduce, last_step = None, 0
    if with_reduce:
        line = Line()
        greet(line)
        pair_in, way_in, way_out = rest[16:19], rest[19:22], rest[22:25]
        reduce = Reduce(line, terms, totals, pair_in, way_in, way_out, *rest[25:])
        last_step = line.size
    else:
        greet(None)
    spread_m = Spread(d_rows_m, sends.at[0], recvs.at[0])
    spread_a = Spread(d_rows_a, sends.at[1], recvs.at[1])
    collect_m = Collect(part_m, near_m, far_out_m, far_in_m, sends.at[2], recvs.at[2])
    collect_a = Collect(part_a, near_a, far_out_a, far_in_a, sends.at[3], recvs.at[3])
    d_vec[...] = jnp.zeros_like(d_vec)
    d_qkv_bias[...] = jnp.zeros_like(d_qkv_bias)
    d_up_bias[...] = jnp.zeros_like(d_up_bias)

    def mod_row(image, piece):
        return mod_ref[image, pl.ds(piece, 1), :]

    def start_down(image):
        d_res = d_res_ref[image]
        d_mod[image, pl.ds(5, 1), :] = jnp.sum(d_res * down_ref[image], axis=0, keepdims=True)
        d_down = d_res * mod_row(image, 5)
        d_vec[1:2, :] += jnp.sum(d_down, axis=0, keepdims=True)
        spread_m.put(image, d_down.astype(jnp.bfloat16))

    def feed(image):
        spread_m.wait(image)
        d_act = dot_nt(d_rows_m[image], w_down_ref[...])
        act, slope = gelu_slope(upper_ref[image])
        act_low[image] = act.astype(jnp.bfloat16)
        d_up = d_act * slope
        d_up_bias[...] += jnp.sum(d_up, axis=0, keepdims=True)
        d_up_low = d_up.astype(jnp.bfloat16)
        d_upper[image] = d_up_low
        collect_m.put(image, dot_nt(d_up_low, w_up_ref[...]))

    def rows_of(ref, width):
        return ref[...].reshape(images * tokens, width)

    def feed_weights():
        tile = 256

        def step(index, carry):
            at = pl.ds(pl.multiple_of(index * tile, tile), tile)
            grad = dot_tn(
                act_low[:, :, at].reshape(images * tokens, tile), rows_of(d_rows_m, D)
            )
            d_out[pl.ds(pl.multiple_of(group_width + index * tile, 64), tile), :] = grad.astype(
                jnp.bfloat16
            )
            grad = dot_tn(
                rows_m[:, :, at].reshape(images * tokens, tile), rows_of(d_upper, units)
            )
            d_w_up[pl.ds(pl.multiple_of(index * tile, tile), tile), :] = grad.astype(jnp.bfloat16)
            return carry

        lax.fori_loop(0, units // tile, step, 0)

    def middle(image):
        d_value, d_shift, d_scale = norm_pull(
            mid_ref[image], mod_row(image, 4), collect_m.take(image)
        )
        d_mod[image, pl.ds(3, 1), :] = d_shift
        d_mod[image, pl.ds(4, 1), :] = d_scale
        d_value = d_res_ref[image] + d_value
        d_mid[image] = d_value
        d_mod[image, pl.ds(2, 1), :] = jnp.sum(d_value * branch_ref[image], axis=0, keepdims=True)
        d_branch = d_value * mod_row(image, 2)
        d_vec[0:1, :] += jnp.sum(d_branch, axis=0, keepdims=True)
        spread_a.put(image, d_branch.astype(jnp.bfloat16))

    def attend(image):
        spread_a.wait(image)
        d_mixed = dot_nt(d_rows_a[image], w_attn_ref[...]).astype(jnp.bfloat16)
        qkv = qkv_ref[image]
        d_queries, d_keys, d_values = [], [], []
        scale_dot = HEAD_DIM ** (-0.5)
        for head in range(group_width // HEAD_DIM):
            queries = head_slice(qkv[:, :group_width], head)
            keys_in = head_slice(qkv[:, group_width : 2 * group_width], head)
            values_in = head_slice(qkv[:, 2 * group_width :], head)
            d_head = head_slice(d_mixed, head)
            probs = soft_rows(queries, keys_in)
            d_probs = dot_nt(d_head, values_in)
            d_values.append(dot_tn(probs.astype(jnp.bfloat16), d_head))
            inner = jnp.sum(probs * d_probs, axis=-1, keepdims=True)
            d_scores = (probs * (d_probs - inner)).astype(jnp.bfloat16)
            d_queries.append(dot_nn(d_scores, keys_in) * scale_dot)
            d_keys.append(dot_tn(d_scores, queries) * scale_dot)
        joined = jnp.concatenate(d_queries + d_keys + d_values, axis=1)
        d_qkv_bias[...] += jnp.sum(joined, axis=0, keepdims=True)
        joined = joined.astype(jnp.bfloat16)
        d_qkv[image] = joined
        collect_a.put(image, dot_nt(joined, w_qkv_ref[...]))

    def attend_weights():
        d_out[0:group_width, :] = dot_tn(
            rows_of(mixed_ref, group_width), rows_of(d_rows_a, D)
        ).astype(jnp.bfloat16)
        tile = 256

        def step(index, carry):
            at = pl.ds(pl.multiple_of(index * tile, tile), tile)
            grad = dot_tn(
                rows_a[:, :, at].reshape(images * tokens, tile), rows_of(d_qkv, qkv_width)
            )
            d_w_qkv[at, :] = grad.astype(jnp.bfloat16)
            return carry

        lax.fori_loop(0, D // tile, step, 0)

    def finish(image):
        d_value, d_shift, d_scale = norm_pull(
            res_ref[image], mod_row(image, 1), collect_a.take(image)
        )
        d_mod[image, pl.ds(0, 1), :] = d_shift
        d_mod[image, pl.ds(1, 1), :] = d_scale
        d_res_out[image] = d_mid[image] + d_value

    def close(image):
        spread_a.close(image)
        spread_m.close(image)
        collect_a.close(image)
        collect_m.close(image)

    each(images, start_down)
    if with_reduce:
        reduce.start()
    each(images, spread_m.forward)
    each(images, feed)
    run_ticks(reduce, 0, min(1, last_step - 1))
    each(images, collect_m.forward)
    feed_weights()
    run_ticks(reduce, 1, min(2, last_step - 1))
    each(images, middle)
    each(images, spread_a.forward)
    each(images, attend)
    each(images, collect_a.forward)
    run_ticks(reduce, 2, min(3, last_step - 1))
    attend_weights()
    each(images, finish)
    each(images, close)
    if with_reduce:
        each(max(last_step - 4, 0), lambda step: reduce.tick(step + 3))
        reduce.finish()


def backward_layer(d_residual, mod_vec, saved, weights, terms):
    images, count, _ = d_residual.shape
    tokens = 4 * count
    low, full = jnp.bfloat16, jnp.float32
    w_qkv, w_up, w_out = weights
    group_width, units = w_qkv.shape[1] // 3, w_up.shape[1]
    shapes = [
        ((images, count, D), full),
        ((D, 3 * group_width), low),
        ((D, units), low),
        ((group_width + units, D), low),
        ((images, 6, D), full),
        ((2, D), full),
        ((1, 3 * group_width), full),
        ((1, units), full),
    ]
    scratch = [
        pltpu.SemaphoreType.DMA((4, images, 3)),
        pltpu.SemaphoreType.DMA((4, images, 3)),
    ]
    if terms:
        spots = lax.axis_size("dp") // 2
        blocks = [term.shape[1:] for term in terms]
        shapes += [(block, full) for block in blocks]
        scratch += [pltpu.VMEM((spots,) + block, low) for block in blocks]
        scratch += [pltpu.VMEM((2, spots) + block, low) for block in blocks]
        scratch += [pltpu.VMEM((2, spots) + block, low) for block in blocks]
        scratch += [
            pltpu.SemaphoreType.DMA((3, spots, 3)),
            pltpu.SemaphoreType.DMA((3, spots, 3)),
        ]
    return pl.pallas_call(
        backward_kernel,
        out_shape=[jax.ShapeDtypeStruct(*shape) for shape in shapes],
        in_specs=[pl.BlockSpec(memory_space=pltpu.VMEM)] * (14 + len(terms)),
        out_specs=[pl.BlockSpec(memory_space=pltpu.VMEM)] * len(shapes),
        scratch_shapes=[
            pltpu.VMEM((images, count, D), full),
            pltpu.VMEM((images, tokens, D), low),
            pltpu.VMEM((images, tokens, D), low),
            pltpu.VMEM((images, tokens, units), low),
            pltpu.VMEM((images, tokens, units), low),
            pltpu.VMEM((images, tokens, 3 * group_width), low),
        ]
        + collect_scratch(images, tokens)
        + collect_scratch(images, tokens)
        + scratch,
        compiler_params=pltpu.CompilerParams(
            collective_id=21 if terms else 23, has_side_effects=True, vmem_limit_bytes=ACT_VMEM
        ),
        cost_estimate=pl.CostEstimate(
            flops=60 * 10**9, bytes_accessed=25 * 2**20, transcendentals=0
        ),
        name="block_backward",
    )(d_residual, mod_vec, *saved, *weights, *terms)


def dense_nt(left_op, right_op):
    return lax.dot_general(
        left_op,
        right_op,
        (((1,), (1,)), ((), ())),
        precision=PRECISE,
        preferred_element_type=jnp.float32,
    )


def dense_tn(left_op, right_op):
    return lax.dot_general(
        left_op,
        right_op,
        (((0,), (0,)), ((), ())),
        precision=PRECISE,
        preferred_element_type=jnp.float32,
    )


def chosen(shape, rule, kind):
    row = lax.broadcasted_iota(jnp.int32, shape, 0)
    col = lax.broadcasted_iota(jnp.int32, shape, 1)
    return jnp.where(rule(row, col), 1.0, 0.0).astype(kind)


def fold(values):
    groups = values.shape[-2] // 8
    pieces = [values[..., 8 * at : 8 * at + 8, :] for at in range(groups)]
    used = groups * values.shape[-1]
    if used % 128:
        pieces.append(jnp.zeros(values.shape[:-2] + (8, 128 - used % 128), values.dtype))
    return jnp.concatenate(pieces, axis=-1)


def folded_lanes(cols, count):
    return -(-(cols // 8 * count) // 128) * 128


def unfold(values, cols, count):
    pieces = [values[..., at * count : (at + 1) * count] for at in range(cols // 8)]
    return jnp.concatenate(pieces, axis=-2)


def slots_of(images):
    return -(-LAYERS * images // 16) * 16


def head_kernel(
    images,
    small_ref,
    feats_ref,
    table_ref,
    time_ref,
    second_ref,
    shift_ref,
    scale_ref,
    bias_ref,
    mod_ref,
    *rest,
):
    shards = rest[0:3]
    (
        small_all,
        feats_out,
        pre_time_out,
        hidden_out,
        pre_signal_out,
        signal_out,
        final_all,
        mod_all,
    ) = rest[3:11]
    wholes = rest[11:14]
    (
        feats_all,
        hidden_own,
        hidden_all,
        signal_own,
        signal_all,
        final_own,
        mod_part,
        mod_in,
        mod_own,
        small_dp,
    ) = rest[14:24]
    crowds = [rest[24 + 3 * index : 27 + 3 * index] for index in range(8)]
    gather_sems = rest[48:]
    dp_size = lax.axis_size("dp")
    tensor_size = lax.axis_size("tensor")
    dp_rank = lax.axis_index("dp")
    images_all = images * dp_size
    slots = mod_own.shape[0]
    greet_group("all")
    gather = Gather(Line(), [shard.at[0] for shard in shards], wholes, *gather_sems)
    feats = Crowd("dp", lambda place: feats_ref, feats_all, *crowds[0])
    small = Crowd("dp", lambda place: small_ref, small_dp, *crowds[1])
    small_spread = Crowd("tensor", lambda place: small_dp, small_all, *crowds[7])
    hidden = Crowd("all", lambda place: hidden_own, hidden_all, *crowds[2])
    signal = Crowd("all", lambda place: signal_own, signal_all, *crowds[3])
    final = Crowd("all", lambda place: final_own.at[place // tensor_size], final_all, *crowds[4])
    mod_sum = Crowd("dp", lambda place: mod_part.at[place], mod_in, *crowds[5])
    line = gather.line
    first, last = line.at == 0, line.at == line.size - 1
    feats.start()
    gather.start()
    feats.wait()
    pick = chosen(
        (images_all, 8 * dp_size),
        lambda row, col: (row // images == col // 8) & (lax.rem(row, images) == lax.rem(col, 8)),
        jnp.float32,
    )
    feats_sum = dense(pick, feats_all[...].reshape(8 * dp_size, feats_all.shape[2]))
    feats_out[...] = feats_sum
    pre_time = dense_nt(time_ref[...], feats_sum[:, 0:FREQ]) + bias_ref[:, 1:2]
    pre_time_out[...] = pre_time
    hidden_own[...] = fold(jax.nn.silu(pre_time))
    hidden.start()
    class_lanes = -(-CLASSES // 128) * 128
    labels = jnp.round(feats_sum[:, FREQ : FREQ + 1]).astype(jnp.int32)
    lane = lax.broadcasted_iota(jnp.int32, (images_all, class_lanes), 1)
    onehot = jnp.where(lane == labels, 1.0, 0.0)
    class_part = dense_nt(table_ref[:, 0:class_lanes], onehot) + bias_ref[:, 2:3]
    small.start()
    for way in (UP, DOWN):
        gather.hand_on(1, way)
    gather.hand_over(1, UP)
    gather.hand_over(1, DOWN, first)
    hidden.wait()
    cols = second_ref.shape[0]
    hidden_full = unfold(hidden_all[...], cols, images_all).reshape(D, images_all)
    hidden_out[...] = hidden_full
    pre_signal = dense(second_ref[...], hidden_full) + class_part
    pre_signal_out[...] = pre_signal
    signal_own[...] = fold(jax.nn.silu(pre_signal))
    signal.start()
    for way in (UP, DOWN):
        gather.hand_on(2, way)
    gather.hand_over(1, DOWN, jnp.logical_not(first))
    gather.hand_over(2, UP, last)
    gather.hand_over(2, DOWN, first)
    small.wait()
    small_spread.start()
    signal.wait()
    signal_full = unfold(signal_all[...], cols, images_all).reshape(D, images_all)
    signal_out[...] = signal_full
    mod_rows = mod_ref.shape[1]
    own_rows = pl.ds(pl.multiple_of(dp_rank * mod_rows, 8), mod_rows)
    signal_low = signal_out[own_rows, :].astype(jnp.bfloat16)
    total = None
    for layer_idx in range(LAYERS):
        pick = chosen(
            (images_all, dp_size * slots),
            lambda row, col: (
                (row // images == col // slots)
                & (lax.rem(row, images) + layer_idx * images == lax.rem(col, slots))
            ),
            jnp.bfloat16,
        )
        placed = dot_nn(signal_low, pick).astype(jnp.bfloat16)
        term = dot_tn(placed, mod_ref[layer_idx])
        total = term if total is None else total + term
    mod_part[...] = total.reshape(mod_part.shape)
    mod_sum.start()
    gather.hand_over(2, UP, jnp.logical_not(last))
    gather.hand_over(2, DOWN, jnp.logical_not(first))
    finals = jnp.concatenate(
        [
            dense(shift_ref[...], signal_full) + bias_ref[:, 3:4],
            dense(scale_ref[...], signal_full) + bias_ref[:, 4:5],
            jnp.zeros((128 - 2 * shift_ref.shape[0], images_all), jnp.float32),
        ],
        axis=0,
    )
    pick = chosen(
        (8 * dp_size, images_all),
        lambda row, col: (row // 8 == col // images) & (lax.rem(row, 8) == lax.rem(col, images)),
        jnp.float32,
    )
    final_own[...] = dense_nt(pick, finals).reshape(final_own.shape)
    final.start()
    run_ticks(gather, 3, min(4, dp_size // 2))
    mod_sum.wait()
    mod_own[...] = jnp.sum(mod_in[...], axis=0)
    mod_spread = Crowd("tensor", lambda place: mod_own, mod_all, *crowds[6])
    mod_spread.start()
    each(max(dp_size // 2 - 4, 0), lambda step: gather.tick(step + 4))
    small_spread.wait()
    final.wait()
    mod_spread.wait()
    gather.finish()


def head_call(small, feats, table, times, second, shift, scale, bias, mod_low, shards, images):
    dp_size, tensor_size = lax.axis_size("dp"), lax.axis_size("tensor")
    size = dp_size * tensor_size
    images_all = images * dp_size
    cols = table.shape[0]
    slots = slots_of(images)
    folded = folded_lanes(cols, images_all)
    full, low = jnp.float32, jnp.bfloat16
    shapes = [
        ((tensor_size, dp_size) + small.shape, full),
        ((images_all, feats.shape[1]), full),
        ((cols, images_all), full),
        ((D, images_all), full),
        ((cols, images_all), full),
        ((D, images_all), full),
        ((size, 8, 128), full),
        ((tensor_size, slots, mod_low.shape[2]), full),
    ] + [((dp_size,) + shard.shape[1:], low) for shard in shards]
    scratch = [
        pltpu.VMEM((dp_size,) + feats.shape, full),
        pltpu.VMEM((8, folded), full),
        pltpu.VMEM((size, 8, folded), full),
        pltpu.VMEM((8, folded), full),
        pltpu.VMEM((size, 8, folded), full),
        pltpu.VMEM((dp_size, 8, 128), full),
        pltpu.VMEM((dp_size, slots, mod_low.shape[2]), full),
        pltpu.VMEM((dp_size, slots, mod_low.shape[2]), full),
        pltpu.VMEM((slots, mod_low.shape[2]), full),
        pltpu.VMEM((dp_size,) + small.shape, full),
    ]
    for count in (dp_size, dp_size, size, size, size, dp_size, tensor_size, tensor_size):
        scratch += crowd_scratch(count)
    scratch += [
        pltpu.SemaphoreType.DMA((3, dp_size // 2, 3)),
        pltpu.SemaphoreType.DMA((3, dp_size // 2, 3)),
        pltpu.SemaphoreType.DMA((3,)),
    ]
    return pl.pallas_call(
        functools.partial(head_kernel, images),
        out_shape=[jax.ShapeDtypeStruct(*shape) for shape in shapes],
        in_specs=[pl.BlockSpec(memory_space=pltpu.VMEM)] * 9
        + [pl.BlockSpec(memory_space=pl.ANY)] * len(shards),
        out_specs=[pl.BlockSpec(memory_space=pltpu.VMEM)] * len(shapes),
        scratch_shapes=scratch,
        compiler_params=pltpu.CompilerParams(
            collective_id=30, has_side_effects=True, vmem_limit_bytes=ACT_VMEM
        ),
        name="head",
    )(small, feats, table, times, second, shift, scale, bias, mod_low, *shards)


def square_sum(values):
    return jnp.sum(jnp.sum(values * values, axis=0, keepdims=True), axis=1, keepdims=True)


def tail_kernel(
    images,
    final_at,
    row_ref,
    mod_ref,
    weight_ref,
    second_ref,
    shift_ref,
    scale_ref,
    pre_signal_ref,
    pre_time_ref,
    feats_ref,
    hidden_ref,
    signal_ref,
    loss_ref,
    *rest,
):
    terms, others = rest[0:3], rest[3 : 3 * LAYERS]
    rest = rest[3 * LAYERS :]
    (
        row_sums,
        vector_sums,
        class_grad,
        time_grad,
        second_grad,
        shift_grad,
        scale_grad,
        mod_grad,
        scalar_sums,
    ) = rest[0:9]
    totals = rest[9:12]
    (
        row_in,
        row_mid,
        row_fin,
        mod_in,
        mod_low,
        d_mod_all,
        signal_part,
        signal_out,
        signal_in,
        hidden_out,
        hidden_in,
        scalar_own,
        scalar_in,
    ) = rest[12:25]
    pair_in, way_in, way_out = rest[25:28], rest[28:31], rest[31:34]
    crowds = [rest[34 + 3 * index : 37 + 3 * index] for index in range(7)]
    reduce_sems = rest[55:]
    dp_size = lax.axis_size("dp")
    tensor_size = lax.axis_size("tensor")
    places = dp_size * tensor_size
    dp_rank = lax.axis_index("dp")
    images_all = images * dp_size
    cols, lanes = row_ref.shape[2:]
    mod_rows = weight_ref.shape[1]
    slots = mod_low.shape[0]
    last_step = dp_size // 2
    greet_group("all")
    reduce = Reduce(Line(), terms, totals, pair_in, way_in, way_out, *reduce_sems)
    mod_sum = Crowd("tensor", lambda place: mod_ref.at[place], mod_in, *crowds[0])
    rows = Crowd("tensor", lambda place: row_ref.at[:, place], row_in, *crowds[1])
    mod_spread = Crowd("dp", lambda place: mod_low, d_mod_all, *crowds[2])
    signal = Crowd("all", lambda place: signal_out.at[place], signal_in, *crowds[3])
    hidden = Crowd("all", lambda place: hidden_out.at[place], hidden_in, *crowds[4])
    row_cross = Crowd("dp", lambda place: row_mid.at[place], row_fin, *crowds[5])
    scalars = Crowd("all", lambda place: scalar_own, scalar_in, *crowds[6])
    mod_sum.start()
    rows.start()
    reduce.send_pair(0)
    mod_sum.wait()
    mod_low[...] = jnp.sum(mod_in[...], axis=0).astype(jnp.bfloat16)
    mod_spread.start()
    rows.wait()
    row_mid[...] = jnp.sum(row_in[...], axis=0)
    row_cross.start()
    reduce.send_pair(1)
    other_squares = sum(square_sum(other[...]) for other in others)
    row_cross.wait()
    row_total = jnp.sum(row_fin[...], axis=0)
    row_sums[...] = row_total
    joined = jnp.concatenate([row_fin[at] for at in range(dp_size)], axis=1)

    def final_of(piece):
        return dense(
            joined,
            chosen(
                (dp_size * lanes, images_all),
                lambda row, col: (
                    (row // lanes == col // images)
                    & (lax.rem(row, lanes) == final_at + piece * images + lax.rem(col, images))
                ),
                jnp.float32,
            ),
        )

    d_shift, d_scale = final_of(0), final_of(1)
    signal_part[...] = dense_tn(shift_ref[...], d_shift) + dense_tn(scale_ref[...], d_scale)
    mod_spread.wait()
    d_mod = d_mod_all[...].reshape(dp_size * slots, mod_low.shape[1])
    own_rows = pl.ds(pl.multiple_of(dp_rank * mod_rows, 8), mod_rows)

    def layer_pick(layer_idx, kind):
        return chosen(
            (dp_size * slots, images_all),
            lambda row, col: (
                (row // slots == col // images)
                & (lax.rem(row, slots) == layer_idx * images + lax.rem(col, images))
            ),
            kind,
        )

    for layer_idx in range(LAYERS):
        signal_part[own_rows, :] += dense(
            dot_nt(weight_ref[layer_idx], d_mod), layer_pick(layer_idx, jnp.float32)
        )
    signal_out[...] = fold(signal_part[...].reshape(places, cols, images_all))
    signal.start()
    reduce.send_pair(2)
    run_ticks(reduce, 0, min(1, last_step - 1))
    signal_low = signal_ref[own_rows, :].astype(jnp.bfloat16)
    for layer_idx in range(LAYERS):
        placed = dot_nt(signal_low, layer_pick(layer_idx, jnp.bfloat16)).astype(jnp.bfloat16)
        grad = dot_nn(placed, d_mod)
        mod_grad[layer_idx] = grad
        other_squares = other_squares + square_sum(grad)
    grad = dense_nt(d_shift, signal_ref[...])
    shift_grad[...] = grad
    other_squares = other_squares + square_sum(grad)
    grad = dense_nt(d_scale, signal_ref[...])
    scale_grad[...] = grad
    other_squares = other_squares + square_sum(grad)
    lane = lax.broadcasted_iota(jnp.int32, row_total.shape, 1)
    other_squares = other_squares + square_sum(jnp.where(lane < final_at, row_total, 0.0))
    signal.wait()
    d_signal = unfold(jnp.sum(signal_in[...], axis=0), cols, images_all)
    d_signal = d_signal * silu_slope(pre_signal_ref[...])
    d_hidden = dense_tn(second_ref[...], d_signal)
    hidden_out[...] = fold(d_hidden.reshape(places, cols, images_all))
    hidden.start()
    each(max(last_step - 3, 0), lambda step: reduce.send_pair(step + 3))
    run_ticks(reduce, 1, min(2, last_step - 1))
    labels = jnp.round(feats_ref[:, FREQ : FREQ + 1]).astype(jnp.int32)
    class_lane = lax.broadcasted_iota(jnp.int32, (images_all, class_grad.shape[1]), 1)
    grad = dense(d_signal, jnp.where(class_lane == labels, 1.0, 0.0))
    class_grad[...] = grad
    other_squares = other_squares + square_sum(grad)
    grad = dense_nt(d_signal, hidden_ref[...])
    second_grad[...] = grad
    other_squares = other_squares + square_sum(grad)
    hidden.wait()
    d_hidden = unfold(jnp.sum(hidden_in[...], axis=0), cols, images_all)
    d_hidden = d_hidden * silu_slope(pre_time_ref[...])
    grad = dense(d_hidden, feats_ref[:, 0:FREQ])
    time_grad[...] = grad
    other_squares = other_squares + square_sum(grad)
    vectors = [
        jnp.sum(values, axis=1, keepdims=True) for values in (d_hidden, d_signal, d_shift, d_scale)
    ]
    lane = lax.broadcasted_iota(jnp.int32, vector_sums.shape, 1)
    grad = sum(jnp.where(lane == at, vector, 0.0) for at, vector in enumerate(vectors))
    vector_sums[...] = grad
    other_squares = other_squares + square_sum(grad)
    run_ticks(reduce, 2, min(3, last_step - 1))
    each(max(last_step - 4, 0), lambda step: reduce.tick(step + 3))
    reduce.finish()
    for total in totals:
        other_squares = other_squares + square_sum(total[...])
    lane = lax.broadcasted_iota(jnp.int32, scalar_own.shape, 1)
    scalar_own[...] = jnp.where(lane == 0, loss_ref[...], other_squares)
    scalars.start()
    scalars.wait()
    scalar_sums[...] = jnp.sum(scalar_in[...], axis=0)


def tail_call(
    rows, mods, mod_low, second, shift, scale, pre_signal, pre_time, feats, hidden, signal, loss,
    terms, others, images, at,
):
    dp_size, tensor_size = lax.axis_size("dp"), lax.axis_size("tensor")
    size = dp_size * tensor_size
    images_all = images * dp_size
    cols, lanes = rows.shape[2:]
    folded = folded_lanes(cols, images_all)
    full, low = jnp.float32, jnp.bfloat16
    spots = dp_size // 2
    blocks = [term.shape[1:] for term in terms]
    shapes = [
        ((cols, lanes), full),
        ((cols, 128), full),
        ((cols, -(-CLASSES // 128) * 128), full),
        ((cols, FREQ), full),
        ((cols, D), full),
        ((cols, D), full),
        ((cols, D), full),
        (mod_low.shape, full),
        ((8, 128), full),
    ] + [(block, full) for block in blocks]
    scratch = [
        pltpu.VMEM((tensor_size, dp_size, cols, lanes), full),
        pltpu.VMEM((dp_size, cols, lanes), full),
        pltpu.VMEM((dp_size, cols, lanes), full),
        pltpu.VMEM(mods.shape, full),
        pltpu.VMEM(mods.shape[1:], low),
        pltpu.VMEM((dp_size,) + mods.shape[1:], low),
        pltpu.VMEM((D, images_all), full),
        pltpu.VMEM((size, 8, folded), full),
        pltpu.VMEM((size, 8, folded), full),
        pltpu.VMEM((size, 8, folded), full),
        pltpu.VMEM((size, 8, folded), full),
        pltpu.VMEM((8, 128), full),
        pltpu.VMEM((size, 8, 128), full),
    ]
    scratch += [pltpu.VMEM((spots,) + block, low) for block in blocks]
    scratch += [pltpu.VMEM((2, spots) + block, low) for block in blocks]
    scratch += [pltpu.VMEM((2, spots) + block, low) for block in blocks]
    for count in (tensor_size, tensor_size, dp_size, size, size, dp_size, size):
        scratch += crowd_scratch(count)
    scratch += [
        pltpu.SemaphoreType.DMA((3, spots, 3)),
        pltpu.SemaphoreType.DMA((3, spots, 3)),
    ]
    return pl.pallas_call(
        functools.partial(tail_kernel, images, at),
        out_shape=[jax.ShapeDtypeStruct(*shape) for shape in shapes],
        in_specs=[pl.BlockSpec(memory_space=pltpu.VMEM)] * (12 + len(terms) + len(others)),
        out_specs=[pl.BlockSpec(memory_space=pltpu.VMEM)] * len(shapes),
        scratch_shapes=scratch,
        compiler_params=pltpu.CompilerParams(
            collective_id=31, has_side_effects=True, vmem_limit_bytes=ACT_VMEM
        ),
        name="tail",
    )(
        rows, mods, mod_low, second, shift, scale, pre_signal, pre_time, feats, hidden, signal,
        loss, *terms, *others,
    )


def adam_update(weight, first, second, grad, factor, first_fix, second_fix):
    clipped = grad * factor
    first_new = BETA_ONE * first + (1.0 - BETA_ONE) * clipped
    second_new = BETA_TWO * second + (1.0 - BETA_TWO) * clipped * clipped
    step_size = first_new / first_fix / (jnp.sqrt(second_new / second_fix) + ADAM_EPS)
    change = -LEARN_RATE * (step_size + DECAY * weight)
    master = weight + change
    return (master, first_new, second_new, master.astype(jnp.bfloat16), change)


def local(
    latents,
    target_noise,
    timesteps,
    labels,
    step_count,
    embed_table,
    layer_in,
    layer_out,
    layer_ada,
    embed_first,
    embed_second,
    input_first,
    input_second,
    output_first,
    output_second,
    mod_first,
    mod_second,
):
    tensor_size = lax.axis_size("tensor")
    tensor_rank = lax.axis_index("tensor")
    images = latents.shape[0]
    grid_side = SIDE // PATCH
    local_rows = grid_side // tensor_size
    tokens_all = grid_side * grid_side
    heads_local = HEADS // tensor_size
    group_width = heads_local * HEAD_DIM
    unit_count = FF // tensor_size
    patch_in = PATCH * PATCH * CHANNELS
    count_all = images * lax.axis_size("dp") * tokens_all * patch_in
    patch_start, time_start, second_start, final_start, head_start, vector_start, layer_start = (
        table_starts()
    )
    layer_rows = 10 + FF // D
    dp_rank = lax.axis_index("dp")
    dp_size = lax.axis_size("dp")
    place_count = dp_size * tensor_size
    images_all = images * dp_size
    table_cols = lax.reduce_precision(embed_table.T, 8, 7)
    cols = table_cols.shape[0]
    mod_rows = layer_ada.shape[1]
    mod_cols = layer_ada.shape[2]
    mod_low = layer_ada.astype(jnp.bfloat16)

    def col_block(row_start, row_count):
        return table_cols[:, row_start : row_start + row_count]

    vector_count = 5 + LAYERS * layer_rows
    small_count = 2 * patch_in + vector_count
    lanes = -(-(small_count + 2 * images) // 128) * 128
    shards_in = layer_in[:, :, 0].astype(jnp.bfloat16)
    shards = (
        shards_in[:, :, : 3 * group_width],
        shards_in[:, :, 3 * group_width :],
        layer_out[:, 0].astype(jnp.bfloat16),
    )
    second_cols = col_block(second_start, D)
    shift_cols = col_block(final_start, D)
    scale_cols = col_block(final_start + D, D)
    fused = cols % 8 == 0 and images <= 8
    if fused:
        small_send = jnp.concatenate(
            [
                col_block(patch_start, patch_in),
                col_block(head_start, patch_in + vector_count),
                jnp.zeros((cols, lanes - small_count), jnp.float32),
            ],
            axis=1,
        )
        feats_send = jnp.concatenate(
            [
                time_features(timesteps),
                jnp.broadcast_to(labels.astype(jnp.float32)[:, None], (images, 128)),
            ],
            axis=1,
        )
        feats_send = jnp.pad(feats_send, ((0, 8 - images), (0, 0)))
        outs = head_call(
            small_send,
            feats_send,
            table_cols,
            col_block(time_start, FREQ),
            second_cols,
            shift_cols,
            scale_cols,
            col_block(vector_start, 5),
            mod_low,
            shards,
            images,
        )
        small_all, feats_all, pre_time, hidden, pre_signal, signal, final_all, mod_full = outs[:8]
        wholes = outs[8:]
        small_all = small_all.transpose(1, 0, 2, 3)
        time_feats = feats_all[:, :FREQ]
        labels_all = jnp.round(feats_all[:, FREQ]).astype(jnp.int32)
        signal_low = lax.dynamic_slice_in_dim(
            signal.astype(jnp.bfloat16), dp_rank * mod_rows, mod_rows, 0
        )
        final_own = final_all[:, :images, : 2 * cols].reshape(place_count, images, 2, cols)
        final_own = final_own.transpose(2, 1, 0, 3).reshape(2, images, D)
        mod_full = mod_full[:, : LAYERS * images].reshape(tensor_size, LAYERS, images, mod_cols)
        mod_full = mod_full.transpose(1, 2, 0, 3).reshape(LAYERS, images, tensor_size * mod_cols)
    else:
        scalar_lanes = jnp.concatenate([timesteps, labels]).astype(jnp.float32)
        small_send = jnp.concatenate(
            [
                col_block(patch_start, patch_in),
                col_block(head_start, patch_in + vector_count),
                jnp.broadcast_to(scalar_lanes[None, :], (cols, 2 * images)),
                jnp.zeros((cols, lanes - small_count - 2 * images), jnp.float32),
            ],
            axis=1,
        )
        small_all = exchange(small_send, "all", False, 1)
        scalars_all = small_all[::tensor_size, 0, small_count : small_count + 2 * images].astype(
            jnp.int32
        )
        timesteps_all = scalars_all[:, :images].reshape(images_all)
        labels_all = scalars_all[:, images:].reshape(images_all)
        time_feats = time_features(timesteps_all)
        onehot = (labels_all[:, None] == jnp.arange(CLASSES, dtype=jnp.int32)[None, :]).astype(
            jnp.float32
        )
        pre_time = dense(col_block(time_start, FREQ), time_feats.T) + col_block(vector_start + 1, 1)
        hidden = exchange(jax.nn.silu(pre_time), "all", False, 2).reshape(D, images_all)
        pre_signal = (
            dense(second_cols, hidden)
            + col_block(vector_start + 2, 1)
            + dense(col_block(0, CLASSES), onehot.T)
        )
        signal = exchange(jax.nn.silu(pre_signal), "all", False, 3).reshape(D, images_all)
        final_send = jnp.concatenate(
            [
                dense(shift_cols, signal) + col_block(vector_start + 3, 1),
                dense(scale_cols, signal) + col_block(vector_start + 4, 1),
            ],
            axis=0,
        )
        final_all = exchange(final_send, "all", False, 4).reshape(place_count, 2, cols, images_all)
        final_own = lax.dynamic_slice_in_dim(final_all, dp_rank * images, images, 3)
        final_own = final_own.transpose(1, 3, 0, 2).reshape(2, images, D)
        signal_low = lax.dynamic_slice_in_dim(
            signal.astype(jnp.bfloat16), dp_rank * mod_rows, mod_rows, 0
        )
        mod_part = jnp.einsum("db,lde->ble", signal_low, mod_low, preferred_element_type=jnp.float32)
        mod_part = mod_part.reshape(dp_size, images * LAYERS, mod_cols)
        mod_local = jnp.sum(exchange(mod_part, "dp", True, 5), axis=0)
        mod_full = exchange(mod_local, "tensor", False, 6)
        mod_full = mod_full.reshape(tensor_size, images, LAYERS, mod_cols)
        mod_full = mod_full.transpose(2, 1, 0, 3).reshape(LAYERS, images, tensor_size * mod_cols)
        wholes = [lax.all_gather(shard[0], "dp") for shard in shards]
    small_rows = small_all.reshape(D, lanes).T
    patch_w = small_rows[0:patch_in]
    head_w = small_rows[patch_in : 2 * patch_in]
    vectors = small_rows[2 * patch_in : 2 * patch_in + 5]
    bias_all = small_rows[2 * patch_in + 5 : small_count]
    onehot = (labels_all[:, None] == jnp.arange(CLASSES, dtype=jnp.int32)[None, :]).astype(
        jnp.float32
    )
    final_shift, final_scale = final_own[0], final_own[1]
    pixels = patchify(latents, local_rows)
    targets = patchify(target_noise, local_rows)
    keep_coef, drop_coef = noise_levels(timesteps)
    noisy = keep_coef[:, None, None] * pixels + drop_coef[:, None, None] * targets
    residual = (
        jnp.einsum("btp,pd->btd", noisy, patch_w, precision=PRECISE)
        + vectors[0]
        + position_table(tensor_rank * local_rows, local_rows)[None]
    )
    saved_acts = []
    bias_all = bias_all.reshape(LAYERS, layer_rows, D)
    mod_vecs = mod_full.reshape(LAYERS, images, 6, D) + bias_all[:, None, 0:6]
    part_bias = lax.dynamic_slice_in_dim(
        bias_all[:, 8:10], tensor_rank * group_width, group_width, 2
    )
    qkv_bias = jnp.concatenate(
        [part_bias[:, 0], jnp.zeros((LAYERS, group_width), jnp.float32), part_bias[:, 1]], axis=1
    )
    up_bias = lax.dynamic_slice_in_dim(
        bias_all[:, 10:].reshape(LAYERS, FF), tensor_rank * unit_count, unit_count, 1
    )
    for layer_idx in range(LAYERS):
        weights = (
            wholes[0].reshape(D, 3 * group_width),
            wholes[1].reshape(D, unit_count),
            wholes[2].reshape(group_width + unit_count, D),
        )
        outs = forward_layer(
            residual,
            mod_vecs[layer_idx],
            bias_all[layer_idx, 6:8],
            qkv_bias[layer_idx : layer_idx + 1],
            up_bias[layer_idx : layer_idx + 1],
            *weights,
            shards if layer_idx + 1 < LAYERS else (),
            layer_idx,
        )
        wholes = outs[9:]
        saved_acts.append((mod_vecs[layer_idx], (residual,) + tuple(outs[1:9]), weights))
        residual = outs[0]
    final_in, final_norm_pull = jax.vjp(modulate, residual, final_shift, final_scale)
    predicted = jnp.einsum("btd,pd->btp", final_in, head_w, precision=PRECISE)
    error_all = predicted - targets
    loss_part = jnp.sum(error_all * error_all) / count_all
    d_pred = 2.0 * error_all / count_all
    d_head = jnp.einsum("btp,btd->pd", d_pred, final_in, precision=PRECISE)
    d_final = jnp.einsum("btp,pd->btd", d_pred, head_w, precision=PRECISE)
    d_residual, d_final_shift, d_final_scale = final_norm_pull(d_final)
    totals = []
    terms = ()
    bias_parts = []
    for layer_idx in reversed(range(LAYERS)):
        mod_vec, saved, weights = saved_acts[layer_idx]
        outs = backward_layer(d_residual, mod_vec, saved, weights, terms)
        d_residual, d_w_qkv, d_w_up, d_w_out, d_mod_vec, d_vec, d_qkv_bias, d_up_bias = outs[:8]
        if terms:
            totals.insert(0, outs[8:])
        terms = [
            term.reshape((dp_size, -1) + term.shape[1:]) for term in (d_w_qkv, d_w_up, d_w_out)
        ]
        bias_parts.insert(0, (d_mod_vec, d_vec, d_qkv_bias, d_up_bias))
    d_mods, d_vecs, d_qkv_rows, d_up_rows = [jnp.stack(parts) for parts in zip(*bias_parts)]
    part_rows = jnp.stack([d_qkv_rows[:, 0, :group_width], d_qkv_rows[:, 0, 2 * group_width :]], 1)
    bias_blocks = jnp.concatenate(
        [
            jnp.sum(d_mods, axis=1),
            d_vecs,
            lax.dynamic_update_slice_in_dim(
                jnp.zeros((LAYERS, 2, D), jnp.float32), part_rows, tensor_rank * group_width, 2
            ),
            lax.dynamic_update_slice_in_dim(
                jnp.zeros((LAYERS, FF), jnp.float32), d_up_rows[:, 0], tensor_rank * unit_count, 1
            ).reshape(LAYERS, FF // D, D),
        ],
        axis=1,
    ).reshape(LAYERS * layer_rows, D)
    d_patch_w = jnp.einsum("btp,btd->pd", noisy, d_residual, precision=PRECISE)
    d_patch_b = jnp.sum(d_residual, axis=(0, 1))
    row_parts = jnp.concatenate(
        [d_patch_w, d_head, d_patch_b[None], bias_blocks, d_final_shift, d_final_scale],
        axis=0,
    )
    row_count = row_parts.shape[0]
    row_lanes = -(-row_count // 128) * 128
    row_parts = jnp.pad(row_parts, ((0, row_lanes - row_count), (0, 0)))
    final_at = row_count - 2 * images
    row_send = row_parts.T.reshape(dp_size, tensor_size, cols, row_lanes)
    mod_send = d_mods.reshape(LAYERS * images, tensor_size, mod_cols)
    mod_send = mod_send.transpose(1, 0, 2)
    if fused:
        slots = slots_of(images)
        outs = tail_call(
            row_send,
            jnp.pad(mod_send, ((0, 0), (0, slots - LAYERS * images), (0, 0))),
            mod_low,
            second_cols,
            shift_cols,
            scale_cols,
            pre_signal,
            pre_time,
            feats_all,
            hidden,
            signal,
            loss_part.reshape(1, 1),
            terms,
            [block for total in totals for block in total],
            images,
            final_at,
        )
        row_sums, vector_sums, class_grad, time_grad, second_grad, shift_grad, scale_grad = outs[:7]
        mod_grad, scalar_sums = outs[7:9]
        totals.insert(0, outs[9:])
        vector_sums = vector_sums[:, 0:4]
        class_grad = class_grad[:, :CLASSES]
        scalar_sums = scalar_sums[0]
    else:
        totals.insert(
            0,
            [
                lax.psum_scatter(term, "dp", scatter_dimension=0).astype(jnp.float32)
                for term in terms
            ],
        )
        row_all = exchange(row_send.reshape(place_count, cols, row_lanes), "all", True, 7)
        row_sums = jnp.sum(row_all, axis=0)
        final_sums = jnp.sum(
            row_all[:, :, final_at:row_count].reshape(dp_size, tensor_size, cols, 2, images), axis=1
        )
        final_sums = final_sums.transpose(2, 1, 0, 3).reshape(2, cols, images_all)
        d_shift_cols, d_scale_cols = final_sums[0], final_sums[1]
        d_mod_own = jnp.sum(exchange(mod_send, "tensor", True, 8), axis=0)
        d_mod_low = exchange(d_mod_own.astype(jnp.bfloat16), "dp", False, 9)
        d_mod_low = d_mod_low.reshape(dp_size, LAYERS, images, mod_cols)
        d_mod_low = d_mod_low.transpose(1, 0, 2, 3).reshape(LAYERS, images_all, mod_cols)
        d_signal_rows = jnp.einsum(
            "lbe,lde->db", d_mod_low, mod_low, preferred_element_type=jnp.float32
        )
        d_signal_part = dense(shift_cols.T, d_shift_cols) + dense(scale_cols.T, d_scale_cols)
        d_signal_part = d_signal_part + lax.dynamic_update_slice_in_dim(
            jnp.zeros((D, images_all), jnp.float32), d_signal_rows, dp_rank * mod_rows, 0
        )
        d_signal_cols = jnp.sum(
            exchange(d_signal_part.reshape(place_count, cols, images_all), "all", True, 10), axis=0
        )
        d_pre_signal = d_signal_cols * silu_slope(pre_signal)
        d_hidden_part = dense(second_cols.T, d_pre_signal)
        d_hidden_cols = jnp.sum(
            exchange(d_hidden_part.reshape(place_count, cols, images_all), "all", True, 11), axis=0
        )
        d_hidden = d_hidden_cols * silu_slope(pre_time)
        mod_grad = jnp.einsum(
            "db,lbe->lde", signal_low, d_mod_low, preferred_element_type=jnp.float32
        )
        class_grad = dense(d_pre_signal, onehot)
        time_grad = dense(d_hidden, time_feats)
        second_grad = dense(d_pre_signal, hidden.T)
        shift_grad = dense(d_shift_cols, signal.T)
        scale_grad = dense(d_scale_cols, signal.T)
        vector_sums = jnp.stack(
            [
                jnp.sum(values, axis=1)
                for values in (d_hidden, d_pre_signal, d_shift_cols, d_scale_cols)
            ],
            axis=1,
        )
    table_grad = jnp.concatenate(
        [
            class_grad,
            row_sums[:, 0:patch_in],
            time_grad,
            second_grad,
            shift_grad,
            scale_grad,
            row_sums[:, patch_in : 2 * patch_in + 1],
            vector_sums,
            row_sums[:, 2 * patch_in + 1 : final_at],
        ],
        axis=1,
    )
    input_grad = jnp.stack([jnp.concatenate(total[0:2], axis=1) for total in totals])
    input_grad = input_grad.reshape(layer_in.shape)
    output_grad = jnp.stack([total[2] for total in totals]).reshape(layer_out.shape)
    if not fused:
        local_squares = (
            jnp.sum(table_grad * table_grad)
            + jnp.sum(input_grad * input_grad)
            + jnp.sum(output_grad * output_grad)
            + jnp.sum(mod_grad * mod_grad)
        )
        scalar_send = jnp.where(
            lax.broadcasted_iota(jnp.int32, (8, 128), 1) == 0, loss_part, local_squares
        )
        scalar_sums = jnp.sum(exchange(scalar_send, "all", False, 12)[:, 0, 0:2], axis=0)
    loss_value = scalar_sums[0]
    square_total = scalar_sums[1]
    grad_norm = jnp.sqrt(square_total)
    factor = jnp.minimum(1.0, CLIP_NORM / grad_norm)
    first_fix = 1.0 - BETA_ONE ** step_count.astype(jnp.float32)
    second_fix = 1.0 - BETA_TWO ** step_count.astype(jnp.float32)
    embed_out = adam_update(
        embed_table.T, embed_first.T, embed_second.T, table_grad, factor, first_fix, second_fix
    )
    input_out = adam_update(
        layer_in, input_first, input_second, input_grad, factor, first_fix, second_fix
    )
    output_out = adam_update(
        layer_out, output_first, output_second, output_grad, factor, first_fix, second_fix
    )
    mod_out = adam_update(layer_ada, mod_first, mod_second, mod_grad, factor, first_fix, second_fix)
    return (
        (loss_value, grad_norm, embed_out[4].T, embed_out[1].T, embed_out[2].T)
        + input_out[0:4]
        + output_out[0:4]
        + mod_out[0:4]
    )


def solution(mesh):
    placed = (
        P("dp", "tensor"),
        P("dp", "tensor"),
        P("dp"),
        P("dp"),
        P(),
        P(None, ("dp", "tensor")),
        P(None, "dp", "tensor", None),
        P(None, "tensor", "dp", None),
        P(None, "dp", "tensor"),
        P(None, ("dp", "tensor")),
        P(None, ("dp", "tensor")),
        P(None, "dp", "tensor", None),
        P(None, "dp", "tensor", None),
        P(None, "tensor", "dp", None),
        P(None, "tensor", "dp", None),
        P(None, "dp", "tensor"),
        P(None, "dp", "tensor"),
    )
    return jax.shard_map(
        local,
        mesh=mesh,
        in_specs=placed,
        out_specs=(
            P(),
            P(),
            P(None, ("dp", "tensor")),
            P(None, ("dp", "tensor")),
            P(None, ("dp", "tensor")),
            P(None, "dp", "tensor", None),
            P(None, "dp", "tensor", None),
            P(None, "dp", "tensor", None),
            P(None, "dp", "tensor", None),
            P(None, "tensor", "dp", None),
            P(None, "tensor", "dp", None),
            P(None, "tensor", "dp", None),
            P(None, "tensor", "dp", None),
            P(None, "dp", "tensor"),
            P(None, "dp", "tensor"),
            P(None, "dp", "tensor"),
            P(None, "dp", "tensor"),
        ),
        check_vma=False,
    )
```

```python
import functools
import math

import jax
import jax.numpy as jnp
from jax import lax
from jax.experimental import pallas as pl
from jax.experimental.pallas import tpu as pltpu
from jax.sharding import PartitionSpec as P

D = 768
HEADS = 12
HEAD_DIM = 64
FF = 3072
CLASSES = 1001
FREQ = 256
CHANNELS = 4
PATCH = 2
SIDE = 32
LAYERS = 3


EPS_NORM = 1e-06
LEARN_RATE = 0.01
DECAY = 0.01
BETA_ONE = 0.5
BETA_TWO = 0.5
ADAM_EPS = 1e-08
CLIP_NORM = 0.25
PRECISE = lax.Precision.HIGHEST


def dense(left_op, right_op):
    return jnp.dot(left_op, right_op, precision=PRECISE, preferred_element_type=jnp.float32)


def layer_norm(values):
    center = values - jnp.mean(values, axis=-1, keepdims=True)
    return center * lax.rsqrt(jnp.mean(center * center, axis=-1, keepdims=True) + EPS_NORM)


def modulate(values, shift_vec, scale_vec):
    return layer_norm(values) * (1.0 + scale_vec[:, None, :]) + shift_vec[:, None, :]


def gelu_tanh(values):
    return jax.nn.gelu(values, approximate=True)


def silu_slope(values):
    sigmoid_val = jax.nn.sigmoid(values)
    return sigmoid_val * (1.0 + values * (1.0 - sigmoid_val))


def time_features(step_ints):
    half_width = FREQ // 2
    frequency = jnp.exp(-math.log(10000.0) * jnp.arange(half_width, dtype=jnp.float32) / half_width)
    angles = step_ints.astype(jnp.float32)[:, None] * frequency[None, :]
    return jnp.concatenate([jnp.cos(angles), jnp.sin(angles)], axis=1)


def noise_levels(step_ints):
    base_cos = math.cos(0.008 / 1.008 * math.pi / 2)
    angles = (step_ints.astype(jnp.float32) / 1000.0 + 0.008) / 1.008 * (math.pi / 2)
    signal_level = jnp.cos(angles) ** 2 / base_cos**2
    return (jnp.sqrt(signal_level), jnp.sqrt(1.0 - signal_level))


def position_table(first_row, row_count):
    grid_side = SIDE // PATCH
    quarter = D // 4
    omegas = jnp.exp(-math.log(10000.0) * jnp.arange(quarter, dtype=jnp.float32) / quarter)
    token_index = jnp.arange(row_count * grid_side, dtype=jnp.int32)
    row_angle = (first_row + token_index // grid_side).astype(jnp.float32)[:, None] * omegas[
        None, :
    ]
    col_angle = (token_index % grid_side).astype(jnp.float32)[:, None] * omegas[None, :]
    return jnp.concatenate(
        [jnp.sin(row_angle), jnp.cos(row_angle), jnp.sin(col_angle), jnp.cos(col_angle)], axis=1
    )


def patchify(flat_pixels, row_count):
    grid_side = SIDE // PATCH
    shaped = flat_pixels.reshape(flat_pixels.shape[0], row_count, PATCH, grid_side, PATCH, CHANNELS)
    return shaped.transpose(0, 1, 3, 2, 4, 5).reshape(
        flat_pixels.shape[0], row_count * grid_side, PATCH * PATCH * CHANNELS
    )


def table_starts():
    patch_in = PATCH * PATCH * CHANNELS
    patch_start = CLASSES
    time_start = patch_start + patch_in
    second_start = time_start + FREQ
    final_start = second_start + D
    head_start = final_start + 2 * D
    vector_start = head_start + patch_in
    layer_start = vector_start + 5
    return (
        patch_start,
        time_start,
        second_start,
        final_start,
        head_start,
        vector_start,
        layer_start,
    )


def group_place(group):
    if group == "all":
        width = lax.axis_size("tensor")
        place = lax.axis_index("dp") * width + lax.axis_index("tensor")
        size = lax.axis_size("dp") * width
        return place, size, lambda at: {"dp": at // width, "tensor": lax.rem(at, width)}
    return lax.axis_index(group), lax.axis_size(group), lambda at: {group: at}


def greet_group(group):
    place, size, coords = group_place(group)
    barrier = pltpu.get_barrier_semaphore()

    def greet_one(step, carry):
        peer = coords(lax.rem(place + step, size))
        pl.semaphore_signal(barrier, inc=1, device_id=peer, device_id_type=pl.DeviceIdType.MESH)
        return carry

    lax.fori_loop(1, size, greet_one, 0)
    pl.semaphore_wait(barrier, size - 1)


def greet_groups(*groups):
    barrier = pltpu.get_barrier_semaphore()
    count = 0
    for group in groups:
        place, size, coords = group_place(group)

        def greet_one(step, carry, place=place, size=size, coords=coords):
            peer = coords(lax.rem(place + step, size))
            pl.semaphore_signal(barrier, inc=1, device_id=peer, device_id_type=pl.DeviceIdType.MESH)
            return carry

        lax.fori_loop(1, size, greet_one, 0)
        count += size - 1
    pl.semaphore_wait(barrier, count)


class Crowd:
    def __init__(self, group, source_at, target, send_sems, recv_sems, local_sem):
        self.place, self.size, self.coords = group_place(group)
        self.source_at, self.target = source_at, target
        self.sends, self.recvs, self.local_sem = send_sems, recv_sems, local_sem

    def copy_to(self, step):
        there = lax.rem(self.place + step, self.size)
        return pltpu.make_async_remote_copy(
            src_ref=self.source_at(there),
            dst_ref=self.target.at[self.place],
            send_sem=self.sends.at[step],
            recv_sem=self.recvs.at[step],
            device_id=self.coords(there),
            device_id_type=pl.DeviceIdType.MESH,
        )

    def own_copy(self):
        return pltpu.make_async_copy(
            self.source_at(self.place), self.target.at[self.place], self.local_sem
        )

    def start(self):
        def begin(step, carry):
            self.copy_to(step).start()
            return carry

        lax.fori_loop(1, self.size, begin, 0)
        self.own_copy().start()

    def wait(self):
        def finish(step, carry):
            self.copy_to(step).wait()
            return carry

        self.own_copy().wait()
        lax.fori_loop(1, self.size, finish, 0)


class Relay:
    def __init__(self, source_at, middle, whole, sems_dp, sems_tensor):
        self.first = Crowd("dp", source_at, middle, *sems_dp)
        self.second = Crowd("tensor", lambda place: middle, whole, *sems_tensor)

    def start(self):
        self.first.start()

    def hand_on(self):
        self.first.wait()
        self.second.start()

    def wait(self):
        self.second.wait()


class Funnel:
    def __init__(self, source, across, middle, along, sems_tensor, sems_dp):
        self.across, self.middle, self.along = across, middle, along
        self.first = Crowd("tensor", lambda place: source.at[:, place], across, *sems_tensor)
        self.second = Crowd("dp", lambda place: middle.at[place], along, *sems_dp)

    def start(self):
        self.first.start()

    def hand_on(self):
        self.first.wait()
        self.middle[...] = jnp.sum(self.across[...], axis=0)
        self.second.start()

    def take(self):
        self.second.wait()
        return jnp.sum(self.along[...], axis=0)


def crowd_scratch(size):
    return [
        pltpu.SemaphoreType.DMA((size,)),
        pltpu.SemaphoreType.DMA((size,)),
        pltpu.SemaphoreType.DMA,
    ]


def exchange_kernel(group, spread, source, target, send_sems, recv_sems, local_sem):
    greet_group(group)
    crowd = Crowd(
        group,
        lambda place: source.at[place] if spread else source,
        target,
        send_sems,
        recv_sems,
        local_sem,
    )
    crowd.start()
    crowd.wait()


def exchange(values, group, spread, call_id):
    if group == "all":
        size = lax.axis_size("dp") * lax.axis_size("tensor")
    else:
        size = lax.axis_size(group)
    block = values.shape[1:] if spread else values.shape
    return pl.pallas_call(
        functools.partial(exchange_kernel, group, spread),
        out_shape=jax.ShapeDtypeStruct((size,) + block, values.dtype),
        in_specs=[pl.BlockSpec(memory_space=pltpu.VMEM)],
        out_specs=pl.BlockSpec(memory_space=pltpu.VMEM),
        scratch_shapes=crowd_scratch(size),
        compiler_params=pltpu.CompilerParams(
            collective_id=call_id, has_side_effects=True, vmem_limit_bytes=32 * 2**20
        ),
        name="exchange_" + group,
    )(values)


MESH = pl.DeviceIdType.MESH
ACT_VMEM = 60 * 2**20


def dot_nn(left_op, right_op):
    return jnp.dot(left_op, right_op, preferred_element_type=jnp.float32)


def dot_nt(left_op, right_op):
    return lax.dot_general(
        left_op, right_op, (((1,), (1,)), ((), ())), preferred_element_type=jnp.float32
    )


def dot_tn(left_op, right_op):
    return lax.dot_general(
        left_op, right_op, (((0,), (0,)), ((), ())), preferred_element_type=jnp.float32
    )


def square_sum(values):
    return jnp.sum(jnp.sum(values * values, axis=0, keepdims=True), axis=1, keepdims=True)


def norm_parts(values):
    center = values - jnp.mean(values, axis=-1, keepdims=True)
    rstd = lax.rsqrt(jnp.mean(center * center, axis=-1, keepdims=True) + EPS_NORM)
    return center * rstd, rstd


def greet(line):
    rank = lax.axis_index("tensor")
    half = lax.axis_size("tensor") // 2
    core_peer = {"tensor": rank + 1 - 2 * lax.rem(rank, 2)}
    chip_peer = {"tensor": lax.rem(rank + half, 2 * half)}
    barrier = pltpu.get_barrier_semaphore()
    for peer in (core_peer, chip_peer):
        pl.semaphore_signal(barrier, inc=1, device_id=peer, device_id_type=MESH)
    count = 2
    if line is not None:
        line.greet()
        count = count + line.answers()
    pl.semaphore_wait(barrier, count)


class Spread:
    def __init__(self, rows_ref, send_sems, recv_sems):
        self.rows, self.send, self.recv = rows_ref, send_sems, recv_sems
        self.rank = lax.axis_index("tensor")
        self.own_core = lax.rem(self.rank, 2)
        self.core_peer = self.rank + 1 - 2 * self.own_core
        self.chip_peer = lax.rem(self.rank + 2, 4)
        self.count = rows_ref.shape[1] // 4

    def block(self, image, owner):
        return self.rows.at[image, pl.ds(pl.multiple_of(owner * self.count, 16), self.count), :]

    def copy(self, image, owner, peer, which):
        return pltpu.make_async_remote_copy(
            src_ref=self.block(image, owner),
            dst_ref=self.block(image, owner),
            send_sem=self.send.at[image, which],
            recv_sem=self.recv.at[image, which],
            device_id={"tensor": peer},
            device_id_type=MESH,
        )

    def put(self, image, values):
        self.rows[image, pl.ds(pl.multiple_of(self.rank * self.count, 16), self.count), :] = values
        self.copy(image, self.rank, self.chip_peer, 0).start()
        self.copy(image, self.rank, self.core_peer, 1).start()

    def forward(self, image):
        self.copy(image, self.rank, self.chip_peer, 0).wait_recv()
        self.copy(image, self.chip_peer, self.core_peer, 2).start()

    def wait(self, image):
        self.copy(image, self.rank, self.core_peer, 1).wait_recv()
        self.copy(image, self.chip_peer, self.core_peer, 2).wait_recv()

    def close(self, image):
        self.copy(image, self.rank, self.chip_peer, 0).wait_send()
        self.copy(image, self.rank, self.core_peer, 1).wait_send()
        self.copy(image, self.chip_peer, self.core_peer, 2).wait_send()


class Collect:
    def __init__(self, part, near, far_out, far_in, send_sems, recv_sems):
        self.part, self.near, self.far_out, self.far_in = part, near, far_out, far_in
        self.send, self.recv = send_sems, recv_sems
        self.rank = lax.axis_index("tensor")
        self.own_core = lax.rem(self.rank, 2)
        self.own_chip = self.rank // 2
        self.core_peer = self.rank + 1 - 2 * self.own_core
        self.chip_peer = lax.rem(self.rank + 2, 4)
        self.count = part.shape[1] // 4

    def block(self, image, owner):
        return self.part.at[image, pl.ds(pl.multiple_of(owner * self.count, 16), self.count), :]

    def near_copy(self, image, far):
        chip = 1 - self.own_chip if far else self.own_chip
        return pltpu.make_async_remote_copy(
            src_ref=self.block(image, 2 * chip + 1 - self.own_core),
            dst_ref=self.near.at[image, far],
            send_sem=self.send.at[image, far],
            recv_sem=self.recv.at[image, far],
            device_id={"tensor": self.core_peer},
            device_id_type=MESH,
        )

    def far_copy(self, image):
        return pltpu.make_async_remote_copy(
            src_ref=self.far_out.at[image],
            dst_ref=self.far_in.at[image],
            send_sem=self.send.at[image, 2],
            recv_sem=self.recv.at[image, 2],
            device_id={"tensor": self.chip_peer},
            device_id_type=MESH,
        )

    def put(self, image, values):
        self.part[image] = values.astype(jnp.bfloat16)
        self.near_copy(image, 1).start()
        self.near_copy(image, 0).start()

    def load(self, image, owner):
        at = pl.ds(pl.multiple_of(owner * self.count, 16), self.count)
        return self.part[image, at, :].astype(jnp.float32)

    def forward(self, image):
        self.near_copy(image, 1).wait_recv()
        total = self.load(image, self.chip_peer) + self.near[image, 1].astype(jnp.float32)
        self.far_out[image] = total.astype(jnp.bfloat16)
        self.far_copy(image).start()

    def take(self, image):
        self.near_copy(image, 0).wait_recv()
        total = self.load(image, self.rank) + self.near[image, 0].astype(jnp.float32)
        self.far_copy(image).wait_recv()
        return total + self.far_in[image].astype(jnp.float32)

    def close(self, image):
        self.near_copy(image, 1).wait_send()
        self.near_copy(image, 0).wait_send()
        self.far_copy(image).wait_send()


def collect_scratch(images, tokens):
    count = tokens // 4
    return [
        pltpu.VMEM((images, tokens, D), jnp.bfloat16),
        pltpu.VMEM((images, 2, count, D), jnp.bfloat16),
        pltpu.VMEM((images, count, D), jnp.bfloat16),
        pltpu.VMEM((images, count, D), jnp.bfloat16),
    ]


def each(count, body):
    def step(index, carry):
        body(index)
        return carry

    lax.fori_loop(0, count, step, 0)


class Moves:
    def __init__(self, pairs, sems):
        self.copies = [
            pltpu.make_async_copy(source, target, sems.at[at])
            for at, (source, target) in enumerate(pairs)
        ]

    def start(self, *which):
        for at in which:
            self.copies[at].start()

    def wait(self, *which):
        for at in which:
            self.copies[at].wait()


class Line:
    def __init__(self):
        self.size = lax.axis_size("dp") // 2
        self.place = lax.axis_index("dp")
        self.at = self.place // 2
        self.side = lax.rem(self.place, 2)
        self.pair = self.place + 1 - 2 * self.side
        self.has_up = self.at + 1 < self.size
        self.has_down = self.at > 0

    def greet(self):
        barrier = pltpu.get_barrier_semaphore()
        pl.semaphore_signal(barrier, inc=1, device_id={"dp": self.pair}, device_id_type=MESH)

        @pl.when(self.has_up)
        def _():
            up = {"dp": self.place + 2}
            pl.semaphore_signal(barrier, inc=1, device_id=up, device_id_type=MESH)

        @pl.when(self.has_down)
        def _():
            down = {"dp": self.place - 2}
            pl.semaphore_signal(barrier, inc=1, device_id=down, device_id_type=MESH)

    def answers(self):
        return 1 + self.has_up.astype(jnp.int32) + self.has_down.astype(jnp.int32)


UP, DOWN, PAIR = 0, 1, 2


class Gather:
    def __init__(self, line, shards, wholes, sends, recvs, local_sems):
        self.line, self.shards, self.wholes = line, shards, wholes
        self.sends, self.recvs, self.local_sems = sends, recvs, local_sems

    def copy(self, part, way, step, owner, fresh=False):
        line = self.line
        there = {UP: line.place + 2, DOWN: line.place - 2, PAIR: line.pair}[way]
        return pltpu.make_async_remote_copy(
            src_ref=self.shards[part] if fresh else self.wholes[part].at[owner],
            dst_ref=self.wholes[part].at[owner],
            send_sem=self.sends.at[way, step, part],
            recv_sem=self.recvs.at[way, step, part],
            device_id={"dp": there},
            device_id_type=MESH,
        )

    def local_copy(self, part):
        return pltpu.make_async_copy(
            self.shards[part], self.wholes[part].at[self.line.place], self.local_sems.at[part]
        )

    def start(self):
        line = self.line
        parts = range(len(self.shards))

        @pl.when(line.has_up)
        def _():
            for part in parts:
                self.copy(part, UP, 0, line.place, True).start()

        @pl.when(line.has_down)
        def _():
            for part in parts:
                self.copy(part, DOWN, 0, line.place, True).start()

        for part in parts:
            self.copy(part, PAIR, line.at, line.place, True).start()
            self.local_copy(part).start()

    def came(self, way, step):
        there = -step if way == UP else step
        spot = self.line.at + there
        return self.line.place + 2 * there, spot, (spot >= 0) & (spot < self.line.size)

    def hand_on(self, step, way):
        line = self.line
        owner, _, real = self.came(way, step)
        can = line.has_up if way == UP else line.has_down

        @pl.when(real)
        def _():
            for part in range(len(self.shards)):
                self.copy(part, way, step - 1, owner).wait_recv()

            @pl.when(can)
            def _():
                for part in range(len(self.shards)):
                    self.copy(part, way, step, owner).start()

    def hand_over(self, step, way, when=True):
        owner, spot, real = self.came(way, step)

        @pl.when(real & when)
        def _():
            for part in range(len(self.shards)):
                self.copy(part, PAIR, spot, owner).start()

    def tick(self, step):
        for way in (UP, DOWN):
            self.hand_on(step, way)
            self.hand_over(step, way)

    def finish(self):
        line = self.line
        parts = range(len(self.shards))
        for part in parts:
            self.local_copy(part).wait()

        def side(spot):
            for part in parts:
                self.copy(part, PAIR, spot, 2 * spot + line.side).wait()

        each(line.size, side)

        def along(step):
            for way, there, can in ((UP, -step, line.has_up), (DOWN, step, line.has_down)):
                spot = line.at + there

                @pl.when((spot >= 0) & (spot < line.size) & can)
                def _(way=way, there=there):
                    for part in parts:
                        self.copy(part, way, step, line.place + 2 * there).wait_send()

        each(line.size, along)


class Reduce:
    def __init__(self, line, terms, totals, own, pair_in, way_in, way_out, sends, recvs, own_sems):
        self.line, self.terms, self.totals, self.own = line, terms, totals, own
        self.own_sems = own_sems
        self.pair_in, self.way_in, self.way_out = pair_in, way_in, way_out
        self.sends, self.recvs = sends, recvs

    def pair_copy(self, part, spot):
        return pltpu.make_async_remote_copy(
            src_ref=self.terms[part].at[2 * spot + 1 - self.line.side],
            dst_ref=self.pair_in[part].at[spot],
            send_sem=self.sends.at[PAIR, spot, part],
            recv_sem=self.recvs.at[PAIR, spot, part],
            device_id={"dp": self.line.pair},
            device_id_type=MESH,
        )

    def way_copy(self, part, way, spot):
        there = self.line.place + 2 if way == UP else self.line.place - 2
        return pltpu.make_async_remote_copy(
            src_ref=self.way_out[part].at[way, spot],
            dst_ref=self.way_in[part].at[way, spot],
            send_sem=self.sends.at[way, spot, part],
            recv_sem=self.recvs.at[way, spot, part],
            device_id={"dp": there},
            device_id_type=MESH,
        )

    def start(self):
        self.load_own()
        each(self.line.size, self.send_pair)

    def own_copy(self, part, spot):
        return pltpu.make_async_copy(
            self.terms[part].at[2 * spot + self.line.side],
            self.own[part].at[spot],
            self.own_sems.at[part, spot],
        )

    def load_own(self):
        def load(spot):
            for part in range(len(self.terms)):
                self.own_copy(part, spot).start()

        each(self.line.size, load)

    def wait_own(self):
        def wait(spot):
            for part in range(len(self.terms)):
                self.own_copy(part, spot).wait()

        each(self.line.size, wait)

    def send_pair(self, step):
        line = self.line
        far = line.size - 1 - step

        @pl.when(line.at + far < line.size)
        def _():
            for part in range(len(self.terms)):
                self.pair_copy(part, line.at + far).start()

        @pl.when((line.at - far >= 0) & (far > 0))
        def _():
            for part in range(len(self.terms)):
                self.pair_copy(part, line.at - far).start()

    def pair_sum(self, part, spot):
        own = self.own[part][spot].astype(jnp.float32)
        return own + self.pair_in[part][spot].astype(jnp.float32)

    def pass_on(self, way, spot, more):
        for part in range(len(self.terms)):
            self.pair_copy(part, spot).wait_recv()
            self.way_out[part][way, spot] = self.pair_sum(part, spot).astype(jnp.bfloat16)

            @pl.when(more)
            def _(part=part):
                self.way_copy(part, way, spot).wait_recv()
                self.way_out[part][way, spot] = (
                    self.pair_sum(part, spot) + self.way_in[part][way, spot].astype(jnp.float32)
                ).astype(jnp.bfloat16)

            self.way_copy(part, way, spot).start()

    def tick(self, step):
        line = self.line
        far = line.size - 1 - step

        @pl.when(line.at + far < line.size)
        def _():
            self.pass_on(UP, line.at + far, line.has_down)

        @pl.when(line.at - far >= 0)
        def _():
            self.pass_on(DOWN, line.at - far, line.has_up)

    def finish(self):
        line = self.line
        spot = line.at
        for part in range(len(self.terms)):
            self.pair_copy(part, spot).wait_recv()
            self.totals[part][...] = self.pair_sum(part, spot)
        for way, can in ((UP, line.has_down), (DOWN, line.has_up)):

            @pl.when(can)
            def _(way=way):
                for part in range(len(self.terms)):
                    self.way_copy(part, way, spot).wait_recv()
                    self.totals[part][...] += self.way_in[part][way, spot].astype(jnp.float32)

        def close(spot):
            for part in range(len(self.terms)):
                self.pair_copy(part, spot).wait_send()
            for way, passed in ((UP, spot > line.at), (DOWN, spot < line.at)):

                @pl.when(passed)
                def _(way=way):
                    for part in range(len(self.terms)):
                        self.way_copy(part, way, spot).wait_send()

        each(line.size, close)


def run_ticks(task, first, last):
    if task is not None:
        for step in range(first, last):
            task.tick(step)


def head_slice(matrix, head):
    return matrix[:, head * HEAD_DIM : (head + 1) * HEAD_DIM]


def soft_rows(queries, keys_in):
    scores = dot_nt(queries, keys_in) * (HEAD_DIM ** (-0.5))
    exponent = jnp.exp(scores - jnp.max(scores, axis=-1, keepdims=True))
    return exponent / jnp.sum(exponent, axis=-1, keepdims=True)


def forward_kernel(
    layer_idx,
    res_ref,
    mod_ref,
    vec_ref,
    qkv_bias_ref,
    up_bias_ref,
    w_qkv_far,
    w_up_far,
    w_out_far,
    *rest,
):
    with_gather = len(rest) > 31
    shards, rest = (rest[:3], rest[3:]) if with_gather else ((), rest)
    res_out, kept = rest[0], rest[1:9]
    wholes, rest = (rest[9:12], rest[12:]) if with_gather else ((), rest[9:])
    rows_a, qkv_out, mixed_out, branch_out, mid_out, rows_m, upper_out, down_out = rest[:8]
    w_qkv_ref, w_up_ref, w_out_ref = rest[8:11]
    (
        part_a,
        near_a,
        far_out_a,
        far_in_a,
        part_m,
        near_m,
        far_out_m,
        far_in_m,
        sends,
        recvs,
        move_sems,
    ) = rest[11:22]
    group_width = w_qkv_ref.shape[1] // 3
    w_attn_ref, w_down_ref = w_out_ref.at[0:group_width, :], w_out_ref.at[group_width:, :]
    far = (w_qkv_far, w_out_far, w_up_far)
    pairs = list(zip(far, (w_qkv_ref, w_out_ref, w_up_ref))) + list(zip(rest[:8], kept))
    moves = Moves(pairs, move_sems)
    moves.start(0, 1, 2)
    images = res_ref.shape[0]
    gather, last_step = None, 0
    if with_gather:
        line = Line()
        greet(line)
        own = [shard.at[layer_idx + 1] for shard in shards]
        gather = Gather(line, own, wholes, *rest[22:])
        last_step = line.size
    else:
        greet(None)
    spread_a = Spread(rows_a, sends.at[0], recvs.at[0])
    spread_m = Spread(rows_m, sends.at[1], recvs.at[1])
    collect_a = Collect(part_a, near_a, far_out_a, far_in_a, sends.at[2], recvs.at[2])
    collect_m = Collect(part_m, near_m, far_out_m, far_in_m, sends.at[3], recvs.at[3])

    def mod_row(image, piece):
        return mod_ref[image, pl.ds(piece, 1), :]

    def start_norm(image):
        normed, _ = norm_parts(res_ref[image])
        normed = normed * (1.0 + mod_row(image, 1)) + mod_row(image, 0)
        spread_a.put(image, normed.astype(jnp.bfloat16))

    def attend(image):
        spread_a.wait(image)
        rows = rows_a[image]
        projected = dot_nn(rows, w_qkv_ref[...]) + qkv_bias_ref[...]
        qkv = projected.astype(jnp.bfloat16)
        qkv_out[image] = qkv
        heads = []
        for head in range(group_width // HEAD_DIM):
            probs = soft_rows(
                head_slice(qkv[:, :group_width], head),
                head_slice(qkv[:, group_width : 2 * group_width], head),
            )
            heads.append(
                dot_nn(probs.astype(jnp.bfloat16), head_slice(qkv[:, 2 * group_width :], head))
            )
        mixed = jnp.concatenate(heads, axis=1).astype(jnp.bfloat16)
        mixed_out[image] = mixed
        collect_a.put(image, dot_nn(mixed, w_attn_ref[...]))

    def middle(image):
        branch = collect_a.take(image) + vec_ref[0:1, :]
        branch_out[image] = branch
        mid = res_ref[image] + mod_row(image, 2) * branch
        mid_out[image] = mid
        normed, _ = norm_parts(mid)
        normed = normed * (1.0 + mod_row(image, 4)) + mod_row(image, 3)
        spread_m.put(image, normed.astype(jnp.bfloat16))

    def feed(image):
        spread_m.wait(image)
        upper = dot_nn(rows_m[image], w_up_ref[...]) + up_bias_ref[...]
        upper_out[image] = upper
        collect_m.put(image, dot_nn(gelu_tanh(upper).astype(jnp.bfloat16), w_down_ref[...]))

    def finish(image):
        down = collect_m.take(image) + vec_ref[1:2, :]
        down_out[image] = down
        res_out[image] = mid_out[image] + mod_row(image, 5) * down

    def close(image):
        spread_a.close(image)
        spread_m.close(image)
        collect_a.close(image)
        collect_m.close(image)

    if with_gather:
        gather.start()
    each(images, start_norm)
    each(images, spread_a.forward)
    moves.wait(0, 1)
    each(images, attend)
    moves.start(3, 4, 5)
    run_ticks(gather, 1, min(2, last_step))
    each(images, collect_a.forward)
    each(images, middle)
    moves.start(6, 7)
    each(images, spread_m.forward)
    run_ticks(gather, 2, min(3, last_step))
    moves.wait(2)
    each(images, feed)
    moves.start(8, 9)
    run_ticks(gather, 3, min(4, last_step))
    each(images, collect_m.forward)
    each(images, finish)
    moves.start(10)
    each(images, close)
    moves.wait(*range(3, 11))
    if with_gather:
        each(max(last_step - 4, 0), lambda step: gather.tick(step + 4))
        gather.finish()


def forward_layer(
    residual, mod_vec, vec_bias, qkv_bias, up_bias, w_qkv, w_up, w_out, shards, layer_idx
):
    images, count, _ = residual.shape
    tokens = 4 * count
    low, full = jnp.bfloat16, jnp.float32
    shapes = [
        ((images, count, D), full),
        ((images, tokens, D), low),
        ((images, tokens, w_qkv.shape[1]), low),
        ((images, tokens, w_qkv.shape[1] // 3), low),
        ((images, count, D), full),
        ((images, count, D), full),
        ((images, tokens, D), low),
        ((images, tokens, w_up.shape[1]), full),
        ((images, count, D), full),
    ]
    scratch = [
        pltpu.SemaphoreType.DMA((4, images, 3)),
        pltpu.SemaphoreType.DMA((4, images, 3)),
        pltpu.SemaphoreType.DMA((11,)),
    ]
    near = [pltpu.VMEM(*shape) for shape in shapes[1:]]
    near += [pltpu.VMEM(weight.shape, low) for weight in (w_qkv, w_up, w_out)]
    if shards:
        dp_size = lax.axis_size("dp")
        shapes += [((dp_size,) + shard.shape[1:], low) for shard in shards]
        scratch += [
            pltpu.SemaphoreType.DMA((3, dp_size // 2, 3)),
            pltpu.SemaphoreType.DMA((3, dp_size // 2, 3)),
            pltpu.SemaphoreType.DMA((3,)),
        ]
    return pl.pallas_call(
        functools.partial(forward_kernel, layer_idx),
        out_shape=[jax.ShapeDtypeStruct(*shape) for shape in shapes],
        in_specs=[pl.BlockSpec(memory_space=pltpu.VMEM)] * 5
        + [pl.BlockSpec(memory_space=pl.ANY)] * (3 + len(shards)),
        out_specs=[pl.BlockSpec(memory_space=pltpu.VMEM)]
        + [pl.BlockSpec(memory_space=pl.ANY)] * (len(shapes) - 1),
        scratch_shapes=near
        + collect_scratch(images, tokens)
        + collect_scratch(images, tokens)
        + scratch,
        compiler_params=pltpu.CompilerParams(
            collective_id=16 + layer_idx, has_side_effects=True, vmem_limit_bytes=ACT_VMEM
        ),
        cost_estimate=pl.CostEstimate(
            flops=30 * 10**9, bytes_accessed=15 * 2**20, transcendentals=0
        ),
        name="block_forward",
    )(residual, mod_vec, vec_bias, qkv_bias, up_bias, w_qkv, w_up, w_out, *shards)


def gelu_slope(values):
    root = math.sqrt(2.0 / math.pi)
    square = values * values
    tanh = jnp.tanh(root * (values + 0.044715 * values * square))
    half = 0.5 * (1.0 + tanh)
    slope = half + 0.5 * values * (1.0 - tanh * tanh) * root * (1.0 + 3.0 * 0.044715 * square)
    return values * half, slope


def norm_pull(values, scale_row, d_normed):
    normed, rstd = norm_parts(values)
    d_shift = jnp.sum(d_normed, axis=0, keepdims=True)
    d_scale = jnp.sum(d_normed * normed, axis=0, keepdims=True)
    inner = d_normed * (1.0 + scale_row)
    mean_one = jnp.mean(inner, axis=-1, keepdims=True)
    mean_two = jnp.mean(inner * normed, axis=-1, keepdims=True)
    return (inner - mean_one - normed * mean_two) * rstd, d_shift, d_scale


def backward_kernel(d_res_ref, mod_ref, *rest):
    kept, rest = rest[:12], rest[12:]
    with_reduce = len(rest) > 40
    terms, rest = (rest[:3], rest[3:]) if with_reduce else ((), rest)
    d_res_out, d_far, (d_mod, d_vec, d_qkv_bias, d_up_bias) = rest[0], rest[1:4], rest[4:8]
    totals, square_out = (rest[8:11], rest[11]) if with_reduce else ((), None)
    rest = rest[12:] if with_reduce else rest[8:]
    (
        res_ref,
        rows_a,
        qkv_ref,
        mixed_ref,
        branch_ref,
        mid_ref,
        rows_m,
        upper_ref,
        down_ref,
        w_qkv_ref,
        w_up_ref,
        w_out_ref,
        d_w_qkv,
        d_w_up,
        d_out,
    ) = rest[:15]
    (
        d_mid,
        d_rows_m,
        d_rows_a,
        act_low,
        d_upper,
        d_qkv,
        part_a,
        near_a,
        far_out_a,
        far_in_a,
        part_m,
        near_m,
        far_out_m,
        far_in_m,
        sends,
        recvs,
        move_sems,
    ) = rest[15:32]
    group_width = w_qkv_ref.shape[1] // 3
    w_attn_ref, w_down_ref = w_out_ref.at[0:group_width, :], w_out_ref.at[group_width:, :]
    pairs = list(zip(kept, rest[:12])) + list(zip(rest[12:15], d_far))
    moves = Moves(pairs, move_sems)
    moves.start(8, 11, 7, 10, 6, 5, 4, 2, 9, 3, 1, 0)
    images = res_ref.shape[0]
    tokens = rows_a.shape[1]
    qkv_width = 3 * group_width
    units = w_up_ref.shape[1]
    reduce, last_step = None, 0
    if with_reduce:
        line = Line()
        greet(line)
        own, pair_in, way_in, way_out = rest[32:35], rest[35:38], rest[38:41], rest[41:44]
        reduce = Reduce(line, terms, totals, own, pair_in, way_in, way_out, *rest[44:])
        last_step = line.size
    else:
        greet(None)
    spread_m = Spread(d_rows_m, sends.at[0], recvs.at[0])
    spread_a = Spread(d_rows_a, sends.at[1], recvs.at[1])
    collect_m = Collect(part_m, near_m, far_out_m, far_in_m, sends.at[2], recvs.at[2])
    collect_a = Collect(part_a, near_a, far_out_a, far_in_a, sends.at[3], recvs.at[3])
    d_vec[...] = jnp.zeros_like(d_vec)
    d_qkv_bias[...] = jnp.zeros_like(d_qkv_bias)
    d_up_bias[...] = jnp.zeros_like(d_up_bias)

    def mod_row(image, piece):
        return mod_ref[image, pl.ds(piece, 1), :]

    def start_down(image):
        d_res = d_res_ref[image]
        d_mod[image, pl.ds(5, 1), :] = jnp.sum(d_res * down_ref[image], axis=0, keepdims=True)
        d_down = d_res * mod_row(image, 5)
        d_vec[1:2, :] += jnp.sum(d_down, axis=0, keepdims=True)
        spread_m.put(image, d_down.astype(jnp.bfloat16))

    def feed(image):
        spread_m.wait(image)
        d_act = dot_nt(d_rows_m[image], w_down_ref[...])
        act, slope = gelu_slope(upper_ref[image])
        act_low[image] = act.astype(jnp.bfloat16)
        d_up = d_act * slope
        d_up_bias[...] += jnp.sum(d_up, axis=0, keepdims=True)
        d_up_low = d_up.astype(jnp.bfloat16)
        d_upper[image] = d_up_low
        collect_m.put(image, dot_nt(d_up_low, w_up_ref[...]))

    def rows_of(ref, width):
        return ref[...].reshape(images * tokens, width)

    def feed_weights():
        tile = 256

        def step(index, carry):
            at = pl.ds(pl.multiple_of(index * tile, tile), tile)
            grad = dot_tn(
                act_low[:, :, at].reshape(images * tokens, tile), rows_of(d_rows_m, D)
            )
            d_out[pl.ds(pl.multiple_of(group_width + index * tile, 64), tile), :] = grad.astype(
                jnp.bfloat16
            )
            grad = dot_tn(
                rows_m[:, :, at].reshape(images * tokens, tile), rows_of(d_upper, units)
            )
            d_w_up[pl.ds(pl.multiple_of(index * tile, tile), tile), :] = grad.astype(jnp.bfloat16)
            return carry

        lax.fori_loop(0, units // tile, step, 0)

    def middle(image):
        d_value, d_shift, d_scale = norm_pull(
            mid_ref[image], mod_row(image, 4), collect_m.take(image)
        )
        d_mod[image, pl.ds(3, 1), :] = d_shift
        d_mod[image, pl.ds(4, 1), :] = d_scale
        d_value = d_res_ref[image] + d_value
        d_mid[image] = d_value
        d_mod[image, pl.ds(2, 1), :] = jnp.sum(d_value * branch_ref[image], axis=0, keepdims=True)
        d_branch = d_value * mod_row(image, 2)
        d_vec[0:1, :] += jnp.sum(d_branch, axis=0, keepdims=True)
        spread_a.put(image, d_branch.astype(jnp.bfloat16))

    def attend(image):
        spread_a.wait(image)
        d_mixed = dot_nt(d_rows_a[image], w_attn_ref[...]).astype(jnp.bfloat16)
        qkv = qkv_ref[image]
        d_queries, d_keys, d_values = [], [], []
        scale_dot = HEAD_DIM ** (-0.5)
        for head in range(group_width // HEAD_DIM):
            queries = head_slice(qkv[:, :group_width], head)
            keys_in = head_slice(qkv[:, group_width : 2 * group_width], head)
            values_in = head_slice(qkv[:, 2 * group_width :], head)
            d_head = head_slice(d_mixed, head)
            probs = soft_rows(queries, keys_in)
            d_probs = dot_nt(d_head, values_in)
            d_values.append(dot_tn(probs.astype(jnp.bfloat16), d_head))
            inner = jnp.sum(probs * d_probs, axis=-1, keepdims=True)
            d_scores = (probs * (d_probs - inner)).astype(jnp.bfloat16)
            d_queries.append(dot_nn(d_scores, keys_in) * scale_dot)
            d_keys.append(dot_tn(d_scores, queries) * scale_dot)
        joined = jnp.concatenate(d_queries + d_keys + d_values, axis=1)
        d_qkv_bias[...] += jnp.sum(joined, axis=0, keepdims=True)
        joined = joined.astype(jnp.bfloat16)
        d_qkv[image] = joined
        collect_a.put(image, dot_nt(joined, w_qkv_ref[...]))

    def attend_weights():
        d_out[0:group_width, :] = dot_tn(
            rows_of(mixed_ref, group_width), rows_of(d_rows_a, D)
        ).astype(jnp.bfloat16)
        tile = 256

        def step(index, carry):
            at = pl.ds(pl.multiple_of(index * tile, tile), tile)
            grad = dot_tn(
                rows_a[:, :, at].reshape(images * tokens, tile), rows_of(d_qkv, qkv_width)
            )
            d_w_qkv[at, :] = grad.astype(jnp.bfloat16)
            return carry

        lax.fori_loop(0, D // tile, step, 0)

    def finish(image):
        d_value, d_shift, d_scale = norm_pull(
            res_ref[image], mod_row(image, 1), collect_a.take(image)
        )
        d_mod[image, pl.ds(0, 1), :] = d_shift
        d_mod[image, pl.ds(1, 1), :] = d_scale
        d_res_out[image] = d_mid[image] + d_value

    def close(image):
        spread_a.close(image)
        spread_m.close(image)
        collect_a.close(image)
        collect_m.close(image)

    if with_reduce:
        reduce.start()
    moves.wait(8)
    each(images, start_down)
    each(images, spread_m.forward)
    moves.wait(11, 7, 10)
    each(images, feed)
    if with_reduce:
        reduce.wait_own()
    run_ticks(reduce, 0, min(1, last_step - 1))
    each(images, collect_m.forward)
    moves.wait(6)
    feed_weights()
    moves.start(13)
    run_ticks(reduce, 1, min(2, last_step - 1))
    moves.wait(5, 4)
    each(images, middle)
    each(images, spread_a.forward)
    moves.wait(2, 9)
    each(images, attend)
    each(images, collect_a.forward)
    run_ticks(reduce, 2, min(3, last_step - 1))
    moves.wait(3, 1)
    attend_weights()
    moves.start(12, 14)
    moves.wait(0)
    each(images, finish)
    each(images, close)
    if with_reduce:
        each(max(last_step - 4, 0), lambda step: reduce.tick(step + 3))
        reduce.finish()
        square_out[...] = jnp.broadcast_to(
            sum(square_sum(total[...]) for total in totals), square_out.shape
        )
    moves.wait(12, 13, 14)


def backward_layer(d_residual, mod_vec, saved, weights, terms):
    images, count, _ = d_residual.shape
    tokens = 4 * count
    low, full = jnp.bfloat16, jnp.float32
    w_qkv, w_up, w_out = weights
    group_width, units = w_qkv.shape[1] // 3, w_up.shape[1]
    shapes = [
        ((images, count, D), full),
        ((D, 3 * group_width), low),
        ((D, units), low),
        ((group_width + units, D), low),
        ((images, 6, D), full),
        ((2, D), full),
        ((1, 3 * group_width), full),
        ((1, units), full),
    ]
    scratch = [
        pltpu.SemaphoreType.DMA((4, images, 3)),
        pltpu.SemaphoreType.DMA((4, images, 3)),
        pltpu.SemaphoreType.DMA((15,)),
    ]
    near = [pltpu.VMEM(kept.shape, kept.dtype) for kept in tuple(saved) + tuple(weights)]
    near += [pltpu.VMEM(*shape) for shape in shapes[1:4]]
    if terms:
        spots = lax.axis_size("dp") // 2
        blocks = [term.shape[1:] for term in terms]
        shapes += [(block, full) for block in blocks] + [((8, 128), full)]
        scratch += [pltpu.VMEM((spots,) + block, low) for block in blocks]
        scratch += [pltpu.VMEM((spots,) + block, low) for block in blocks]
        scratch += [pltpu.VMEM((2, spots) + block, low) for block in blocks]
        scratch += [pltpu.VMEM((2, spots) + block, low) for block in blocks]
        scratch += [
            pltpu.SemaphoreType.DMA((3, spots, 3)),
            pltpu.SemaphoreType.DMA((3, spots, 3)),
            pltpu.SemaphoreType.DMA((3, spots)),
        ]
    return pl.pallas_call(
        backward_kernel,
        out_shape=[jax.ShapeDtypeStruct(*shape) for shape in shapes],
        in_specs=[pl.BlockSpec(memory_space=pltpu.VMEM)] * 2
        + [pl.BlockSpec(memory_space=pl.ANY)] * (12 + len(terms)),
        out_specs=[pl.BlockSpec(memory_space=pltpu.VMEM)]
        + [pl.BlockSpec(memory_space=pl.ANY)] * 3
        + [pl.BlockSpec(memory_space=pltpu.VMEM)] * (len(shapes) - 4),
        scratch_shapes=near
        + [
            pltpu.VMEM((images, count, D), full),
            pltpu.VMEM((images, tokens, D), low),
            pltpu.VMEM((images, tokens, D), low),
            pltpu.VMEM((images, tokens, units), low),
            pltpu.VMEM((images, tokens, units), low),
            pltpu.VMEM((images, tokens, 3 * group_width), low),
        ]
        + collect_scratch(images, tokens)
        + collect_scratch(images, tokens)
        + scratch,
        compiler_params=pltpu.CompilerParams(
            collective_id=21 if terms else 23, has_side_effects=True, vmem_limit_bytes=ACT_VMEM
        ),
        cost_estimate=pl.CostEstimate(
            flops=60 * 10**9, bytes_accessed=25 * 2**20, transcendentals=0
        ),
        name="block_backward",
    )(d_residual, mod_vec, *saved, *weights, *terms)


def dense_nt(left_op, right_op):
    return lax.dot_general(
        left_op,
        right_op,
        (((1,), (1,)), ((), ())),
        precision=PRECISE,
        preferred_element_type=jnp.float32,
    )


def dense_tn(left_op, right_op):
    return lax.dot_general(
        left_op,
        right_op,
        (((0,), (0,)), ((), ())),
        precision=PRECISE,
        preferred_element_type=jnp.float32,
    )


def chosen(shape, rule, kind):
    row = lax.broadcasted_iota(jnp.int32, shape, 0)
    col = lax.broadcasted_iota(jnp.int32, shape, 1)
    return jnp.where(rule(row, col), 1.0, 0.0).astype(kind)


def fold(values):
    groups = values.shape[-2] // 8
    pieces = [values[..., 8 * at : 8 * at + 8, :] for at in range(groups)]
    used = groups * values.shape[-1]
    if used % 128:
        pieces.append(jnp.zeros(values.shape[:-2] + (8, 128 - used % 128), values.dtype))
    return jnp.concatenate(pieces, axis=-1)


def folded_lanes(cols, count):
    return -(-(cols // 8 * count) // 128) * 128


def unfold_all(values, cols, count):
    ordered = [
        values[tensor_at, dp_at]
        for dp_at in range(values.shape[1])
        for tensor_at in range(values.shape[0])
    ]
    return jnp.concatenate([unfold(value, cols, count) for value in ordered], axis=0)


def unfold(values, cols, count):
    pieces = [values[..., at * count : (at + 1) * count] for at in range(cols // 8)]
    return jnp.concatenate(pieces, axis=-2)


def slots_of(images):
    return -(-LAYERS * images // 16) * 16


def head_kernel(
    images,
    small_ref,
    feats_ref,
    table_ref,
    time_ref,
    second_ref,
    shift_ref,
    scale_ref,
    bias_ref,
    mod_ref,
    *rest,
):
    shards = rest[0:3]
    (
        small_all,
        feats_out,
        pre_time_out,
        hidden_out,
        pre_signal_out,
        signal_out,
        final_all,
        mod_all,
    ) = rest[3:11]
    wholes = rest[11:14]
    (
        feats_all,
        hidden_own,
        hidden_dp,
        hidden_all,
        signal_own,
        signal_dp,
        signal_all,
        final_own,
        final_dp,
        mod_part,
        mod_in,
        mod_own,
        small_dp,
    ) = rest[14:27]
    crowds = [rest[27 + 3 * index : 30 + 3 * index] for index in range(11)]
    gather_sems = rest[60:]
    dp_size = lax.axis_size("dp")
    tensor_size = lax.axis_size("tensor")
    dp_rank = lax.axis_index("dp")
    images_all = images * dp_size
    slots = mod_own.shape[0]
    greet_groups("dp", "tensor")
    gather = Gather(Line(), [shard.at[0] for shard in shards], wholes, *gather_sems)
    feats = Crowd("dp", lambda place: feats_ref, feats_all, *crowds[0])
    mod_sum = Crowd("dp", lambda place: mod_part.at[place], mod_in, *crowds[1])
    mod_spread = Crowd("tensor", lambda place: mod_own, mod_all, *crowds[2])
    small = Relay(lambda place: small_ref, small_dp, small_all, *crowds[3:5])
    hidden = Relay(lambda place: hidden_own, hidden_dp, hidden_all, *crowds[5:7])
    signal = Relay(lambda place: signal_own, signal_dp, signal_all, *crowds[7:9])
    final = Relay(lambda place: final_own.at[place], final_dp, final_all, *crowds[9:11])
    line = gather.line
    first, last = line.at == 0, line.at == line.size - 1
    feats.start()
    gather.start()
    feats.wait()
    pick = chosen(
        (images_all, 8 * dp_size),
        lambda row, col: (row // images == col // 8) & (lax.rem(row, images) == lax.rem(col, 8)),
        jnp.float32,
    )
    feats_sum = dense(pick, feats_all[...].reshape(8 * dp_size, feats_all.shape[2]))
    feats_out[...] = feats_sum
    pre_time = dense_nt(time_ref[...], feats_sum[:, 0:FREQ]) + bias_ref[:, 1:2]
    pre_time_out[...] = pre_time
    hidden_own[...] = fold(jax.nn.silu(pre_time))
    hidden.start()
    class_lanes = -(-CLASSES // 128) * 128
    labels = jnp.round(feats_sum[:, FREQ : FREQ + 1]).astype(jnp.int32)
    lane = lax.broadcasted_iota(jnp.int32, (images_all, class_lanes), 1)
    onehot = jnp.where(lane == labels, 1.0, 0.0)
    class_part = dense_nt(table_ref[:, 0:class_lanes], onehot) + bias_ref[:, 2:3]
    small.start()
    hidden.hand_on()
    for way in (UP, DOWN):
        gather.hand_on(1, way)
    gather.hand_over(1, UP)
    gather.hand_over(1, DOWN, first)
    hidden.wait()
    cols = second_ref.shape[0]
    hidden_full = unfold_all(hidden_all[...], cols, images_all)
    hidden_out[...] = hidden_full
    pre_signal = dense(second_ref[...], hidden_full) + class_part
    pre_signal_out[...] = pre_signal
    signal_own[...] = fold(jax.nn.silu(pre_signal))
    signal.start()
    small.hand_on()
    signal.hand_on()
    for way in (UP, DOWN):
        gather.hand_on(2, way)
    gather.hand_over(1, DOWN, jnp.logical_not(first))
    gather.hand_over(2, UP, last)
    gather.hand_over(2, DOWN, first)
    signal.wait()
    signal_full = unfold_all(signal_all[...], cols, images_all)
    signal_out[...] = signal_full
    mod_rows = mod_ref.shape[1]
    own_rows = pl.ds(pl.multiple_of(dp_rank * mod_rows, 8), mod_rows)
    signal_low = signal_out[own_rows, :].astype(jnp.bfloat16)
    total = None
    for layer_idx in range(LAYERS):
        pick = chosen(
            (images_all, dp_size * slots),
            lambda row, col: (
                (row // images == col // slots)
                & (lax.rem(row, images) + layer_idx * images == lax.rem(col, slots))
            ),
            jnp.bfloat16,
        )
        placed = dot_nn(signal_low, pick).astype(jnp.bfloat16)
        term = dot_tn(placed, mod_ref[layer_idx])
        total = term if total is None else total + term
    mod_part[...] = total.reshape(mod_part.shape).astype(mod_part.dtype)
    mod_sum.start()
    gather.hand_over(2, UP, jnp.logical_not(last))
    gather.hand_over(2, DOWN, jnp.logical_not(first))
    finals = jnp.concatenate(
        [
            dense(shift_ref[...], signal_full) + bias_ref[:, 3:4],
            dense(scale_ref[...], signal_full) + bias_ref[:, 4:5],
            jnp.zeros((128 - 2 * shift_ref.shape[0], images_all), jnp.float32),
        ],
        axis=0,
    )
    pick = chosen(
        (8 * dp_size, images_all),
        lambda row, col: (row // 8 == col // images) & (lax.rem(row, 8) == lax.rem(col, images)),
        jnp.float32,
    )
    final_own[...] = dense_nt(pick, finals).reshape(final_own.shape)
    final.start()
    run_ticks(gather, 3, min(4, dp_size // 2))
    mod_sum.wait()
    mod_own[...] = jnp.sum(mod_in[...].astype(jnp.float32), axis=0)
    mod_spread.start()
    final.hand_on()
    each(max(dp_size // 2 - 4, 0), lambda step: gather.tick(step + 4))
    small.wait()
    final.wait()
    mod_spread.wait()
    gather.finish()


def head_call(small, feats, table, times, second, shift, scale, bias, mod_low, shards, images):
    dp_size, tensor_size = lax.axis_size("dp"), lax.axis_size("tensor")
    images_all = images * dp_size
    cols = table.shape[0]
    slots = slots_of(images)
    folded = folded_lanes(cols, images_all)
    full, low = jnp.float32, jnp.bfloat16
    shapes = [
        ((tensor_size, dp_size) + small.shape, full),
        ((images_all, feats.shape[1]), full),
        ((cols, images_all), full),
        ((D, images_all), full),
        ((cols, images_all), full),
        ((D, images_all), full),
        ((tensor_size, dp_size, 8, 128), full),
        ((tensor_size, slots, mod_low.shape[2]), full),
    ] + [((dp_size,) + shard.shape[1:], low) for shard in shards]
    scratch = [
        pltpu.VMEM((dp_size,) + feats.shape, full),
        pltpu.VMEM((8, folded), full),
        pltpu.VMEM((dp_size, 8, folded), full),
        pltpu.VMEM((tensor_size, dp_size, 8, folded), full),
        pltpu.VMEM((8, folded), full),
        pltpu.VMEM((dp_size, 8, folded), full),
        pltpu.VMEM((tensor_size, dp_size, 8, folded), full),
        pltpu.VMEM((dp_size, 8, 128), full),
        pltpu.VMEM((dp_size, 8, 128), full),
        pltpu.VMEM((dp_size, slots, mod_low.shape[2]), low),
        pltpu.VMEM((dp_size, slots, mod_low.shape[2]), low),
        pltpu.VMEM((slots, mod_low.shape[2]), full),
        pltpu.VMEM((dp_size,) + small.shape, full),
    ]
    for count in (dp_size, dp_size) + (tensor_size, dp_size) * 4 + (tensor_size,):
        scratch += crowd_scratch(count)
    scratch += [
        pltpu.SemaphoreType.DMA((3, dp_size // 2, 3)),
        pltpu.SemaphoreType.DMA((3, dp_size // 2, 3)),
        pltpu.SemaphoreType.DMA((3,)),
    ]
    return pl.pallas_call(
        functools.partial(head_kernel, images),
        out_shape=[jax.ShapeDtypeStruct(*shape) for shape in shapes],
        in_specs=[pl.BlockSpec(memory_space=pltpu.VMEM)] * 9
        + [pl.BlockSpec(memory_space=pl.ANY)] * len(shards),
        out_specs=[pl.BlockSpec(memory_space=pltpu.VMEM)] * 8
        + [pl.BlockSpec(memory_space=pl.ANY)] * len(shards),
        scratch_shapes=scratch,
        compiler_params=pltpu.CompilerParams(
            collective_id=30, has_side_effects=True, vmem_limit_bytes=ACT_VMEM
        ),
        name="head",
    )(small, feats, table, times, second, shift, scale, bias, mod_low, *shards)


def tail_kernel(
    images,
    final_at,
    row_ref,
    mod_ref,
    weight_ref,
    second_ref,
    shift_ref,
    scale_ref,
    pre_signal_ref,
    pre_time_ref,
    feats_ref,
    hidden_ref,
    signal_ref,
    loss_ref,
    *rest,
):
    terms, others = rest[0:3], rest[3 : 2 + LAYERS]
    rest = rest[2 + LAYERS :]
    (
        row_sums,
        vector_sums,
        class_grad,
        time_grad,
        second_grad,
        shift_grad,
        scale_grad,
        mod_grad,
        scalar_sums,
    ) = rest[0:9]
    totals = rest[9:12]
    (
        row_in,
        row_mid,
        row_fin,
        mod_in,
        mod_low,
        d_mod_all,
        signal_part,
        scalar_own,
        scalar_in,
        scalar_mid,
        scalar_fin,
    ) = rest[12:23]
    signal_refs, hidden_refs = rest[23:27], rest[27:31]
    own, pair_in, way_in, way_out = rest[31:34], rest[34:37], rest[37:40], rest[40:43]
    crowds = [rest[43 + 3 * index : 46 + 3 * index] for index in range(10)]
    reduce_sems = rest[73:]
    signal_out, hidden_out = signal_refs[0], hidden_refs[0]
    dp_size = lax.axis_size("dp")
    tensor_size = lax.axis_size("tensor")
    places = dp_size * tensor_size
    dp_rank = lax.axis_index("dp")
    images_all = images * dp_size
    cols, lanes = row_ref.shape[2:]
    mod_rows = weight_ref.shape[1]
    slots = mod_low.shape[0]
    last_step = dp_size // 2
    greet_groups("tensor", "dp")
    reduce = Reduce(Line(), terms, totals, own, pair_in, way_in, way_out, *reduce_sems)
    mod_sum = Crowd("tensor", lambda place: mod_ref.at[place], mod_in, *crowds[0])
    mod_spread = Crowd("dp", lambda place: mod_low, d_mod_all, *crowds[1])
    rows = Funnel(row_ref, row_in, row_mid, row_fin, *crowds[2:4])
    signal = Funnel(*signal_refs, *crowds[4:6])
    hidden = Funnel(*hidden_refs, *crowds[6:8])
    scalars = Crowd("tensor", lambda place: scalar_own, scalar_in, *crowds[8])
    scalars_dp = Crowd("dp", lambda place: scalar_mid, scalar_fin, *crowds[9])
    mod_sum.start()
    rows.start()
    reduce.send_pair(0)
    reduce.load_own()
    mod_sum.wait()
    mod_low[...] = jnp.sum(mod_in[...], axis=0).astype(jnp.bfloat16)
    mod_spread.start()
    rows.hand_on()
    reduce.send_pair(1)
    other_squares = sum(other[0:1, 0:1] for other in others)
    reduce.wait_own()
    row_total = rows.take()
    row_sums[...] = row_total
    joined = jnp.concatenate([row_fin[at] for at in range(dp_size)], axis=1)

    def final_of(piece):
        return dense(
            joined,
            chosen(
                (dp_size * lanes, images_all),
                lambda row, col: (
                    (row // lanes == col // images)
                    & (lax.rem(row, lanes) == final_at + piece * images + lax.rem(col, images))
                ),
                jnp.float32,
            ),
        )

    d_shift, d_scale = final_of(0), final_of(1)
    signal_part[...] = dense_tn(shift_ref[...], d_shift) + dense_tn(scale_ref[...], d_scale)
    mod_spread.wait()
    d_mod = d_mod_all[...].reshape(dp_size * slots, mod_low.shape[1])
    own_rows = pl.ds(pl.multiple_of(dp_rank * mod_rows, 8), mod_rows)

    def layer_pick(layer_idx, kind):
        return chosen(
            (dp_size * slots, images_all),
            lambda row, col: (
                (row // slots == col // images)
                & (lax.rem(row, slots) == layer_idx * images + lax.rem(col, images))
            ),
            kind,
        )

    for layer_idx in range(LAYERS):
        signal_part[own_rows, :] += dense(
            dot_nt(weight_ref[layer_idx], d_mod), layer_pick(layer_idx, jnp.float32)
        )
    signal_out[...] = fold(signal_part[...].reshape(places, cols, images_all)).reshape(
        signal_out.shape
    )
    signal.start()
    signal.hand_on()
    reduce.send_pair(2)
    run_ticks(reduce, 0, min(1, last_step - 1))
    signal_low = signal_ref[own_rows, :].astype(jnp.bfloat16)
    for layer_idx in range(LAYERS):
        placed = dot_nt(signal_low, layer_pick(layer_idx, jnp.bfloat16)).astype(jnp.bfloat16)
        grad = dot_nn(placed, d_mod)
        mod_grad[layer_idx] = grad
        other_squares = other_squares + square_sum(grad)
    grad = dense_nt(d_shift, signal_ref[...])
    shift_grad[...] = grad
    other_squares = other_squares + square_sum(grad)
    grad = dense_nt(d_scale, signal_ref[...])
    scale_grad[...] = grad
    other_squares = other_squares + square_sum(grad)
    lane = lax.broadcasted_iota(jnp.int32, row_total.shape, 1)
    other_squares = other_squares + square_sum(jnp.where(lane < final_at, row_total, 0.0))
    d_signal = unfold(signal.take(), cols, images_all)
    d_signal = d_signal * silu_slope(pre_signal_ref[...])
    d_hidden = dense_tn(second_ref[...], d_signal)
    hidden_out[...] = fold(d_hidden.reshape(places, cols, images_all)).reshape(hidden_out.shape)
    hidden.start()
    hidden.hand_on()
    each(max(last_step - 3, 0), lambda step: reduce.send_pair(step + 3))
    run_ticks(reduce, 1, min(2, last_step - 1))
    labels = jnp.round(feats_ref[:, FREQ : FREQ + 1]).astype(jnp.int32)
    class_lane = lax.broadcasted_iota(jnp.int32, (images_all, class_grad.shape[1]), 1)
    grad = dense(d_signal, jnp.where(class_lane == labels, 1.0, 0.0))
    class_grad[...] = grad
    other_squares = other_squares + square_sum(grad)
    grad = dense_nt(d_signal, hidden_ref[...])
    second_grad[...] = grad
    other_squares = other_squares + square_sum(grad)
    d_hidden = unfold(hidden.take(), cols, images_all)
    d_hidden = d_hidden * silu_slope(pre_time_ref[...])
    grad = dense(d_hidden, feats_ref[:, 0:FREQ])
    time_grad[...] = grad
    other_squares = other_squares + square_sum(grad)
    vectors = [
        jnp.sum(values, axis=1, keepdims=True) for values in (d_hidden, d_signal, d_shift, d_scale)
    ]
    lane = lax.broadcasted_iota(jnp.int32, vector_sums.shape, 1)
    grad = sum(jnp.where(lane == at, vector, 0.0) for at, vector in enumerate(vectors))
    vector_sums[...] = grad
    other_squares = other_squares + square_sum(grad)
    run_ticks(reduce, 2, min(3, last_step - 1))
    each(max(last_step - 4, 0), lambda step: reduce.tick(step + 3))
    reduce.finish()
    for total in totals:
        other_squares = other_squares + square_sum(total[...])
    lane = lax.broadcasted_iota(jnp.int32, scalar_own.shape, 1)
    scalar_own[...] = jnp.where(lane == 0, loss_ref[...], other_squares)
    scalars.start()
    scalars.wait()
    scalar_mid[...] = jnp.sum(scalar_in[...], axis=0)
    scalars_dp.start()
    scalars_dp.wait()
    scalar_sums[...] = jnp.sum(scalar_fin[...], axis=0)


def tail_call(
    rows, mods, mod_low, second, shift, scale, pre_signal, pre_time, feats, hidden, signal, loss,
    terms, others, images, at,
):
    dp_size, tensor_size = lax.axis_size("dp"), lax.axis_size("tensor")
    images_all = images * dp_size
    cols, lanes = rows.shape[2:]
    folded = folded_lanes(cols, images_all)
    full, low = jnp.float32, jnp.bfloat16
    spots = dp_size // 2
    blocks = [term.shape[1:] for term in terms]
    shapes = [
        ((cols, lanes), full),
        ((cols, 128), full),
        ((cols, -(-CLASSES // 128) * 128), full),
        ((cols, FREQ), full),
        ((cols, D), full),
        ((cols, D), full),
        ((cols, D), full),
        (mod_low.shape, full),
        ((8, 128), full),
    ] + [(block, full) for block in blocks]
    scratch = [
        pltpu.VMEM((tensor_size, dp_size, cols, lanes), full),
        pltpu.VMEM((dp_size, cols, lanes), full),
        pltpu.VMEM((dp_size, cols, lanes), full),
        pltpu.VMEM(mods.shape, full),
        pltpu.VMEM(mods.shape[1:], low),
        pltpu.VMEM((dp_size,) + mods.shape[1:], low),
        pltpu.VMEM((D, images_all), full),
        pltpu.VMEM((8, 128), full),
        pltpu.VMEM((tensor_size, 8, 128), full),
        pltpu.VMEM((8, 128), full),
        pltpu.VMEM((dp_size, 8, 128), full),
    ]
    for _ in range(2):
        scratch += [
            pltpu.VMEM((dp_size, tensor_size, 8, folded), full),
            pltpu.VMEM((tensor_size, dp_size, 8, folded), full),
            pltpu.VMEM((dp_size, 8, folded), full),
            pltpu.VMEM((dp_size, 8, folded), full),
        ]
    scratch += [pltpu.VMEM((spots,) + block, low) for block in blocks]
    scratch += [pltpu.VMEM((spots,) + block, low) for block in blocks]
    scratch += [pltpu.VMEM((2, spots) + block, low) for block in blocks]
    scratch += [pltpu.VMEM((2, spots) + block, low) for block in blocks]
    for count in (tensor_size, dp_size) * 5:
        scratch += crowd_scratch(count)
    scratch += [
        pltpu.SemaphoreType.DMA((3, spots, 3)),
        pltpu.SemaphoreType.DMA((3, spots, 3)),
        pltpu.SemaphoreType.DMA((3, spots)),
    ]
    return pl.pallas_call(
        functools.partial(tail_kernel, images, at),
        out_shape=[jax.ShapeDtypeStruct(*shape) for shape in shapes],
        in_specs=[pl.BlockSpec(memory_space=pltpu.VMEM)] * 12
        + [pl.BlockSpec(memory_space=pl.ANY)] * len(terms)
        + [pl.BlockSpec(memory_space=pltpu.VMEM)] * len(others),
        out_specs=[pl.BlockSpec(memory_space=pltpu.VMEM)] * len(shapes),
        scratch_shapes=scratch,
        compiler_params=pltpu.CompilerParams(
            collective_id=31, has_side_effects=True, vmem_limit_bytes=ACT_VMEM
        ),
        name="tail",
    )(
        rows, mods, mod_low, second, shift, scale, pre_signal, pre_time, feats, hidden, signal,
        loss, *terms, *others,
    )


def adam_update(weight, first, second, grad, factor, first_fix, second_fix):
    clipped = grad * factor
    first_new = BETA_ONE * first + (1.0 - BETA_ONE) * clipped
    second_new = BETA_TWO * second + (1.0 - BETA_TWO) * clipped * clipped
    step_size = first_new / first_fix / (jnp.sqrt(second_new / second_fix) + ADAM_EPS)
    change = -LEARN_RATE * (step_size + DECAY * weight)
    master = weight + change
    return (master, first_new, second_new, master.astype(jnp.bfloat16), change)


def local(
    latents,
    target_noise,
    timesteps,
    labels,
    step_count,
    embed_table,
    layer_in,
    layer_out,
    layer_ada,
    embed_first,
    embed_second,
    input_first,
    input_second,
    output_first,
    output_second,
    mod_first,
    mod_second,
):
    tensor_size = lax.axis_size("tensor")
    tensor_rank = lax.axis_index("tensor")
    images = latents.shape[0]
    grid_side = SIDE // PATCH
    local_rows = grid_side // tensor_size
    tokens_all = grid_side * grid_side
    heads_local = HEADS // tensor_size
    group_width = heads_local * HEAD_DIM
    unit_count = FF // tensor_size
    patch_in = PATCH * PATCH * CHANNELS
    count_all = images * lax.axis_size("dp") * tokens_all * patch_in
    patch_start, time_start, second_start, final_start, head_start, vector_start, layer_start = (
        table_starts()
    )
    layer_rows = 10 + FF // D
    dp_rank = lax.axis_index("dp")
    dp_size = lax.axis_size("dp")
    place_count = dp_size * tensor_size
    images_all = images * dp_size
    table_cols = lax.reduce_precision(embed_table.T, 8, 7)
    cols = table_cols.shape[0]
    mod_rows = layer_ada.shape[1]
    mod_cols = layer_ada.shape[2]
    mod_low = layer_ada.astype(jnp.bfloat16)

    def col_block(row_start, row_count):
        return table_cols[:, row_start : row_start + row_count]

    vector_count = 5 + LAYERS * layer_rows
    small_count = 2 * patch_in + vector_count
    lanes = -(-(small_count + 2 * images) // 128) * 128
    shards_in = layer_in[:, :, 0].astype(jnp.bfloat16)
    shards = (
        shards_in[:, :, : 3 * group_width],
        shards_in[:, :, 3 * group_width :],
        layer_out[:, 0].astype(jnp.bfloat16),
    )
    second_cols = col_block(second_start, D)
    shift_cols = col_block(final_start, D)
    scale_cols = col_block(final_start + D, D)
    fused = cols % 8 == 0 and images <= 8
    if fused:
        small_send = jnp.concatenate(
            [
                col_block(patch_start, patch_in),
                col_block(head_start, patch_in + vector_count),
                jnp.zeros((cols, lanes - small_count), jnp.float32),
            ],
            axis=1,
        )
        feats_send = jnp.concatenate(
            [
                time_features(timesteps),
                jnp.broadcast_to(labels.astype(jnp.float32)[:, None], (images, 128)),
            ],
            axis=1,
        )
        feats_send = jnp.pad(feats_send, ((0, 8 - images), (0, 0)))
        outs = head_call(
            small_send,
            feats_send,
            table_cols,
            col_block(time_start, FREQ),
            second_cols,
            shift_cols,
            scale_cols,
            col_block(vector_start, 5),
            mod_low,
            shards,
            images,
        )
        small_all, feats_all, pre_time, hidden, pre_signal, signal, final_all, mod_full = outs[:8]
        wholes = outs[8:]
        small_all = small_all.transpose(1, 0, 2, 3)
        time_feats = feats_all[:, :FREQ]
        labels_all = jnp.round(feats_all[:, FREQ]).astype(jnp.int32)
        signal_low = lax.dynamic_slice_in_dim(
            signal.astype(jnp.bfloat16), dp_rank * mod_rows, mod_rows, 0
        )
        final_all = final_all.transpose(1, 0, 2, 3)[:, :, :images, : 2 * cols]
        final_own = final_all.reshape(place_count, images, 2, cols)
        final_own = final_own.transpose(2, 1, 0, 3).reshape(2, images, D)
        mod_full = mod_full[:, : LAYERS * images].reshape(tensor_size, LAYERS, images, mod_cols)
        mod_full = mod_full.transpose(1, 2, 0, 3).reshape(LAYERS, images, tensor_size * mod_cols)
    else:
        scalar_lanes = jnp.concatenate([timesteps, labels]).astype(jnp.float32)
        small_send = jnp.concatenate(
            [
                col_block(patch_start, patch_in),
                col_block(head_start, patch_in + vector_count),
                jnp.broadcast_to(scalar_lanes[None, :], (cols, 2 * images)),
                jnp.zeros((cols, lanes - small_count - 2 * images), jnp.float32),
            ],
            axis=1,
        )
        small_all = exchange(small_send, "all", False, 1)
        scalars_all = small_all[::tensor_size, 0, small_count : small_count + 2 * images].astype(
            jnp.int32
        )
        timesteps_all = scalars_all[:, :images].reshape(images_all)
        labels_all = scalars_all[:, images:].reshape(images_all)
        time_feats = time_features(timesteps_all)
        onehot = (labels_all[:, None] == jnp.arange(CLASSES, dtype=jnp.int32)[None, :]).astype(
            jnp.float32
        )
        pre_time = dense(col_block(time_start, FREQ), time_feats.T) + col_block(vector_start + 1, 1)
        hidden = exchange(jax.nn.silu(pre_time), "all", False, 2).reshape(D, images_all)
        pre_signal = (
            dense(second_cols, hidden)
            + col_block(vector_start + 2, 1)
            + dense(col_block(0, CLASSES), onehot.T)
        )
        signal = exchange(jax.nn.silu(pre_signal), "all", False, 3).reshape(D, images_all)
        final_send = jnp.concatenate(
            [
                dense(shift_cols, signal) + col_block(vector_start + 3, 1),
                dense(scale_cols, signal) + col_block(vector_start + 4, 1),
            ],
            axis=0,
        )
        final_all = exchange(final_send, "all", False, 4).reshape(place_count, 2, cols, images_all)
        final_own = lax.dynamic_slice_in_dim(final_all, dp_rank * images, images, 3)
        final_own = final_own.transpose(1, 3, 0, 2).reshape(2, images, D)
        signal_low = lax.dynamic_slice_in_dim(
            signal.astype(jnp.bfloat16), dp_rank * mod_rows, mod_rows, 0
        )
        mod_part = jnp.einsum("db,lde->ble", signal_low, mod_low, preferred_element_type=jnp.float32)
        mod_part = mod_part.reshape(dp_size, images * LAYERS, mod_cols)
        mod_local = jnp.sum(exchange(mod_part, "dp", True, 5), axis=0)
        mod_full = exchange(mod_local, "tensor", False, 6)
        mod_full = mod_full.reshape(tensor_size, images, LAYERS, mod_cols)
        mod_full = mod_full.transpose(2, 1, 0, 3).reshape(LAYERS, images, tensor_size * mod_cols)
        wholes = [lax.all_gather(shard[0], "dp") for shard in shards]
    small_rows = small_all.reshape(D, lanes).T
    patch_w = small_rows[0:patch_in]
    head_w = small_rows[patch_in : 2 * patch_in]
    vectors = small_rows[2 * patch_in : 2 * patch_in + 5]
    bias_all = small_rows[2 * patch_in + 5 : small_count]
    onehot = (labels_all[:, None] == jnp.arange(CLASSES, dtype=jnp.int32)[None, :]).astype(
        jnp.float32
    )
    final_shift, final_scale = final_own[0], final_own[1]
    pixels = patchify(latents, local_rows)
    targets = patchify(target_noise, local_rows)
    keep_coef, drop_coef = noise_levels(timesteps)
    noisy = keep_coef[:, None, None] * pixels + drop_coef[:, None, None] * targets
    residual = (
        jnp.einsum("btp,pd->btd", noisy, patch_w, precision=PRECISE)
        + vectors[0]
        + position_table(tensor_rank * local_rows, local_rows)[None]
    )
    saved_acts = []
    bias_all = bias_all.reshape(LAYERS, layer_rows, D)
    mod_vecs = mod_full.reshape(LAYERS, images, 6, D) + bias_all[:, None, 0:6]
    part_bias = lax.dynamic_slice_in_dim(
        bias_all[:, 8:10], tensor_rank * group_width, group_width, 2
    )
    qkv_bias = jnp.concatenate(
        [part_bias[:, 0], jnp.zeros((LAYERS, group_width), jnp.float32), part_bias[:, 1]], axis=1
    )
    up_bias = lax.dynamic_slice_in_dim(
        bias_all[:, 10:].reshape(LAYERS, FF), tensor_rank * unit_count, unit_count, 1
    )
    for layer_idx in range(LAYERS):
        weights = (
            wholes[0].reshape(D, 3 * group_width),
            wholes[1].reshape(D, unit_count),
            wholes[2].reshape(group_width + unit_count, D),
        )
        outs = forward_layer(
            residual,
            mod_vecs[layer_idx],
            bias_all[layer_idx, 6:8],
            qkv_bias[layer_idx : layer_idx + 1],
            up_bias[layer_idx : layer_idx + 1],
            *weights,
            shards if layer_idx + 1 < LAYERS else (),
            layer_idx,
        )
        wholes = outs[9:]
        saved_acts.append((mod_vecs[layer_idx], (residual,) + tuple(outs[1:9]), weights))
        residual = outs[0]
    final_in, final_norm_pull = jax.vjp(modulate, residual, final_shift, final_scale)
    predicted = jnp.einsum("btd,pd->btp", final_in, head_w, precision=PRECISE)
    error_all = predicted - targets
    loss_part = jnp.sum(error_all * error_all) / count_all
    d_pred = 2.0 * error_all / count_all
    d_head = jnp.einsum("btp,btd->pd", d_pred, final_in, precision=PRECISE)
    d_final = jnp.einsum("btp,pd->btd", d_pred, head_w, precision=PRECISE)
    d_residual, d_final_shift, d_final_scale = final_norm_pull(d_final)
    totals = []
    squares = []
    terms = ()
    bias_parts = []
    for layer_idx in reversed(range(LAYERS)):
        mod_vec, saved, weights = saved_acts[layer_idx]
        outs = backward_layer(d_residual, mod_vec, saved, weights, terms)
        d_residual, d_w_qkv, d_w_up, d_w_out, d_mod_vec, d_vec, d_qkv_bias, d_up_bias = outs[:8]
        if terms:
            totals.insert(0, outs[8:11])
            squares.append(outs[11])
        terms = [
            term.reshape((dp_size, -1) + term.shape[1:]) for term in (d_w_qkv, d_w_up, d_w_out)
        ]
        bias_parts.insert(0, (d_mod_vec, d_vec, d_qkv_bias, d_up_bias))
    d_mods, d_vecs, d_qkv_rows, d_up_rows = [jnp.stack(parts) for parts in zip(*bias_parts)]
    part_rows = jnp.stack([d_qkv_rows[:, 0, :group_width], d_qkv_rows[:, 0, 2 * group_width :]], 1)
    bias_blocks = jnp.concatenate(
        [
            jnp.sum(d_mods, axis=1),
            d_vecs,
            lax.dynamic_update_slice_in_dim(
                jnp.zeros((LAYERS, 2, D), jnp.float32), part_rows, tensor_rank * group_width, 2
            ),
            lax.dynamic_update_slice_in_dim(
                jnp.zeros((LAYERS, FF), jnp.float32), d_up_rows[:, 0], tensor_rank * unit_count, 1
            ).reshape(LAYERS, FF // D, D),
        ],
        axis=1,
    ).reshape(LAYERS * layer_rows, D)
    d_patch_w = jnp.einsum("btp,btd->pd", noisy, d_residual, precision=PRECISE)
    d_patch_b = jnp.sum(d_residual, axis=(0, 1))
    row_parts = jnp.concatenate(
        [d_patch_w, d_head, d_patch_b[None], bias_blocks, d_final_shift, d_final_scale],
        axis=0,
    )
    row_count = row_parts.shape[0]
    row_lanes = -(-row_count // 128) * 128
    row_parts = jnp.pad(row_parts, ((0, row_lanes - row_count), (0, 0)))
    final_at = row_count - 2 * images
    row_send = row_parts.T.reshape(dp_size, tensor_size, cols, row_lanes)
    mod_send = d_mods.reshape(LAYERS * images, tensor_size, mod_cols)
    mod_send = mod_send.transpose(1, 0, 2)
    if fused:
        slots = slots_of(images)
        outs = tail_call(
            row_send,
            jnp.pad(mod_send, ((0, 0), (0, slots - LAYERS * images), (0, 0))),
            mod_low,
            second_cols,
            shift_cols,
            scale_cols,
            pre_signal,
            pre_time,
            feats_all,
            hidden,
            signal,
            loss_part.reshape(1, 1),
            terms,
            squares,
            images,
            final_at,
        )
        row_sums, vector_sums, class_grad, time_grad, second_grad, shift_grad, scale_grad = outs[:7]
        mod_grad, scalar_sums = outs[7:9]
        totals.insert(0, outs[9:])
        vector_sums = vector_sums[:, 0:4]
        class_grad = class_grad[:, :CLASSES]
        scalar_sums = scalar_sums[0]
    else:
        totals.insert(
            0,
            [
                lax.psum_scatter(term, "dp", scatter_dimension=0).astype(jnp.float32)
                for term in terms
            ],
        )
        row_all = exchange(row_send.reshape(place_count, cols, row_lanes), "all", True, 7)
        row_sums = jnp.sum(row_all, axis=0)
        final_sums = jnp.sum(
            row_all[:, :, final_at:row_count].reshape(dp_size, tensor_size, cols, 2, images), axis=1
        )
        final_sums = final_sums.transpose(2, 1, 0, 3).reshape(2, cols, images_all)
        d_shift_cols, d_scale_cols = final_sums[0], final_sums[1]
        d_mod_own = jnp.sum(exchange(mod_send, "tensor", True, 8), axis=0)
        d_mod_low = exchange(d_mod_own.astype(jnp.bfloat16), "dp", False, 9)
        d_mod_low = d_mod_low.reshape(dp_size, LAYERS, images, mod_cols)
        d_mod_low = d_mod_low.transpose(1, 0, 2, 3).reshape(LAYERS, images_all, mod_cols)
        d_signal_rows = jnp.einsum(
            "lbe,lde->db", d_mod_low, mod_low, preferred_element_type=jnp.float32
        )
        d_signal_part = dense(shift_cols.T, d_shift_cols) + dense(scale_cols.T, d_scale_cols)
        d_signal_part = d_signal_part + lax.dynamic_update_slice_in_dim(
            jnp.zeros((D, images_all), jnp.float32), d_signal_rows, dp_rank * mod_rows, 0
        )
        d_signal_cols = jnp.sum(
            exchange(d_signal_part.reshape(place_count, cols, images_all), "all", True, 10), axis=0
        )
        d_pre_signal = d_signal_cols * silu_slope(pre_signal)
        d_hidden_part = dense(second_cols.T, d_pre_signal)
        d_hidden_cols = jnp.sum(
            exchange(d_hidden_part.reshape(place_count, cols, images_all), "all", True, 11), axis=0
        )
        d_hidden = d_hidden_cols * silu_slope(pre_time)
        mod_grad = jnp.einsum(
            "db,lbe->lde", signal_low, d_mod_low, preferred_element_type=jnp.float32
        )
        class_grad = dense(d_pre_signal, onehot)
        time_grad = dense(d_hidden, time_feats)
        second_grad = dense(d_pre_signal, hidden.T)
        shift_grad = dense(d_shift_cols, signal.T)
        scale_grad = dense(d_scale_cols, signal.T)
        vector_sums = jnp.stack(
            [
                jnp.sum(values, axis=1)
                for values in (d_hidden, d_pre_signal, d_shift_cols, d_scale_cols)
            ],
            axis=1,
        )
    table_grad = jnp.concatenate(
        [
            class_grad,
            row_sums[:, 0:patch_in],
            time_grad,
            second_grad,
            shift_grad,
            scale_grad,
            row_sums[:, patch_in : 2 * patch_in + 1],
            vector_sums,
            row_sums[:, 2 * patch_in + 1 : final_at],
        ],
        axis=1,
    )
    input_grad = jnp.stack([jnp.concatenate(total[0:2], axis=1) for total in totals])
    input_grad = input_grad.reshape(layer_in.shape)
    output_grad = jnp.stack([total[2] for total in totals]).reshape(layer_out.shape)
    if not fused:
        local_squares = (
            jnp.sum(table_grad * table_grad)
            + jnp.sum(input_grad * input_grad)
            + jnp.sum(output_grad * output_grad)
            + jnp.sum(mod_grad * mod_grad)
        )
        scalar_send = jnp.where(
            lax.broadcasted_iota(jnp.int32, (8, 128), 1) == 0, loss_part, local_squares
        )
        scalar_sums = jnp.sum(exchange(scalar_send, "all", False, 12)[:, 0, 0:2], axis=0)
    loss_value = scalar_sums[0]
    square_total = scalar_sums[1]
    grad_norm = jnp.sqrt(square_total)
    factor = jnp.minimum(1.0, CLIP_NORM / grad_norm)
    first_fix = 1.0 - BETA_ONE ** step_count.astype(jnp.float32)
    second_fix = 1.0 - BETA_TWO ** step_count.astype(jnp.float32)
    embed_out = adam_update(
        embed_table.T, embed_first.T, embed_second.T, table_grad, factor, first_fix, second_fix
    )
    input_out = adam_update(
        layer_in, input_first, input_second, input_grad, factor, first_fix, second_fix
    )
    output_out = adam_update(
        layer_out, output_first, output_second, output_grad, factor, first_fix, second_fix
    )
    mod_out = adam_update(layer_ada, mod_first, mod_second, mod_grad, factor, first_fix, second_fix)
    return (
        (loss_value, grad_norm, embed_out[4].T, embed_out[1].T, embed_out[2].T)
        + input_out[0:4]
        + output_out[0:4]
        + mod_out[0:4]
    )


def solution(mesh):
    placed = (
        P("dp", "tensor"),
        P("dp", "tensor"),
        P("dp"),
        P("dp"),
        P(),
        P(None, ("dp", "tensor")),
        P(None, "dp", "tensor", None),
        P(None, "tensor", "dp", None),
        P(None, "dp", "tensor"),
        P(None, ("dp", "tensor")),
        P(None, ("dp", "tensor")),
        P(None, "dp", "tensor", None),
        P(None, "dp", "tensor", None),
        P(None, "tensor", "dp", None),
        P(None, "tensor", "dp", None),
        P(None, "dp", "tensor"),
        P(None, "dp", "tensor"),
    )
    return jax.shard_map(
        local,
        mesh=mesh,
        in_specs=placed,
        out_specs=(
            P(),
            P(),
            P(None, ("dp", "tensor")),
            P(None, ("dp", "tensor")),
            P(None, ("dp", "tensor")),
            P(None, "dp", "tensor", None),
            P(None, "dp", "tensor", None),
            P(None, "dp", "tensor", None),
            P(None, "dp", "tensor", None),
            P(None, "tensor", "dp", None),
            P(None, "tensor", "dp", None),
            P(None, "tensor", "dp", None),
            P(None, "tensor", "dp", None),
            P(None, "dp", "tensor"),
            P(None, "dp", "tensor"),
            P(None, "dp", "tensor"),
            P(None, "dp", "tensor"),
        ),
        check_vma=False,
    )
```

```python
import functools
import math

import jax
import jax.numpy as jnp
from jax import lax
from jax.experimental import pallas as pl
from jax.experimental.pallas import tpu as pltpu
from jax.sharding import PartitionSpec as P

D = 768
HEADS = 12
HEAD_DIM = 64
FF = 3072
CLASSES = 1001
FREQ = 256
CHANNELS = 4
PATCH = 2
SIDE = 32
LAYERS = 3


EPS_NORM = 1e-06
LEARN_RATE = 0.01
DECAY = 0.01
BETA_ONE = 0.5
BETA_TWO = 0.5
ADAM_EPS = 1e-08
CLIP_NORM = 0.25
PRECISE = lax.Precision.HIGHEST


def dense(left_op, right_op):
    return jnp.dot(left_op, right_op, precision=PRECISE, preferred_element_type=jnp.float32)


def layer_norm(values):
    center = values - jnp.mean(values, axis=-1, keepdims=True)
    return center * lax.rsqrt(jnp.mean(center * center, axis=-1, keepdims=True) + EPS_NORM)


def modulate(values, shift_vec, scale_vec):
    return layer_norm(values) * (1.0 + scale_vec[:, None, :]) + shift_vec[:, None, :]


def gelu_tanh(values):
    return jax.nn.gelu(values, approximate=True)


def silu_slope(values):
    sigmoid_val = jax.nn.sigmoid(values)
    return sigmoid_val * (1.0 + values * (1.0 - sigmoid_val))


def time_features(step_ints):
    half_width = FREQ // 2
    frequency = jnp.exp(-math.log(10000.0) * jnp.arange(half_width, dtype=jnp.float32) / half_width)
    angles = step_ints.astype(jnp.float32)[:, None] * frequency[None, :]
    return jnp.concatenate([jnp.cos(angles), jnp.sin(angles)], axis=1)


def noise_levels(step_ints):
    base_cos = math.cos(0.008 / 1.008 * math.pi / 2)
    angles = (step_ints.astype(jnp.float32) / 1000.0 + 0.008) / 1.008 * (math.pi / 2)
    signal_level = jnp.cos(angles) ** 2 / base_cos**2
    return (jnp.sqrt(signal_level), jnp.sqrt(1.0 - signal_level))


def position_table(first_row, row_count):
    grid_side = SIDE // PATCH
    quarter = D // 4
    omegas = jnp.exp(-math.log(10000.0) * jnp.arange(quarter, dtype=jnp.float32) / quarter)
    token_index = jnp.arange(row_count * grid_side, dtype=jnp.int32)
    row_angle = (first_row + token_index // grid_side).astype(jnp.float32)[:, None] * omegas[
        None, :
    ]
    col_angle = (token_index % grid_side).astype(jnp.float32)[:, None] * omegas[None, :]
    return jnp.concatenate(
        [jnp.sin(row_angle), jnp.cos(row_angle), jnp.sin(col_angle), jnp.cos(col_angle)], axis=1
    )


def patchify(flat_pixels, row_count):
    grid_side = SIDE // PATCH
    shaped = flat_pixels.reshape(flat_pixels.shape[0], row_count, PATCH, grid_side, PATCH, CHANNELS)
    return shaped.transpose(0, 1, 3, 2, 4, 5).reshape(
        flat_pixels.shape[0], row_count * grid_side, PATCH * PATCH * CHANNELS
    )


def table_starts():
    patch_in = PATCH * PATCH * CHANNELS
    patch_start = CLASSES
    time_start = patch_start + patch_in
    second_start = time_start + FREQ
    final_start = second_start + D
    head_start = final_start + 2 * D
    vector_start = head_start + patch_in
    layer_start = vector_start + 5
    return (
        patch_start,
        time_start,
        second_start,
        final_start,
        head_start,
        vector_start,
        layer_start,
    )


def group_place(group):
    if group == "all":
        width = lax.axis_size("tensor")
        place = lax.axis_index("dp") * width + lax.axis_index("tensor")
        size = lax.axis_size("dp") * width
        return place, size, lambda at: {"dp": at // width, "tensor": lax.rem(at, width)}
    return lax.axis_index(group), lax.axis_size(group), lambda at: {group: at}


def greet_group(group):
    place, size, coords = group_place(group)
    barrier = pltpu.get_barrier_semaphore()

    def greet_one(step, carry):
        peer = coords(lax.rem(place + step, size))
        pl.semaphore_signal(barrier, inc=1, device_id=peer, device_id_type=pl.DeviceIdType.MESH)
        return carry

    lax.fori_loop(1, size, greet_one, 0)
    pl.semaphore_wait(barrier, size - 1)


def greet_groups(*groups):
    barrier = pltpu.get_barrier_semaphore()
    count = 0
    for group in groups:
        place, size, coords = group_place(group)

        def greet_one(step, carry, place=place, size=size, coords=coords):
            peer = coords(lax.rem(place + step, size))
            pl.semaphore_signal(barrier, inc=1, device_id=peer, device_id_type=pl.DeviceIdType.MESH)
            return carry

        lax.fori_loop(1, size, greet_one, 0)
        count += size - 1
    pl.semaphore_wait(barrier, count)


class Crowd:
    def __init__(self, group, source_at, target, send_sems, recv_sems, local_sem):
        self.place, self.size, self.coords = group_place(group)
        self.source_at, self.target = source_at, target
        self.sends, self.recvs, self.local_sem = send_sems, recv_sems, local_sem

    def copy_to(self, step):
        there = lax.rem(self.place + step, self.size)
        return pltpu.make_async_remote_copy(
            src_ref=self.source_at(there),
            dst_ref=self.target.at[self.place],
            send_sem=self.sends.at[step],
            recv_sem=self.recvs.at[step],
            device_id=self.coords(there),
            device_id_type=pl.DeviceIdType.MESH,
        )

    def own_copy(self):
        return pltpu.make_async_copy(
            self.source_at(self.place), self.target.at[self.place], self.local_sem
        )

    def start(self):
        def begin(step, carry):
            self.copy_to(step).start()
            return carry

        lax.fori_loop(1, self.size, begin, 0)
        self.own_copy().start()

    def wait(self):
        def finish(step, carry):
            self.copy_to(step).wait()
            return carry

        self.own_copy().wait()
        lax.fori_loop(1, self.size, finish, 0)


class Relay:
    def __init__(self, source_at, middle, whole, sems_dp, sems_tensor):
        self.first = Crowd("dp", source_at, middle, *sems_dp)
        self.second = Crowd("tensor", lambda place: middle, whole, *sems_tensor)

    def start(self):
        self.first.start()

    def hand_on(self):
        self.first.wait()
        self.second.start()

    def wait(self):
        self.second.wait()


class Funnel:
    def __init__(self, source, across, middle, along, sems_tensor, sems_dp):
        self.across, self.middle, self.along = across, middle, along
        self.first = Crowd("tensor", lambda place: source.at[:, place], across, *sems_tensor)
        self.second = Crowd("dp", lambda place: middle.at[place], along, *sems_dp)

    def start(self):
        self.first.start()

    def hand_on(self):
        self.first.wait()
        self.middle[...] = jnp.sum(self.across[...], axis=0)
        self.second.start()

    def take(self):
        self.second.wait()
        return jnp.sum(self.along[...], axis=0)


def crowd_scratch(size):
    return [
        pltpu.SemaphoreType.DMA((size,)),
        pltpu.SemaphoreType.DMA((size,)),
        pltpu.SemaphoreType.DMA,
    ]


def exchange_kernel(group, spread, source, target, send_sems, recv_sems, local_sem):
    greet_group(group)
    crowd = Crowd(
        group,
        lambda place: source.at[place] if spread else source,
        target,
        send_sems,
        recv_sems,
        local_sem,
    )
    crowd.start()
    crowd.wait()


def exchange(values, group, spread, call_id):
    if group == "all":
        size = lax.axis_size("dp") * lax.axis_size("tensor")
    else:
        size = lax.axis_size(group)
    block = values.shape[1:] if spread else values.shape
    return pl.pallas_call(
        functools.partial(exchange_kernel, group, spread),
        out_shape=jax.ShapeDtypeStruct((size,) + block, values.dtype),
        in_specs=[pl.BlockSpec(memory_space=pltpu.VMEM)],
        out_specs=pl.BlockSpec(memory_space=pltpu.VMEM),
        scratch_shapes=crowd_scratch(size),
        compiler_params=pltpu.CompilerParams(
            collective_id=call_id, has_side_effects=True, vmem_limit_bytes=32 * 2**20
        ),
        name="exchange_" + group,
    )(values)


MESH = pl.DeviceIdType.MESH
ACT_VMEM = 60 * 2**20


def dot_nn(left_op, right_op):
    return jnp.dot(left_op, right_op, preferred_element_type=jnp.float32)


def dot_nt(left_op, right_op):
    return lax.dot_general(
        left_op, right_op, (((1,), (1,)), ((), ())), preferred_element_type=jnp.float32
    )


def dot_tn(left_op, right_op):
    return lax.dot_general(
        left_op, right_op, (((0,), (0,)), ((), ())), preferred_element_type=jnp.float32
    )


def square_sum(values):
    return jnp.sum(jnp.sum(values * values, axis=0, keepdims=True), axis=1, keepdims=True)


def norm_parts(values):
    center = values - jnp.mean(values, axis=-1, keepdims=True)
    rstd = lax.rsqrt(jnp.mean(center * center, axis=-1, keepdims=True) + EPS_NORM)
    return center * rstd, rstd


def greet(line):
    rank = lax.axis_index("tensor")
    half = lax.axis_size("tensor") // 2
    core_peer = {"tensor": rank + 1 - 2 * lax.rem(rank, 2)}
    chip_peer = {"tensor": lax.rem(rank + half, 2 * half)}
    barrier = pltpu.get_barrier_semaphore()
    for peer in (core_peer, chip_peer):
        pl.semaphore_signal(barrier, inc=1, device_id=peer, device_id_type=MESH)
    count = 2
    if line is not None:
        line.greet()
        count = count + line.answers()
    pl.semaphore_wait(barrier, count)


class Spread:
    def __init__(self, rows_ref, send_sems, recv_sems):
        self.rows, self.send, self.recv = rows_ref, send_sems, recv_sems
        self.rank = lax.axis_index("tensor")
        self.own_core = lax.rem(self.rank, 2)
        self.core_peer = self.rank + 1 - 2 * self.own_core
        self.chip_peer = lax.rem(self.rank + 2, 4)
        self.count = rows_ref.shape[1] // 4

    def block(self, image, owner):
        return self.rows.at[image, pl.ds(pl.multiple_of(owner * self.count, 16), self.count), :]

    def copy(self, image, owner, peer, which):
        return pltpu.make_async_remote_copy(
            src_ref=self.block(image, owner),
            dst_ref=self.block(image, owner),
            send_sem=self.send.at[image, which],
            recv_sem=self.recv.at[image, which],
            device_id={"tensor": peer},
            device_id_type=MESH,
        )

    def put(self, image, values):
        self.rows[image, pl.ds(pl.multiple_of(self.rank * self.count, 16), self.count), :] = values
        self.copy(image, self.rank, self.chip_peer, 0).start()
        self.copy(image, self.rank, self.core_peer, 1).start()

    def forward(self, image):
        self.copy(image, self.rank, self.chip_peer, 0).wait_recv()
        self.copy(image, self.chip_peer, self.core_peer, 2).start()

    def wait(self, image):
        self.copy(image, self.rank, self.core_peer, 1).wait_recv()
        self.copy(image, self.chip_peer, self.core_peer, 2).wait_recv()

    def close(self, image):
        self.copy(image, self.rank, self.chip_peer, 0).wait_send()
        self.copy(image, self.rank, self.core_peer, 1).wait_send()
        self.copy(image, self.chip_peer, self.core_peer, 2).wait_send()


class Collect:
    def __init__(self, part, near, far_out, far_in, send_sems, recv_sems):
        self.part, self.near, self.far_out, self.far_in = part, near, far_out, far_in
        self.send, self.recv = send_sems, recv_sems
        self.rank = lax.axis_index("tensor")
        self.own_core = lax.rem(self.rank, 2)
        self.own_chip = self.rank // 2
        self.core_peer = self.rank + 1 - 2 * self.own_core
        self.chip_peer = lax.rem(self.rank + 2, 4)
        self.count = part.shape[1] // 4

    def block(self, image, owner):
        return self.part.at[image, pl.ds(pl.multiple_of(owner * self.count, 16), self.count), :]

    def near_copy(self, image, far):
        chip = 1 - self.own_chip if far else self.own_chip
        return pltpu.make_async_remote_copy(
            src_ref=self.block(image, 2 * chip + 1 - self.own_core),
            dst_ref=self.near.at[image, far],
            send_sem=self.send.at[image, far],
            recv_sem=self.recv.at[image, far],
            device_id={"tensor": self.core_peer},
            device_id_type=MESH,
        )

    def far_copy(self, image):
        return pltpu.make_async_remote_copy(
            src_ref=self.far_out.at[image],
            dst_ref=self.far_in.at[image],
            send_sem=self.send.at[image, 2],
            recv_sem=self.recv.at[image, 2],
            device_id={"tensor": self.chip_peer},
            device_id_type=MESH,
        )

    def put(self, image, values):
        self.part[image] = values.astype(jnp.bfloat16)
        self.near_copy(image, 1).start()
        self.near_copy(image, 0).start()

    def load(self, image, owner):
        at = pl.ds(pl.multiple_of(owner * self.count, 16), self.count)
        return self.part[image, at, :].astype(jnp.float32)

    def forward(self, image):
        self.near_copy(image, 1).wait_recv()
        total = self.load(image, self.chip_peer) + self.near[image, 1].astype(jnp.float32)
        self.far_out[image] = total.astype(jnp.bfloat16)
        self.far_copy(image).start()

    def take(self, image):
        self.near_copy(image, 0).wait_recv()
        total = self.load(image, self.rank) + self.near[image, 0].astype(jnp.float32)
        self.far_copy(image).wait_recv()
        return total + self.far_in[image].astype(jnp.float32)

    def close(self, image):
        self.near_copy(image, 1).wait_send()
        self.near_copy(image, 0).wait_send()
        self.far_copy(image).wait_send()


def collect_scratch(images, tokens):
    count = tokens // 4
    return [
        pltpu.VMEM((images, tokens, D), jnp.bfloat16),
        pltpu.VMEM((images, 2, count, D), jnp.bfloat16),
        pltpu.VMEM((images, count, D), jnp.bfloat16),
        pltpu.VMEM((images, count, D), jnp.bfloat16),
    ]


def each(count, body):
    def step(index, carry):
        body(index)
        return carry

    lax.fori_loop(0, count, step, 0)


class Moves:
    def __init__(self, pairs, sems):
        self.copies = [
            pltpu.make_async_copy(source, target, sems.at[at])
            for at, (source, target) in enumerate(pairs)
        ]

    def start(self, *which):
        for at in which:
            self.copies[at].start()

    def wait(self, *which):
        for at in which:
            self.copies[at].wait()


class Line:
    def __init__(self):
        self.size = lax.axis_size("dp") // 2
        self.place = lax.axis_index("dp")
        self.at = self.place // 2
        self.side = lax.rem(self.place, 2)
        self.pair = self.place + 1 - 2 * self.side
        self.has_up = self.at + 1 < self.size
        self.has_down = self.at > 0

    def greet(self):
        barrier = pltpu.get_barrier_semaphore()
        pl.semaphore_signal(barrier, inc=1, device_id={"dp": self.pair}, device_id_type=MESH)

        @pl.when(self.has_up)
        def _():
            up = {"dp": self.place + 2}
            pl.semaphore_signal(barrier, inc=1, device_id=up, device_id_type=MESH)

        @pl.when(self.has_down)
        def _():
            down = {"dp": self.place - 2}
            pl.semaphore_signal(barrier, inc=1, device_id=down, device_id_type=MESH)

    def answers(self):
        return 1 + self.has_up.astype(jnp.int32) + self.has_down.astype(jnp.int32)


UP, DOWN, PAIR = 0, 1, 2


class Gather:
    def __init__(self, line, shards, wholes, sends, recvs, local_sems):
        self.line, self.shards, self.wholes = line, shards, wholes
        self.sends, self.recvs, self.local_sems = sends, recvs, local_sems

    def copy(self, part, way, step, owner, fresh=False):
        line = self.line
        there = {UP: line.place + 2, DOWN: line.place - 2, PAIR: line.pair}[way]
        return pltpu.make_async_remote_copy(
            src_ref=self.shards[part] if fresh else self.wholes[part].at[owner],
            dst_ref=self.wholes[part].at[owner],
            send_sem=self.sends.at[way, step, part],
            recv_sem=self.recvs.at[way, step, part],
            device_id={"dp": there},
            device_id_type=MESH,
        )

    def local_copy(self, part):
        return pltpu.make_async_copy(
            self.shards[part], self.wholes[part].at[self.line.place], self.local_sems.at[part]
        )

    def start(self):
        line = self.line
        parts = range(len(self.shards))

        @pl.when(line.has_up)
        def _():
            for part in parts:
                self.copy(part, UP, 0, line.place, True).start()

        @pl.when(line.has_down)
        def _():
            for part in parts:
                self.copy(part, DOWN, 0, line.place, True).start()

        for part in parts:
            self.copy(part, PAIR, line.at, line.place, True).start()
            self.local_copy(part).start()

    def came(self, way, step):
        there = -step if way == UP else step
        spot = self.line.at + there
        return self.line.place + 2 * there, spot, (spot >= 0) & (spot < self.line.size)

    def hand_on(self, step, way):
        line = self.line
        owner, _, real = self.came(way, step)
        can = line.has_up if way == UP else line.has_down

        @pl.when(real)
        def _():
            for part in range(len(self.shards)):
                self.copy(part, way, step - 1, owner).wait_recv()

            @pl.when(can)
            def _():
                for part in range(len(self.shards)):
                    self.copy(part, way, step, owner).start()

    def hand_over(self, step, way, when=True):
        owner, spot, real = self.came(way, step)

        @pl.when(real & when)
        def _():
            for part in range(len(self.shards)):
                self.copy(part, PAIR, spot, owner).start()

    def tick(self, step):
        for way in (UP, DOWN):
            self.hand_on(step, way)
            self.hand_over(step, way)

    def finish(self):
        line = self.line
        parts = range(len(self.shards))
        for part in parts:
            self.local_copy(part).wait()

        def side(spot):
            for part in parts:
                self.copy(part, PAIR, spot, 2 * spot + line.side).wait()

        each(line.size, side)

        def along(step):
            for way, there, can in ((UP, -step, line.has_up), (DOWN, step, line.has_down)):
                spot = line.at + there

                @pl.when((spot >= 0) & (spot < line.size) & can)
                def _(way=way, there=there):
                    for part in parts:
                        self.copy(part, way, step, line.place + 2 * there).wait_send()

        each(line.size, along)


class Reduce:
    def __init__(self, line, terms, totals, own, pair_in, way_in, way_out, sends, recvs, own_sems):
        self.line, self.terms, self.totals, self.own = line, terms, totals, own
        self.own_sems = own_sems
        self.pair_in, self.way_in, self.way_out = pair_in, way_in, way_out
        self.sends, self.recvs = sends, recvs

    def pair_copy(self, part, spot):
        return pltpu.make_async_remote_copy(
            src_ref=self.terms[part].at[2 * spot + 1 - self.line.side],
            dst_ref=self.pair_in[part].at[spot],
            send_sem=self.sends.at[PAIR, spot, part],
            recv_sem=self.recvs.at[PAIR, spot, part],
            device_id={"dp": self.line.pair},
            device_id_type=MESH,
        )

    def way_copy(self, part, way, spot):
        there = self.line.place + 2 if way == UP else self.line.place - 2
        return pltpu.make_async_remote_copy(
            src_ref=self.way_out[part].at[way, spot],
            dst_ref=self.way_in[part].at[way, spot],
            send_sem=self.sends.at[way, spot, part],
            recv_sem=self.recvs.at[way, spot, part],
            device_id={"dp": there},
            device_id_type=MESH,
        )

    def start(self):
        self.load_own()
        each(self.line.size, self.send_pair)

    def own_copy(self, part, spot):
        return pltpu.make_async_copy(
            self.terms[part].at[2 * spot + self.line.side],
            self.own[part].at[spot],
            self.own_sems.at[part, spot],
        )

    def load_own(self):
        def load(spot):
            for part in range(len(self.terms)):
                self.own_copy(part, spot).start()

        each(self.line.size, load)

    def wait_own(self):
        def wait(spot):
            for part in range(len(self.terms)):
                self.own_copy(part, spot).wait()

        each(self.line.size, wait)

    def send_pair(self, step):
        line = self.line
        far = line.size - 1 - step

        @pl.when(line.at + far < line.size)
        def _():
            for part in range(len(self.terms)):
                self.pair_copy(part, line.at + far).start()

        @pl.when((line.at - far >= 0) & (far > 0))
        def _():
            for part in range(len(self.terms)):
                self.pair_copy(part, line.at - far).start()

    def pair_sum(self, part, spot):
        own = self.own[part][spot].astype(jnp.float32)
        return own + self.pair_in[part][spot].astype(jnp.float32)

    def pass_on(self, way, spot, more):
        for part in range(len(self.terms)):
            self.pair_copy(part, spot).wait_recv()
            self.way_out[part][way, spot] = self.pair_sum(part, spot).astype(jnp.bfloat16)

            @pl.when(more)
            def _(part=part):
                self.way_copy(part, way, spot).wait_recv()
                self.way_out[part][way, spot] = (
                    self.pair_sum(part, spot) + self.way_in[part][way, spot].astype(jnp.float32)
                ).astype(jnp.bfloat16)

            self.way_copy(part, way, spot).start()

    def tick(self, step):
        line = self.line
        far = line.size - 1 - step

        @pl.when(line.at + far < line.size)
        def _():
            self.pass_on(UP, line.at + far, line.has_down)

        @pl.when(line.at - far >= 0)
        def _():
            self.pass_on(DOWN, line.at - far, line.has_up)

    def finish(self):
        line = self.line
        spot = line.at
        for part in range(len(self.terms)):
            self.pair_copy(part, spot).wait_recv()
            self.totals[part][...] = self.pair_sum(part, spot)
        for way, can in ((UP, line.has_down), (DOWN, line.has_up)):

            @pl.when(can)
            def _(way=way):
                for part in range(len(self.terms)):
                    self.way_copy(part, way, spot).wait_recv()
                    self.totals[part][...] += self.way_in[part][way, spot].astype(jnp.float32)

        def close(spot):
            for part in range(len(self.terms)):
                self.pair_copy(part, spot).wait_send()
            for way, passed in ((UP, spot > line.at), (DOWN, spot < line.at)):

                @pl.when(passed)
                def _(way=way):
                    for part in range(len(self.terms)):
                        self.way_copy(part, way, spot).wait_send()

        each(line.size, close)


def run_ticks(task, first, last):
    if task is not None:
        for step in range(first, last):
            task.tick(step)


def head_slice(matrix, head):
    return matrix[:, head * HEAD_DIM : (head + 1) * HEAD_DIM]


def soft_rows(queries, keys_in):
    scores = dot_nt(queries, keys_in) * (HEAD_DIM ** (-0.5))
    exponent = jnp.exp(scores - jnp.max(scores, axis=-1, keepdims=True))
    return exponent / jnp.sum(exponent, axis=-1, keepdims=True)


def forward_kernel(
    layer_idx,
    res_ref,
    mod_ref,
    vec_ref,
    qkv_bias_ref,
    up_bias_ref,
    w_qkv_far,
    w_up_far,
    w_out_far,
    *rest,
):
    with_gather = len(rest) > 31
    shards, rest = (rest[:3], rest[3:]) if with_gather else ((), rest)
    res_out, kept = rest[0], rest[1:9]
    wholes, rest = (rest[9:12], rest[12:]) if with_gather else ((), rest[9:])
    rows_a, qkv_out, mixed_out, branch_out, mid_out, rows_m, upper_out, down_out = rest[:8]
    w_qkv_ref, w_up_ref, w_out_ref = rest[8:11]
    (
        part_a,
        near_a,
        far_out_a,
        far_in_a,
        part_m,
        near_m,
        far_out_m,
        far_in_m,
        sends,
        recvs,
        move_sems,
    ) = rest[11:22]
    group_width = w_qkv_ref.shape[1] // 3
    w_attn_ref, w_down_ref = w_out_ref.at[0:group_width, :], w_out_ref.at[group_width:, :]
    far = (w_qkv_far, w_out_far, w_up_far)
    pairs = list(zip(far, (w_qkv_ref, w_out_ref, w_up_ref))) + list(zip(rest[:8], kept))
    moves = Moves(pairs, move_sems)
    moves.start(0, 1, 2)
    images = res_ref.shape[0]
    gather, last_step = None, 0
    if with_gather:
        line = Line()
        greet(line)
        own = [shard.at[layer_idx + 1] for shard in shards]
        gather = Gather(line, own, wholes, *rest[22:])
        last_step = line.size
    else:
        greet(None)
    spread_a = Spread(rows_a, sends.at[0], recvs.at[0])
    spread_m = Spread(rows_m, sends.at[1], recvs.at[1])
    collect_a = Collect(part_a, near_a, far_out_a, far_in_a, sends.at[2], recvs.at[2])
    collect_m = Collect(part_m, near_m, far_out_m, far_in_m, sends.at[3], recvs.at[3])

    def mod_row(image, piece):
        return mod_ref[image, pl.ds(piece, 1), :]

    def start_norm(image):
        normed, _ = norm_parts(res_ref[image])
        normed = normed * (1.0 + mod_row(image, 1)) + mod_row(image, 0)
        spread_a.put(image, normed.astype(jnp.bfloat16))

    def attend(image):
        spread_a.wait(image)
        rows = rows_a[image]
        projected = dot_nn(rows, w_qkv_ref[...]) + qkv_bias_ref[...]
        qkv = projected.astype(jnp.bfloat16)
        qkv_out[image] = qkv
        heads = []
        for head in range(group_width // HEAD_DIM):
            probs = soft_rows(
                head_slice(qkv[:, :group_width], head),
                head_slice(qkv[:, group_width : 2 * group_width], head),
            )
            heads.append(
                dot_nn(probs.astype(jnp.bfloat16), head_slice(qkv[:, 2 * group_width :], head))
            )
        mixed = jnp.concatenate(heads, axis=1).astype(jnp.bfloat16)
        mixed_out[image] = mixed
        collect_a.put(image, dot_nn(mixed, w_attn_ref[...]))

    def middle(image):
        branch = collect_a.take(image) + vec_ref[0:1, :]
        branch_out[image] = branch
        mid = res_ref[image] + mod_row(image, 2) * branch
        mid_out[image] = mid
        normed, _ = norm_parts(mid)
        normed = normed * (1.0 + mod_row(image, 4)) + mod_row(image, 3)
        spread_m.put(image, normed.astype(jnp.bfloat16))

    def feed(image):
        spread_m.wait(image)
        upper = dot_nn(rows_m[image], w_up_ref[...]) + up_bias_ref[...]
        upper_out[image] = upper
        collect_m.put(image, dot_nn(gelu_tanh(upper).astype(jnp.bfloat16), w_down_ref[...]))

    def finish(image):
        down = collect_m.take(image) + vec_ref[1:2, :]
        down_out[image] = down
        res_out[image] = mid_out[image] + mod_row(image, 5) * down

    def close(image):
        spread_a.close(image)
        spread_m.close(image)
        collect_a.close(image)
        collect_m.close(image)

    if with_gather:
        gather.start()
    each(images, start_norm)
    each(images, spread_a.forward)
    moves.wait(0, 1)
    each(images, attend)
    moves.start(3, 4, 5)
    run_ticks(gather, 1, min(2, last_step))
    each(images, collect_a.forward)
    each(images, middle)
    moves.start(6, 7)
    each(images, spread_m.forward)
    run_ticks(gather, 2, min(3, last_step))
    moves.wait(2)
    each(images, feed)
    moves.start(8, 9)
    run_ticks(gather, 3, min(4, last_step))
    each(images, collect_m.forward)
    each(images, finish)
    moves.start(10)
    each(images, close)
    moves.wait(*range(3, 11))
    if with_gather:
        each(max(last_step - 4, 0), lambda step: gather.tick(step + 4))
        gather.finish()


def forward_layer(
    residual, mod_vec, vec_bias, qkv_bias, up_bias, w_qkv, w_up, w_out, shards, layer_idx
):
    images, count, _ = residual.shape
    tokens = 4 * count
    low, full = jnp.bfloat16, jnp.float32
    shapes = [
        ((images, count, D), full),
        ((images, tokens, D), low),
        ((images, tokens, w_qkv.shape[1]), low),
        ((images, tokens, w_qkv.shape[1] // 3), low),
        ((images, count, D), full),
        ((images, count, D), full),
        ((images, tokens, D), low),
        ((images, tokens, w_up.shape[1]), full),
        ((images, count, D), full),
    ]
    scratch = [
        pltpu.SemaphoreType.DMA((4, images, 3)),
        pltpu.SemaphoreType.DMA((4, images, 3)),
        pltpu.SemaphoreType.DMA((11,)),
    ]
    near = [pltpu.VMEM(*shape) for shape in shapes[1:]]
    near += [pltpu.VMEM(weight.shape, low) for weight in (w_qkv, w_up, w_out)]
    if shards:
        dp_size = lax.axis_size("dp")
        shapes += [((dp_size,) + shard.shape[1:], low) for shard in shards]
        scratch += [
            pltpu.SemaphoreType.DMA((3, dp_size // 2, 3)),
            pltpu.SemaphoreType.DMA((3, dp_size // 2, 3)),
            pltpu.SemaphoreType.DMA((3,)),
        ]
    return pl.pallas_call(
        functools.partial(forward_kernel, layer_idx),
        out_shape=[jax.ShapeDtypeStruct(*shape) for shape in shapes],
        in_specs=[pl.BlockSpec(memory_space=pltpu.VMEM)] * 5
        + [pl.BlockSpec(memory_space=pl.ANY)] * (3 + len(shards)),
        out_specs=[pl.BlockSpec(memory_space=pltpu.VMEM)]
        + [pl.BlockSpec(memory_space=pl.ANY)] * (len(shapes) - 1),
        scratch_shapes=near
        + collect_scratch(images, tokens)
        + collect_scratch(images, tokens)
        + scratch,
        compiler_params=pltpu.CompilerParams(
            collective_id=16 + layer_idx, has_side_effects=True, vmem_limit_bytes=ACT_VMEM
        ),
        cost_estimate=pl.CostEstimate(
            flops=30 * 10**9, bytes_accessed=15 * 2**20, transcendentals=0
        ),
        name="block_forward",
    )(residual, mod_vec, vec_bias, qkv_bias, up_bias, w_qkv, w_up, w_out, *shards)


def flat(ref):
    value = ref[...]
    return value.reshape(-1, value.shape[-1])


def forward_all_kernel(
    res_ref,
    mod_ref,
    vec_ref,
    qkv_bias_ref,
    up_bias_ref,
    qkv_far,
    up_far,
    out_far,
    *rest,
):
    shards, res_out, kept_far, whole_far = rest[0:3], rest[3], rest[4:13], rest[13:16]
    kept, rest = rest[16:25], rest[25:]
    res_all, rows_a_all, qkv_all, mixed_all, branch_all, mid_all, rows_m_all, upper_all, down_all = kept
    w_qkv_all, w_up_all, w_blocks_all, w_out_all = rest[0:4]
    part_a, near_a, far_out_a, far_in_a, part_m, near_m, far_out_m, far_in_m = rest[4:12]
    sends, recvs, keep_sems, load_sems, whole_sems, gather_sends, gather_recvs, local_sems = rest[12:]
    images = res_ref.shape[0]
    group_width = w_qkv_all.shape[-1] // 3
    line = Line()
    last_step = line.size
    loads = Moves(
        [(qkv_far, w_qkv_all.at[0]), (out_far, w_blocks_all.at[0]), (up_far, w_up_all.at[0])],
        load_sems,
    )
    loads.start(0, 1, 2)
    greet(line)
    gathers = [None]
    for layer_idx in range(1, LAYERS):
        gathers.append(
            Gather(
                line,
                [shard.at[layer_idx] for shard in shards],
                [whole.at[layer_idx] for whole in (w_qkv_all, w_up_all, w_blocks_all)],
                gather_sends.at[layer_idx],
                gather_recvs.at[layer_idx],
                local_sems.at[layer_idx],
            )
        )
    gathers.append(None)

    def join_blocks(layer_idx):
        rows = w_blocks_all.shape[2]
        for pair in range(w_blocks_all.shape[1] // 2):
            halves = [
                w_blocks_all[layer_idx, 2 * pair + side].astype(jnp.float32) for side in range(2)
            ]
            w_out_all[layer_idx, 2 * rows * pair : 2 * rows * (pair + 1), :] = jnp.concatenate(
                halves, axis=0
            ).astype(jnp.bfloat16)

    def mod_row(layer_idx, image, piece):
        return mod_ref[layer_idx, image, pl.ds(piece, 1), :]

    for layer_idx in range(LAYERS):
        res, rows_a, qkv_out, mixed_out, branch_out, mid_out, rows_m, upper_out, down_out = [
            ref.at[layer_idx] for ref in kept
        ]
        w_qkv, w_up, w_out = w_qkv_all.at[layer_idx], w_up_all.at[layer_idx], w_out_all.at[layer_idx]
        w_attn, w_down = w_out.at[0:group_width, :], w_out.at[group_width:, :]
        spread_a = Spread(rows_a, sends.at[layer_idx, 0], recvs.at[layer_idx, 0])
        spread_m = Spread(rows_m, sends.at[layer_idx, 1], recvs.at[layer_idx, 1])
        collect_a = Collect(
            part_a,
            near_a.at[layer_idx],
            far_out_a.at[layer_idx],
            far_in_a.at[layer_idx],
            sends.at[layer_idx, 2],
            recvs.at[layer_idx, 2],
        )
        collect_m = Collect(
            part_m,
            near_m.at[layer_idx],
            far_out_m.at[layer_idx],
            far_in_m.at[layer_idx],
            sends.at[layer_idx, 3],
            recvs.at[layer_idx, 3],
        )
        keep = Moves(
            [(ref.at[layer_idx], far.at[layer_idx]) for ref, far in zip(kept, kept_far)],
            keep_sems.at[layer_idx],
        )
        keep_whole = Moves(
            [
                (ref.at[layer_idx], far.at[layer_idx])
                for ref, far in zip((w_qkv_all, w_up_all, w_out_all), whole_far)
            ],
            whole_sems.at[layer_idx],
        )
        gather = gathers[layer_idx + 1]

        def start_norm(image, at, values, target):
            normed, _ = norm_parts(values)
            normed = normed * (1.0 + mod_row(at, image, 1)) + mod_row(at, image, 0)
            target.put(image, normed.astype(jnp.bfloat16))

        def first_norm(image, res=res, spread_a=spread_a):
            res[image] = res_ref[image]
            start_norm(image, 0, res_ref[image], spread_a)

        def attend(image):
            spread_a.wait(image)
            projected = dot_nn(rows_a[image], flat(w_qkv)) + qkv_bias_ref[layer_idx]
            qkv = projected.astype(jnp.bfloat16)
            qkv_out[image] = qkv
            heads = []
            for head in range(group_width // HEAD_DIM):
                probs = soft_rows(
                    head_slice(qkv[:, :group_width], head),
                    head_slice(qkv[:, group_width : 2 * group_width], head),
                )
                heads.append(
                    dot_nn(probs.astype(jnp.bfloat16), head_slice(qkv[:, 2 * group_width :], head))
                )
            mixed = jnp.concatenate(heads, axis=1).astype(jnp.bfloat16)
            mixed_out[image] = mixed
            collect_a.put(image, dot_nn(mixed, w_attn[...]))

        def middle(image):
            branch = collect_a.take(image) + vec_ref[layer_idx, 0:1, :]
            branch_out[image] = branch
            mid = res[image] + mod_row(layer_idx, image, 2) * branch
            mid_out[image] = mid
            normed, _ = norm_parts(mid)
            normed = normed * (1.0 + mod_row(layer_idx, image, 4)) + mod_row(layer_idx, image, 3)
            spread_m.put(image, normed.astype(jnp.bfloat16))

        def feed(image):
            spread_m.wait(image)
            upper = dot_nn(rows_m[image], flat(w_up)) + up_bias_ref[layer_idx]
            upper_out[image] = upper
            collect_m.put(image, dot_nn(gelu_tanh(upper).astype(jnp.bfloat16), w_down[...]))

        def finish(image):
            down = collect_m.take(image) + vec_ref[layer_idx, 1:2, :]
            down_out[image] = down
            value = mid_out[image] + mod_row(layer_idx, image, 5) * down
            if layer_idx + 1 < LAYERS:
                res_all[layer_idx + 1, image] = value
                following = Spread(
                    rows_a_all.at[layer_idx + 1],
                    sends.at[layer_idx + 1, 0],
                    recvs.at[layer_idx + 1, 0],
                )
                start_norm(image, layer_idx + 1, value, following)
            else:
                res_out[image] = value

        def close(image):
            spread_a.close(image)
            spread_m.close(image)
            collect_a.close(image)
            collect_m.close(image)

        if layer_idx == 0:
            gather.start()
            each(images, first_norm)
        each(images, spread_a.forward)
        if layer_idx == 0:
            loads.wait(0, 1)
            join_blocks(0)
        each(images, attend)
        keep.start(0, 1, 2, 3)
        run_ticks(gather, 1, min(2, last_step))
        each(images, collect_a.forward)
        each(images, middle)
        keep.start(4, 5)
        each(images, spread_m.forward)
        run_ticks(gather, 2, min(3, last_step))
        if layer_idx == 0:
            loads.wait(2)
        each(images, feed)
        keep.start(6, 7)
        run_ticks(gather, 3, min(4, last_step))
        each(images, collect_m.forward)
        each(images, finish)
        keep.start(8)
        keep_whole.start(0, 1, 2)
        each(images, close)
        if gather is not None:
            each(max(last_step - 4, 0), lambda step, gather=gather: gather.tick(step + 4))
            if gathers[layer_idx + 2] is not None:
                gathers[layer_idx + 2].start()
            gather.finish()
            join_blocks(layer_idx + 1)
        keep.wait(*range(9))
        keep_whole.wait(0, 1, 2)


def forward_all(residual, mod_vecs, vec_bias, qkv_bias, up_bias, wholes, shards):
    images, count, _ = residual.shape
    tokens = 4 * count
    low, full = jnp.bfloat16, jnp.float32
    dp_size = lax.axis_size("dp")
    qkv_width, units = wholes[0].shape[-1], wholes[1].shape[-1]
    own = (images, count, D)
    kept = [
        (own, full),
        ((images, tokens, D), low),
        ((images, tokens, qkv_width), low),
        ((images, tokens, qkv_width // 3), low),
        (own, full),
        (own, full),
        ((images, tokens, D), low),
        ((images, tokens, units), full),
        (own, full),
    ]
    kept = [((LAYERS,) + shape, kind) for shape, kind in kept]
    out_rows = wholes[2].shape[0] * wholes[2].shape[1]
    matrices = [
        ((LAYERS,) + wholes[0].shape, low),
        ((LAYERS,) + wholes[1].shape, low),
        ((LAYERS, out_rows, D), low),
    ]
    shapes = [(own, full)] + kept + matrices
    collect = [
        pltpu.VMEM((images, tokens, D), low),
        pltpu.VMEM((LAYERS, images, 2, count, D), low),
        pltpu.VMEM((LAYERS, images, count, D), low),
        pltpu.VMEM((LAYERS, images, count, D), low),
    ]
    return pl.pallas_call(
        forward_all_kernel,
        out_shape=[jax.ShapeDtypeStruct(*shape) for shape in shapes],
        in_specs=[pl.BlockSpec(memory_space=pltpu.VMEM)] * 5
        + [pl.BlockSpec(memory_space=pl.ANY)] * 6,
        out_specs=[pl.BlockSpec(memory_space=pltpu.VMEM)]
        + [pl.BlockSpec(memory_space=pl.ANY)] * (len(shapes) - 1),
        scratch_shapes=[pltpu.VMEM(*shape) for shape in kept]
        + [
            pltpu.VMEM(*matrices[0]),
            pltpu.VMEM(*matrices[1]),
            pltpu.VMEM((LAYERS,) + wholes[2].shape, low),
            pltpu.VMEM(*matrices[2]),
        ]
        + collect
        + collect
        + [
            pltpu.SemaphoreType.DMA((LAYERS, 4, images, 3)),
            pltpu.SemaphoreType.DMA((LAYERS, 4, images, 3)),
            pltpu.SemaphoreType.DMA((LAYERS, 9)),
            pltpu.SemaphoreType.DMA((3,)),
            pltpu.SemaphoreType.DMA((LAYERS, 3)),
            pltpu.SemaphoreType.DMA((LAYERS, 3, dp_size // 2, 3)),
            pltpu.SemaphoreType.DMA((LAYERS, 3, dp_size // 2, 3)),
            pltpu.SemaphoreType.DMA((LAYERS, 3)),
        ],
        compiler_params=pltpu.CompilerParams(
            collective_id=24, has_side_effects=True, vmem_limit_bytes=ACT_VMEM
        ),
        name="blocks_forward",
    )(residual, mod_vecs, vec_bias, qkv_bias, up_bias, *wholes, *shards)


def gelu_slope(values):
    root = math.sqrt(2.0 / math.pi)
    square = values * values
    tanh = jnp.tanh(root * (values + 0.044715 * values * square))
    half = 0.5 * (1.0 + tanh)
    slope = half + 0.5 * values * (1.0 - tanh * tanh) * root * (1.0 + 3.0 * 0.044715 * square)
    return values * half, slope


def norm_pull(values, scale_row, d_normed):
    normed, rstd = norm_parts(values)
    d_shift = jnp.sum(d_normed, axis=0, keepdims=True)
    d_scale = jnp.sum(d_normed * normed, axis=0, keepdims=True)
    inner = d_normed * (1.0 + scale_row)
    mean_one = jnp.mean(inner, axis=-1, keepdims=True)
    mean_two = jnp.mean(inner * normed, axis=-1, keepdims=True)
    return (inner - mean_one - normed * mean_two) * rstd, d_shift, d_scale


def backward_kernel(layer_idx, d_res_ref, mod_ref, *rest):
    kept, rest = rest[:12], rest[12:]
    if layer_idx is not None:
        kept = [ref.at[layer_idx] for ref in kept]
    with_reduce = len(rest) > 40
    terms, rest = (rest[:3], rest[3:]) if with_reduce else ((), rest)
    d_res_out, d_far, (d_mod, d_vec, d_qkv_bias, d_up_bias) = rest[0], rest[1:4], rest[4:8]
    totals, square_out = (rest[8:11], rest[11]) if with_reduce else ((), None)
    rest = rest[12:] if with_reduce else rest[8:]
    (
        res_ref,
        rows_a,
        qkv_ref,
        mixed_ref,
        branch_ref,
        mid_ref,
        rows_m,
        upper_ref,
        down_ref,
        w_qkv_ref,
        w_up_ref,
        w_out_ref,
        d_w_qkv,
        d_w_up,
        d_out,
    ) = rest[:15]
    (
        d_mid,
        d_rows_m,
        d_rows_a,
        act_low,
        d_upper,
        d_qkv,
        part_a,
        near_a,
        far_out_a,
        far_in_a,
        part_m,
        near_m,
        far_out_m,
        far_in_m,
        sends,
        recvs,
        move_sems,
    ) = rest[15:32]
    group_width = w_qkv_ref.shape[-1] // 3
    w_attn_ref, w_down_ref = w_out_ref.at[0:group_width, :], w_out_ref.at[group_width:, :]
    pairs = list(zip(kept, rest[:12])) + list(zip(rest[12:15], d_far))
    moves = Moves(pairs, move_sems)
    moves.start(8, 11, 7, 10, 6, 5, 4, 2, 9, 3, 1, 0)
    images = res_ref.shape[0]
    tokens = rows_a.shape[1]
    qkv_width = 3 * group_width
    units = w_up_ref.shape[-1]
    reduce, last_step = None, 0
    if with_reduce:
        line = Line()
        greet(line)
        own, pair_in, way_in, way_out = rest[32:35], rest[35:38], rest[38:41], rest[41:44]
        reduce = Reduce(line, terms, totals, own, pair_in, way_in, way_out, *rest[44:])
        last_step = line.size
    else:
        greet(None)
    spread_m = Spread(d_rows_m, sends.at[0], recvs.at[0])
    spread_a = Spread(d_rows_a, sends.at[1], recvs.at[1])
    collect_m = Collect(part_m, near_m, far_out_m, far_in_m, sends.at[2], recvs.at[2])
    collect_a = Collect(part_a, near_a, far_out_a, far_in_a, sends.at[3], recvs.at[3])
    d_vec[...] = jnp.zeros_like(d_vec)
    d_qkv_bias[...] = jnp.zeros_like(d_qkv_bias)
    d_up_bias[...] = jnp.zeros_like(d_up_bias)

    def mod_row(image, piece):
        return mod_ref[image, pl.ds(piece, 1), :]

    def start_down(image):
        d_res = d_res_ref[image]
        d_mod[image, pl.ds(5, 1), :] = jnp.sum(d_res * down_ref[image], axis=0, keepdims=True)
        d_down = d_res * mod_row(image, 5)
        d_vec[1:2, :] += jnp.sum(d_down, axis=0, keepdims=True)
        spread_m.put(image, d_down.astype(jnp.bfloat16))

    def feed(image):
        spread_m.wait(image)
        d_act = dot_nt(d_rows_m[image], w_down_ref[...])
        act, slope = gelu_slope(upper_ref[image])
        act_low[image] = act.astype(jnp.bfloat16)
        d_up = d_act * slope
        d_up_bias[...] += jnp.sum(d_up, axis=0, keepdims=True)
        d_up_low = d_up.astype(jnp.bfloat16)
        d_upper[image] = d_up_low
        collect_m.put(image, dot_nt(d_up_low, flat(w_up_ref)))

    def rows_of(ref, width):
        return ref[...].reshape(images * tokens, width)

    def feed_weights():
        tile = 256

        def step(index, carry):
            at = pl.ds(pl.multiple_of(index * tile, tile), tile)
            grad = dot_tn(
                act_low[:, :, at].reshape(images * tokens, tile), rows_of(d_rows_m, D)
            )
            d_out[pl.ds(pl.multiple_of(group_width + index * tile, 64), tile), :] = grad.astype(
                jnp.bfloat16
            )
            grad = dot_tn(
                rows_m[:, :, at].reshape(images * tokens, tile), rows_of(d_upper, units)
            )
            d_w_up[pl.ds(pl.multiple_of(index * tile, tile), tile), :] = grad.astype(jnp.bfloat16)
            return carry

        lax.fori_loop(0, units // tile, step, 0)

    def middle(image):
        d_value, d_shift, d_scale = norm_pull(
            mid_ref[image], mod_row(image, 4), collect_m.take(image)
        )
        d_mod[image, pl.ds(3, 1), :] = d_shift
        d_mod[image, pl.ds(4, 1), :] = d_scale
        d_value = d_res_ref[image] + d_value
        d_mid[image] = d_value
        d_mod[image, pl.ds(2, 1), :] = jnp.sum(d_value * branch_ref[image], axis=0, keepdims=True)
        d_branch = d_value * mod_row(image, 2)
        d_vec[0:1, :] += jnp.sum(d_branch, axis=0, keepdims=True)
        spread_a.put(image, d_branch.astype(jnp.bfloat16))

    def attend(image):
        spread_a.wait(image)
        d_mixed = dot_nt(d_rows_a[image], w_attn_ref[...]).astype(jnp.bfloat16)
        qkv = qkv_ref[image]
        d_queries, d_keys, d_values = [], [], []
        scale_dot = HEAD_DIM ** (-0.5)
        for head in range(group_width // HEAD_DIM):
            queries = head_slice(qkv[:, :group_width], head)
            keys_in = head_slice(qkv[:, group_width : 2 * group_width], head)
            values_in = head_slice(qkv[:, 2 * group_width :], head)
            d_head = head_slice(d_mixed, head)
            probs = soft_rows(queries, keys_in)
            d_probs = dot_nt(d_head, values_in)
            d_values.append(dot_tn(probs.astype(jnp.bfloat16), d_head))
            inner = jnp.sum(probs * d_probs, axis=-1, keepdims=True)
            d_scores = (probs * (d_probs - inner)).astype(jnp.bfloat16)
            d_queries.append(dot_nn(d_scores, keys_in) * scale_dot)
            d_keys.append(dot_tn(d_scores, queries) * scale_dot)
        joined = jnp.concatenate(d_queries + d_keys + d_values, axis=1)
        d_qkv_bias[...] += jnp.sum(joined, axis=0, keepdims=True)
        joined = joined.astype(jnp.bfloat16)
        d_qkv[image] = joined
        collect_a.put(image, dot_nt(joined, flat(w_qkv_ref)))

    def attend_weights():
        d_out[0:group_width, :] = dot_tn(
            rows_of(mixed_ref, group_width), rows_of(d_rows_a, D)
        ).astype(jnp.bfloat16)
        tile = 256

        def step(index, carry):
            at = pl.ds(pl.multiple_of(index * tile, tile), tile)
            grad = dot_tn(
                rows_a[:, :, at].reshape(images * tokens, tile), rows_of(d_qkv, qkv_width)
            )
            d_w_qkv[at, :] = grad.astype(jnp.bfloat16)
            return carry

        lax.fori_loop(0, D // tile, step, 0)

    def finish(image):
        d_value, d_shift, d_scale = norm_pull(
            res_ref[image], mod_row(image, 1), collect_a.take(image)
        )
        d_mod[image, pl.ds(0, 1), :] = d_shift
        d_mod[image, pl.ds(1, 1), :] = d_scale
        d_res_out[image] = d_mid[image] + d_value

    def close(image):
        spread_a.close(image)
        spread_m.close(image)
        collect_a.close(image)
        collect_m.close(image)

    if with_reduce:
        reduce.start()
    moves.wait(8)
    each(images, start_down)
    each(images, spread_m.forward)
    moves.wait(11, 7, 10)
    each(images, feed)
    if with_reduce:
        reduce.wait_own()
    run_ticks(reduce, 0, min(1, last_step - 1))
    each(images, collect_m.forward)
    moves.wait(6)
    feed_weights()
    moves.start(13)
    run_ticks(reduce, 1, min(2, last_step - 1))
    moves.wait(5, 4)
    each(images, middle)
    each(images, spread_a.forward)
    moves.wait(2, 9)
    each(images, attend)
    each(images, collect_a.forward)
    run_ticks(reduce, 2, min(3, last_step - 1))
    moves.wait(3, 1)
    attend_weights()
    moves.start(12, 14)
    moves.wait(0)
    each(images, finish)
    each(images, close)
    if with_reduce:
        each(max(last_step - 4, 0), lambda step: reduce.tick(step + 3))
        reduce.finish()
        square_out[...] = jnp.broadcast_to(
            sum(square_sum(total[...]) for total in totals), square_out.shape
        )
    moves.wait(12, 13, 14)


def backward_layer(d_residual, mod_vec, saved, weights, terms, layer_idx, stacked):
    images, count, _ = d_residual.shape
    tokens = 4 * count
    low, full = jnp.bfloat16, jnp.float32
    w_qkv, w_up, w_out = weights
    group_width, units = w_qkv.shape[-1] // 3, w_up.shape[-1]
    shapes = [
        ((images, count, D), full),
        ((D, 3 * group_width), low),
        ((D, units), low),
        ((group_width + units, D), low),
        ((images, 6, D), full),
        ((2, D), full),
        ((1, 3 * group_width), full),
        ((1, units), full),
    ]
    scratch = [
        pltpu.SemaphoreType.DMA((4, images, 3)),
        pltpu.SemaphoreType.DMA((4, images, 3)),
        pltpu.SemaphoreType.DMA((15,)),
    ]
    near = [
        pltpu.VMEM(kept.shape[1:] if stacked else kept.shape, kept.dtype)
        for kept in tuple(saved) + tuple(weights)
    ]
    near += [pltpu.VMEM(*shape) for shape in shapes[1:4]]
    if terms:
        spots = lax.axis_size("dp") // 2
        blocks = [term.shape[1:] for term in terms]
        shapes += [(block, full) for block in blocks] + [((8, 128), full)]
        scratch += [pltpu.VMEM((spots,) + block, low) for block in blocks]
        scratch += [pltpu.VMEM((spots,) + block, low) for block in blocks]
        scratch += [pltpu.VMEM((2, spots) + block, low) for block in blocks]
        scratch += [pltpu.VMEM((2, spots) + block, low) for block in blocks]
        scratch += [
            pltpu.SemaphoreType.DMA((3, spots, 3)),
            pltpu.SemaphoreType.DMA((3, spots, 3)),
            pltpu.SemaphoreType.DMA((3, spots)),
        ]
    return pl.pallas_call(
        functools.partial(backward_kernel, layer_idx if stacked else None),
        out_shape=[jax.ShapeDtypeStruct(*shape) for shape in shapes],
        in_specs=[pl.BlockSpec(memory_space=pltpu.VMEM)] * 2
        + [pl.BlockSpec(memory_space=pl.ANY)] * (12 + len(terms)),
        out_specs=[pl.BlockSpec(memory_space=pltpu.VMEM)]
        + [pl.BlockSpec(memory_space=pl.ANY)] * 3
        + [pl.BlockSpec(memory_space=pltpu.VMEM)] * (len(shapes) - 4),
        scratch_shapes=near
        + [
            pltpu.VMEM((images, count, D), full),
            pltpu.VMEM((images, tokens, D), low),
            pltpu.VMEM((images, tokens, D), low),
            pltpu.VMEM((images, tokens, units), low),
            pltpu.VMEM((images, tokens, units), low),
            pltpu.VMEM((images, tokens, 3 * group_width), low),
        ]
        + collect_scratch(images, tokens)
        + collect_scratch(images, tokens)
        + scratch,
        compiler_params=pltpu.CompilerParams(
            collective_id=20 + layer_idx if stacked else (21 if terms else 23), has_side_effects=True, vmem_limit_bytes=ACT_VMEM
        ),
        cost_estimate=pl.CostEstimate(
            flops=60 * 10**9, bytes_accessed=25 * 2**20, transcendentals=0
        ),
        name="block_backward",
    )(d_residual, mod_vec, *saved, *weights, *terms)


def dense_nt(left_op, right_op):
    return lax.dot_general(
        left_op,
        right_op,
        (((1,), (1,)), ((), ())),
        precision=PRECISE,
        preferred_element_type=jnp.float32,
    )


def dense_tn(left_op, right_op):
    return lax.dot_general(
        left_op,
        right_op,
        (((0,), (0,)), ((), ())),
        precision=PRECISE,
        preferred_element_type=jnp.float32,
    )


def chosen(shape, rule, kind):
    row = lax.broadcasted_iota(jnp.int32, shape, 0)
    col = lax.broadcasted_iota(jnp.int32, shape, 1)
    return jnp.where(rule(row, col), 1.0, 0.0).astype(kind)


def fold(values):
    groups = values.shape[-2] // 8
    pieces = [values[..., 8 * at : 8 * at + 8, :] for at in range(groups)]
    used = groups * values.shape[-1]
    if used % 128:
        pieces.append(jnp.zeros(values.shape[:-2] + (8, 128 - used % 128), values.dtype))
    return jnp.concatenate(pieces, axis=-1)


def folded_lanes(cols, count):
    return -(-(cols // 8 * count) // 128) * 128


def unfold_all(values, cols, count):
    ordered = [
        values[tensor_at, dp_at]
        for dp_at in range(values.shape[1])
        for tensor_at in range(values.shape[0])
    ]
    return jnp.concatenate([unfold(value, cols, count) for value in ordered], axis=0)


def unfold(values, cols, count):
    pieces = [values[..., at * count : (at + 1) * count] for at in range(cols // 8)]
    return jnp.concatenate(pieces, axis=-2)


def slots_of(images):
    return -(-LAYERS * images // 16) * 16


def head_kernel(
    images,
    small_ref,
    feats_ref,
    table_ref,
    time_ref,
    second_ref,
    shift_ref,
    scale_ref,
    bias_ref,
    mod_ref,
    *rest,
):
    shards = rest[0:3]
    (
        small_all,
        feats_out,
        pre_time_out,
        hidden_out,
        pre_signal_out,
        signal_out,
        final_all,
        mod_all,
    ) = rest[3:11]
    wholes = rest[11:14]
    (
        feats_all,
        hidden_own,
        hidden_dp,
        hidden_all,
        signal_own,
        signal_dp,
        signal_all,
        final_own,
        final_dp,
        mod_part,
        mod_in,
        mod_own,
        small_dp,
    ) = rest[14:27]
    crowds = [rest[27 + 3 * index : 30 + 3 * index] for index in range(11)]
    gather_sems = rest[60:]
    dp_size = lax.axis_size("dp")
    tensor_size = lax.axis_size("tensor")
    dp_rank = lax.axis_index("dp")
    images_all = images * dp_size
    slots = mod_own.shape[0]
    greet_groups("dp", "tensor")
    gather = Gather(Line(), [shard.at[0] for shard in shards], wholes, *gather_sems)
    feats = Crowd("dp", lambda place: feats_ref, feats_all, *crowds[0])
    mod_sum = Crowd("dp", lambda place: mod_part.at[place], mod_in, *crowds[1])
    mod_spread = Crowd("tensor", lambda place: mod_own, mod_all, *crowds[2])
    small = Relay(lambda place: small_ref, small_dp, small_all, *crowds[3:5])
    hidden = Relay(lambda place: hidden_own, hidden_dp, hidden_all, *crowds[5:7])
    signal = Relay(lambda place: signal_own, signal_dp, signal_all, *crowds[7:9])
    final = Relay(lambda place: final_own.at[place], final_dp, final_all, *crowds[9:11])
    line = gather.line
    first, last = line.at == 0, line.at == line.size - 1
    feats.start()
    gather.start()
    feats.wait()
    pick = chosen(
        (images_all, 8 * dp_size),
        lambda row, col: (row // images == col // 8) & (lax.rem(row, images) == lax.rem(col, 8)),
        jnp.float32,
    )
    feats_sum = dense(pick, feats_all[...].reshape(8 * dp_size, feats_all.shape[2]))
    feats_out[...] = feats_sum
    pre_time = dense_nt(time_ref[...], feats_sum[:, 0:FREQ]) + bias_ref[:, 1:2]
    pre_time_out[...] = pre_time
    hidden_own[...] = fold(jax.nn.silu(pre_time))
    hidden.start()
    class_lanes = -(-CLASSES // 128) * 128
    labels = jnp.round(feats_sum[:, FREQ : FREQ + 1]).astype(jnp.int32)
    lane = lax.broadcasted_iota(jnp.int32, (images_all, class_lanes), 1)
    onehot = jnp.where(lane == labels, 1.0, 0.0)
    class_part = dense_nt(table_ref[:, 0:class_lanes], onehot) + bias_ref[:, 2:3]
    small.start()
    hidden.hand_on()
    for way in (UP, DOWN):
        gather.hand_on(1, way)
    gather.hand_over(1, UP)
    gather.hand_over(1, DOWN, first)
    hidden.wait()
    cols = second_ref.shape[0]
    hidden_full = unfold_all(hidden_all[...], cols, images_all)
    hidden_out[...] = hidden_full
    pre_signal = dense(second_ref[...], hidden_full) + class_part
    pre_signal_out[...] = pre_signal
    signal_own[...] = fold(jax.nn.silu(pre_signal))
    signal.start()
    small.hand_on()
    signal.hand_on()
    for way in (UP, DOWN):
        gather.hand_on(2, way)
    gather.hand_over(1, DOWN, jnp.logical_not(first))
    gather.hand_over(2, UP, last)
    gather.hand_over(2, DOWN, first)
    signal.wait()
    signal_full = unfold_all(signal_all[...], cols, images_all)
    signal_out[...] = signal_full
    mod_rows = mod_ref.shape[1]
    own_rows = pl.ds(pl.multiple_of(dp_rank * mod_rows, 8), mod_rows)
    signal_low = signal_out[own_rows, :].astype(jnp.bfloat16)
    total = None
    for layer_idx in range(LAYERS):
        pick = chosen(
            (images_all, dp_size * slots),
            lambda row, col: (
                (row // images == col // slots)
                & (lax.rem(row, images) + layer_idx * images == lax.rem(col, slots))
            ),
            jnp.bfloat16,
        )
        placed = dot_nn(signal_low, pick).astype(jnp.bfloat16)
        term = dot_tn(placed, mod_ref[layer_idx])
        total = term if total is None else total + term
    mod_part[...] = total.reshape(mod_part.shape).astype(mod_part.dtype)
    mod_sum.start()
    gather.hand_over(2, UP, jnp.logical_not(last))
    gather.hand_over(2, DOWN, jnp.logical_not(first))
    finals = jnp.concatenate(
        [
            dense(shift_ref[...], signal_full) + bias_ref[:, 3:4],
            dense(scale_ref[...], signal_full) + bias_ref[:, 4:5],
            jnp.zeros((128 - 2 * shift_ref.shape[0], images_all), jnp.float32),
        ],
        axis=0,
    )
    pick = chosen(
        (8 * dp_size, images_all),
        lambda row, col: (row // 8 == col // images) & (lax.rem(row, 8) == lax.rem(col, images)),
        jnp.float32,
    )
    final_own[...] = dense_nt(pick, finals).reshape(final_own.shape)
    final.start()
    run_ticks(gather, 3, min(4, dp_size // 2))
    mod_sum.wait()
    mod_own[...] = jnp.sum(mod_in[...].astype(jnp.float32), axis=0)
    mod_spread.start()
    final.hand_on()
    each(max(dp_size // 2 - 4, 0), lambda step: gather.tick(step + 4))
    small.wait()
    final.wait()
    mod_spread.wait()
    gather.finish()


def head_call(small, feats, table, times, second, shift, scale, bias, mod_low, shards, images):
    dp_size, tensor_size = lax.axis_size("dp"), lax.axis_size("tensor")
    images_all = images * dp_size
    cols = table.shape[0]
    slots = slots_of(images)
    folded = folded_lanes(cols, images_all)
    full, low = jnp.float32, jnp.bfloat16
    shapes = [
        ((tensor_size, dp_size) + small.shape, full),
        ((images_all, feats.shape[1]), full),
        ((cols, images_all), full),
        ((D, images_all), full),
        ((cols, images_all), full),
        ((D, images_all), full),
        ((tensor_size, dp_size, 8, 128), full),
        ((tensor_size, slots, mod_low.shape[2]), full),
    ] + [((dp_size,) + shard.shape[1:], low) for shard in shards]
    scratch = [
        pltpu.VMEM((dp_size,) + feats.shape, full),
        pltpu.VMEM((8, folded), full),
        pltpu.VMEM((dp_size, 8, folded), full),
        pltpu.VMEM((tensor_size, dp_size, 8, folded), full),
        pltpu.VMEM((8, folded), full),
        pltpu.VMEM((dp_size, 8, folded), full),
        pltpu.VMEM((tensor_size, dp_size, 8, folded), full),
        pltpu.VMEM((dp_size, 8, 128), full),
        pltpu.VMEM((dp_size, 8, 128), full),
        pltpu.VMEM((dp_size, slots, mod_low.shape[2]), low),
        pltpu.VMEM((dp_size, slots, mod_low.shape[2]), low),
        pltpu.VMEM((slots, mod_low.shape[2]), full),
        pltpu.VMEM((dp_size,) + small.shape, full),
    ]
    for count in (dp_size, dp_size) + (tensor_size, dp_size) * 4 + (tensor_size,):
        scratch += crowd_scratch(count)
    scratch += [
        pltpu.SemaphoreType.DMA((3, dp_size // 2, 3)),
        pltpu.SemaphoreType.DMA((3, dp_size // 2, 3)),
        pltpu.SemaphoreType.DMA((3,)),
    ]
    return pl.pallas_call(
        functools.partial(head_kernel, images),
        out_shape=[jax.ShapeDtypeStruct(*shape) for shape in shapes],
        in_specs=[pl.BlockSpec(memory_space=pltpu.VMEM)] * 9
        + [pl.BlockSpec(memory_space=pl.ANY)] * len(shards),
        out_specs=[pl.BlockSpec(memory_space=pltpu.VMEM)] * 8
        + [pl.BlockSpec(memory_space=pl.ANY)] * len(shards),
        scratch_shapes=scratch,
        compiler_params=pltpu.CompilerParams(
            collective_id=30, has_side_effects=True, vmem_limit_bytes=ACT_VMEM
        ),
        name="head",
    )(small, feats, table, times, second, shift, scale, bias, mod_low, *shards)


def tail_kernel(
    images,
    final_at,
    row_ref,
    mod_ref,
    weight_ref,
    second_ref,
    shift_ref,
    scale_ref,
    pre_signal_ref,
    pre_time_ref,
    feats_ref,
    hidden_ref,
    signal_ref,
    loss_ref,
    *rest,
):
    terms, others = rest[0:3], rest[3 : 2 + LAYERS]
    rest = rest[2 + LAYERS :]
    (
        row_sums,
        vector_sums,
        class_grad,
        time_grad,
        second_grad,
        shift_grad,
        scale_grad,
        mod_grad,
        scalar_sums,
    ) = rest[0:9]
    totals = rest[9:12]
    (
        row_in,
        row_mid,
        row_fin,
        mod_in,
        mod_low,
        d_mod_all,
        signal_part,
        scalar_own,
        scalar_in,
        scalar_mid,
        scalar_fin,
    ) = rest[12:23]
    signal_refs, hidden_refs = rest[23:27], rest[27:31]
    own, pair_in, way_in, way_out = rest[31:34], rest[34:37], rest[37:40], rest[40:43]
    crowds = [rest[43 + 3 * index : 46 + 3 * index] for index in range(10)]
    reduce_sems = rest[73:]
    signal_out, hidden_out = signal_refs[0], hidden_refs[0]
    dp_size = lax.axis_size("dp")
    tensor_size = lax.axis_size("tensor")
    places = dp_size * tensor_size
    dp_rank = lax.axis_index("dp")
    images_all = images * dp_size
    cols, lanes = row_ref.shape[2:]
    mod_rows = weight_ref.shape[1]
    slots = mod_low.shape[0]
    last_step = dp_size // 2
    greet_groups("tensor", "dp")
    reduce = Reduce(Line(), terms, totals, own, pair_in, way_in, way_out, *reduce_sems)
    mod_sum = Crowd("tensor", lambda place: mod_ref.at[place], mod_in, *crowds[0])
    mod_spread = Crowd("dp", lambda place: mod_low, d_mod_all, *crowds[1])
    rows = Funnel(row_ref, row_in, row_mid, row_fin, *crowds[2:4])
    signal = Funnel(*signal_refs, *crowds[4:6])
    hidden = Funnel(*hidden_refs, *crowds[6:8])
    scalars = Crowd("tensor", lambda place: scalar_own, scalar_in, *crowds[8])
    scalars_dp = Crowd("dp", lambda place: scalar_mid, scalar_fin, *crowds[9])
    mod_sum.start()
    rows.start()
    reduce.send_pair(0)
    reduce.load_own()
    mod_sum.wait()
    mod_low[...] = jnp.sum(mod_in[...], axis=0).astype(jnp.bfloat16)
    mod_spread.start()
    rows.hand_on()
    reduce.send_pair(1)
    other_squares = sum(other[0:1, 0:1] for other in others)
    reduce.wait_own()
    row_total = rows.take()
    row_sums[...] = row_total
    joined = jnp.concatenate([row_fin[at] for at in range(dp_size)], axis=1)

    def final_of(piece):
        return dense(
            joined,
            chosen(
                (dp_size * lanes, images_all),
                lambda row, col: (
                    (row // lanes == col // images)
                    & (lax.rem(row, lanes) == final_at + piece * images + lax.rem(col, images))
                ),
                jnp.float32,
            ),
        )

    d_shift, d_scale = final_of(0), final_of(1)
    signal_part[...] = dense_tn(shift_ref[...], d_shift) + dense_tn(scale_ref[...], d_scale)
    mod_spread.wait()
    d_mod = d_mod_all[...].reshape(dp_size * slots, mod_low.shape[1])
    own_rows = pl.ds(pl.multiple_of(dp_rank * mod_rows, 8), mod_rows)

    def layer_pick(layer_idx, kind):
        return chosen(
            (dp_size * slots, images_all),
            lambda row, col: (
                (row // slots == col // images)
                & (lax.rem(row, slots) == layer_idx * images + lax.rem(col, images))
            ),
            kind,
        )

    for layer_idx in range(LAYERS):
        signal_part[own_rows, :] += dense(
            dot_nt(weight_ref[layer_idx], d_mod), layer_pick(layer_idx, jnp.float32)
        )
    signal_out[...] = fold(signal_part[...].reshape(places, cols, images_all)).reshape(
        signal_out.shape
    )
    signal.start()
    signal.hand_on()
    reduce.send_pair(2)
    run_ticks(reduce, 0, min(1, last_step - 1))
    signal_low = signal_ref[own_rows, :].astype(jnp.bfloat16)
    for layer_idx in range(LAYERS):
        placed = dot_nt(signal_low, layer_pick(layer_idx, jnp.bfloat16)).astype(jnp.bfloat16)
        grad = dot_nn(placed, d_mod)
        mod_grad[layer_idx] = grad
        other_squares = other_squares + square_sum(grad)
    grad = dense_nt(d_shift, signal_ref[...])
    shift_grad[...] = grad
    other_squares = other_squares + square_sum(grad)
    grad = dense_nt(d_scale, signal_ref[...])
    scale_grad[...] = grad
    other_squares = other_squares + square_sum(grad)
    lane = lax.broadcasted_iota(jnp.int32, row_total.shape, 1)
    other_squares = other_squares + square_sum(jnp.where(lane < final_at, row_total, 0.0))
    d_signal = unfold(signal.take(), cols, images_all)
    d_signal = d_signal * silu_slope(pre_signal_ref[...])
    d_hidden = dense_tn(second_ref[...], d_signal)
    hidden_out[...] = fold(d_hidden.reshape(places, cols, images_all)).reshape(hidden_out.shape)
    hidden.start()
    hidden.hand_on()
    each(max(last_step - 3, 0), lambda step: reduce.send_pair(step + 3))
    run_ticks(reduce, 1, min(2, last_step - 1))
    labels = jnp.round(feats_ref[:, FREQ : FREQ + 1]).astype(jnp.int32)
    class_lane = lax.broadcasted_iota(jnp.int32, (images_all, class_grad.shape[1]), 1)
    grad = dense(d_signal, jnp.where(class_lane == labels, 1.0, 0.0))
    class_grad[...] = grad
    other_squares = other_squares + square_sum(grad)
    grad = dense_nt(d_signal, hidden_ref[...])
    second_grad[...] = grad
    other_squares = other_squares + square_sum(grad)
    d_hidden = unfold(hidden.take(), cols, images_all)
    d_hidden = d_hidden * silu_slope(pre_time_ref[...])
    grad = dense(d_hidden, feats_ref[:, 0:FREQ])
    time_grad[...] = grad
    other_squares = other_squares + square_sum(grad)
    vectors = [
        jnp.sum(values, axis=1, keepdims=True) for values in (d_hidden, d_signal, d_shift, d_scale)
    ]
    lane = lax.broadcasted_iota(jnp.int32, vector_sums.shape, 1)
    grad = sum(jnp.where(lane == at, vector, 0.0) for at, vector in enumerate(vectors))
    vector_sums[...] = grad
    other_squares = other_squares + square_sum(grad)
    run_ticks(reduce, 2, min(3, last_step - 1))
    each(max(last_step - 4, 0), lambda step: reduce.tick(step + 3))
    reduce.finish()
    for total in totals:
        other_squares = other_squares + square_sum(total[...])
    lane = lax.broadcasted_iota(jnp.int32, scalar_own.shape, 1)
    scalar_own[...] = jnp.where(lane == 0, loss_ref[...], other_squares)
    scalars.start()
    scalars.wait()
    scalar_mid[...] = jnp.sum(scalar_in[...], axis=0)
    scalars_dp.start()
    scalars_dp.wait()
    scalar_sums[...] = jnp.sum(scalar_fin[...], axis=0)


def tail_call(
    rows, mods, mod_low, second, shift, scale, pre_signal, pre_time, feats, hidden, signal, loss,
    terms, others, images, at,
):
    dp_size, tensor_size = lax.axis_size("dp"), lax.axis_size("tensor")
    images_all = images * dp_size
    cols, lanes = rows.shape[2:]
    folded = folded_lanes(cols, images_all)
    full, low = jnp.float32, jnp.bfloat16
    spots = dp_size // 2
    blocks = [term.shape[1:] for term in terms]
    shapes = [
        ((cols, lanes), full),
        ((cols, 128), full),
        ((cols, -(-CLASSES // 128) * 128), full),
        ((cols, FREQ), full),
        ((cols, D), full),
        ((cols, D), full),
        ((cols, D), full),
        (mod_low.shape, full),
        ((8, 128), full),
    ] + [(block, full) for block in blocks]
    scratch = [
        pltpu.VMEM((tensor_size, dp_size, cols, lanes), full),
        pltpu.VMEM((dp_size, cols, lanes), full),
        pltpu.VMEM((dp_size, cols, lanes), full),
        pltpu.VMEM(mods.shape, full),
        pltpu.VMEM(mods.shape[1:], low),
        pltpu.VMEM((dp_size,) + mods.shape[1:], low),
        pltpu.VMEM((D, images_all), full),
        pltpu.VMEM((8, 128), full),
        pltpu.VMEM((tensor_size, 8, 128), full),
        pltpu.VMEM((8, 128), full),
        pltpu.VMEM((dp_size, 8, 128), full),
    ]
    for _ in range(2):
        scratch += [
            pltpu.VMEM((dp_size, tensor_size, 8, folded), full),
            pltpu.VMEM((tensor_size, dp_size, 8, folded), full),
            pltpu.VMEM((dp_size, 8, folded), full),
            pltpu.VMEM((dp_size, 8, folded), full),
        ]
    scratch += [pltpu.VMEM((spots,) + block, low) for block in blocks]
    scratch += [pltpu.VMEM((spots,) + block, low) for block in blocks]
    scratch += [pltpu.VMEM((2, spots) + block, low) for block in blocks]
    scratch += [pltpu.VMEM((2, spots) + block, low) for block in blocks]
    for count in (tensor_size, dp_size) * 5:
        scratch += crowd_scratch(count)
    scratch += [
        pltpu.SemaphoreType.DMA((3, spots, 3)),
        pltpu.SemaphoreType.DMA((3, spots, 3)),
        pltpu.SemaphoreType.DMA((3, spots)),
    ]
    return pl.pallas_call(
        functools.partial(tail_kernel, images, at),
        out_shape=[jax.ShapeDtypeStruct(*shape) for shape in shapes],
        in_specs=[pl.BlockSpec(memory_space=pltpu.VMEM)] * 12
        + [pl.BlockSpec(memory_space=pl.ANY)] * len(terms)
        + [pl.BlockSpec(memory_space=pltpu.VMEM)] * len(others),
        out_specs=[pl.BlockSpec(memory_space=pltpu.VMEM)] * len(shapes),
        scratch_shapes=scratch,
        compiler_params=pltpu.CompilerParams(
            collective_id=31, has_side_effects=True, vmem_limit_bytes=ACT_VMEM
        ),
        name="tail",
    )(
        rows, mods, mod_low, second, shift, scale, pre_signal, pre_time, feats, hidden, signal,
        loss, *terms, *others,
    )


def adam_update(weight, first, second, grad, factor, first_fix, second_fix):
    clipped = grad * factor
    first_new = BETA_ONE * first + (1.0 - BETA_ONE) * clipped
    second_new = BETA_TWO * second + (1.0 - BETA_TWO) * clipped * clipped
    step_size = first_new / first_fix / (jnp.sqrt(second_new / second_fix) + ADAM_EPS)
    change = -LEARN_RATE * (step_size + DECAY * weight)
    master = weight + change
    return (master, first_new, second_new, master.astype(jnp.bfloat16), change)


def local(
    latents,
    target_noise,
    timesteps,
    labels,
    step_count,
    embed_table,
    layer_in,
    layer_out,
    layer_ada,
    embed_first,
    embed_second,
    input_first,
    input_second,
    output_first,
    output_second,
    mod_first,
    mod_second,
):
    tensor_size = lax.axis_size("tensor")
    tensor_rank = lax.axis_index("tensor")
    images = latents.shape[0]
    grid_side = SIDE // PATCH
    local_rows = grid_side // tensor_size
    tokens_all = grid_side * grid_side
    heads_local = HEADS // tensor_size
    group_width = heads_local * HEAD_DIM
    unit_count = FF // tensor_size
    patch_in = PATCH * PATCH * CHANNELS
    count_all = images * lax.axis_size("dp") * tokens_all * patch_in
    patch_start, time_start, second_start, final_start, head_start, vector_start, layer_start = (
        table_starts()
    )
    layer_rows = 10 + FF // D
    dp_rank = lax.axis_index("dp")
    dp_size = lax.axis_size("dp")
    place_count = dp_size * tensor_size
    images_all = images * dp_size
    table_cols = lax.reduce_precision(embed_table.T, 8, 7)
    cols = table_cols.shape[0]
    mod_rows = layer_ada.shape[1]
    mod_cols = layer_ada.shape[2]
    mod_low = layer_ada.astype(jnp.bfloat16)

    def col_block(row_start, row_count):
        return table_cols[:, row_start : row_start + row_count]

    vector_count = 5 + LAYERS * layer_rows
    small_count = 2 * patch_in + vector_count
    lanes = -(-(small_count + 2 * images) // 128) * 128
    shards_in = layer_in[:, :, 0].astype(jnp.bfloat16)
    shards = (
        shards_in[:, :, : 3 * group_width],
        shards_in[:, :, 3 * group_width :],
        layer_out[:, 0].astype(jnp.bfloat16),
    )
    second_cols = col_block(second_start, D)
    shift_cols = col_block(final_start, D)
    scale_cols = col_block(final_start + D, D)
    fused = cols % 8 == 0 and images <= 8
    if fused:
        small_send = jnp.concatenate(
            [
                col_block(patch_start, patch_in),
                col_block(head_start, patch_in + vector_count),
                jnp.zeros((cols, lanes - small_count), jnp.float32),
            ],
            axis=1,
        )
        feats_send = jnp.concatenate(
            [
                time_features(timesteps),
                jnp.broadcast_to(labels.astype(jnp.float32)[:, None], (images, 128)),
            ],
            axis=1,
        )
        feats_send = jnp.pad(feats_send, ((0, 8 - images), (0, 0)))
        outs = head_call(
            small_send,
            feats_send,
            table_cols,
            col_block(time_start, FREQ),
            second_cols,
            shift_cols,
            scale_cols,
            col_block(vector_start, 5),
            mod_low,
            shards,
            images,
        )
        small_all, feats_all, pre_time, hidden, pre_signal, signal, final_all, mod_full = outs[:8]
        wholes = outs[8:]
        small_all = small_all.transpose(1, 0, 2, 3)
        time_feats = feats_all[:, :FREQ]
        labels_all = jnp.round(feats_all[:, FREQ]).astype(jnp.int32)
        signal_low = lax.dynamic_slice_in_dim(
            signal.astype(jnp.bfloat16), dp_rank * mod_rows, mod_rows, 0
        )
        final_all = final_all.transpose(1, 0, 2, 3)[:, :, :images, : 2 * cols]
        final_own = final_all.reshape(place_count, images, 2, cols)
        final_own = final_own.transpose(2, 1, 0, 3).reshape(2, images, D)
        mod_full = mod_full[:, : LAYERS * images].reshape(tensor_size, LAYERS, images, mod_cols)
        mod_full = mod_full.transpose(1, 2, 0, 3).reshape(LAYERS, images, tensor_size * mod_cols)
    else:
        scalar_lanes = jnp.concatenate([timesteps, labels]).astype(jnp.float32)
        small_send = jnp.concatenate(
            [
                col_block(patch_start, patch_in),
                col_block(head_start, patch_in + vector_count),
                jnp.broadcast_to(scalar_lanes[None, :], (cols, 2 * images)),
                jnp.zeros((cols, lanes - small_count - 2 * images), jnp.float32),
            ],
            axis=1,
        )
        small_all = exchange(small_send, "all", False, 1)
        scalars_all = small_all[::tensor_size, 0, small_count : small_count + 2 * images].astype(
            jnp.int32
        )
        timesteps_all = scalars_all[:, :images].reshape(images_all)
        labels_all = scalars_all[:, images:].reshape(images_all)
        time_feats = time_features(timesteps_all)
        onehot = (labels_all[:, None] == jnp.arange(CLASSES, dtype=jnp.int32)[None, :]).astype(
            jnp.float32
        )
        pre_time = dense(col_block(time_start, FREQ), time_feats.T) + col_block(vector_start + 1, 1)
        hidden = exchange(jax.nn.silu(pre_time), "all", False, 2).reshape(D, images_all)
        pre_signal = (
            dense(second_cols, hidden)
            + col_block(vector_start + 2, 1)
            + dense(col_block(0, CLASSES), onehot.T)
        )
        signal = exchange(jax.nn.silu(pre_signal), "all", False, 3).reshape(D, images_all)
        final_send = jnp.concatenate(
            [
                dense(shift_cols, signal) + col_block(vector_start + 3, 1),
                dense(scale_cols, signal) + col_block(vector_start + 4, 1),
            ],
            axis=0,
        )
        final_all = exchange(final_send, "all", False, 4).reshape(place_count, 2, cols, images_all)
        final_own = lax.dynamic_slice_in_dim(final_all, dp_rank * images, images, 3)
        final_own = final_own.transpose(1, 3, 0, 2).reshape(2, images, D)
        signal_low = lax.dynamic_slice_in_dim(
            signal.astype(jnp.bfloat16), dp_rank * mod_rows, mod_rows, 0
        )
        mod_part = jnp.einsum("db,lde->ble", signal_low, mod_low, preferred_element_type=jnp.float32)
        mod_part = mod_part.reshape(dp_size, images * LAYERS, mod_cols)
        mod_local = jnp.sum(exchange(mod_part, "dp", True, 5), axis=0)
        mod_full = exchange(mod_local, "tensor", False, 6)
        mod_full = mod_full.reshape(tensor_size, images, LAYERS, mod_cols)
        mod_full = mod_full.transpose(2, 1, 0, 3).reshape(LAYERS, images, tensor_size * mod_cols)
        wholes = [lax.all_gather(shard[0], "dp") for shard in shards]
    small_rows = small_all.reshape(D, lanes).T
    patch_w = small_rows[0:patch_in]
    head_w = small_rows[patch_in : 2 * patch_in]
    vectors = small_rows[2 * patch_in : 2 * patch_in + 5]
    bias_all = small_rows[2 * patch_in + 5 : small_count]
    onehot = (labels_all[:, None] == jnp.arange(CLASSES, dtype=jnp.int32)[None, :]).astype(
        jnp.float32
    )
    final_shift, final_scale = final_own[0], final_own[1]
    pixels = patchify(latents, local_rows)
    targets = patchify(target_noise, local_rows)
    keep_coef, drop_coef = noise_levels(timesteps)
    noisy = keep_coef[:, None, None] * pixels + drop_coef[:, None, None] * targets
    residual = (
        jnp.einsum("btp,pd->btd", noisy, patch_w, precision=PRECISE)
        + vectors[0]
        + position_table(tensor_rank * local_rows, local_rows)[None]
    )
    saved_acts = []
    bias_all = bias_all.reshape(LAYERS, layer_rows, D)
    mod_vecs = mod_full.reshape(LAYERS, images, 6, D) + bias_all[:, None, 0:6]
    part_bias = lax.dynamic_slice_in_dim(
        bias_all[:, 8:10], tensor_rank * group_width, group_width, 2
    )
    qkv_bias = jnp.concatenate(
        [part_bias[:, 0], jnp.zeros((LAYERS, group_width), jnp.float32), part_bias[:, 1]], axis=1
    )
    up_bias = lax.dynamic_slice_in_dim(
        bias_all[:, 10:].reshape(LAYERS, FF), tensor_rank * unit_count, unit_count, 1
    )
    joined = fused and shards[0].shape[1] % 16 == 0 and shards[2].shape[1] % 8 == 0
    if joined:
        outs = forward_all(
            residual,
            mod_vecs,
            bias_all[:, 6:8],
            qkv_bias[:, None],
            up_bias[:, None],
            wholes,
            shards,
        )
        residual = outs[0]
        saved_acts = [(mod_vecs[layer_idx], outs[1:10], outs[10:13]) for layer_idx in range(LAYERS)]
    else:
        for layer_idx in range(LAYERS):
            weights = (
                wholes[0].reshape(D, 3 * group_width),
                wholes[1].reshape(D, unit_count),
                wholes[2].reshape(group_width + unit_count, D),
            )
            outs = forward_layer(
                residual,
                mod_vecs[layer_idx],
                bias_all[layer_idx, 6:8],
                qkv_bias[layer_idx : layer_idx + 1],
                up_bias[layer_idx : layer_idx + 1],
                *weights,
                shards if layer_idx + 1 < LAYERS else (),
                layer_idx,
            )
            wholes = outs[9:]
            saved_acts.append((mod_vecs[layer_idx], (residual,) + tuple(outs[1:9]), weights))
            residual = outs[0]
    final_in, final_norm_pull = jax.vjp(modulate, residual, final_shift, final_scale)
    predicted = jnp.einsum("btd,pd->btp", final_in, head_w, precision=PRECISE)
    error_all = predicted - targets
    loss_part = jnp.sum(error_all * error_all) / count_all
    d_pred = 2.0 * error_all / count_all
    d_head = jnp.einsum("btp,btd->pd", d_pred, final_in, precision=PRECISE)
    d_final = jnp.einsum("btp,pd->btd", d_pred, head_w, precision=PRECISE)
    d_residual, d_final_shift, d_final_scale = final_norm_pull(d_final)
    totals = []
    squares = []
    terms = ()
    bias_parts = []
    for layer_idx in reversed(range(LAYERS)):
        mod_vec, saved, weights = saved_acts[layer_idx]
        outs = backward_layer(
            d_residual, mod_vec, saved, weights, terms, layer_idx, joined
        )
        d_residual, d_w_qkv, d_w_up, d_w_out, d_mod_vec, d_vec, d_qkv_bias, d_up_bias = outs[:8]
        if terms:
            totals.insert(0, outs[8:11])
            squares.append(outs[11])
        terms = [
            term.reshape((dp_size, -1) + term.shape[1:]) for term in (d_w_qkv, d_w_up, d_w_out)
        ]
        bias_parts.insert(0, (d_mod_vec, d_vec, d_qkv_bias, d_up_bias))
    d_mods, d_vecs, d_qkv_rows, d_up_rows = [jnp.stack(parts) for parts in zip(*bias_parts)]
    part_rows = jnp.stack([d_qkv_rows[:, 0, :group_width], d_qkv_rows[:, 0, 2 * group_width :]], 1)
    bias_blocks = jnp.concatenate(
        [
            jnp.sum(d_mods, axis=1),
            d_vecs,
            lax.dynamic_update_slice_in_dim(
                jnp.zeros((LAYERS, 2, D), jnp.float32), part_rows, tensor_rank * group_width, 2
            ),
            lax.dynamic_update_slice_in_dim(
                jnp.zeros((LAYERS, FF), jnp.float32), d_up_rows[:, 0], tensor_rank * unit_count, 1
            ).reshape(LAYERS, FF // D, D),
        ],
        axis=1,
    ).reshape(LAYERS * layer_rows, D)
    d_patch_w = jnp.einsum("btp,btd->pd", noisy, d_residual, precision=PRECISE)
    d_patch_b = jnp.sum(d_residual, axis=(0, 1))
    row_parts = jnp.concatenate(
        [d_patch_w, d_head, d_patch_b[None], bias_blocks, d_final_shift, d_final_scale],
        axis=0,
    )
    row_count = row_parts.shape[0]
    row_lanes = -(-row_count // 128) * 128
    row_parts = jnp.pad(row_parts, ((0, row_lanes - row_count), (0, 0)))
    final_at = row_count - 2 * images
    row_send = row_parts.T.reshape(dp_size, tensor_size, cols, row_lanes)
    mod_send = d_mods.reshape(LAYERS * images, tensor_size, mod_cols)
    mod_send = mod_send.transpose(1, 0, 2)
    if fused:
        slots = slots_of(images)
        outs = tail_call(
            row_send,
            jnp.pad(mod_send, ((0, 0), (0, slots - LAYERS * images), (0, 0))),
            mod_low,
            second_cols,
            shift_cols,
            scale_cols,
            pre_signal,
            pre_time,
            feats_all,
            hidden,
            signal,
            loss_part.reshape(1, 1),
            terms,
            squares,
            images,
            final_at,
        )
        row_sums, vector_sums, class_grad, time_grad, second_grad, shift_grad, scale_grad = outs[:7]
        mod_grad, scalar_sums = outs[7:9]
        totals.insert(0, outs[9:])
        vector_sums = vector_sums[:, 0:4]
        class_grad = class_grad[:, :CLASSES]
        scalar_sums = scalar_sums[0]
    else:
        totals.insert(
            0,
            [
                lax.psum_scatter(term, "dp", scatter_dimension=0).astype(jnp.float32)
                for term in terms
            ],
        )
        row_all = exchange(row_send.reshape(place_count, cols, row_lanes), "all", True, 7)
        row_sums = jnp.sum(row_all, axis=0)
        final_sums = jnp.sum(
            row_all[:, :, final_at:row_count].reshape(dp_size, tensor_size, cols, 2, images), axis=1
        )
        final_sums = final_sums.transpose(2, 1, 0, 3).reshape(2, cols, images_all)
        d_shift_cols, d_scale_cols = final_sums[0], final_sums[1]
        d_mod_own = jnp.sum(exchange(mod_send, "tensor", True, 8), axis=0)
        d_mod_low = exchange(d_mod_own.astype(jnp.bfloat16), "dp", False, 9)
        d_mod_low = d_mod_low.reshape(dp_size, LAYERS, images, mod_cols)
        d_mod_low = d_mod_low.transpose(1, 0, 2, 3).reshape(LAYERS, images_all, mod_cols)
        d_signal_rows = jnp.einsum(
            "lbe,lde->db", d_mod_low, mod_low, preferred_element_type=jnp.float32
        )
        d_signal_part = dense(shift_cols.T, d_shift_cols) + dense(scale_cols.T, d_scale_cols)
        d_signal_part = d_signal_part + lax.dynamic_update_slice_in_dim(
            jnp.zeros((D, images_all), jnp.float32), d_signal_rows, dp_rank * mod_rows, 0
        )
        d_signal_cols = jnp.sum(
            exchange(d_signal_part.reshape(place_count, cols, images_all), "all", True, 10), axis=0
        )
        d_pre_signal = d_signal_cols * silu_slope(pre_signal)
        d_hidden_part = dense(second_cols.T, d_pre_signal)
        d_hidden_cols = jnp.sum(
            exchange(d_hidden_part.reshape(place_count, cols, images_all), "all", True, 11), axis=0
        )
        d_hidden = d_hidden_cols * silu_slope(pre_time)
        mod_grad = jnp.einsum(
            "db,lbe->lde", signal_low, d_mod_low, preferred_element_type=jnp.float32
        )
        class_grad = dense(d_pre_signal, onehot)
        time_grad = dense(d_hidden, time_feats)
        second_grad = dense(d_pre_signal, hidden.T)
        shift_grad = dense(d_shift_cols, signal.T)
        scale_grad = dense(d_scale_cols, signal.T)
        vector_sums = jnp.stack(
            [
                jnp.sum(values, axis=1)
                for values in (d_hidden, d_pre_signal, d_shift_cols, d_scale_cols)
            ],
            axis=1,
        )
    table_grad = jnp.concatenate(
        [
            class_grad,
            row_sums[:, 0:patch_in],
            time_grad,
            second_grad,
            shift_grad,
            scale_grad,
            row_sums[:, patch_in : 2 * patch_in + 1],
            vector_sums,
            row_sums[:, 2 * patch_in + 1 : final_at],
        ],
        axis=1,
    )
    input_grad = jnp.stack([jnp.concatenate(total[0:2], axis=1) for total in totals])
    input_grad = input_grad.reshape(layer_in.shape)
    output_grad = jnp.stack([total[2] for total in totals]).reshape(layer_out.shape)
    if not fused:
        local_squares = (
            jnp.sum(table_grad * table_grad)
            + jnp.sum(input_grad * input_grad)
            + jnp.sum(output_grad * output_grad)
            + jnp.sum(mod_grad * mod_grad)
        )
        scalar_send = jnp.where(
            lax.broadcasted_iota(jnp.int32, (8, 128), 1) == 0, loss_part, local_squares
        )
        scalar_sums = jnp.sum(exchange(scalar_send, "all", False, 12)[:, 0, 0:2], axis=0)
    loss_value = scalar_sums[0]
    square_total = scalar_sums[1]
    grad_norm = jnp.sqrt(square_total)
    factor = jnp.minimum(1.0, CLIP_NORM / grad_norm)
    first_fix = 1.0 - BETA_ONE ** step_count.astype(jnp.float32)
    second_fix = 1.0 - BETA_TWO ** step_count.astype(jnp.float32)
    embed_out = adam_update(
        embed_table.T, embed_first.T, embed_second.T, table_grad, factor, first_fix, second_fix
    )
    input_out = adam_update(
        layer_in, input_first, input_second, input_grad, factor, first_fix, second_fix
    )
    output_out = adam_update(
        layer_out, output_first, output_second, output_grad, factor, first_fix, second_fix
    )
    mod_out = adam_update(layer_ada, mod_first, mod_second, mod_grad, factor, first_fix, second_fix)
    return (
        (loss_value, grad_norm, embed_out[4].T, embed_out[1].T, embed_out[2].T)
        + input_out[0:4]
        + output_out[0:4]
        + mod_out[0:4]
    )


def solution(mesh):
    placed = (
        P("dp", "tensor"),
        P("dp", "tensor"),
        P("dp"),
        P("dp"),
        P(),
        P(None, ("dp", "tensor")),
        P(None, "dp", "tensor", None),
        P(None, "tensor", "dp", None),
        P(None, "dp", "tensor"),
        P(None, ("dp", "tensor")),
        P(None, ("dp", "tensor")),
        P(None, "dp", "tensor", None),
        P(None, "dp", "tensor", None),
        P(None, "tensor", "dp", None),
        P(None, "tensor", "dp", None),
        P(None, "dp", "tensor"),
        P(None, "dp", "tensor"),
    )
    return jax.shard_map(
        local,
        mesh=mesh,
        in_specs=placed,
        out_specs=(
            P(),
            P(),
            P(None, ("dp", "tensor")),
            P(None, ("dp", "tensor")),
            P(None, ("dp", "tensor")),
            P(None, "dp", "tensor", None),
            P(None, "dp", "tensor", None),
            P(None, "dp", "tensor", None),
            P(None, "dp", "tensor", None),
            P(None, "tensor", "dp", None),
            P(None, "tensor", "dp", None),
            P(None, "tensor", "dp", None),
            P(None, "tensor", "dp", None),
            P(None, "dp", "tensor"),
            P(None, "dp", "tensor"),
            P(None, "dp", "tensor"),
            P(None, "dp", "tensor"),
        ),
        check_vma=False,
    )
```

```python
import functools
import math

import jax
import jax.numpy as jnp
from jax import lax
from jax.experimental import pallas as pl
from jax.experimental.pallas import tpu as pltpu
from jax.sharding import PartitionSpec as P

D = 768
HEADS = 12
HEAD_DIM = 64
FF = 3072
CLASSES = 1001
FREQ = 256
CHANNELS = 4
PATCH = 2
SIDE = 32
LAYERS = 3


EPS_NORM = 1e-06
LEARN_RATE = 0.01
DECAY = 0.01
BETA_ONE = 0.5
BETA_TWO = 0.5
ADAM_EPS = 1e-08
CLIP_NORM = 0.25
PRECISE = lax.Precision.HIGHEST


def dense(left_op, right_op):
    return jnp.dot(left_op, right_op, precision=PRECISE, preferred_element_type=jnp.float32)


def layer_norm(values):
    center = values - jnp.mean(values, axis=-1, keepdims=True)
    return center * lax.rsqrt(jnp.mean(center * center, axis=-1, keepdims=True) + EPS_NORM)


def modulate(values, shift_vec, scale_vec):
    return layer_norm(values) * (1.0 + scale_vec[:, None, :]) + shift_vec[:, None, :]


def gelu_tanh(values):
    return jax.nn.gelu(values, approximate=True)


def silu_slope(values):
    sigmoid_val = jax.nn.sigmoid(values)
    return sigmoid_val * (1.0 + values * (1.0 - sigmoid_val))


def time_features(step_ints):
    half_width = FREQ // 2
    frequency = jnp.exp(-math.log(10000.0) * jnp.arange(half_width, dtype=jnp.float32) / half_width)
    angles = step_ints.astype(jnp.float32)[:, None] * frequency[None, :]
    return jnp.concatenate([jnp.cos(angles), jnp.sin(angles)], axis=1)


def noise_levels(step_ints):
    base_cos = math.cos(0.008 / 1.008 * math.pi / 2)
    angles = (step_ints.astype(jnp.float32) / 1000.0 + 0.008) / 1.008 * (math.pi / 2)
    signal_level = jnp.cos(angles) ** 2 / base_cos**2
    return (jnp.sqrt(signal_level), jnp.sqrt(1.0 - signal_level))


def position_table(first_row, row_count):
    grid_side = SIDE // PATCH
    quarter = D // 4
    omegas = jnp.exp(-math.log(10000.0) * jnp.arange(quarter, dtype=jnp.float32) / quarter)
    token_index = jnp.arange(row_count * grid_side, dtype=jnp.int32)
    row_angle = (first_row + token_index // grid_side).astype(jnp.float32)[:, None] * omegas[
        None, :
    ]
    col_angle = (token_index % grid_side).astype(jnp.float32)[:, None] * omegas[None, :]
    return jnp.concatenate(
        [jnp.sin(row_angle), jnp.cos(row_angle), jnp.sin(col_angle), jnp.cos(col_angle)], axis=1
    )


def patchify(flat_pixels, row_count):
    grid_side = SIDE // PATCH
    shaped = flat_pixels.reshape(flat_pixels.shape[0], row_count, PATCH, grid_side, PATCH, CHANNELS)
    return shaped.transpose(0, 1, 3, 2, 4, 5).reshape(
        flat_pixels.shape[0], row_count * grid_side, PATCH * PATCH * CHANNELS
    )


def table_starts():
    patch_in = PATCH * PATCH * CHANNELS
    patch_start = CLASSES
    time_start = patch_start + patch_in
    second_start = time_start + FREQ
    final_start = second_start + D
    head_start = final_start + 2 * D
    vector_start = head_start + patch_in
    layer_start = vector_start + 5
    return (
        patch_start,
        time_start,
        second_start,
        final_start,
        head_start,
        vector_start,
        layer_start,
    )


def group_place(group):
    if group == "all":
        width = lax.axis_size("tensor")
        place = lax.axis_index("dp") * width + lax.axis_index("tensor")
        size = lax.axis_size("dp") * width
        return place, size, lambda at: {"dp": at // width, "tensor": lax.rem(at, width)}
    return lax.axis_index(group), lax.axis_size(group), lambda at: {group: at}


def greet_group(group):
    place, size, coords = group_place(group)
    barrier = pltpu.get_barrier_semaphore()

    def greet_one(step, carry):
        peer = coords(lax.rem(place + step, size))
        pl.semaphore_signal(barrier, inc=1, device_id=peer, device_id_type=pl.DeviceIdType.MESH)
        return carry

    lax.fori_loop(1, size, greet_one, 0)
    pl.semaphore_wait(barrier, size - 1)


def greet_groups(*groups):
    barrier = pltpu.get_barrier_semaphore()
    count = 0
    for group in groups:
        place, size, coords = group_place(group)

        def greet_one(step, carry, place=place, size=size, coords=coords):
            peer = coords(lax.rem(place + step, size))
            pl.semaphore_signal(barrier, inc=1, device_id=peer, device_id_type=pl.DeviceIdType.MESH)
            return carry

        lax.fori_loop(1, size, greet_one, 0)
        count += size - 1
    pl.semaphore_wait(barrier, count)


class Crowd:
    def __init__(self, group, source_at, target, send_sems, recv_sems, local_sem):
        self.place, self.size, self.coords = group_place(group)
        self.source_at, self.target = source_at, target
        self.sends, self.recvs, self.local_sem = send_sems, recv_sems, local_sem

    def copy_to(self, step):
        there = lax.rem(self.place + step, self.size)
        return pltpu.make_async_remote_copy(
            src_ref=self.source_at(there),
            dst_ref=self.target.at[self.place],
            send_sem=self.sends.at[step],
            recv_sem=self.recvs.at[step],
            device_id=self.coords(there),
            device_id_type=pl.DeviceIdType.MESH,
        )

    def own_copy(self):
        return pltpu.make_async_copy(
            self.source_at(self.place), self.target.at[self.place], self.local_sem
        )

    def start(self):
        def begin(step, carry):
            self.copy_to(step).start()
            return carry

        lax.fori_loop(1, self.size, begin, 0)
        self.own_copy().start()

    def wait(self):
        def finish(step, carry):
            self.copy_to(step).wait()
            return carry

        self.own_copy().wait()
        lax.fori_loop(1, self.size, finish, 0)


class Relay:
    def __init__(self, source_at, middle, whole, sems_dp, sems_tensor):
        self.first = Crowd("dp", source_at, middle, *sems_dp)
        self.second = Crowd("tensor", lambda place: middle, whole, *sems_tensor)

    def start(self):
        self.first.start()

    def hand_on(self):
        self.first.wait()
        self.second.start()

    def wait(self):
        self.second.wait()


class Funnel:
    def __init__(self, source, across, middle, along, sems_tensor, sems_dp):
        self.across, self.middle, self.along = across, middle, along
        self.first = Crowd("tensor", lambda place: source.at[:, place], across, *sems_tensor)
        self.second = Crowd("dp", lambda place: middle.at[place], along, *sems_dp)

    def start(self):
        self.first.start()

    def hand_on(self):
        self.first.wait()
        self.middle[...] = jnp.sum(self.across[...], axis=0)
        self.second.start()

    def take(self):
        self.second.wait()
        return jnp.sum(self.along[...], axis=0)


def crowd_scratch(size):
    return [
        pltpu.SemaphoreType.DMA((size,)),
        pltpu.SemaphoreType.DMA((size,)),
        pltpu.SemaphoreType.DMA,
    ]


def exchange_kernel(group, spread, source, target, send_sems, recv_sems, local_sem):
    greet_group(group)
    crowd = Crowd(
        group,
        lambda place: source.at[place] if spread else source,
        target,
        send_sems,
        recv_sems,
        local_sem,
    )
    crowd.start()
    crowd.wait()


def exchange(values, group, spread, call_id):
    if group == "all":
        size = lax.axis_size("dp") * lax.axis_size("tensor")
    else:
        size = lax.axis_size(group)
    block = values.shape[1:] if spread else values.shape
    return pl.pallas_call(
        functools.partial(exchange_kernel, group, spread),
        out_shape=jax.ShapeDtypeStruct((size,) + block, values.dtype),
        in_specs=[pl.BlockSpec(memory_space=pltpu.VMEM)],
        out_specs=pl.BlockSpec(memory_space=pltpu.VMEM),
        scratch_shapes=crowd_scratch(size),
        compiler_params=pltpu.CompilerParams(
            collective_id=call_id, has_side_effects=True, vmem_limit_bytes=32 * 2**20
        ),
        name="exchange_" + group,
    )(values)


MESH = pl.DeviceIdType.MESH
ACT_VMEM = 60 * 2**20


def dot_nn(left_op, right_op):
    return jnp.dot(left_op, right_op, preferred_element_type=jnp.float32)


def dot_nt(left_op, right_op):
    return lax.dot_general(
        left_op, right_op, (((1,), (1,)), ((), ())), preferred_element_type=jnp.float32
    )


def dot_tn(left_op, right_op):
    return lax.dot_general(
        left_op, right_op, (((0,), (0,)), ((), ())), preferred_element_type=jnp.float32
    )


def square_sum(values):
    return jnp.sum(jnp.sum(values * values, axis=0, keepdims=True), axis=1, keepdims=True)


def norm_parts(values):
    center = values - jnp.mean(values, axis=-1, keepdims=True)
    rstd = lax.rsqrt(jnp.mean(center * center, axis=-1, keepdims=True) + EPS_NORM)
    return center * rstd, rstd


def greet(line):
    rank = lax.axis_index("tensor")
    half = lax.axis_size("tensor") // 2
    core_peer = {"tensor": rank + 1 - 2 * lax.rem(rank, 2)}
    chip_peer = {"tensor": lax.rem(rank + half, 2 * half)}
    barrier = pltpu.get_barrier_semaphore()
    for peer in (core_peer, chip_peer):
        pl.semaphore_signal(barrier, inc=1, device_id=peer, device_id_type=MESH)
    count = 2
    if line is not None:
        line.greet()
        count = count + line.answers()
    pl.semaphore_wait(barrier, count)


class Spread:
    def __init__(self, rows_ref, send_sems, recv_sems):
        self.rows, self.send, self.recv = rows_ref, send_sems, recv_sems
        self.rank = lax.axis_index("tensor")
        self.own_core = lax.rem(self.rank, 2)
        self.core_peer = self.rank + 1 - 2 * self.own_core
        self.chip_peer = lax.rem(self.rank + 2, 4)
        self.count = rows_ref.shape[1] // 4

    def block(self, image, owner):
        return self.rows.at[image, pl.ds(pl.multiple_of(owner * self.count, 16), self.count), :]

    def copy(self, image, owner, peer, which):
        return pltpu.make_async_remote_copy(
            src_ref=self.block(image, owner),
            dst_ref=self.block(image, owner),
            send_sem=self.send.at[image, which],
            recv_sem=self.recv.at[image, which],
            device_id={"tensor": peer},
            device_id_type=MESH,
        )

    def put(self, image, values):
        self.rows[image, pl.ds(pl.multiple_of(self.rank * self.count, 16), self.count), :] = values
        self.copy(image, self.rank, self.chip_peer, 0).start()
        self.copy(image, self.rank, self.core_peer, 1).start()

    def forward(self, image):
        self.copy(image, self.rank, self.chip_peer, 0).wait_recv()
        self.copy(image, self.chip_peer, self.core_peer, 2).start()

    def wait(self, image):
        self.copy(image, self.rank, self.core_peer, 1).wait_recv()
        self.copy(image, self.chip_peer, self.core_peer, 2).wait_recv()

    def close(self, image):
        self.copy(image, self.rank, self.chip_peer, 0).wait_send()
        self.copy(image, self.rank, self.core_peer, 1).wait_send()
        self.copy(image, self.chip_peer, self.core_peer, 2).wait_send()


class Collect:
    def __init__(self, part, near, far_out, far_in, send_sems, recv_sems):
        self.part, self.near, self.far_out, self.far_in = part, near, far_out, far_in
        self.send, self.recv = send_sems, recv_sems
        self.rank = lax.axis_index("tensor")
        self.own_core = lax.rem(self.rank, 2)
        self.own_chip = self.rank // 2
        self.core_peer = self.rank + 1 - 2 * self.own_core
        self.chip_peer = lax.rem(self.rank + 2, 4)
        self.count = part.shape[1] // 4

    def block(self, image, owner):
        return self.part.at[image, pl.ds(pl.multiple_of(owner * self.count, 16), self.count), :]

    def near_copy(self, image, far):
        chip = 1 - self.own_chip if far else self.own_chip
        return pltpu.make_async_remote_copy(
            src_ref=self.block(image, 2 * chip + 1 - self.own_core),
            dst_ref=self.near.at[image, far],
            send_sem=self.send.at[image, far],
            recv_sem=self.recv.at[image, far],
            device_id={"tensor": self.core_peer},
            device_id_type=MESH,
        )

    def far_copy(self, image):
        return pltpu.make_async_remote_copy(
            src_ref=self.far_out.at[image],
            dst_ref=self.far_in.at[image],
            send_sem=self.send.at[image, 2],
            recv_sem=self.recv.at[image, 2],
            device_id={"tensor": self.chip_peer},
            device_id_type=MESH,
        )

    def put(self, image, values):
        self.part[image] = values.astype(jnp.bfloat16)
        self.near_copy(image, 1).start()
        self.near_copy(image, 0).start()

    def load(self, image, owner):
        at = pl.ds(pl.multiple_of(owner * self.count, 16), self.count)
        return self.part[image, at, :].astype(jnp.float32)

    def forward(self, image):
        self.near_copy(image, 1).wait_recv()
        total = self.load(image, self.chip_peer) + self.near[image, 1].astype(jnp.float32)
        self.far_out[image] = total.astype(jnp.bfloat16)
        self.far_copy(image).start()

    def take(self, image):
        self.near_copy(image, 0).wait_recv()
        total = self.load(image, self.rank) + self.near[image, 0].astype(jnp.float32)
        self.far_copy(image).wait_recv()
        return total + self.far_in[image].astype(jnp.float32)

    def close(self, image):
        self.near_copy(image, 1).wait_send()
        self.near_copy(image, 0).wait_send()
        self.far_copy(image).wait_send()


def collect_scratch(images, tokens):
    count = tokens // 4
    return [
        pltpu.VMEM((images, tokens, D), jnp.bfloat16),
        pltpu.VMEM((images, 2, count, D), jnp.bfloat16),
        pltpu.VMEM((images, count, D), jnp.bfloat16),
        pltpu.VMEM((images, count, D), jnp.bfloat16),
    ]


def each(count, body):
    def step(index, carry):
        body(index)
        return carry

    lax.fori_loop(0, count, step, 0)


class Moves:
    def __init__(self, pairs, sems):
        self.copies = [
            pltpu.make_async_copy(source, target, sems.at[at])
            for at, (source, target) in enumerate(pairs)
        ]

    def start(self, *which):
        for at in which:
            self.copies[at].start()

    def wait(self, *which):
        for at in which:
            self.copies[at].wait()


class Line:
    def __init__(self):
        self.size = lax.axis_size("dp") // 2
        self.place = lax.axis_index("dp")
        self.at = self.place // 2
        self.side = lax.rem(self.place, 2)
        self.pair = self.place + 1 - 2 * self.side
        self.has_up = self.at + 1 < self.size
        self.has_down = self.at > 0

    def greet(self):
        barrier = pltpu.get_barrier_semaphore()
        pl.semaphore_signal(barrier, inc=1, device_id={"dp": self.pair}, device_id_type=MESH)

        @pl.when(self.has_up)
        def _():
            up = {"dp": self.place + 2}
            pl.semaphore_signal(barrier, inc=1, device_id=up, device_id_type=MESH)

        @pl.when(self.has_down)
        def _():
            down = {"dp": self.place - 2}
            pl.semaphore_signal(barrier, inc=1, device_id=down, device_id_type=MESH)

    def answers(self):
        return 1 + self.has_up.astype(jnp.int32) + self.has_down.astype(jnp.int32)


UP, DOWN, PAIR = 0, 1, 2


class Gather:
    def __init__(self, line, shards, wholes, sends, recvs, local_sems):
        self.line, self.shards, self.wholes = line, shards, wholes
        self.sends, self.recvs, self.local_sems = sends, recvs, local_sems

    def copy(self, part, way, step, owner, fresh=False):
        line = self.line
        there = {UP: line.place + 2, DOWN: line.place - 2, PAIR: line.pair}[way]
        return pltpu.make_async_remote_copy(
            src_ref=self.shards[part] if fresh else self.wholes[part].at[owner],
            dst_ref=self.wholes[part].at[owner],
            send_sem=self.sends.at[way, step, part],
            recv_sem=self.recvs.at[way, step, part],
            device_id={"dp": there},
            device_id_type=MESH,
        )

    def local_copy(self, part):
        return pltpu.make_async_copy(
            self.shards[part], self.wholes[part].at[self.line.place], self.local_sems.at[part]
        )

    def start(self):
        line = self.line
        parts = range(len(self.shards))

        @pl.when(line.has_up)
        def _():
            for part in parts:
                self.copy(part, UP, 0, line.place, True).start()

        @pl.when(line.has_down)
        def _():
            for part in parts:
                self.copy(part, DOWN, 0, line.place, True).start()

        for part in parts:
            self.copy(part, PAIR, line.at, line.place, True).start()
            self.local_copy(part).start()

    def came(self, way, step):
        there = -step if way == UP else step
        spot = self.line.at + there
        return self.line.place + 2 * there, spot, (spot >= 0) & (spot < self.line.size)

    def hand_on(self, step, way):
        line = self.line
        owner, _, real = self.came(way, step)
        can = line.has_up if way == UP else line.has_down

        @pl.when(real)
        def _():
            for part in range(len(self.shards)):
                self.copy(part, way, step - 1, owner).wait_recv()

            @pl.when(can)
            def _():
                for part in range(len(self.shards)):
                    self.copy(part, way, step, owner).start()

    def hand_over(self, step, way, when=True):
        owner, spot, real = self.came(way, step)

        @pl.when(real & when)
        def _():
            for part in range(len(self.shards)):
                self.copy(part, PAIR, spot, owner).start()

    def tick(self, step):
        for way in (UP, DOWN):
            self.hand_on(step, way)
            self.hand_over(step, way)

    def finish(self):
        line = self.line
        parts = range(len(self.shards))
        for part in parts:
            self.local_copy(part).wait()

        def side(spot):
            for part in parts:
                self.copy(part, PAIR, spot, 2 * spot + line.side).wait()

        each(line.size, side)

        def along(step):
            for way, there, can in ((UP, -step, line.has_up), (DOWN, step, line.has_down)):
                spot = line.at + there

                @pl.when((spot >= 0) & (spot < line.size) & can)
                def _(way=way, there=there):
                    for part in parts:
                        self.copy(part, way, step, line.place + 2 * there).wait_send()

        each(line.size, along)


class Reduce:
    def __init__(self, line, terms, totals, own, pair_in, way_in, way_out, sends, recvs, own_sems):
        self.line, self.terms, self.totals, self.own = line, terms, totals, own
        self.own_sems = own_sems
        self.pair_in, self.way_in, self.way_out = pair_in, way_in, way_out
        self.sends, self.recvs = sends, recvs

    def pair_copy(self, part, spot):
        return pltpu.make_async_remote_copy(
            src_ref=self.terms[part].at[2 * spot + 1 - self.line.side],
            dst_ref=self.pair_in[part].at[spot],
            send_sem=self.sends.at[PAIR, spot, part],
            recv_sem=self.recvs.at[PAIR, spot, part],
            device_id={"dp": self.line.pair},
            device_id_type=MESH,
        )

    def way_copy(self, part, way, spot):
        there = self.line.place + 2 if way == UP else self.line.place - 2
        return pltpu.make_async_remote_copy(
            src_ref=self.way_out[part].at[way, spot],
            dst_ref=self.way_in[part].at[way, spot],
            send_sem=self.sends.at[way, spot, part],
            recv_sem=self.recvs.at[way, spot, part],
            device_id={"dp": there},
            device_id_type=MESH,
        )

    def start(self):
        self.load_own()
        each(self.line.size, self.send_pair)

    def own_copy(self, part, spot):
        return pltpu.make_async_copy(
            self.terms[part].at[2 * spot + self.line.side],
            self.own[part].at[spot],
            self.own_sems.at[part, spot],
        )

    def load_own(self):
        def load(spot):
            for part in range(len(self.terms)):
                self.own_copy(part, spot).start()

        each(self.line.size, load)

    def wait_own(self):
        def wait(spot):
            for part in range(len(self.terms)):
                self.own_copy(part, spot).wait()

        each(self.line.size, wait)

    def send_pair(self, step):
        line = self.line
        far = line.size - 1 - step

        @pl.when(line.at + far < line.size)
        def _():
            for part in range(len(self.terms)):
                self.pair_copy(part, line.at + far).start()

        @pl.when((line.at - far >= 0) & (far > 0))
        def _():
            for part in range(len(self.terms)):
                self.pair_copy(part, line.at - far).start()

    def pair_sum(self, part, spot):
        own = self.own[part][spot].astype(jnp.float32)
        return own + self.pair_in[part][spot].astype(jnp.float32)

    def pass_on(self, way, spot, more):
        for part in range(len(self.terms)):
            self.pair_copy(part, spot).wait_recv()
            self.way_out[part][way, spot] = self.pair_sum(part, spot).astype(jnp.bfloat16)

            @pl.when(more)
            def _(part=part):
                self.way_copy(part, way, spot).wait_recv()
                self.way_out[part][way, spot] = (
                    self.pair_sum(part, spot) + self.way_in[part][way, spot].astype(jnp.float32)
                ).astype(jnp.bfloat16)

            self.way_copy(part, way, spot).start()

    def tick(self, step):
        line = self.line
        far = line.size - 1 - step

        @pl.when(line.at + far < line.size)
        def _():
            self.pass_on(UP, line.at + far, line.has_down)

        @pl.when(line.at - far >= 0)
        def _():
            self.pass_on(DOWN, line.at - far, line.has_up)

    def finish(self):
        line = self.line
        spot = line.at
        for part in range(len(self.terms)):
            self.pair_copy(part, spot).wait_recv()
            self.totals[part][...] = self.pair_sum(part, spot)
        for way, can in ((UP, line.has_down), (DOWN, line.has_up)):

            @pl.when(can)
            def _(way=way):
                for part in range(len(self.terms)):
                    self.way_copy(part, way, spot).wait_recv()
                    self.totals[part][...] += self.way_in[part][way, spot].astype(jnp.float32)

        def close(spot):
            for part in range(len(self.terms)):
                self.pair_copy(part, spot).wait_send()
            for way, passed in ((UP, spot > line.at), (DOWN, spot < line.at)):

                @pl.when(passed)
                def _(way=way):
                    for part in range(len(self.terms)):
                        self.way_copy(part, way, spot).wait_send()

        each(line.size, close)


def run_ticks(task, first, last):
    if task is not None:
        for step in range(first, last):
            task.tick(step)


def head_slice(matrix, head):
    return matrix[:, head * HEAD_DIM : (head + 1) * HEAD_DIM]


def soft_rows(queries, keys_in):
    scores = dot_nt(queries, keys_in) * (HEAD_DIM ** (-0.5))
    exponent = jnp.exp(scores - jnp.max(scores, axis=-1, keepdims=True))
    return exponent / jnp.sum(exponent, axis=-1, keepdims=True)


def forward_kernel(
    layer_idx,
    res_ref,
    mod_ref,
    vec_ref,
    qkv_bias_ref,
    up_bias_ref,
    w_qkv_far,
    w_up_far,
    w_out_far,
    *rest,
):
    with_gather = len(rest) > 31
    shards, rest = (rest[:3], rest[3:]) if with_gather else ((), rest)
    res_out, kept = rest[0], rest[1:9]
    wholes, rest = (rest[9:12], rest[12:]) if with_gather else ((), rest[9:])
    rows_a, qkv_out, mixed_out, branch_out, mid_out, rows_m, upper_out, down_out = rest[:8]
    w_qkv_ref, w_up_ref, w_out_ref = rest[8:11]
    (
        part_a,
        near_a,
        far_out_a,
        far_in_a,
        part_m,
        near_m,
        far_out_m,
        far_in_m,
        sends,
        recvs,
        move_sems,
    ) = rest[11:22]
    group_width = w_qkv_ref.shape[1] // 3
    w_attn_ref, w_down_ref = w_out_ref.at[0:group_width, :], w_out_ref.at[group_width:, :]
    far = (w_qkv_far, w_out_far, w_up_far)
    pairs = list(zip(far, (w_qkv_ref, w_out_ref, w_up_ref))) + list(zip(rest[:8], kept))
    moves = Moves(pairs, move_sems)
    moves.start(0, 1, 2)
    images = res_ref.shape[0]
    gather, last_step = None, 0
    if with_gather:
        line = Line()
        greet(line)
        own = [shard.at[layer_idx + 1] for shard in shards]
        gather = Gather(line, own, wholes, *rest[22:])
        last_step = line.size
    else:
        greet(None)
    spread_a = Spread(rows_a, sends.at[0], recvs.at[0])
    spread_m = Spread(rows_m, sends.at[1], recvs.at[1])
    collect_a = Collect(part_a, near_a, far_out_a, far_in_a, sends.at[2], recvs.at[2])
    collect_m = Collect(part_m, near_m, far_out_m, far_in_m, sends.at[3], recvs.at[3])

    def mod_row(image, piece):
        return mod_ref[image, pl.ds(piece, 1), :]

    def start_norm(image):
        normed, _ = norm_parts(res_ref[image])
        normed = normed * (1.0 + mod_row(image, 1)) + mod_row(image, 0)
        spread_a.put(image, normed.astype(jnp.bfloat16))

    def attend(image):
        spread_a.wait(image)
        rows = rows_a[image]
        projected = dot_nn(rows, w_qkv_ref[...]) + qkv_bias_ref[...]
        qkv = projected.astype(jnp.bfloat16)
        qkv_out[image] = qkv
        heads = []
        for head in range(group_width // HEAD_DIM):
            probs = soft_rows(
                head_slice(qkv[:, :group_width], head),
                head_slice(qkv[:, group_width : 2 * group_width], head),
            )
            heads.append(
                dot_nn(probs.astype(jnp.bfloat16), head_slice(qkv[:, 2 * group_width :], head))
            )
        mixed = jnp.concatenate(heads, axis=1).astype(jnp.bfloat16)
        mixed_out[image] = mixed
        collect_a.put(image, dot_nn(mixed, w_attn_ref[...]))

    def middle(image):
        branch = collect_a.take(image) + vec_ref[0:1, :]
        branch_out[image] = branch
        mid = res_ref[image] + mod_row(image, 2) * branch
        mid_out[image] = mid
        normed, _ = norm_parts(mid)
        normed = normed * (1.0 + mod_row(image, 4)) + mod_row(image, 3)
        spread_m.put(image, normed.astype(jnp.bfloat16))

    def feed(image):
        spread_m.wait(image)
        upper = dot_nn(rows_m[image], w_up_ref[...]) + up_bias_ref[...]
        upper_out[image] = upper
        collect_m.put(image, dot_nn(gelu_tanh(upper).astype(jnp.bfloat16), w_down_ref[...]))

    def finish(image):
        down = collect_m.take(image) + vec_ref[1:2, :]
        down_out[image] = down
        res_out[image] = mid_out[image] + mod_row(image, 5) * down

    def close(image):
        spread_a.close(image)
        spread_m.close(image)
        collect_a.close(image)
        collect_m.close(image)

    if with_gather:
        gather.start()
    each(images, start_norm)
    each(images, spread_a.forward)
    moves.wait(0, 1)
    each(images, attend)
    moves.start(3, 4, 5)
    run_ticks(gather, 1, min(2, last_step))
    each(images, collect_a.forward)
    each(images, middle)
    moves.start(6, 7)
    each(images, spread_m.forward)
    run_ticks(gather, 2, min(3, last_step))
    moves.wait(2)
    each(images, feed)
    moves.start(8, 9)
    run_ticks(gather, 3, min(4, last_step))
    each(images, collect_m.forward)
    each(images, finish)
    moves.start(10)
    each(images, close)
    moves.wait(*range(3, 11))
    if with_gather:
        each(max(last_step - 4, 0), lambda step: gather.tick(step + 4))
        gather.finish()


def forward_layer(
    residual, mod_vec, vec_bias, qkv_bias, up_bias, w_qkv, w_up, w_out, shards, layer_idx
):
    images, count, _ = residual.shape
    tokens = 4 * count
    low, full = jnp.bfloat16, jnp.float32
    shapes = [
        ((images, count, D), full),
        ((images, tokens, D), low),
        ((images, tokens, w_qkv.shape[1]), low),
        ((images, tokens, w_qkv.shape[1] // 3), low),
        ((images, count, D), full),
        ((images, count, D), full),
        ((images, tokens, D), low),
        ((images, tokens, w_up.shape[1]), full),
        ((images, count, D), full),
    ]
    scratch = [
        pltpu.SemaphoreType.DMA((4, images, 3)),
        pltpu.SemaphoreType.DMA((4, images, 3)),
        pltpu.SemaphoreType.DMA((11,)),
    ]
    near = [pltpu.VMEM(*shape) for shape in shapes[1:]]
    near += [pltpu.VMEM(weight.shape, low) for weight in (w_qkv, w_up, w_out)]
    if shards:
        dp_size = lax.axis_size("dp")
        shapes += [((dp_size,) + shard.shape[1:], low) for shard in shards]
        scratch += [
            pltpu.SemaphoreType.DMA((3, dp_size // 2, 3)),
            pltpu.SemaphoreType.DMA((3, dp_size // 2, 3)),
            pltpu.SemaphoreType.DMA((3,)),
        ]
    return pl.pallas_call(
        functools.partial(forward_kernel, layer_idx),
        out_shape=[jax.ShapeDtypeStruct(*shape) for shape in shapes],
        in_specs=[pl.BlockSpec(memory_space=pltpu.VMEM)] * 5
        + [pl.BlockSpec(memory_space=pl.ANY)] * (3 + len(shards)),
        out_specs=[pl.BlockSpec(memory_space=pltpu.VMEM)]
        + [pl.BlockSpec(memory_space=pl.ANY)] * (len(shapes) - 1),
        scratch_shapes=near
        + collect_scratch(images, tokens)
        + collect_scratch(images, tokens)
        + scratch,
        compiler_params=pltpu.CompilerParams(
            collective_id=16 + layer_idx, has_side_effects=True, vmem_limit_bytes=ACT_VMEM
        ),
        cost_estimate=pl.CostEstimate(
            flops=30 * 10**9, bytes_accessed=15 * 2**20, transcendentals=0
        ),
        name="block_forward",
    )(residual, mod_vec, vec_bias, qkv_bias, up_bias, w_qkv, w_up, w_out, *shards)


def flat(ref):
    value = ref[...]
    return value.reshape(-1, value.shape[-1])


def forward_all_kernel(
    count_all,
    res_ref,
    mod_ref,
    vec_ref,
    qkv_bias_ref,
    up_bias_ref,
    final_shift_ref,
    final_scale_ref,
    head_ref,
    targets_ref,
    qkv_far,
    up_far,
    out_far,
    *rest,
):
    shards, rest = rest[0:3], rest[3:]
    d_res_out, d_head_out, loss_out, d_shift_out, d_scale_out = rest[0:5]
    kept_far, whole_far = rest[5:14], rest[14:17]
    kept, rest = rest[17:26], rest[26:]
    res_all, rows_a_all, qkv_all, mixed_all, branch_all, mid_all, rows_m_all, upper_all, down_all = kept
    w_qkv_all, w_up_all, w_blocks_all, w_out_all = rest[0:4]
    part_a, near_a, far_out_a, far_in_a, part_m, near_m, far_out_m, far_in_m = rest[4:12]
    sends, recvs, keep_sems, load_sems, whole_sems, gather_sends, gather_recvs, local_sems = rest[12:]
    images = res_ref.shape[0]
    group_width = w_qkv_all.shape[-1] // 3
    line = Line()
    last_step = line.size
    loads = Moves(
        [(qkv_far, w_qkv_all.at[0]), (out_far, w_blocks_all.at[0]), (up_far, w_up_all.at[0])],
        load_sems,
    )
    loads.start(0, 1, 2)
    greet(line)
    gathers = [None]
    for layer_idx in range(1, LAYERS):
        gathers.append(
            Gather(
                line,
                [shard.at[layer_idx] for shard in shards],
                [whole.at[layer_idx] for whole in (w_qkv_all, w_up_all, w_blocks_all)],
                gather_sends.at[layer_idx],
                gather_recvs.at[layer_idx],
                local_sems.at[layer_idx],
            )
        )
    gathers.append(None)

    def join_blocks(layer_idx):
        rows = w_blocks_all.shape[2]
        for pair in range(w_blocks_all.shape[1] // 2):
            halves = [
                w_blocks_all[layer_idx, 2 * pair + side].astype(jnp.float32) for side in range(2)
            ]
            w_out_all[layer_idx, 2 * rows * pair : 2 * rows * (pair + 1), :] = jnp.concatenate(
                halves, axis=0
            ).astype(jnp.bfloat16)

    def mod_row(layer_idx, image, piece):
        return mod_ref[layer_idx, image, pl.ds(piece, 1), :]

    d_head_out[...] = jnp.zeros_like(d_head_out)
    loss_out[...] = jnp.zeros_like(loss_out)

    def final_loss(image, value):
        normed, _ = norm_parts(value)
        final_in = normed * (1.0 + final_scale_ref[image]) + final_shift_ref[image]
        error_all = dense_nt(final_in, head_ref[...]) - targets_ref[image]
        loss_out[...] += square_sum(error_all) / count_all
        d_pred = 2.0 * error_all / count_all
        d_head_out[...] += dense_tn(d_pred, final_in)
        d_value, d_shift, d_scale = norm_pull(
            value, final_scale_ref[image], dense(d_pred, head_ref[...])
        )
        d_shift_out[image] = d_shift
        d_scale_out[image] = d_scale
        d_res_out[image] = d_value

    for layer_idx in range(LAYERS):
        res, rows_a, qkv_out, mixed_out, branch_out, mid_out, rows_m, upper_out, down_out = [
            ref.at[layer_idx] for ref in kept
        ]
        w_qkv, w_up, w_out = w_qkv_all.at[layer_idx], w_up_all.at[layer_idx], w_out_all.at[layer_idx]
        w_attn, w_down = w_out.at[0:group_width, :], w_out.at[group_width:, :]
        spread_a = Spread(rows_a, sends.at[layer_idx, 0], recvs.at[layer_idx, 0])
        spread_m = Spread(rows_m, sends.at[layer_idx, 1], recvs.at[layer_idx, 1])
        collect_a = Collect(
            part_a,
            near_a.at[layer_idx],
            far_out_a.at[layer_idx],
            far_in_a.at[layer_idx],
            sends.at[layer_idx, 2],
            recvs.at[layer_idx, 2],
        )
        collect_m = Collect(
            part_m,
            near_m.at[layer_idx],
            far_out_m.at[layer_idx],
            far_in_m.at[layer_idx],
            sends.at[layer_idx, 3],
            recvs.at[layer_idx, 3],
        )
        keep = Moves(
            [(ref.at[layer_idx], far.at[layer_idx]) for ref, far in zip(kept, kept_far)],
            keep_sems.at[layer_idx],
        )
        keep_whole = Moves(
            [
                (ref.at[layer_idx], far.at[layer_idx])
                for ref, far in zip((w_qkv_all, w_up_all, w_out_all), whole_far)
            ],
            whole_sems.at[layer_idx],
        )
        gather = gathers[layer_idx + 1]

        def start_norm(image, at, values, target):
            normed, _ = norm_parts(values)
            normed = normed * (1.0 + mod_row(at, image, 1)) + mod_row(at, image, 0)
            target.put(image, normed.astype(jnp.bfloat16))

        def first_norm(image, res=res, spread_a=spread_a):
            res[image] = res_ref[image]
            start_norm(image, 0, res_ref[image], spread_a)

        def attend(image):
            spread_a.wait(image)
            projected = dot_nn(rows_a[image], flat(w_qkv)) + qkv_bias_ref[layer_idx]
            qkv = projected.astype(jnp.bfloat16)
            qkv_out[image] = qkv
            heads = []
            for head in range(group_width // HEAD_DIM):
                probs = soft_rows(
                    head_slice(qkv[:, :group_width], head),
                    head_slice(qkv[:, group_width : 2 * group_width], head),
                )
                heads.append(
                    dot_nn(probs.astype(jnp.bfloat16), head_slice(qkv[:, 2 * group_width :], head))
                )
            mixed = jnp.concatenate(heads, axis=1).astype(jnp.bfloat16)
            mixed_out[image] = mixed
            collect_a.put(image, dot_nn(mixed, w_attn[...]))

        def middle(image):
            branch = collect_a.take(image) + vec_ref[layer_idx, 0:1, :]
            branch_out[image] = branch
            mid = res[image] + mod_row(layer_idx, image, 2) * branch
            mid_out[image] = mid
            normed, _ = norm_parts(mid)
            normed = normed * (1.0 + mod_row(layer_idx, image, 4)) + mod_row(layer_idx, image, 3)
            spread_m.put(image, normed.astype(jnp.bfloat16))

        def feed(image):
            spread_m.wait(image)
            upper = dot_nn(rows_m[image], flat(w_up)) + up_bias_ref[layer_idx]
            upper_out[image] = upper
            collect_m.put(image, dot_nn(gelu_tanh(upper).astype(jnp.bfloat16), w_down[...]))

        def finish(image):
            down = collect_m.take(image) + vec_ref[layer_idx, 1:2, :]
            down_out[image] = down
            value = mid_out[image] + mod_row(layer_idx, image, 5) * down
            if layer_idx + 1 < LAYERS:
                res_all[layer_idx + 1, image] = value
                following = Spread(
                    rows_a_all.at[layer_idx + 1],
                    sends.at[layer_idx + 1, 0],
                    recvs.at[layer_idx + 1, 0],
                )
                start_norm(image, layer_idx + 1, value, following)
            else:
                final_loss(image, value)

        def close(image):
            spread_a.close(image)
            spread_m.close(image)
            collect_a.close(image)
            collect_m.close(image)

        if layer_idx == 0:
            gather.start()
            each(images, first_norm)
        each(images, spread_a.forward)
        if layer_idx == 0:
            loads.wait(0, 1)
            join_blocks(0)
        each(images, attend)
        keep.start(0, 1, 2, 3)
        run_ticks(gather, 1, min(2, last_step))
        each(images, collect_a.forward)
        each(images, middle)
        keep.start(4, 5)
        each(images, spread_m.forward)
        run_ticks(gather, 2, min(3, last_step))
        if layer_idx == 0:
            loads.wait(2)
        each(images, feed)
        keep.start(6, 7)
        run_ticks(gather, 3, min(4, last_step))
        each(images, collect_m.forward)
        each(images, finish)
        keep.start(8)
        keep_whole.start(0, 1, 2)
        each(images, close)
        if gather is not None:
            each(max(last_step - 4, 0), lambda step, gather=gather: gather.tick(step + 4))
            if gathers[layer_idx + 2] is not None:
                gathers[layer_idx + 2].start()
            gather.finish()
            join_blocks(layer_idx + 1)
        keep.wait(*range(9))
        keep_whole.wait(0, 1, 2)


def forward_all(
    count_all, residual, mod_vecs, vec_bias, qkv_bias, up_bias, finals, wholes, shards
):
    images, count, _ = residual.shape
    tokens = 4 * count
    low, full = jnp.bfloat16, jnp.float32
    dp_size = lax.axis_size("dp")
    qkv_width, units = wholes[0].shape[-1], wholes[1].shape[-1]
    own = (images, count, D)
    kept = [
        (own, full),
        ((images, tokens, D), low),
        ((images, tokens, qkv_width), low),
        ((images, tokens, qkv_width // 3), low),
        (own, full),
        (own, full),
        ((images, tokens, D), low),
        ((images, tokens, units), full),
        (own, full),
    ]
    kept = [((LAYERS,) + shape, kind) for shape, kind in kept]
    out_rows = wholes[2].shape[0] * wholes[2].shape[1]
    matrices = [
        ((LAYERS,) + wholes[0].shape, low),
        ((LAYERS,) + wholes[1].shape, low),
        ((LAYERS, out_rows, D), low),
    ]
    shapes = [(own, full), (finals[2].shape, full), ((1, 1), full)]
    shapes += [(finals[0].shape, full), (finals[1].shape, full)]
    shapes += kept + matrices
    collect = [
        pltpu.VMEM((images, tokens, D), low),
        pltpu.VMEM((LAYERS, images, 2, count, D), low),
        pltpu.VMEM((LAYERS, images, count, D), low),
        pltpu.VMEM((LAYERS, images, count, D), low),
    ]
    return pl.pallas_call(
        functools.partial(forward_all_kernel, count_all),
        out_shape=[jax.ShapeDtypeStruct(*shape) for shape in shapes],
        in_specs=[pl.BlockSpec(memory_space=pltpu.VMEM)] * 9
        + [pl.BlockSpec(memory_space=pl.ANY)] * 6,
        out_specs=[pl.BlockSpec(memory_space=pltpu.VMEM)] * 5
        + [pl.BlockSpec(memory_space=pl.ANY)] * (len(shapes) - 5),
        scratch_shapes=[pltpu.VMEM(*shape) for shape in kept]
        + [
            pltpu.VMEM(*matrices[0]),
            pltpu.VMEM(*matrices[1]),
            pltpu.VMEM((LAYERS,) + wholes[2].shape, low),
            pltpu.VMEM(*matrices[2]),
        ]
        + collect
        + collect
        + [
            pltpu.SemaphoreType.DMA((LAYERS, 4, images, 3)),
            pltpu.SemaphoreType.DMA((LAYERS, 4, images, 3)),
            pltpu.SemaphoreType.DMA((LAYERS, 9)),
            pltpu.SemaphoreType.DMA((3,)),
            pltpu.SemaphoreType.DMA((LAYERS, 3)),
            pltpu.SemaphoreType.DMA((LAYERS, 3, dp_size // 2, 3)),
            pltpu.SemaphoreType.DMA((LAYERS, 3, dp_size // 2, 3)),
            pltpu.SemaphoreType.DMA((LAYERS, 3)),
        ],
        compiler_params=pltpu.CompilerParams(
            collective_id=24, has_side_effects=True, vmem_limit_bytes=ACT_VMEM
        ),
        name="blocks_forward",
    )(residual, mod_vecs, vec_bias, qkv_bias, up_bias, *finals, *wholes, *shards)


def gelu_slope(values):
    root = math.sqrt(2.0 / math.pi)
    square = values * values
    tanh = jnp.tanh(root * (values + 0.044715 * values * square))
    half = 0.5 * (1.0 + tanh)
    slope = half + 0.5 * values * (1.0 - tanh * tanh) * root * (1.0 + 3.0 * 0.044715 * square)
    return values * half, slope


def norm_pull(values, scale_row, d_normed):
    normed, rstd = norm_parts(values)
    d_shift = jnp.sum(d_normed, axis=0, keepdims=True)
    d_scale = jnp.sum(d_normed * normed, axis=0, keepdims=True)
    inner = d_normed * (1.0 + scale_row)
    mean_one = jnp.mean(inner, axis=-1, keepdims=True)
    mean_two = jnp.mean(inner * normed, axis=-1, keepdims=True)
    return (inner - mean_one - normed * mean_two) * rstd, d_shift, d_scale


def backward_kernel(layer_idx, d_res_ref, mod_ref, *rest):
    kept, rest = rest[:12], rest[12:]
    if layer_idx is not None:
        kept = [ref.at[layer_idx] for ref in kept]
    with_reduce = len(rest) > 40
    terms, rest = (rest[:3], rest[3:]) if with_reduce else ((), rest)
    d_res_out, d_far, (d_mod, d_vec, d_qkv_bias, d_up_bias) = rest[0], rest[1:4], rest[4:8]
    totals, square_out = (rest[8:11], rest[11]) if with_reduce else ((), None)
    rest = rest[12:] if with_reduce else rest[8:]
    (
        res_ref,
        rows_a,
        qkv_ref,
        mixed_ref,
        branch_ref,
        mid_ref,
        rows_m,
        upper_ref,
        down_ref,
        w_qkv_ref,
        w_up_ref,
        w_out_ref,
        d_w_qkv,
        d_w_up,
        d_out,
    ) = rest[:15]
    (
        d_mid,
        d_rows_m,
        d_rows_a,
        act_low,
        d_upper,
        d_qkv,
        part_a,
        near_a,
        far_out_a,
        far_in_a,
        part_m,
        near_m,
        far_out_m,
        far_in_m,
        sends,
        recvs,
        move_sems,
    ) = rest[15:32]
    group_width = w_qkv_ref.shape[-1] // 3
    w_attn_ref, w_down_ref = w_out_ref.at[0:group_width, :], w_out_ref.at[group_width:, :]
    pairs = list(zip(kept, rest[:12])) + list(zip(rest[12:15], d_far))
    moves = Moves(pairs, move_sems)
    moves.start(8, 11, 7, 10, 6, 5, 4, 2, 9, 3, 1, 0)
    images = res_ref.shape[0]
    tokens = rows_a.shape[1]
    qkv_width = 3 * group_width
    units = w_up_ref.shape[-1]
    reduce, last_step = None, 0
    if with_reduce:
        line = Line()
        greet(line)
        own, pair_in, way_in, way_out = rest[32:35], rest[35:38], rest[38:41], rest[41:44]
        reduce = Reduce(line, terms, totals, own, pair_in, way_in, way_out, *rest[44:])
        last_step = line.size
    else:
        greet(None)
    spread_m = Spread(d_rows_m, sends.at[0], recvs.at[0])
    spread_a = Spread(d_rows_a, sends.at[1], recvs.at[1])
    collect_m = Collect(part_m, near_m, far_out_m, far_in_m, sends.at[2], recvs.at[2])
    collect_a = Collect(part_a, near_a, far_out_a, far_in_a, sends.at[3], recvs.at[3])
    d_vec[...] = jnp.zeros_like(d_vec)
    d_qkv_bias[...] = jnp.zeros_like(d_qkv_bias)
    d_up_bias[...] = jnp.zeros_like(d_up_bias)

    def mod_row(image, piece):
        return mod_ref[image, pl.ds(piece, 1), :]

    def start_down(image):
        d_res = d_res_ref[image]
        d_mod[image, pl.ds(5, 1), :] = jnp.sum(d_res * down_ref[image], axis=0, keepdims=True)
        d_down = d_res * mod_row(image, 5)
        d_vec[1:2, :] += jnp.sum(d_down, axis=0, keepdims=True)
        spread_m.put(image, d_down.astype(jnp.bfloat16))

    def feed(image):
        spread_m.wait(image)
        d_act = dot_nt(d_rows_m[image], w_down_ref[...])
        act, slope = gelu_slope(upper_ref[image])
        act_low[image] = act.astype(jnp.bfloat16)
        d_up = d_act * slope
        d_up_bias[...] += jnp.sum(d_up, axis=0, keepdims=True)
        d_up_low = d_up.astype(jnp.bfloat16)
        d_upper[image] = d_up_low
        collect_m.put(image, dot_nt(d_up_low, flat(w_up_ref)))

    def rows_of(ref, width):
        return ref[...].reshape(images * tokens, width)

    def feed_weights():
        tile = 256

        def step(index, carry):
            at = pl.ds(pl.multiple_of(index * tile, tile), tile)
            grad = dot_tn(
                act_low[:, :, at].reshape(images * tokens, tile), rows_of(d_rows_m, D)
            )
            d_out[pl.ds(pl.multiple_of(group_width + index * tile, 64), tile), :] = grad.astype(
                jnp.bfloat16
            )
            grad = dot_tn(
                rows_m[:, :, at].reshape(images * tokens, tile), rows_of(d_upper, units)
            )
            d_w_up[pl.ds(pl.multiple_of(index * tile, tile), tile), :] = grad.astype(jnp.bfloat16)
            return carry

        lax.fori_loop(0, units // tile, step, 0)

    def middle(image):
        d_value, d_shift, d_scale = norm_pull(
            mid_ref[image], mod_row(image, 4), collect_m.take(image)
        )
        d_mod[image, pl.ds(3, 1), :] = d_shift
        d_mod[image, pl.ds(4, 1), :] = d_scale
        d_value = d_res_ref[image] + d_value
        d_mid[image] = d_value
        d_mod[image, pl.ds(2, 1), :] = jnp.sum(d_value * branch_ref[image], axis=0, keepdims=True)
        d_branch = d_value * mod_row(image, 2)
        d_vec[0:1, :] += jnp.sum(d_branch, axis=0, keepdims=True)
        spread_a.put(image, d_branch.astype(jnp.bfloat16))

    def attend(image):
        spread_a.wait(image)
        d_mixed = dot_nt(d_rows_a[image], w_attn_ref[...]).astype(jnp.bfloat16)
        qkv = qkv_ref[image]
        d_queries, d_keys, d_values = [], [], []
        scale_dot = HEAD_DIM ** (-0.5)
        for head in range(group_width // HEAD_DIM):
            queries = head_slice(qkv[:, :group_width], head)
            keys_in = head_slice(qkv[:, group_width : 2 * group_width], head)
            values_in = head_slice(qkv[:, 2 * group_width :], head)
            d_head = head_slice(d_mixed, head)
            probs = soft_rows(queries, keys_in)
            d_probs = dot_nt(d_head, values_in)
            d_values.append(dot_tn(probs.astype(jnp.bfloat16), d_head))
            inner = jnp.sum(probs * d_probs, axis=-1, keepdims=True)
            d_scores = (probs * (d_probs - inner)).astype(jnp.bfloat16)
            d_queries.append(dot_nn(d_scores, keys_in) * scale_dot)
            d_keys.append(dot_tn(d_scores, queries) * scale_dot)
        joined = jnp.concatenate(d_queries + d_keys + d_values, axis=1)
        d_qkv_bias[...] += jnp.sum(joined, axis=0, keepdims=True)
        joined = joined.astype(jnp.bfloat16)
        d_qkv[image] = joined
        collect_a.put(image, dot_nt(joined, flat(w_qkv_ref)))

    def attend_weights():
        d_out[0:group_width, :] = dot_tn(
            rows_of(mixed_ref, group_width), rows_of(d_rows_a, D)
        ).astype(jnp.bfloat16)
        tile = 256

        def step(index, carry):
            at = pl.ds(pl.multiple_of(index * tile, tile), tile)
            grad = dot_tn(
                rows_a[:, :, at].reshape(images * tokens, tile), rows_of(d_qkv, qkv_width)
            )
            d_w_qkv[at, :] = grad.astype(jnp.bfloat16)
            return carry

        lax.fori_loop(0, D // tile, step, 0)

    def finish(image):
        d_value, d_shift, d_scale = norm_pull(
            res_ref[image], mod_row(image, 1), collect_a.take(image)
        )
        d_mod[image, pl.ds(0, 1), :] = d_shift
        d_mod[image, pl.ds(1, 1), :] = d_scale
        d_res_out[image] = d_mid[image] + d_value

    def close(image):
        spread_a.close(image)
        spread_m.close(image)
        collect_a.close(image)
        collect_m.close(image)

    if with_reduce:
        reduce.start()
    moves.wait(8)
    each(images, start_down)
    each(images, spread_m.forward)
    moves.wait(11, 7, 10)
    each(images, feed)
    if with_reduce:
        reduce.wait_own()
    run_ticks(reduce, 0, min(1, last_step - 1))
    each(images, collect_m.forward)
    moves.wait(6)
    feed_weights()
    moves.start(13)
    run_ticks(reduce, 1, min(2, last_step - 1))
    moves.wait(5, 4)
    each(images, middle)
    each(images, spread_a.forward)
    moves.wait(2, 9)
    each(images, attend)
    each(images, collect_a.forward)
    run_ticks(reduce, 2, min(3, last_step - 1))
    moves.wait(3, 1)
    attend_weights()
    moves.start(12, 14)
    moves.wait(0)
    each(images, finish)
    each(images, close)
    if with_reduce:
        each(max(last_step - 4, 0), lambda step: reduce.tick(step + 3))
        reduce.finish()
        square_out[...] = jnp.broadcast_to(
            sum(square_sum(total[...]) for total in totals), square_out.shape
        )
    moves.wait(12, 13, 14)


def backward_layer(d_residual, mod_vec, saved, weights, terms, layer_idx, stacked):
    images, count, _ = d_residual.shape
    tokens = 4 * count
    low, full = jnp.bfloat16, jnp.float32
    w_qkv, w_up, w_out = weights
    group_width, units = w_qkv.shape[-1] // 3, w_up.shape[-1]
    shapes = [
        ((images, count, D), full),
        ((D, 3 * group_width), low),
        ((D, units), low),
        ((group_width + units, D), low),
        ((images, 6, D), full),
        ((2, D), full),
        ((1, 3 * group_width), full),
        ((1, units), full),
    ]
    scratch = [
        pltpu.SemaphoreType.DMA((4, images, 3)),
        pltpu.SemaphoreType.DMA((4, images, 3)),
        pltpu.SemaphoreType.DMA((15,)),
    ]
    near = [
        pltpu.VMEM(kept.shape[1:] if stacked else kept.shape, kept.dtype)
        for kept in tuple(saved) + tuple(weights)
    ]
    near += [pltpu.VMEM(*shape) for shape in shapes[1:4]]
    if terms:
        spots = lax.axis_size("dp") // 2
        blocks = [term.shape[1:] for term in terms]
        shapes += [(block, full) for block in blocks] + [((8, 128), full)]
        scratch += [pltpu.VMEM((spots,) + block, low) for block in blocks]
        scratch += [pltpu.VMEM((spots,) + block, low) for block in blocks]
        scratch += [pltpu.VMEM((2, spots) + block, low) for block in blocks]
        scratch += [pltpu.VMEM((2, spots) + block, low) for block in blocks]
        scratch += [
            pltpu.SemaphoreType.DMA((3, spots, 3)),
            pltpu.SemaphoreType.DMA((3, spots, 3)),
            pltpu.SemaphoreType.DMA((3, spots)),
        ]
    return pl.pallas_call(
        functools.partial(backward_kernel, layer_idx if stacked else None),
        out_shape=[jax.ShapeDtypeStruct(*shape) for shape in shapes],
        in_specs=[pl.BlockSpec(memory_space=pltpu.VMEM)] * 2
        + [pl.BlockSpec(memory_space=pl.ANY)] * (12 + len(terms)),
        out_specs=[pl.BlockSpec(memory_space=pltpu.VMEM)]
        + [pl.BlockSpec(memory_space=pl.ANY)] * 3
        + [pl.BlockSpec(memory_space=pltpu.VMEM)] * (len(shapes) - 4),
        scratch_shapes=near
        + [
            pltpu.VMEM((images, count, D), full),
            pltpu.VMEM((images, tokens, D), low),
            pltpu.VMEM((images, tokens, D), low),
            pltpu.VMEM((images, tokens, units), low),
            pltpu.VMEM((images, tokens, units), low),
            pltpu.VMEM((images, tokens, 3 * group_width), low),
        ]
        + collect_scratch(images, tokens)
        + collect_scratch(images, tokens)
        + scratch,
        compiler_params=pltpu.CompilerParams(
            collective_id=20 + layer_idx if stacked else (21 if terms else 23), has_side_effects=True, vmem_limit_bytes=ACT_VMEM
        ),
        cost_estimate=pl.CostEstimate(
            flops=60 * 10**9, bytes_accessed=25 * 2**20, transcendentals=0
        ),
        name="block_backward",
    )(d_residual, mod_vec, *saved, *weights, *terms)


def dense_nt(left_op, right_op):
    return lax.dot_general(
        left_op,
        right_op,
        (((1,), (1,)), ((), ())),
        precision=PRECISE,
        preferred_element_type=jnp.float32,
    )


def dense_tn(left_op, right_op):
    return lax.dot_general(
        left_op,
        right_op,
        (((0,), (0,)), ((), ())),
        precision=PRECISE,
        preferred_element_type=jnp.float32,
    )


def chosen(shape, rule, kind):
    row = lax.broadcasted_iota(jnp.int32, shape, 0)
    col = lax.broadcasted_iota(jnp.int32, shape, 1)
    return jnp.where(rule(row, col), 1.0, 0.0).astype(kind)


def fold(values):
    groups = values.shape[-2] // 8
    pieces = [values[..., 8 * at : 8 * at + 8, :] for at in range(groups)]
    used = groups * values.shape[-1]
    if used % 128:
        pieces.append(jnp.zeros(values.shape[:-2] + (8, 128 - used % 128), values.dtype))
    return jnp.concatenate(pieces, axis=-1)


def folded_lanes(cols, count):
    return -(-(cols // 8 * count) // 128) * 128


def unfold_all(values, cols, count):
    ordered = [
        values[tensor_at, dp_at]
        for dp_at in range(values.shape[1])
        for tensor_at in range(values.shape[0])
    ]
    return jnp.concatenate([unfold(value, cols, count) for value in ordered], axis=0)


def unfold(values, cols, count):
    pieces = [values[..., at * count : (at + 1) * count] for at in range(cols // 8)]
    return jnp.concatenate(pieces, axis=-2)


def slots_of(images):
    return -(-LAYERS * images // 16) * 16


def head_kernel(
    images,
    small_ref,
    feats_ref,
    table_ref,
    time_ref,
    second_ref,
    shift_ref,
    scale_ref,
    bias_ref,
    mod_ref,
    *rest,
):
    shards = rest[0:3]
    (
        small_all,
        feats_out,
        pre_time_out,
        hidden_out,
        pre_signal_out,
        signal_out,
        final_all,
        mod_all,
    ) = rest[3:11]
    wholes = rest[11:14]
    (
        feats_all,
        hidden_own,
        hidden_dp,
        hidden_all,
        signal_own,
        signal_dp,
        signal_all,
        final_own,
        final_dp,
        mod_part,
        mod_in,
        mod_own,
        small_dp,
    ) = rest[14:27]
    crowds = [rest[27 + 3 * index : 30 + 3 * index] for index in range(11)]
    gather_sems = rest[60:]
    dp_size = lax.axis_size("dp")
    tensor_size = lax.axis_size("tensor")
    dp_rank = lax.axis_index("dp")
    images_all = images * dp_size
    slots = mod_own.shape[0]
    greet_groups("dp", "tensor")
    gather = Gather(Line(), [shard.at[0] for shard in shards], wholes, *gather_sems)
    feats = Crowd("dp", lambda place: feats_ref, feats_all, *crowds[0])
    mod_sum = Crowd("dp", lambda place: mod_part.at[place], mod_in, *crowds[1])
    mod_spread = Crowd("tensor", lambda place: mod_own, mod_all, *crowds[2])
    small = Relay(lambda place: small_ref, small_dp, small_all, *crowds[3:5])
    hidden = Relay(lambda place: hidden_own, hidden_dp, hidden_all, *crowds[5:7])
    signal = Relay(lambda place: signal_own, signal_dp, signal_all, *crowds[7:9])
    final = Relay(lambda place: final_own.at[place], final_dp, final_all, *crowds[9:11])
    line = gather.line
    first, last = line.at == 0, line.at == line.size - 1
    feats.start()
    gather.start()
    feats.wait()
    pick = chosen(
        (images_all, 8 * dp_size),
        lambda row, col: (row // images == col // 8) & (lax.rem(row, images) == lax.rem(col, 8)),
        jnp.float32,
    )
    feats_sum = dense(pick, feats_all[...].reshape(8 * dp_size, feats_all.shape[2]))
    feats_out[...] = feats_sum
    pre_time = dense_nt(time_ref[...], feats_sum[:, 0:FREQ]) + bias_ref[:, 1:2]
    pre_time_out[...] = pre_time
    hidden_own[...] = fold(jax.nn.silu(pre_time))
    hidden.start()
    class_lanes = -(-CLASSES // 128) * 128
    labels = jnp.round(feats_sum[:, FREQ : FREQ + 1]).astype(jnp.int32)
    lane = lax.broadcasted_iota(jnp.int32, (images_all, class_lanes), 1)
    onehot = jnp.where(lane == labels, 1.0, 0.0)
    class_part = dense_nt(table_ref[:, 0:class_lanes], onehot) + bias_ref[:, 2:3]
    small.start()
    hidden.hand_on()
    for way in (UP, DOWN):
        gather.hand_on(1, way)
    gather.hand_over(1, UP)
    gather.hand_over(1, DOWN, first)
    hidden.wait()
    cols = second_ref.shape[0]
    hidden_full = unfold_all(hidden_all[...], cols, images_all)
    hidden_out[...] = hidden_full
    pre_signal = dense(second_ref[...], hidden_full) + class_part
    pre_signal_out[...] = pre_signal
    signal_own[...] = fold(jax.nn.silu(pre_signal))
    signal.start()
    small.hand_on()
    signal.hand_on()
    for way in (UP, DOWN):
        gather.hand_on(2, way)
    gather.hand_over(1, DOWN, jnp.logical_not(first))
    gather.hand_over(2, UP, last)
    gather.hand_over(2, DOWN, first)
    signal.wait()
    signal_full = unfold_all(signal_all[...], cols, images_all)
    signal_out[...] = signal_full
    mod_rows = mod_ref.shape[1]
    own_rows = pl.ds(pl.multiple_of(dp_rank * mod_rows, 8), mod_rows)
    signal_low = signal_out[own_rows, :].astype(jnp.bfloat16)
    total = None
    for layer_idx in range(LAYERS):
        pick = chosen(
            (images_all, dp_size * slots),
            lambda row, col: (
                (row // images == col // slots)
                & (lax.rem(row, images) + layer_idx * images == lax.rem(col, slots))
            ),
            jnp.bfloat16,
        )
        placed = dot_nn(signal_low, pick).astype(jnp.bfloat16)
        term = dot_tn(placed, mod_ref[layer_idx])
        total = term if total is None else total + term
    mod_part[...] = total.reshape(mod_part.shape).astype(mod_part.dtype)
    mod_sum.start()
    gather.hand_over(2, UP, jnp.logical_not(last))
    gather.hand_over(2, DOWN, jnp.logical_not(first))
    finals = jnp.concatenate(
        [
            dense(shift_ref[...], signal_full) + bias_ref[:, 3:4],
            dense(scale_ref[...], signal_full) + bias_ref[:, 4:5],
            jnp.zeros((128 - 2 * shift_ref.shape[0], images_all), jnp.float32),
        ],
        axis=0,
    )
    pick = chosen(
        (8 * dp_size, images_all),
        lambda row, col: (row // 8 == col // images) & (lax.rem(row, 8) == lax.rem(col, images)),
        jnp.float32,
    )
    final_own[...] = dense_nt(pick, finals).reshape(final_own.shape)
    final.start()
    run_ticks(gather, 3, min(4, dp_size // 2))
    mod_sum.wait()
    mod_own[...] = jnp.sum(mod_in[...].astype(jnp.float32), axis=0)
    mod_spread.start()
    final.hand_on()
    each(max(dp_size // 2 - 4, 0), lambda step: gather.tick(step + 4))
    small.wait()
    final.wait()
    mod_spread.wait()
    gather.finish()


def head_call(small, feats, table, times, second, shift, scale, bias, mod_low, shards, images):
    dp_size, tensor_size = lax.axis_size("dp"), lax.axis_size("tensor")
    images_all = images * dp_size
    cols = table.shape[0]
    slots = slots_of(images)
    folded = folded_lanes(cols, images_all)
    full, low = jnp.float32, jnp.bfloat16
    shapes = [
        ((tensor_size, dp_size) + small.shape, full),
        ((images_all, feats.shape[1]), full),
        ((cols, images_all), full),
        ((D, images_all), full),
        ((cols, images_all), full),
        ((D, images_all), full),
        ((tensor_size, dp_size, 8, 128), full),
        ((tensor_size, slots, mod_low.shape[2]), full),
    ] + [((dp_size,) + shard.shape[1:], low) for shard in shards]
    scratch = [
        pltpu.VMEM((dp_size,) + feats.shape, full),
        pltpu.VMEM((8, folded), full),
        pltpu.VMEM((dp_size, 8, folded), full),
        pltpu.VMEM((tensor_size, dp_size, 8, folded), full),
        pltpu.VMEM((8, folded), full),
        pltpu.VMEM((dp_size, 8, folded), full),
        pltpu.VMEM((tensor_size, dp_size, 8, folded), full),
        pltpu.VMEM((dp_size, 8, 128), full),
        pltpu.VMEM((dp_size, 8, 128), full),
        pltpu.VMEM((dp_size, slots, mod_low.shape[2]), low),
        pltpu.VMEM((dp_size, slots, mod_low.shape[2]), low),
        pltpu.VMEM((slots, mod_low.shape[2]), full),
        pltpu.VMEM((dp_size,) + small.shape, full),
    ]
    for count in (dp_size, dp_size) + (tensor_size, dp_size) * 4 + (tensor_size,):
        scratch += crowd_scratch(count)
    scratch += [
        pltpu.SemaphoreType.DMA((3, dp_size // 2, 3)),
        pltpu.SemaphoreType.DMA((3, dp_size // 2, 3)),
        pltpu.SemaphoreType.DMA((3,)),
    ]
    return pl.pallas_call(
        functools.partial(head_kernel, images),
        out_shape=[jax.ShapeDtypeStruct(*shape) for shape in shapes],
        in_specs=[pl.BlockSpec(memory_space=pltpu.VMEM)] * 9
        + [pl.BlockSpec(memory_space=pl.ANY)] * len(shards),
        out_specs=[pl.BlockSpec(memory_space=pltpu.VMEM)] * 8
        + [pl.BlockSpec(memory_space=pl.ANY)] * len(shards),
        scratch_shapes=scratch,
        compiler_params=pltpu.CompilerParams(
            collective_id=30, has_side_effects=True, vmem_limit_bytes=ACT_VMEM
        ),
        name="head",
    )(small, feats, table, times, second, shift, scale, bias, mod_low, *shards)


def tail_kernel(
    images,
    final_at,
    row_ref,
    mod_ref,
    weight_ref,
    second_ref,
    shift_ref,
    scale_ref,
    pre_signal_ref,
    pre_time_ref,
    feats_ref,
    hidden_ref,
    signal_ref,
    loss_ref,
    *rest,
):
    terms, others = rest[0:3], rest[3 : 2 + LAYERS]
    rest = rest[2 + LAYERS :]
    table_grad, mod_grad, scalar_sums = rest[0:3]
    totals, rest = rest[3:6], rest[6:]
    (
        row_in,
        row_mid,
        row_fin,
        mod_in,
        mod_low,
        d_mod_all,
        signal_part,
        scalar_own,
        scalar_in,
        scalar_mid,
        scalar_fin,
    ) = rest[0:11]
    signal_refs, hidden_refs = rest[11:15], rest[15:19]
    own, pair_in, way_in, way_out = rest[19:22], rest[22:25], rest[25:28], rest[28:31]
    crowds = [rest[31 + 3 * index : 34 + 3 * index] for index in range(10)]
    reduce_sems = rest[61:]
    signal_out, hidden_out = signal_refs[0], hidden_refs[0]
    dp_size = lax.axis_size("dp")
    tensor_size = lax.axis_size("tensor")
    places = dp_size * tensor_size
    dp_rank = lax.axis_index("dp")
    images_all = images * dp_size
    cols, lanes = row_ref.shape[2:]
    mod_rows = weight_ref.shape[1]
    slots = mod_low.shape[0]
    last_step = dp_size // 2
    greet_groups("tensor", "dp")
    reduce = Reduce(Line(), terms, totals, own, pair_in, way_in, way_out, *reduce_sems)
    mod_sum = Crowd("tensor", lambda place: mod_ref.at[place], mod_in, *crowds[0])
    mod_spread = Crowd("dp", lambda place: mod_low, d_mod_all, *crowds[1])
    rows = Funnel(row_ref, row_in, row_mid, row_fin, *crowds[2:4])
    signal = Funnel(*signal_refs, *crowds[4:6])
    hidden = Funnel(*hidden_refs, *crowds[6:8])
    scalars = Crowd("tensor", lambda place: scalar_own, scalar_in, *crowds[8])
    scalars_dp = Crowd("dp", lambda place: scalar_mid, scalar_fin, *crowds[9])
    mod_sum.start()
    rows.start()
    reduce.send_pair(0)
    reduce.load_own()
    mod_sum.wait()
    mod_low[...] = jnp.sum(mod_in[...], axis=0).astype(jnp.bfloat16)
    mod_spread.start()
    rows.hand_on()
    reduce.send_pair(1)
    other_squares = sum(other[0:1, 0:1] for other in others)
    reduce.wait_own()
    row_total = rows.take()
    patch_start, time_start, second_start, final_start, head_start, vector_start, layer_start = (
        table_starts()
    )
    patch_in = time_start - patch_start
    layer_at = 2 * patch_in + 1

    def put(start, values):
        table_grad[:, start : start + values.shape[1]] = values

    put(patch_start, row_total[:, 0:patch_in])
    put(head_start, row_total[:, patch_in:layer_at])
    put(layer_start, row_total[:, layer_at:final_at])
    joined = jnp.concatenate([row_fin[at] for at in range(dp_size)], axis=1)

    def final_of(piece):
        return dense(
            joined,
            chosen(
                (dp_size * lanes, images_all),
                lambda row, col: (
                    (row // lanes == col // images)
                    & (lax.rem(row, lanes) == final_at + piece * images + lax.rem(col, images))
                ),
                jnp.float32,
            ),
        )

    d_shift, d_scale = final_of(0), final_of(1)
    signal_part[...] = dense_tn(shift_ref[...], d_shift) + dense_tn(scale_ref[...], d_scale)
    mod_spread.wait()
    d_mod = d_mod_all[...].reshape(dp_size * slots, mod_low.shape[1])
    own_rows = pl.ds(pl.multiple_of(dp_rank * mod_rows, 8), mod_rows)

    def layer_pick(layer_idx, kind):
        return chosen(
            (dp_size * slots, images_all),
            lambda row, col: (
                (row // slots == col // images)
                & (lax.rem(row, slots) == layer_idx * images + lax.rem(col, images))
            ),
            kind,
        )

    for layer_idx in range(LAYERS):
        signal_part[own_rows, :] += dense(
            dot_nt(weight_ref[layer_idx], d_mod), layer_pick(layer_idx, jnp.float32)
        )
    signal_out[...] = fold(signal_part[...].reshape(places, cols, images_all)).reshape(
        signal_out.shape
    )
    signal.start()
    signal.hand_on()
    reduce.send_pair(2)
    run_ticks(reduce, 0, min(1, last_step - 1))
    signal_low = signal_ref[own_rows, :].astype(jnp.bfloat16)
    for layer_idx in range(LAYERS):
        placed = dot_nt(signal_low, layer_pick(layer_idx, jnp.bfloat16)).astype(jnp.bfloat16)
        grad = dot_nn(placed, d_mod)
        mod_grad[layer_idx] = grad
        other_squares = other_squares + square_sum(grad)
    grad = dense_nt(d_shift, signal_ref[...])
    put(final_start, grad)
    other_squares = other_squares + square_sum(grad)
    grad = dense_nt(d_scale, signal_ref[...])
    put(final_start + D, grad)
    other_squares = other_squares + square_sum(grad)
    lane = lax.broadcasted_iota(jnp.int32, row_total.shape, 1)
    other_squares = other_squares + square_sum(jnp.where(lane < final_at, row_total, 0.0))
    d_signal = unfold(signal.take(), cols, images_all)
    d_signal = d_signal * silu_slope(pre_signal_ref[...])
    d_hidden = dense_tn(second_ref[...], d_signal)
    hidden_out[...] = fold(d_hidden.reshape(places, cols, images_all)).reshape(hidden_out.shape)
    hidden.start()
    hidden.hand_on()
    each(max(last_step - 3, 0), lambda step: reduce.send_pair(step + 3))
    run_ticks(reduce, 1, min(2, last_step - 1))
    labels = jnp.round(feats_ref[:, FREQ : FREQ + 1]).astype(jnp.int32)
    class_lane = lax.broadcasted_iota(jnp.int32, (images_all, -(-CLASSES // 128) * 128), 1)
    grad = dense(d_signal, jnp.where(class_lane == labels, 1.0, 0.0))
    put(0, grad[:, 0:CLASSES])
    other_squares = other_squares + square_sum(grad)
    grad = dense_nt(d_signal, hidden_ref[...])
    put(second_start, grad)
    other_squares = other_squares + square_sum(grad)
    d_hidden = unfold(hidden.take(), cols, images_all)
    d_hidden = d_hidden * silu_slope(pre_time_ref[...])
    grad = dense(d_hidden, feats_ref[:, 0:FREQ])
    put(time_start, grad)
    other_squares = other_squares + square_sum(grad)
    vectors = [
        jnp.sum(values, axis=1, keepdims=True) for values in (d_hidden, d_signal, d_shift, d_scale)
    ]
    lane = lax.broadcasted_iota(jnp.int32, (cols, 128), 1)
    grad = sum(jnp.where(lane == at, vector, 0.0) for at, vector in enumerate(vectors))
    put(vector_start + 1, grad[:, 0:4])
    other_squares = other_squares + square_sum(grad)
    run_ticks(reduce, 2, min(3, last_step - 1))
    each(max(last_step - 4, 0), lambda step: reduce.tick(step + 3))
    reduce.finish()
    for total in totals:
        other_squares = other_squares + square_sum(total[...])
    lane = lax.broadcasted_iota(jnp.int32, scalar_own.shape, 1)
    scalar_own[...] = jnp.where(lane == 0, loss_ref[...], other_squares)
    scalars.start()
    scalars.wait()
    scalar_mid[...] = jnp.sum(scalar_in[...], axis=0)
    scalars_dp.start()
    scalars_dp.wait()
    scalar_sums[...] = jnp.sum(scalar_fin[...], axis=0)


def tail_call(
    rows, mods, mod_low, second, shift, scale, pre_signal, pre_time, feats, hidden, signal, loss,
    terms, others, images, at,
):
    dp_size, tensor_size = lax.axis_size("dp"), lax.axis_size("tensor")
    images_all = images * dp_size
    cols, lanes = rows.shape[2:]
    folded = folded_lanes(cols, images_all)
    full, low = jnp.float32, jnp.bfloat16
    spots = dp_size // 2
    blocks = [term.shape[1:] for term in terms]
    table_rows = table_starts()[-1] + LAYERS * (10 + FF // D)
    shapes = [
        ((cols, table_rows), full),
        (mod_low.shape, full),
        ((8, 128), full),
    ] + [(block, full) for block in blocks]
    scratch = [
        pltpu.VMEM((tensor_size, dp_size, cols, lanes), full),
        pltpu.VMEM((dp_size, cols, lanes), full),
        pltpu.VMEM((dp_size, cols, lanes), full),
        pltpu.VMEM(mods.shape, full),
        pltpu.VMEM(mods.shape[1:], low),
        pltpu.VMEM((dp_size,) + mods.shape[1:], low),
        pltpu.VMEM((D, images_all), full),
        pltpu.VMEM((8, 128), full),
        pltpu.VMEM((tensor_size, 8, 128), full),
        pltpu.VMEM((8, 128), full),
        pltpu.VMEM((dp_size, 8, 128), full),
    ]
    for _ in range(2):
        scratch += [
            pltpu.VMEM((dp_size, tensor_size, 8, folded), full),
            pltpu.VMEM((tensor_size, dp_size, 8, folded), full),
            pltpu.VMEM((dp_size, 8, folded), full),
            pltpu.VMEM((dp_size, 8, folded), full),
        ]
    scratch += [pltpu.VMEM((spots,) + block, low) for block in blocks]
    scratch += [pltpu.VMEM((spots,) + block, low) for block in blocks]
    scratch += [pltpu.VMEM((2, spots) + block, low) for block in blocks]
    scratch += [pltpu.VMEM((2, spots) + block, low) for block in blocks]
    for count in (tensor_size, dp_size) * 5:
        scratch += crowd_scratch(count)
    scratch += [
        pltpu.SemaphoreType.DMA((3, spots, 3)),
        pltpu.SemaphoreType.DMA((3, spots, 3)),
        pltpu.SemaphoreType.DMA((3, spots)),
    ]
    return pl.pallas_call(
        functools.partial(tail_kernel, images, at),
        out_shape=[jax.ShapeDtypeStruct(*shape) for shape in shapes],
        in_specs=[pl.BlockSpec(memory_space=pltpu.VMEM)] * 12
        + [pl.BlockSpec(memory_space=pl.ANY)] * len(terms)
        + [pl.BlockSpec(memory_space=pltpu.VMEM)] * len(others),
        out_specs=[pl.BlockSpec(memory_space=pltpu.VMEM)] * len(shapes),
        scratch_shapes=scratch,
        compiler_params=pltpu.CompilerParams(
            collective_id=31, has_side_effects=True, vmem_limit_bytes=ACT_VMEM
        ),
        name="tail",
    )(
        rows, mods, mod_low, second, shift, scale, pre_signal, pre_time, feats, hidden, signal,
        loss, *terms, *others,
    )


def adam_update(weight, first, second, grad, factor, first_fix, second_fix):
    clipped = grad * factor
    first_new = BETA_ONE * first + (1.0 - BETA_ONE) * clipped
    second_new = BETA_TWO * second + (1.0 - BETA_TWO) * clipped * clipped
    step_size = first_new / first_fix / (jnp.sqrt(second_new / second_fix) + ADAM_EPS)
    change = -LEARN_RATE * (step_size + DECAY * weight)
    master = weight + change
    return (master, first_new, second_new, master.astype(jnp.bfloat16), change)


def local(
    latents,
    target_noise,
    timesteps,
    labels,
    step_count,
    embed_table,
    layer_in,
    layer_out,
    layer_ada,
    embed_first,
    embed_second,
    input_first,
    input_second,
    output_first,
    output_second,
    mod_first,
    mod_second,
):
    tensor_size = lax.axis_size("tensor")
    tensor_rank = lax.axis_index("tensor")
    images = latents.shape[0]
    grid_side = SIDE // PATCH
    local_rows = grid_side // tensor_size
    tokens_all = grid_side * grid_side
    heads_local = HEADS // tensor_size
    group_width = heads_local * HEAD_DIM
    unit_count = FF // tensor_size
    patch_in = PATCH * PATCH * CHANNELS
    count_all = images * lax.axis_size("dp") * tokens_all * patch_in
    patch_start, time_start, second_start, final_start, head_start, vector_start, layer_start = (
        table_starts()
    )
    layer_rows = 10 + FF // D
    dp_rank = lax.axis_index("dp")
    dp_size = lax.axis_size("dp")
    place_count = dp_size * tensor_size
    images_all = images * dp_size
    table_cols = lax.reduce_precision(embed_table.T, 8, 7)
    cols = table_cols.shape[0]
    mod_rows = layer_ada.shape[1]
    mod_cols = layer_ada.shape[2]
    mod_low = layer_ada.astype(jnp.bfloat16)

    def col_block(row_start, row_count):
        return table_cols[:, row_start : row_start + row_count]

    vector_count = 5 + LAYERS * layer_rows
    small_count = 2 * patch_in + vector_count
    lanes = -(-(small_count + 2 * images) // 128) * 128
    shards_in = layer_in[:, :, 0].astype(jnp.bfloat16)
    shards = (
        shards_in[:, :, : 3 * group_width],
        shards_in[:, :, 3 * group_width :],
        layer_out[:, 0].astype(jnp.bfloat16),
    )
    second_cols = col_block(second_start, D)
    shift_cols = col_block(final_start, D)
    scale_cols = col_block(final_start + D, D)
    fused = cols % 8 == 0 and images <= 8
    if fused:
        small_send = jnp.concatenate(
            [
                col_block(patch_start, patch_in),
                col_block(head_start, patch_in + vector_count),
                jnp.zeros((cols, lanes - small_count), jnp.float32),
            ],
            axis=1,
        )
        feats_send = jnp.concatenate(
            [
                time_features(timesteps),
                jnp.broadcast_to(labels.astype(jnp.float32)[:, None], (images, 128)),
            ],
            axis=1,
        )
        feats_send = jnp.pad(feats_send, ((0, 8 - images), (0, 0)))
        outs = head_call(
            small_send,
            feats_send,
            table_cols,
            col_block(time_start, FREQ),
            second_cols,
            shift_cols,
            scale_cols,
            col_block(vector_start, 5),
            mod_low,
            shards,
            images,
        )
        small_all, feats_all, pre_time, hidden, pre_signal, signal, final_all, mod_full = outs[:8]
        wholes = outs[8:]
        small_all = small_all.transpose(1, 0, 2, 3)
        time_feats = feats_all[:, :FREQ]
        labels_all = jnp.round(feats_all[:, FREQ]).astype(jnp.int32)
        signal_low = lax.dynamic_slice_in_dim(
            signal.astype(jnp.bfloat16), dp_rank * mod_rows, mod_rows, 0
        )
        final_all = final_all.transpose(1, 0, 2, 3)[:, :, :images, : 2 * cols]
        final_own = final_all.reshape(place_count, images, 2, cols)
        final_own = final_own.transpose(2, 1, 0, 3).reshape(2, images, D)
        mod_full = mod_full[:, : LAYERS * images].reshape(tensor_size, LAYERS, images, mod_cols)
        mod_full = mod_full.transpose(1, 2, 0, 3).reshape(LAYERS, images, tensor_size * mod_cols)
    else:
        scalar_lanes = jnp.concatenate([timesteps, labels]).astype(jnp.float32)
        small_send = jnp.concatenate(
            [
                col_block(patch_start, patch_in),
                col_block(head_start, patch_in + vector_count),
                jnp.broadcast_to(scalar_lanes[None, :], (cols, 2 * images)),
                jnp.zeros((cols, lanes - small_count - 2 * images), jnp.float32),
            ],
            axis=1,
        )
        small_all = exchange(small_send, "all", False, 1)
        scalars_all = small_all[::tensor_size, 0, small_count : small_count + 2 * images].astype(
            jnp.int32
        )
        timesteps_all = scalars_all[:, :images].reshape(images_all)
        labels_all = scalars_all[:, images:].reshape(images_all)
        time_feats = time_features(timesteps_all)
        onehot = (labels_all[:, None] == jnp.arange(CLASSES, dtype=jnp.int32)[None, :]).astype(
            jnp.float32
        )
        pre_time = dense(col_block(time_start, FREQ), time_feats.T) + col_block(vector_start + 1, 1)
        hidden = exchange(jax.nn.silu(pre_time), "all", False, 2).reshape(D, images_all)
        pre_signal = (
            dense(second_cols, hidden)
            + col_block(vector_start + 2, 1)
            + dense(col_block(0, CLASSES), onehot.T)
        )
        signal = exchange(jax.nn.silu(pre_signal), "all", False, 3).reshape(D, images_all)
        final_send = jnp.concatenate(
            [
                dense(shift_cols, signal) + col_block(vector_start + 3, 1),
                dense(scale_cols, signal) + col_block(vector_start + 4, 1),
            ],
            axis=0,
        )
        final_all = exchange(final_send, "all", False, 4).reshape(place_count, 2, cols, images_all)
        final_own = lax.dynamic_slice_in_dim(final_all, dp_rank * images, images, 3)
        final_own = final_own.transpose(1, 3, 0, 2).reshape(2, images, D)
        signal_low = lax.dynamic_slice_in_dim(
            signal.astype(jnp.bfloat16), dp_rank * mod_rows, mod_rows, 0
        )
        mod_part = jnp.einsum("db,lde->ble", signal_low, mod_low, preferred_element_type=jnp.float32)
        mod_part = mod_part.reshape(dp_size, images * LAYERS, mod_cols)
        mod_local = jnp.sum(exchange(mod_part, "dp", True, 5), axis=0)
        mod_full = exchange(mod_local, "tensor", False, 6)
        mod_full = mod_full.reshape(tensor_size, images, LAYERS, mod_cols)
        mod_full = mod_full.transpose(2, 1, 0, 3).reshape(LAYERS, images, tensor_size * mod_cols)
        wholes = [lax.all_gather(shard[0], "dp") for shard in shards]
    small_rows = small_all.reshape(D, lanes).T
    patch_w = small_rows[0:patch_in]
    head_w = small_rows[patch_in : 2 * patch_in]
    vectors = small_rows[2 * patch_in : 2 * patch_in + 5]
    bias_all = small_rows[2 * patch_in + 5 : small_count]
    onehot = (labels_all[:, None] == jnp.arange(CLASSES, dtype=jnp.int32)[None, :]).astype(
        jnp.float32
    )
    final_shift, final_scale = final_own[0], final_own[1]
    pixels = patchify(latents, local_rows)
    targets = patchify(target_noise, local_rows)
    keep_coef, drop_coef = noise_levels(timesteps)
    noisy = keep_coef[:, None, None] * pixels + drop_coef[:, None, None] * targets
    residual = (
        jnp.einsum("btp,pd->btd", noisy, patch_w, precision=PRECISE)
        + vectors[0]
        + position_table(tensor_rank * local_rows, local_rows)[None]
    )
    saved_acts = []
    bias_all = bias_all.reshape(LAYERS, layer_rows, D)
    mod_vecs = mod_full.reshape(LAYERS, images, 6, D) + bias_all[:, None, 0:6]
    part_bias = lax.dynamic_slice_in_dim(
        bias_all[:, 8:10], tensor_rank * group_width, group_width, 2
    )
    qkv_bias = jnp.concatenate(
        [part_bias[:, 0], jnp.zeros((LAYERS, group_width), jnp.float32), part_bias[:, 1]], axis=1
    )
    up_bias = lax.dynamic_slice_in_dim(
        bias_all[:, 10:].reshape(LAYERS, FF), tensor_rank * unit_count, unit_count, 1
    )
    joined = fused and shards[0].shape[1] % 16 == 0 and shards[2].shape[1] % 8 == 0
    if joined:
        outs = forward_all(
            count_all,
            residual,
            mod_vecs,
            bias_all[:, 6:8],
            qkv_bias[:, None],
            up_bias[:, None],
            (final_shift[:, None], final_scale[:, None], head_w, targets),
            wholes,
            shards,
        )
        d_residual, d_head, loss_part, d_final_shift, d_final_scale = outs[:5]
        loss_part = loss_part[0, 0]
        d_final_shift, d_final_scale = d_final_shift[:, 0], d_final_scale[:, 0]
        saved_acts = [
            (mod_vecs[layer_idx], outs[5:14], outs[14:17]) for layer_idx in range(LAYERS)
        ]
    else:
        for layer_idx in range(LAYERS):
            weights = (
                wholes[0].reshape(D, 3 * group_width),
                wholes[1].reshape(D, unit_count),
                wholes[2].reshape(group_width + unit_count, D),
            )
            outs = forward_layer(
                residual,
                mod_vecs[layer_idx],
                bias_all[layer_idx, 6:8],
                qkv_bias[layer_idx : layer_idx + 1],
                up_bias[layer_idx : layer_idx + 1],
                *weights,
                shards if layer_idx + 1 < LAYERS else (),
                layer_idx,
            )
            wholes = outs[9:]
            saved_acts.append((mod_vecs[layer_idx], (residual,) + tuple(outs[1:9]), weights))
            residual = outs[0]
        final_in, final_norm_pull = jax.vjp(modulate, residual, final_shift, final_scale)
        predicted = jnp.einsum("btd,pd->btp", final_in, head_w, precision=PRECISE)
        error_all = predicted - targets
        loss_part = jnp.sum(error_all * error_all) / count_all
        d_pred = 2.0 * error_all / count_all
        d_head = jnp.einsum("btp,btd->pd", d_pred, final_in, precision=PRECISE)
        d_final = jnp.einsum("btp,pd->btd", d_pred, head_w, precision=PRECISE)
        d_residual, d_final_shift, d_final_scale = final_norm_pull(d_final)
    totals = []
    squares = []
    terms = ()
    bias_parts = []
    for layer_idx in reversed(range(LAYERS)):
        mod_vec, saved, weights = saved_acts[layer_idx]
        outs = backward_layer(
            d_residual, mod_vec, saved, weights, terms, layer_idx, joined
        )
        d_residual, d_w_qkv, d_w_up, d_w_out, d_mod_vec, d_vec, d_qkv_bias, d_up_bias = outs[:8]
        if terms:
            totals.insert(0, outs[8:11])
            squares.append(outs[11])
        terms = [
            term.reshape((dp_size, -1) + term.shape[1:]) for term in (d_w_qkv, d_w_up, d_w_out)
        ]
        bias_parts.insert(0, (d_mod_vec, d_vec, d_qkv_bias, d_up_bias))
    d_mods, d_vecs, d_qkv_rows, d_up_rows = [jnp.stack(parts) for parts in zip(*bias_parts)]
    part_rows = jnp.stack([d_qkv_rows[:, 0, :group_width], d_qkv_rows[:, 0, 2 * group_width :]], 1)
    bias_blocks = jnp.concatenate(
        [
            jnp.sum(d_mods, axis=1),
            d_vecs,
            lax.dynamic_update_slice_in_dim(
                jnp.zeros((LAYERS, 2, D), jnp.float32), part_rows, tensor_rank * group_width, 2
            ),
            lax.dynamic_update_slice_in_dim(
                jnp.zeros((LAYERS, FF), jnp.float32), d_up_rows[:, 0], tensor_rank * unit_count, 1
            ).reshape(LAYERS, FF // D, D),
        ],
        axis=1,
    ).reshape(LAYERS * layer_rows, D)
    d_patch_w = jnp.einsum("btp,btd->pd", noisy, d_residual, precision=PRECISE)
    d_patch_b = jnp.sum(d_residual, axis=(0, 1))
    row_parts = jnp.concatenate(
        [d_patch_w, d_head, d_patch_b[None], bias_blocks, d_final_shift, d_final_scale],
        axis=0,
    )
    row_count = row_parts.shape[0]
    row_lanes = -(-row_count // 128) * 128
    row_parts = jnp.pad(row_parts, ((0, row_lanes - row_count), (0, 0)))
    final_at = row_count - 2 * images
    row_send = row_parts.T.reshape(dp_size, tensor_size, cols, row_lanes)
    mod_send = d_mods.reshape(LAYERS * images, tensor_size, mod_cols)
    mod_send = mod_send.transpose(1, 0, 2)
    if fused:
        slots = slots_of(images)
        outs = tail_call(
            row_send,
            jnp.pad(mod_send, ((0, 0), (0, slots - LAYERS * images), (0, 0))),
            mod_low,
            second_cols,
            shift_cols,
            scale_cols,
            pre_signal,
            pre_time,
            feats_all,
            hidden,
            signal,
            loss_part.reshape(1, 1),
            terms,
            squares,
            images,
            final_at,
        )
        table_grad, mod_grad, scalar_sums = outs[:3]
        totals.insert(0, outs[3:])
        scalar_sums = scalar_sums[0]
    else:
        totals.insert(
            0,
            [
                lax.psum_scatter(term, "dp", scatter_dimension=0).astype(jnp.float32)
                for term in terms
            ],
        )
        row_all = exchange(row_send.reshape(place_count, cols, row_lanes), "all", True, 7)
        row_sums = jnp.sum(row_all, axis=0)
        final_sums = jnp.sum(
            row_all[:, :, final_at:row_count].reshape(dp_size, tensor_size, cols, 2, images), axis=1
        )
        final_sums = final_sums.transpose(2, 1, 0, 3).reshape(2, cols, images_all)
        d_shift_cols, d_scale_cols = final_sums[0], final_sums[1]
        d_mod_own = jnp.sum(exchange(mod_send, "tensor", True, 8), axis=0)
        d_mod_low = exchange(d_mod_own.astype(jnp.bfloat16), "dp", False, 9)
        d_mod_low = d_mod_low.reshape(dp_size, LAYERS, images, mod_cols)
        d_mod_low = d_mod_low.transpose(1, 0, 2, 3).reshape(LAYERS, images_all, mod_cols)
        d_signal_rows = jnp.einsum(
            "lbe,lde->db", d_mod_low, mod_low, preferred_element_type=jnp.float32
        )
        d_signal_part = dense(shift_cols.T, d_shift_cols) + dense(scale_cols.T, d_scale_cols)
        d_signal_part = d_signal_part + lax.dynamic_update_slice_in_dim(
            jnp.zeros((D, images_all), jnp.float32), d_signal_rows, dp_rank * mod_rows, 0
        )
        d_signal_cols = jnp.sum(
            exchange(d_signal_part.reshape(place_count, cols, images_all), "all", True, 10), axis=0
        )
        d_pre_signal = d_signal_cols * silu_slope(pre_signal)
        d_hidden_part = dense(second_cols.T, d_pre_signal)
        d_hidden_cols = jnp.sum(
            exchange(d_hidden_part.reshape(place_count, cols, images_all), "all", True, 11), axis=0
        )
        d_hidden = d_hidden_cols * silu_slope(pre_time)
        mod_grad = jnp.einsum(
            "db,lbe->lde", signal_low, d_mod_low, preferred_element_type=jnp.float32
        )
        class_grad = dense(d_pre_signal, onehot)
        time_grad = dense(d_hidden, time_feats)
        second_grad = dense(d_pre_signal, hidden.T)
        shift_grad = dense(d_shift_cols, signal.T)
        scale_grad = dense(d_scale_cols, signal.T)
        vector_sums = jnp.stack(
            [
                jnp.sum(values, axis=1)
                for values in (d_hidden, d_pre_signal, d_shift_cols, d_scale_cols)
            ],
            axis=1,
        )
        table_grad = jnp.concatenate(
            [
                class_grad,
                row_sums[:, 0:patch_in],
                time_grad,
                second_grad,
                shift_grad,
                scale_grad,
                row_sums[:, patch_in : 2 * patch_in + 1],
                vector_sums,
                row_sums[:, 2 * patch_in + 1 : final_at],
            ],
            axis=1,
        )
    input_grad = jnp.stack([jnp.concatenate(total[0:2], axis=1) for total in totals])
    input_grad = input_grad.reshape(layer_in.shape)
    output_grad = jnp.stack([total[2] for total in totals]).reshape(layer_out.shape)
    if not fused:
        local_squares = (
            jnp.sum(table_grad * table_grad)
            + jnp.sum(input_grad * input_grad)
            + jnp.sum(output_grad * output_grad)
            + jnp.sum(mod_grad * mod_grad)
        )
        scalar_send = jnp.where(
            lax.broadcasted_iota(jnp.int32, (8, 128), 1) == 0, loss_part, local_squares
        )
        scalar_sums = jnp.sum(exchange(scalar_send, "all", False, 12)[:, 0, 0:2], axis=0)
    loss_value = scalar_sums[0]
    square_total = scalar_sums[1]
    grad_norm = jnp.sqrt(square_total)
    factor = jnp.minimum(1.0, CLIP_NORM / grad_norm)
    first_fix = 1.0 - BETA_ONE ** step_count.astype(jnp.float32)
    second_fix = 1.0 - BETA_TWO ** step_count.astype(jnp.float32)
    embed_out = adam_update(
        embed_table.T, embed_first.T, embed_second.T, table_grad, factor, first_fix, second_fix
    )
    input_out = adam_update(
        layer_in, input_first, input_second, input_grad, factor, first_fix, second_fix
    )
    output_out = adam_update(
        layer_out, output_first, output_second, output_grad, factor, first_fix, second_fix
    )
    mod_out = adam_update(layer_ada, mod_first, mod_second, mod_grad, factor, first_fix, second_fix)
    return (
        (loss_value, grad_norm, embed_out[4].T, embed_out[1].T, embed_out[2].T)
        + input_out[0:4]
        + output_out[0:4]
        + mod_out[0:4]
    )


def solution(mesh):
    placed = (
        P("dp", "tensor"),
        P("dp", "tensor"),
        P("dp"),
        P("dp"),
        P(),
        P(None, ("dp", "tensor")),
        P(None, "dp", "tensor", None),
        P(None, "tensor", "dp", None),
        P(None, "dp", "tensor"),
        P(None, ("dp", "tensor")),
        P(None, ("dp", "tensor")),
        P(None, "dp", "tensor", None),
        P(None, "dp", "tensor", None),
        P(None, "tensor", "dp", None),
        P(None, "tensor", "dp", None),
        P(None, "dp", "tensor"),
        P(None, "dp", "tensor"),
    )
    return jax.shard_map(
        local,
        mesh=mesh,
        in_specs=placed,
        out_specs=(
            P(),
            P(),
            P(None, ("dp", "tensor")),
            P(None, ("dp", "tensor")),
            P(None, ("dp", "tensor")),
            P(None, "dp", "tensor", None),
            P(None, "dp", "tensor", None),
            P(None, "dp", "tensor", None),
            P(None, "dp", "tensor", None),
            P(None, "tensor", "dp", None),
            P(None, "tensor", "dp", None),
            P(None, "tensor", "dp", None),
            P(None, "tensor", "dp", None),
            P(None, "dp", "tensor"),
            P(None, "dp", "tensor"),
            P(None, "dp", "tensor"),
            P(None, "dp", "tensor"),
        ),
        check_vma=False,
    )
```

```python
import functools
import math

import jax
import jax.numpy as jnp
from jax import lax
from jax.experimental import pallas as pl
from jax.experimental.pallas import tpu as pltpu
from jax.sharding import PartitionSpec as P

D = 768
HEADS = 12
HEAD_DIM = 64
FF = 3072
CLASSES = 1001
FREQ = 256
CHANNELS = 4
PATCH = 2
SIDE = 32
LAYERS = 3


EPS_NORM = 1e-06
LEARN_RATE = 0.01
DECAY = 0.01
BETA_ONE = 0.5
BETA_TWO = 0.5
ADAM_EPS = 1e-08
CLIP_NORM = 0.25
PRECISE = lax.Precision.HIGHEST


def dense(left_op, right_op):
    return jnp.dot(left_op, right_op, precision=PRECISE, preferred_element_type=jnp.float32)


def layer_norm(values):
    center = values - jnp.mean(values, axis=-1, keepdims=True)
    return center * lax.rsqrt(jnp.mean(center * center, axis=-1, keepdims=True) + EPS_NORM)


def modulate(values, shift_vec, scale_vec):
    return layer_norm(values) * (1.0 + scale_vec[:, None, :]) + shift_vec[:, None, :]


def gelu_tanh(values):
    return jax.nn.gelu(values, approximate=True)


def silu_slope(values):
    sigmoid_val = jax.nn.sigmoid(values)
    return sigmoid_val * (1.0 + values * (1.0 - sigmoid_val))


def time_features(step_ints):
    half_width = FREQ // 2
    frequency = jnp.exp(-math.log(10000.0) * jnp.arange(half_width, dtype=jnp.float32) / half_width)
    angles = step_ints.astype(jnp.float32)[:, None] * frequency[None, :]
    return jnp.concatenate([jnp.cos(angles), jnp.sin(angles)], axis=1)


def noise_levels(step_ints):
    base_cos = math.cos(0.008 / 1.008 * math.pi / 2)
    angles = (step_ints.astype(jnp.float32) / 1000.0 + 0.008) / 1.008 * (math.pi / 2)
    signal_level = jnp.cos(angles) ** 2 / base_cos**2
    return (jnp.sqrt(signal_level), jnp.sqrt(1.0 - signal_level))


def position_table(first_row, row_count):
    grid_side = SIDE // PATCH
    quarter = D // 4
    omegas = jnp.exp(-math.log(10000.0) * jnp.arange(quarter, dtype=jnp.float32) / quarter)
    token_index = jnp.arange(row_count * grid_side, dtype=jnp.int32)
    row_angle = (first_row + token_index // grid_side).astype(jnp.float32)[:, None] * omegas[
        None, :
    ]
    col_angle = (token_index % grid_side).astype(jnp.float32)[:, None] * omegas[None, :]
    return jnp.concatenate(
        [jnp.sin(row_angle), jnp.cos(row_angle), jnp.sin(col_angle), jnp.cos(col_angle)], axis=1
    )


def patchify(flat_pixels, row_count):
    grid_side = SIDE // PATCH
    shaped = flat_pixels.reshape(flat_pixels.shape[0], row_count, PATCH, grid_side, PATCH, CHANNELS)
    return shaped.transpose(0, 1, 3, 2, 4, 5).reshape(
        flat_pixels.shape[0], row_count * grid_side, PATCH * PATCH * CHANNELS
    )


def table_starts():
    patch_in = PATCH * PATCH * CHANNELS
    patch_start = CLASSES
    time_start = patch_start + patch_in
    second_start = time_start + FREQ
    final_start = second_start + D
    head_start = final_start + 2 * D
    vector_start = head_start + patch_in
    layer_start = vector_start + 5
    return (
        patch_start,
        time_start,
        second_start,
        final_start,
        head_start,
        vector_start,
        layer_start,
    )


def group_place(group):
    if group == "all":
        width = lax.axis_size("tensor")
        place = lax.axis_index("dp") * width + lax.axis_index("tensor")
        size = lax.axis_size("dp") * width
        return place, size, lambda at: {"dp": at // width, "tensor": lax.rem(at, width)}
    return lax.axis_index(group), lax.axis_size(group), lambda at: {group: at}


def greet_group(group):
    place, size, coords = group_place(group)
    barrier = pltpu.get_barrier_semaphore()

    def greet_one(step, carry):
        peer = coords(lax.rem(place + step, size))
        pl.semaphore_signal(barrier, inc=1, device_id=peer, device_id_type=pl.DeviceIdType.MESH)
        return carry

    lax.fori_loop(1, size, greet_one, 0)
    pl.semaphore_wait(barrier, size - 1)


def greet_groups(*groups):
    barrier = pltpu.get_barrier_semaphore()
    count = 0
    for group in groups:
        place, size, coords = group_place(group)

        def greet_one(step, carry, place=place, size=size, coords=coords):
            peer = coords(lax.rem(place + step, size))
            pl.semaphore_signal(barrier, inc=1, device_id=peer, device_id_type=pl.DeviceIdType.MESH)
            return carry

        lax.fori_loop(1, size, greet_one, 0)
        count += size - 1
    pl.semaphore_wait(barrier, count)


class Crowd:
    def __init__(self, group, source_at, target, send_sems, recv_sems, local_sem):
        self.place, self.size, self.coords = group_place(group)
        self.source_at, self.target = source_at, target
        self.sends, self.recvs, self.local_sem = send_sems, recv_sems, local_sem

    def copy_to(self, step):
        there = lax.rem(self.place + step, self.size)
        return pltpu.make_async_remote_copy(
            src_ref=self.source_at(there),
            dst_ref=self.target.at[self.place],
            send_sem=self.sends.at[step],
            recv_sem=self.recvs.at[step],
            device_id=self.coords(there),
            device_id_type=pl.DeviceIdType.MESH,
        )

    def own_copy(self):
        return pltpu.make_async_copy(
            self.source_at(self.place), self.target.at[self.place], self.local_sem
        )

    def start(self):
        def begin(step, carry):
            self.copy_to(step).start()
            return carry

        lax.fori_loop(1, self.size, begin, 0)
        self.own_copy().start()

    def wait(self):
        def finish(step, carry):
            self.copy_to(step).wait()
            return carry

        self.own_copy().wait()
        lax.fori_loop(1, self.size, finish, 0)


class Relay:
    def __init__(self, source_at, middle, whole, sems_dp, sems_tensor):
        self.first = Crowd("dp", source_at, middle, *sems_dp)
        self.second = Crowd("tensor", lambda place: middle, whole, *sems_tensor)

    def start(self):
        self.first.start()

    def hand_on(self):
        self.first.wait()
        self.second.start()

    def wait(self):
        self.second.wait()


class Funnel:
    def __init__(self, source, across, middle, along, sems_tensor, sems_dp):
        self.across, self.middle, self.along = across, middle, along
        self.first = Crowd("tensor", lambda place: source.at[:, place], across, *sems_tensor)
        self.second = Crowd("dp", lambda place: middle.at[place], along, *sems_dp)

    def start(self):
        self.first.start()

    def hand_on(self):
        self.first.wait()
        self.middle[...] = jnp.sum(self.across[...], axis=0)
        self.second.start()

    def take(self):
        self.second.wait()
        return jnp.sum(self.along[...], axis=0)


def crowd_scratch(size):
    return [
        pltpu.SemaphoreType.DMA((size,)),
        pltpu.SemaphoreType.DMA((size,)),
        pltpu.SemaphoreType.DMA,
    ]


def exchange_kernel(group, spread, source, target, send_sems, recv_sems, local_sem):
    greet_group(group)
    crowd = Crowd(
        group,
        lambda place: source.at[place] if spread else source,
        target,
        send_sems,
        recv_sems,
        local_sem,
    )
    crowd.start()
    crowd.wait()


def exchange(values, group, spread, call_id):
    if group == "all":
        size = lax.axis_size("dp") * lax.axis_size("tensor")
    else:
        size = lax.axis_size(group)
    block = values.shape[1:] if spread else values.shape
    return pl.pallas_call(
        functools.partial(exchange_kernel, group, spread),
        out_shape=jax.ShapeDtypeStruct((size,) + block, values.dtype),
        in_specs=[pl.BlockSpec(memory_space=pltpu.VMEM)],
        out_specs=pl.BlockSpec(memory_space=pltpu.VMEM),
        scratch_shapes=crowd_scratch(size),
        compiler_params=pltpu.CompilerParams(
            collective_id=call_id, has_side_effects=True, vmem_limit_bytes=32 * 2**20
        ),
        name="exchange_" + group,
    )(values)


MESH = pl.DeviceIdType.MESH
ACT_VMEM = 60 * 2**20


def dot_nn(left_op, right_op):
    return jnp.dot(left_op, right_op, preferred_element_type=jnp.float32)


def dot_nt(left_op, right_op):
    return lax.dot_general(
        left_op, right_op, (((1,), (1,)), ((), ())), preferred_element_type=jnp.float32
    )


def dot_tn(left_op, right_op):
    return lax.dot_general(
        left_op, right_op, (((0,), (0,)), ((), ())), preferred_element_type=jnp.float32
    )


def square_sum(values):
    return jnp.sum(jnp.sum(values * values, axis=0, keepdims=True), axis=1, keepdims=True)


def norm_parts(values):
    center = values - jnp.mean(values, axis=-1, keepdims=True)
    rstd = lax.rsqrt(jnp.mean(center * center, axis=-1, keepdims=True) + EPS_NORM)
    return center * rstd, rstd


def greet(line):
    rank = lax.axis_index("tensor")
    half = lax.axis_size("tensor") // 2
    core_peer = {"tensor": rank + 1 - 2 * lax.rem(rank, 2)}
    chip_peer = {"tensor": lax.rem(rank + half, 2 * half)}
    barrier = pltpu.get_barrier_semaphore()
    for peer in (core_peer, chip_peer):
        pl.semaphore_signal(barrier, inc=1, device_id=peer, device_id_type=MESH)
    count = 2
    if line is not None:
        line.greet()
        count = count + line.answers()
    pl.semaphore_wait(barrier, count)


class Spread:
    def __init__(self, rows_ref, send_sems, recv_sems):
        self.rows, self.send, self.recv = rows_ref, send_sems, recv_sems
        self.rank = lax.axis_index("tensor")
        self.own_core = lax.rem(self.rank, 2)
        self.core_peer = self.rank + 1 - 2 * self.own_core
        self.chip_peer = lax.rem(self.rank + 2, 4)
        self.count = rows_ref.shape[1] // 4

    def block(self, image, owner):
        return self.rows.at[image, pl.ds(pl.multiple_of(owner * self.count, 16), self.count), :]

    def copy(self, image, owner, peer, which):
        return pltpu.make_async_remote_copy(
            src_ref=self.block(image, owner),
            dst_ref=self.block(image, owner),
            send_sem=self.send.at[image, which],
            recv_sem=self.recv.at[image, which],
            device_id={"tensor": peer},
            device_id_type=MESH,
        )

    def put(self, image, values):
        self.rows[image, pl.ds(pl.multiple_of(self.rank * self.count, 16), self.count), :] = values
        self.copy(image, self.rank, self.chip_peer, 0).start()
        self.copy(image, self.rank, self.core_peer, 1).start()

    def forward(self, image):
        self.copy(image, self.rank, self.chip_peer, 0).wait_recv()
        self.copy(image, self.chip_peer, self.core_peer, 2).start()

    def wait(self, image):
        self.copy(image, self.rank, self.core_peer, 1).wait_recv()
        self.copy(image, self.chip_peer, self.core_peer, 2).wait_recv()

    def close(self, image):
        self.copy(image, self.rank, self.chip_peer, 0).wait_send()
        self.copy(image, self.rank, self.core_peer, 1).wait_send()
        self.copy(image, self.chip_peer, self.core_peer, 2).wait_send()


class Collect:
    def __init__(self, part, near, far_out, far_in, send_sems, recv_sems):
        self.part, self.near, self.far_out, self.far_in = part, near, far_out, far_in
        self.send, self.recv = send_sems, recv_sems
        self.rank = lax.axis_index("tensor")
        self.own_core = lax.rem(self.rank, 2)
        self.own_chip = self.rank // 2
        self.core_peer = self.rank + 1 - 2 * self.own_core
        self.chip_peer = lax.rem(self.rank + 2, 4)
        self.count = part.shape[1] // 4

    def block(self, image, owner):
        return self.part.at[image, pl.ds(pl.multiple_of(owner * self.count, 16), self.count), :]

    def near_copy(self, image, far):
        chip = 1 - self.own_chip if far else self.own_chip
        return pltpu.make_async_remote_copy(
            src_ref=self.block(image, 2 * chip + 1 - self.own_core),
            dst_ref=self.near.at[image, far],
            send_sem=self.send.at[image, far],
            recv_sem=self.recv.at[image, far],
            device_id={"tensor": self.core_peer},
            device_id_type=MESH,
        )

    def far_copy(self, image):
        return pltpu.make_async_remote_copy(
            src_ref=self.far_out.at[image],
            dst_ref=self.far_in.at[image],
            send_sem=self.send.at[image, 2],
            recv_sem=self.recv.at[image, 2],
            device_id={"tensor": self.chip_peer},
            device_id_type=MESH,
        )

    def put(self, image, values):
        self.part[image] = values.astype(jnp.bfloat16)
        self.near_copy(image, 1).start()
        self.near_copy(image, 0).start()

    def load(self, image, owner):
        at = pl.ds(pl.multiple_of(owner * self.count, 16), self.count)
        return self.part[image, at, :].astype(jnp.float32)

    def forward(self, image):
        self.near_copy(image, 1).wait_recv()
        total = self.load(image, self.chip_peer) + self.near[image, 1].astype(jnp.float32)
        self.far_out[image] = total.astype(jnp.bfloat16)
        self.far_copy(image).start()

    def take(self, image):
        self.near_copy(image, 0).wait_recv()
        total = self.load(image, self.rank) + self.near[image, 0].astype(jnp.float32)
        self.far_copy(image).wait_recv()
        return total + self.far_in[image].astype(jnp.float32)

    def close(self, image):
        self.near_copy(image, 1).wait_send()
        self.near_copy(image, 0).wait_send()
        self.far_copy(image).wait_send()


def collect_scratch(images, tokens):
    count = tokens // 4
    return [
        pltpu.VMEM((images, tokens, D), jnp.bfloat16),
        pltpu.VMEM((images, 2, count, D), jnp.bfloat16),
        pltpu.VMEM((images, count, D), jnp.bfloat16),
        pltpu.VMEM((images, count, D), jnp.bfloat16),
    ]


def each(count, body):
    def step(index, carry):
        body(index)
        return carry

    lax.fori_loop(0, count, step, 0)


class Moves:
    def __init__(self, pairs, sems):
        self.copies = [
            pltpu.make_async_copy(source, target, sems.at[at])
            for at, (source, target) in enumerate(pairs)
        ]

    def start(self, *which):
        for at in which:
            self.copies[at].start()

    def wait(self, *which):
        for at in which:
            self.copies[at].wait()


class Line:
    def __init__(self):
        self.size = lax.axis_size("dp") // 2
        self.place = lax.axis_index("dp")
        self.at = self.place // 2
        self.side = lax.rem(self.place, 2)
        self.pair = self.place + 1 - 2 * self.side
        self.has_up = self.at + 1 < self.size
        self.has_down = self.at > 0

    def greet(self):
        barrier = pltpu.get_barrier_semaphore()
        pl.semaphore_signal(barrier, inc=1, device_id={"dp": self.pair}, device_id_type=MESH)

        @pl.when(self.has_up)
        def _():
            up = {"dp": self.place + 2}
            pl.semaphore_signal(barrier, inc=1, device_id=up, device_id_type=MESH)

        @pl.when(self.has_down)
        def _():
            down = {"dp": self.place - 2}
            pl.semaphore_signal(barrier, inc=1, device_id=down, device_id_type=MESH)

    def answers(self):
        return 1 + self.has_up.astype(jnp.int32) + self.has_down.astype(jnp.int32)


UP, DOWN, PAIR = 0, 1, 2


class Gather:
    def __init__(self, line, shards, wholes, sends, recvs, local_sems):
        self.line, self.shards, self.wholes = line, shards, wholes
        self.sends, self.recvs, self.local_sems = sends, recvs, local_sems

    def copy(self, part, way, step, owner, fresh=False):
        line = self.line
        there = {UP: line.place + 2, DOWN: line.place - 2, PAIR: line.pair}[way]
        return pltpu.make_async_remote_copy(
            src_ref=self.shards[part] if fresh else self.wholes[part].at[owner],
            dst_ref=self.wholes[part].at[owner],
            send_sem=self.sends.at[way, step, part],
            recv_sem=self.recvs.at[way, step, part],
            device_id={"dp": there},
            device_id_type=MESH,
        )

    def local_copy(self, part):
        return pltpu.make_async_copy(
            self.shards[part], self.wholes[part].at[self.line.place], self.local_sems.at[part]
        )

    def start(self):
        line = self.line
        parts = range(len(self.shards))

        @pl.when(line.has_up)
        def _():
            for part in parts:
                self.copy(part, UP, 0, line.place, True).start()

        @pl.when(line.has_down)
        def _():
            for part in parts:
                self.copy(part, DOWN, 0, line.place, True).start()

        for part in parts:
            self.copy(part, PAIR, line.at, line.place, True).start()
            self.local_copy(part).start()

    def came(self, way, step):
        there = -step if way == UP else step
        spot = self.line.at + there
        return self.line.place + 2 * there, spot, (spot >= 0) & (spot < self.line.size)

    def hand_on(self, step, way):
        line = self.line
        owner, _, real = self.came(way, step)
        can = line.has_up if way == UP else line.has_down

        @pl.when(real)
        def _():
            for part in range(len(self.shards)):
                self.copy(part, way, step - 1, owner).wait_recv()

            @pl.when(can)
            def _():
                for part in range(len(self.shards)):
                    self.copy(part, way, step, owner).start()

    def hand_over(self, step, way, when=True):
        owner, spot, real = self.came(way, step)

        @pl.when(real & when)
        def _():
            for part in range(len(self.shards)):
                self.copy(part, PAIR, spot, owner).start()

    def tick(self, step):
        for way in (UP, DOWN):
            self.hand_on(step, way)
            self.hand_over(step, way)

    def finish(self):
        line = self.line
        parts = range(len(self.shards))
        for part in parts:
            self.local_copy(part).wait()

        def side(spot):
            for part in parts:
                self.copy(part, PAIR, spot, 2 * spot + line.side).wait()

        each(line.size, side)

        def along(step):
            for way, there, can in ((UP, -step, line.has_up), (DOWN, step, line.has_down)):
                spot = line.at + there

                @pl.when((spot >= 0) & (spot < line.size) & can)
                def _(way=way, there=there):
                    for part in parts:
                        self.copy(part, way, step, line.place + 2 * there).wait_send()

        each(line.size, along)


class Reduce:
    def __init__(self, line, terms, totals, own, pair_in, way_in, way_out, sends, recvs, own_sems):
        self.line, self.terms, self.totals, self.own = line, terms, totals, own
        self.own_sems = own_sems
        self.pair_in, self.way_in, self.way_out = pair_in, way_in, way_out
        self.sends, self.recvs = sends, recvs

    def pair_copy(self, part, spot):
        return pltpu.make_async_remote_copy(
            src_ref=self.terms[part].at[2 * spot + 1 - self.line.side],
            dst_ref=self.pair_in[part].at[spot],
            send_sem=self.sends.at[PAIR, spot, part],
            recv_sem=self.recvs.at[PAIR, spot, part],
            device_id={"dp": self.line.pair},
            device_id_type=MESH,
        )

    def way_copy(self, part, way, spot):
        there = self.line.place + 2 if way == UP else self.line.place - 2
        return pltpu.make_async_remote_copy(
            src_ref=self.way_out[part].at[way, spot],
            dst_ref=self.way_in[part].at[way, spot],
            send_sem=self.sends.at[way, spot, part],
            recv_sem=self.recvs.at[way, spot, part],
            device_id={"dp": there},
            device_id_type=MESH,
        )

    def start(self):
        self.load_own()
        each(self.line.size, self.send_pair)

    def own_copy(self, part, spot):
        return pltpu.make_async_copy(
            self.terms[part].at[2 * spot + self.line.side],
            self.own[part].at[spot],
            self.own_sems.at[part, spot],
        )

    def load_own(self):
        def load(spot):
            for part in range(len(self.terms)):
                self.own_copy(part, spot).start()

        each(self.line.size, load)

    def wait_own(self):
        def wait(spot):
            for part in range(len(self.terms)):
                self.own_copy(part, spot).wait()

        each(self.line.size, wait)

    def send_pair(self, step):
        line = self.line
        far = line.size - 1 - step

        @pl.when(line.at + far < line.size)
        def _():
            for part in range(len(self.terms)):
                self.pair_copy(part, line.at + far).start()

        @pl.when((line.at - far >= 0) & (far > 0))
        def _():
            for part in range(len(self.terms)):
                self.pair_copy(part, line.at - far).start()

    def pair_sum(self, part, spot):
        own = self.own[part][spot].astype(jnp.float32)
        return own + self.pair_in[part][spot].astype(jnp.float32)

    def pass_on(self, way, spot, more):
        for part in range(len(self.terms)):
            self.pair_copy(part, spot).wait_recv()
            self.way_out[part][way, spot] = self.pair_sum(part, spot).astype(jnp.bfloat16)

            @pl.when(more)
            def _(part=part):
                self.way_copy(part, way, spot).wait_recv()
                self.way_out[part][way, spot] = (
                    self.pair_sum(part, spot) + self.way_in[part][way, spot].astype(jnp.float32)
                ).astype(jnp.bfloat16)

            self.way_copy(part, way, spot).start()

    def tick(self, step):
        line = self.line
        far = line.size - 1 - step

        @pl.when(line.at + far < line.size)
        def _():
            self.pass_on(UP, line.at + far, line.has_down)

        @pl.when(line.at - far >= 0)
        def _():
            self.pass_on(DOWN, line.at - far, line.has_up)

    def finish(self):
        line = self.line
        spot = line.at
        for part in range(len(self.terms)):
            self.pair_copy(part, spot).wait_recv()
            self.totals[part][...] = self.pair_sum(part, spot)
        for way, can in ((UP, line.has_down), (DOWN, line.has_up)):

            @pl.when(can)
            def _(way=way):
                for part in range(len(self.terms)):
                    self.way_copy(part, way, spot).wait_recv()
                    self.totals[part][...] += self.way_in[part][way, spot].astype(jnp.float32)

        def close(spot):
            for part in range(len(self.terms)):
                self.pair_copy(part, spot).wait_send()
            for way, passed in ((UP, spot > line.at), (DOWN, spot < line.at)):

                @pl.when(passed)
                def _(way=way):
                    for part in range(len(self.terms)):
                        self.way_copy(part, way, spot).wait_send()

        each(line.size, close)


def run_ticks(task, first, last):
    if task is not None:
        for step in range(first, last):
            task.tick(step)


def head_slice(matrix, head):
    return matrix[:, head * HEAD_DIM : (head + 1) * HEAD_DIM]


def soft_rows(queries, keys_in):
    scores = dot_nt(queries, keys_in) * (HEAD_DIM ** (-0.5))
    exponent = jnp.exp(scores - jnp.max(scores, axis=-1, keepdims=True))
    return exponent / jnp.sum(exponent, axis=-1, keepdims=True)


def forward_kernel(
    layer_idx,
    res_ref,
    mod_ref,
    vec_ref,
    qkv_bias_ref,
    up_bias_ref,
    w_qkv_far,
    w_up_far,
    w_out_far,
    *rest,
):
    with_gather = len(rest) > 31
    shards, rest = (rest[:3], rest[3:]) if with_gather else ((), rest)
    res_out, kept = rest[0], rest[1:9]
    wholes, rest = (rest[9:12], rest[12:]) if with_gather else ((), rest[9:])
    rows_a, qkv_out, mixed_out, branch_out, mid_out, rows_m, upper_out, down_out = rest[:8]
    w_qkv_ref, w_up_ref, w_out_ref = rest[8:11]
    (
        part_a,
        near_a,
        far_out_a,
        far_in_a,
        part_m,
        near_m,
        far_out_m,
        far_in_m,
        sends,
        recvs,
        move_sems,
    ) = rest[11:22]
    group_width = w_qkv_ref.shape[1] // 3
    w_attn_ref, w_down_ref = w_out_ref.at[0:group_width, :], w_out_ref.at[group_width:, :]
    far = (w_qkv_far, w_out_far, w_up_far)
    pairs = list(zip(far, (w_qkv_ref, w_out_ref, w_up_ref))) + list(zip(rest[:8], kept))
    moves = Moves(pairs, move_sems)
    moves.start(0, 1, 2)
    images = res_ref.shape[0]
    gather, last_step = None, 0
    if with_gather:
        line = Line()
        greet(line)
        own = [shard.at[layer_idx + 1] for shard in shards]
        gather = Gather(line, own, wholes, *rest[22:])
        last_step = line.size
    else:
        greet(None)
    spread_a = Spread(rows_a, sends.at[0], recvs.at[0])
    spread_m = Spread(rows_m, sends.at[1], recvs.at[1])
    collect_a = Collect(part_a, near_a, far_out_a, far_in_a, sends.at[2], recvs.at[2])
    collect_m = Collect(part_m, near_m, far_out_m, far_in_m, sends.at[3], recvs.at[3])

    def mod_row(image, piece):
        return mod_ref[image, pl.ds(piece, 1), :]

    def start_norm(image):
        normed, _ = norm_parts(res_ref[image])
        normed = normed * (1.0 + mod_row(image, 1)) + mod_row(image, 0)
        spread_a.put(image, normed.astype(jnp.bfloat16))

    def attend(image):
        spread_a.wait(image)
        rows = rows_a[image]
        projected = dot_nn(rows, w_qkv_ref[...]) + qkv_bias_ref[...]
        qkv = projected.astype(jnp.bfloat16)
        qkv_out[image] = qkv
        heads = []
        for head in range(group_width // HEAD_DIM):
            probs = soft_rows(
                head_slice(qkv[:, :group_width], head),
                head_slice(qkv[:, group_width : 2 * group_width], head),
            )
            heads.append(
                dot_nn(probs.astype(jnp.bfloat16), head_slice(qkv[:, 2 * group_width :], head))
            )
        mixed = jnp.concatenate(heads, axis=1).astype(jnp.bfloat16)
        mixed_out[image] = mixed
        collect_a.put(image, dot_nn(mixed, w_attn_ref[...]))

    def middle(image):
        branch = collect_a.take(image) + vec_ref[0:1, :]
        branch_out[image] = branch
        mid = res_ref[image] + mod_row(image, 2) * branch
        mid_out[image] = mid
        normed, _ = norm_parts(mid)
        normed = normed * (1.0 + mod_row(image, 4)) + mod_row(image, 3)
        spread_m.put(image, normed.astype(jnp.bfloat16))

    def feed(image):
        spread_m.wait(image)
        upper = dot_nn(rows_m[image], w_up_ref[...]) + up_bias_ref[...]
        upper_out[image] = upper
        collect_m.put(image, dot_nn(gelu_tanh(upper).astype(jnp.bfloat16), w_down_ref[...]))

    def finish(image):
        down = collect_m.take(image) + vec_ref[1:2, :]
        down_out[image] = down
        res_out[image] = mid_out[image] + mod_row(image, 5) * down

    def close(image):
        spread_a.close(image)
        spread_m.close(image)
        collect_a.close(image)
        collect_m.close(image)

    if with_gather:
        gather.start()
    each(images, start_norm)
    each(images, spread_a.forward)
    moves.wait(0, 1)
    each(images, attend)
    moves.start(3, 4, 5)
    run_ticks(gather, 1, min(2, last_step))
    each(images, collect_a.forward)
    each(images, middle)
    moves.start(6, 7)
    each(images, spread_m.forward)
    run_ticks(gather, 2, min(3, last_step))
    moves.wait(2)
    each(images, feed)
    moves.start(8, 9)
    run_ticks(gather, 3, min(4, last_step))
    each(images, collect_m.forward)
    each(images, finish)
    moves.start(10)
    each(images, close)
    moves.wait(*range(3, 11))
    if with_gather:
        each(max(last_step - 4, 0), lambda step: gather.tick(step + 4))
        gather.finish()


def forward_layer(
    residual, mod_vec, vec_bias, qkv_bias, up_bias, w_qkv, w_up, w_out, shards, layer_idx
):
    images, count, _ = residual.shape
    tokens = 4 * count
    low, full = jnp.bfloat16, jnp.float32
    shapes = [
        ((images, count, D), full),
        ((images, tokens, D), low),
        ((images, tokens, w_qkv.shape[1]), low),
        ((images, tokens, w_qkv.shape[1] // 3), low),
        ((images, count, D), full),
        ((images, count, D), full),
        ((images, tokens, D), low),
        ((images, tokens, w_up.shape[1]), full),
        ((images, count, D), full),
    ]
    scratch = [
        pltpu.SemaphoreType.DMA((4, images, 3)),
        pltpu.SemaphoreType.DMA((4, images, 3)),
        pltpu.SemaphoreType.DMA((11,)),
    ]
    near = [pltpu.VMEM(*shape) for shape in shapes[1:]]
    near += [pltpu.VMEM(weight.shape, low) for weight in (w_qkv, w_up, w_out)]
    if shards:
        dp_size = lax.axis_size("dp")
        shapes += [((dp_size,) + shard.shape[1:], low) for shard in shards]
        scratch += [
            pltpu.SemaphoreType.DMA((3, dp_size // 2, 3)),
            pltpu.SemaphoreType.DMA((3, dp_size // 2, 3)),
            pltpu.SemaphoreType.DMA((3,)),
        ]
    return pl.pallas_call(
        functools.partial(forward_kernel, layer_idx),
        out_shape=[jax.ShapeDtypeStruct(*shape) for shape in shapes],
        in_specs=[pl.BlockSpec(memory_space=pltpu.VMEM)] * 5
        + [pl.BlockSpec(memory_space=pl.ANY)] * (3 + len(shards)),
        out_specs=[pl.BlockSpec(memory_space=pltpu.VMEM)]
        + [pl.BlockSpec(memory_space=pl.ANY)] * (len(shapes) - 1),
        scratch_shapes=near
        + collect_scratch(images, tokens)
        + collect_scratch(images, tokens)
        + scratch,
        compiler_params=pltpu.CompilerParams(
            collective_id=16 + layer_idx, has_side_effects=True, vmem_limit_bytes=ACT_VMEM
        ),
        cost_estimate=pl.CostEstimate(
            flops=30 * 10**9, bytes_accessed=15 * 2**20, transcendentals=0
        ),
        name="block_forward",
    )(residual, mod_vec, vec_bias, qkv_bias, up_bias, w_qkv, w_up, w_out, *shards)


def flat(ref):
    value = ref[...]
    return value.reshape(-1, value.shape[-1])


def forward_all_kernel(
    count_all,
    res_ref,
    mod_ref,
    vec_ref,
    qkv_bias_ref,
    up_bias_ref,
    final_shift_ref,
    final_scale_ref,
    head_ref,
    targets_ref,
    qkv_far,
    up_far,
    out_far,
    *rest,
):
    shards, rest = rest[0:3], rest[3:]
    d_res_out, d_head_out, loss_out, d_shift_out, d_scale_out = rest[0:5]
    kept_far, whole_far = rest[5:14], rest[14:17]
    kept, rest = rest[17:26], rest[26:]
    res_all, rows_a_all, qkv_all, mixed_all, branch_all, mid_all, rows_m_all, upper_all, down_all = kept
    w_qkv_all, w_up_all, w_blocks_all, w_out_all = rest[0:4]
    part_a, near_a, far_out_a, far_in_a, part_m, near_m, far_out_m, far_in_m = rest[4:12]
    sends, recvs, keep_sems, load_sems, whole_sems, gather_sends, gather_recvs, local_sems = rest[12:]
    images = res_ref.shape[0]
    group_width = w_qkv_all.shape[-1] // 3
    line = Line()
    last_step = line.size
    loads = Moves(
        [(qkv_far, w_qkv_all.at[0]), (out_far, w_blocks_all.at[0]), (up_far, w_up_all.at[0])],
        load_sems,
    )
    loads.start(0, 1, 2)
    greet(line)
    gathers = [None]
    for layer_idx in range(1, LAYERS):
        gathers.append(
            Gather(
                line,
                [shard.at[layer_idx] for shard in shards],
                [whole.at[layer_idx] for whole in (w_qkv_all, w_up_all, w_blocks_all)],
                gather_sends.at[layer_idx],
                gather_recvs.at[layer_idx],
                local_sems.at[layer_idx],
            )
        )
    gathers.append(None)

    def join_blocks(layer_idx):
        rows = w_blocks_all.shape[2]
        for pair in range(w_blocks_all.shape[1] // 2):
            halves = [
                w_blocks_all[layer_idx, 2 * pair + side].astype(jnp.float32) for side in range(2)
            ]
            w_out_all[layer_idx, 2 * rows * pair : 2 * rows * (pair + 1), :] = jnp.concatenate(
                halves, axis=0
            ).astype(jnp.bfloat16)

    def mod_row(layer_idx, image, piece):
        return mod_ref[layer_idx, image, pl.ds(piece, 1), :]

    d_head_out[...] = jnp.zeros_like(d_head_out)
    loss_out[...] = jnp.zeros_like(loss_out)

    def final_loss(image, value):
        normed, _ = norm_parts(value)
        final_in = normed * (1.0 + final_scale_ref[image]) + final_shift_ref[image]
        error_all = dense_nt(final_in, head_ref[...]) - targets_ref[image]
        loss_out[...] += square_sum(error_all) / count_all
        d_pred = 2.0 * error_all / count_all
        d_head_out[...] += dense_tn(d_pred, final_in)
        d_value, d_shift, d_scale = norm_pull(
            value, final_scale_ref[image], dense(d_pred, head_ref[...])
        )
        d_shift_out[image] = d_shift
        d_scale_out[image] = d_scale
        d_res_out[image] = d_value

    for layer_idx in range(LAYERS):
        res, rows_a, qkv_out, mixed_out, branch_out, mid_out, rows_m, upper_out, down_out = [
            ref.at[layer_idx] for ref in kept
        ]
        w_qkv, w_up, w_out = w_qkv_all.at[layer_idx], w_up_all.at[layer_idx], w_out_all.at[layer_idx]
        w_attn, w_down = w_out.at[0:group_width, :], w_out.at[group_width:, :]
        spread_a = Spread(rows_a, sends.at[layer_idx, 0], recvs.at[layer_idx, 0])
        spread_m = Spread(rows_m, sends.at[layer_idx, 1], recvs.at[layer_idx, 1])
        collect_a = Collect(
            part_a,
            near_a.at[layer_idx],
            far_out_a.at[layer_idx],
            far_in_a.at[layer_idx],
            sends.at[layer_idx, 2],
            recvs.at[layer_idx, 2],
        )
        collect_m = Collect(
            part_m,
            near_m.at[layer_idx],
            far_out_m.at[layer_idx],
            far_in_m.at[layer_idx],
            sends.at[layer_idx, 3],
            recvs.at[layer_idx, 3],
        )
        keep = Moves(
            [(ref.at[layer_idx], far.at[layer_idx]) for ref, far in zip(kept, kept_far)],
            keep_sems.at[layer_idx],
        )
        keep_whole = Moves(
            [
                (ref.at[layer_idx], far.at[layer_idx])
                for ref, far in zip((w_qkv_all, w_up_all, w_out_all), whole_far)
            ],
            whole_sems.at[layer_idx],
        )
        gather = gathers[layer_idx + 1]

        def start_norm(image, at, values, target):
            normed, _ = norm_parts(values)
            normed = normed * (1.0 + mod_row(at, image, 1)) + mod_row(at, image, 0)
            target.put(image, normed.astype(jnp.bfloat16))

        def first_norm(image, res=res, spread_a=spread_a):
            res[image] = res_ref[image]
            start_norm(image, 0, res_ref[image], spread_a)

        def attend(image):
            spread_a.wait(image)
            projected = dot_nn(rows_a[image], flat(w_qkv)) + qkv_bias_ref[layer_idx]
            qkv = projected.astype(jnp.bfloat16)
            qkv_out[image] = qkv
            heads = []
            for head in range(group_width // HEAD_DIM):
                probs = soft_rows(
                    head_slice(qkv[:, :group_width], head),
                    head_slice(qkv[:, group_width : 2 * group_width], head),
                )
                heads.append(
                    dot_nn(probs.astype(jnp.bfloat16), head_slice(qkv[:, 2 * group_width :], head))
                )
            mixed = jnp.concatenate(heads, axis=1).astype(jnp.bfloat16)
            mixed_out[image] = mixed
            collect_a.put(image, dot_nn(mixed, w_attn[...]))

        def middle(image):
            branch = collect_a.take(image) + vec_ref[layer_idx, 0:1, :]
            branch_out[image] = branch
            mid = res[image] + mod_row(layer_idx, image, 2) * branch
            mid_out[image] = mid
            normed, _ = norm_parts(mid)
            normed = normed * (1.0 + mod_row(layer_idx, image, 4)) + mod_row(layer_idx, image, 3)
            spread_m.put(image, normed.astype(jnp.bfloat16))

        def feed(image):
            spread_m.wait(image)
            upper = dot_nn(rows_m[image], flat(w_up)) + up_bias_ref[layer_idx]
            upper_out[image] = upper
            collect_m.put(image, dot_nn(gelu_tanh(upper).astype(jnp.bfloat16), w_down[...]))

        def finish(image):
            down = collect_m.take(image) + vec_ref[layer_idx, 1:2, :]
            down_out[image] = down
            value = mid_out[image] + mod_row(layer_idx, image, 5) * down
            if layer_idx + 1 < LAYERS:
                res_all[layer_idx + 1, image] = value
                following = Spread(
                    rows_a_all.at[layer_idx + 1],
                    sends.at[layer_idx + 1, 0],
                    recvs.at[layer_idx + 1, 0],
                )
                start_norm(image, layer_idx + 1, value, following)
            else:
                final_loss(image, value)

        def close(image):
            spread_a.close(image)
            spread_m.close(image)
            collect_a.close(image)
            collect_m.close(image)

        if layer_idx == 0:
            gather.start()
            each(images, first_norm)
        if layer_idx > 0:
            run_ticks(gather, 1, min(2, last_step))
        each(images, spread_a.forward)
        if layer_idx == 0:
            loads.wait(0, 1)
            join_blocks(0)
        each(images, attend)
        keep.start(0, 1, 2, 3)
        at = 1 if layer_idx == 0 else 2
        run_ticks(gather, at, min(at + 1, last_step))
        each(images, collect_a.forward)
        each(images, middle)
        keep.start(4, 5)
        each(images, spread_m.forward)
        at = 2 if layer_idx == 0 else 3
        run_ticks(gather, at, min(at + 1, last_step))
        if layer_idx == 0:
            loads.wait(2)
        each(images, feed)
        keep.start(6, 7)
        if layer_idx == 0:
            run_ticks(gather, 3, min(4, last_step))
        if gather is not None and gathers[layer_idx + 2] is not None:
            gathers[layer_idx + 2].start()
        each(images, collect_m.forward)
        each(images, finish)
        keep.start(8)
        keep_whole.start(0, 1, 2)
        each(images, close)
        if gather is not None:
            each(max(last_step - 4, 0), lambda step, gather=gather: gather.tick(step + 4))
            gather.finish()
            join_blocks(layer_idx + 1)
        keep.wait(*range(9))
        keep_whole.wait(0, 1, 2)


def forward_all(
    count_all, residual, mod_vecs, vec_bias, qkv_bias, up_bias, finals, wholes, shards
):
    images, count, _ = residual.shape
    tokens = 4 * count
    low, full = jnp.bfloat16, jnp.float32
    dp_size = lax.axis_size("dp")
    qkv_width, units = wholes[0].shape[-1], wholes[1].shape[-1]
    own = (images, count, D)
    kept = [
        (own, full),
        ((images, tokens, D), low),
        ((images, tokens, qkv_width), low),
        ((images, tokens, qkv_width // 3), low),
        (own, full),
        (own, full),
        ((images, tokens, D), low),
        ((images, tokens, units), full),
        (own, full),
    ]
    kept = [((LAYERS,) + shape, kind) for shape, kind in kept]
    out_rows = wholes[2].shape[0] * wholes[2].shape[1]
    matrices = [
        ((LAYERS,) + wholes[0].shape, low),
        ((LAYERS,) + wholes[1].shape, low),
        ((LAYERS, out_rows, D), low),
    ]
    shapes = [(own, full), (finals[2].shape, full), ((1, 1), full)]
    shapes += [(finals[0].shape, full), (finals[1].shape, full)]
    shapes += kept + matrices
    collect = [
        pltpu.VMEM((images, tokens, D), low),
        pltpu.VMEM((LAYERS, images, 2, count, D), low),
        pltpu.VMEM((LAYERS, images, count, D), low),
        pltpu.VMEM((LAYERS, images, count, D), low),
    ]
    return pl.pallas_call(
        functools.partial(forward_all_kernel, count_all),
        out_shape=[jax.ShapeDtypeStruct(*shape) for shape in shapes],
        in_specs=[pl.BlockSpec(memory_space=pltpu.VMEM)] * 9
        + [pl.BlockSpec(memory_space=pl.ANY)] * 6,
        out_specs=[pl.BlockSpec(memory_space=pltpu.VMEM)] * 5
        + [pl.BlockSpec(memory_space=pl.ANY)] * (len(shapes) - 5),
        scratch_shapes=[pltpu.VMEM(*shape) for shape in kept]
        + [
            pltpu.VMEM(*matrices[0]),
            pltpu.VMEM(*matrices[1]),
            pltpu.VMEM((LAYERS,) + wholes[2].shape, low),
            pltpu.VMEM(*matrices[2]),
        ]
        + collect
        + collect
        + [
            pltpu.SemaphoreType.DMA((LAYERS, 4, images, 3)),
            pltpu.SemaphoreType.DMA((LAYERS, 4, images, 3)),
            pltpu.SemaphoreType.DMA((LAYERS, 9)),
            pltpu.SemaphoreType.DMA((3,)),
            pltpu.SemaphoreType.DMA((LAYERS, 3)),
            pltpu.SemaphoreType.DMA((LAYERS, 3, dp_size // 2, 3)),
            pltpu.SemaphoreType.DMA((LAYERS, 3, dp_size // 2, 3)),
            pltpu.SemaphoreType.DMA((LAYERS, 3)),
        ],
        compiler_params=pltpu.CompilerParams(
            collective_id=24, has_side_effects=True, vmem_limit_bytes=ACT_VMEM
        ),
        name="blocks_forward",
    )(residual, mod_vecs, vec_bias, qkv_bias, up_bias, *finals, *wholes, *shards)


def gelu_slope(values):
    root = math.sqrt(2.0 / math.pi)
    square = values * values
    tanh = jnp.tanh(root * (values + 0.044715 * values * square))
    half = 0.5 * (1.0 + tanh)
    slope = half + 0.5 * values * (1.0 - tanh * tanh) * root * (1.0 + 3.0 * 0.044715 * square)
    return values * half, slope


def norm_pull(values, scale_row, d_normed):
    normed, rstd = norm_parts(values)
    d_shift = jnp.sum(d_normed, axis=0, keepdims=True)
    d_scale = jnp.sum(d_normed * normed, axis=0, keepdims=True)
    inner = d_normed * (1.0 + scale_row)
    mean_one = jnp.mean(inner, axis=-1, keepdims=True)
    mean_two = jnp.mean(inner * normed, axis=-1, keepdims=True)
    return (inner - mean_one - normed * mean_two) * rstd, d_shift, d_scale


def backward_kernel(layer_idx, d_res_ref, mod_ref, *rest):
    kept, rest = rest[:12], rest[12:]
    if layer_idx is not None:
        kept = [ref.at[layer_idx] for ref in kept]
    with_reduce = len(rest) > 40
    terms, rest = (rest[:3], rest[3:]) if with_reduce else ((), rest)
    d_res_out, d_far, (d_mod, d_vec, d_qkv_bias, d_up_bias) = rest[0], rest[1:4], rest[4:8]
    totals, square_out = (rest[8:11], rest[11]) if with_reduce else ((), None)
    rest = rest[12:] if with_reduce else rest[8:]
    (
        res_ref,
        rows_a,
        qkv_ref,
        mixed_ref,
        branch_ref,
        mid_ref,
        rows_m,
        upper_ref,
        down_ref,
        w_qkv_ref,
        w_up_ref,
        w_out_ref,
        d_w_qkv,
        d_w_up,
        d_out,
    ) = rest[:15]
    (
        d_mid,
        d_rows_m,
        d_rows_a,
        act_low,
        d_upper,
        d_qkv,
        part_a,
        near_a,
        far_out_a,
        far_in_a,
        part_m,
        near_m,
        far_out_m,
        far_in_m,
        sends,
        recvs,
        move_sems,
    ) = rest[15:32]
    group_width = w_qkv_ref.shape[-1] // 3
    w_attn_ref, w_down_ref = w_out_ref.at[0:group_width, :], w_out_ref.at[group_width:, :]
    pairs = list(zip(kept, rest[:12])) + list(zip(rest[12:15], d_far))
    moves = Moves(pairs, move_sems)
    moves.start(8, 11, 7, 10, 6, 5, 4, 2, 9, 3, 1, 0)
    images = res_ref.shape[0]
    tokens = rows_a.shape[1]
    qkv_width = 3 * group_width
    units = w_up_ref.shape[-1]
    reduce, last_step = None, 0
    if with_reduce:
        line = Line()
        greet(line)
        own, pair_in, way_in, way_out = rest[32:35], rest[35:38], rest[38:41], rest[41:44]
        reduce = Reduce(line, terms, totals, own, pair_in, way_in, way_out, *rest[44:])
        last_step = line.size
    else:
        greet(None)
    spread_m = Spread(d_rows_m, sends.at[0], recvs.at[0])
    spread_a = Spread(d_rows_a, sends.at[1], recvs.at[1])
    collect_m = Collect(part_m, near_m, far_out_m, far_in_m, sends.at[2], recvs.at[2])
    collect_a = Collect(part_a, near_a, far_out_a, far_in_a, sends.at[3], recvs.at[3])
    d_vec[...] = jnp.zeros_like(d_vec)
    d_qkv_bias[...] = jnp.zeros_like(d_qkv_bias)
    d_up_bias[...] = jnp.zeros_like(d_up_bias)

    def mod_row(image, piece):
        return mod_ref[image, pl.ds(piece, 1), :]

    def start_down(image):
        d_res = d_res_ref[image]
        d_mod[image, pl.ds(5, 1), :] = jnp.sum(d_res * down_ref[image], axis=0, keepdims=True)
        d_down = d_res * mod_row(image, 5)
        d_vec[1:2, :] += jnp.sum(d_down, axis=0, keepdims=True)
        spread_m.put(image, d_down.astype(jnp.bfloat16))

    def feed(image):
        spread_m.wait(image)
        d_act = dot_nt(d_rows_m[image], w_down_ref[...])
        act, slope = gelu_slope(upper_ref[image])
        act_low[image] = act.astype(jnp.bfloat16)
        d_up = d_act * slope
        d_up_bias[...] += jnp.sum(d_up, axis=0, keepdims=True)
        d_up_low = d_up.astype(jnp.bfloat16)
        d_upper[image] = d_up_low
        collect_m.put(image, dot_nt(d_up_low, flat(w_up_ref)))

    def rows_of(ref, width):
        return ref[...].reshape(images * tokens, width)

    def feed_weights():
        tile = 256

        def step(index, carry):
            at = pl.ds(pl.multiple_of(index * tile, tile), tile)
            grad = dot_tn(
                act_low[:, :, at].reshape(images * tokens, tile), rows_of(d_rows_m, D)
            )
            d_out[pl.ds(pl.multiple_of(group_width + index * tile, 64), tile), :] = grad.astype(
                jnp.bfloat16
            )
            grad = dot_tn(
                rows_m[:, :, at].reshape(images * tokens, tile), rows_of(d_upper, units)
            )
            d_w_up[pl.ds(pl.multiple_of(index * tile, tile), tile), :] = grad.astype(jnp.bfloat16)
            return carry

        lax.fori_loop(0, units // tile, step, 0)

    def middle(image):
        d_value, d_shift, d_scale = norm_pull(
            mid_ref[image], mod_row(image, 4), collect_m.take(image)
        )
        d_mod[image, pl.ds(3, 1), :] = d_shift
        d_mod[image, pl.ds(4, 1), :] = d_scale
        d_value = d_res_ref[image] + d_value
        d_mid[image] = d_value
        d_mod[image, pl.ds(2, 1), :] = jnp.sum(d_value * branch_ref[image], axis=0, keepdims=True)
        d_branch = d_value * mod_row(image, 2)
        d_vec[0:1, :] += jnp.sum(d_branch, axis=0, keepdims=True)
        spread_a.put(image, d_branch.astype(jnp.bfloat16))

    def attend(image):
        spread_a.wait(image)
        d_mixed = dot_nt(d_rows_a[image], w_attn_ref[...]).astype(jnp.bfloat16)
        qkv = qkv_ref[image]
        d_queries, d_keys, d_values = [], [], []
        scale_dot = HEAD_DIM ** (-0.5)
        for head in range(group_width // HEAD_DIM):
            queries = head_slice(qkv[:, :group_width], head)
            keys_in = head_slice(qkv[:, group_width : 2 * group_width], head)
            values_in = head_slice(qkv[:, 2 * group_width :], head)
            d_head = head_slice(d_mixed, head)
            probs = soft_rows(queries, keys_in)
            d_probs = dot_nt(d_head, values_in)
            d_values.append(dot_tn(probs.astype(jnp.bfloat16), d_head))
            inner = jnp.sum(probs * d_probs, axis=-1, keepdims=True)
            d_scores = (probs * (d_probs - inner)).astype(jnp.bfloat16)
            d_queries.append(dot_nn(d_scores, keys_in) * scale_dot)
            d_keys.append(dot_tn(d_scores, queries) * scale_dot)
        joined = jnp.concatenate(d_queries + d_keys + d_values, axis=1)
        d_qkv_bias[...] += jnp.sum(joined, axis=0, keepdims=True)
        joined = joined.astype(jnp.bfloat16)
        d_qkv[image] = joined
        collect_a.put(image, dot_nt(joined, flat(w_qkv_ref)))

    def attend_weights():
        d_out[0:group_width, :] = dot_tn(
            rows_of(mixed_ref, group_width), rows_of(d_rows_a, D)
        ).astype(jnp.bfloat16)
        tile = 256

        def step(index, carry):
            at = pl.ds(pl.multiple_of(index * tile, tile), tile)
            grad = dot_tn(
                rows_a[:, :, at].reshape(images * tokens, tile), rows_of(d_qkv, qkv_width)
            )
            d_w_qkv[at, :] = grad.astype(jnp.bfloat16)
            return carry

        lax.fori_loop(0, D // tile, step, 0)

    def finish(image):
        d_value, d_shift, d_scale = norm_pull(
            res_ref[image], mod_row(image, 1), collect_a.take(image)
        )
        d_mod[image, pl.ds(0, 1), :] = d_shift
        d_mod[image, pl.ds(1, 1), :] = d_scale
        d_res_out[image] = d_mid[image] + d_value

    def close(image):
        spread_a.close(image)
        spread_m.close(image)
        collect_a.close(image)
        collect_m.close(image)

    if with_reduce:
        reduce.start()
    moves.wait(8)
    each(images, start_down)
    each(images, spread_m.forward)
    moves.wait(11, 7, 10)
    each(images, feed)
    if with_reduce:
        reduce.wait_own()
    run_ticks(reduce, 0, min(1, last_step - 1))
    each(images, collect_m.forward)
    moves.wait(6)
    feed_weights()
    moves.start(13)
    moves.wait(5, 4)
    each(images - 1, middle)
    run_ticks(reduce, 1, min(2, last_step - 1))
    middle(images - 1)
    each(images, spread_a.forward)
    moves.wait(2, 9)
    each(images - 1, attend)
    run_ticks(reduce, 2, min(3, last_step - 1))
    attend(images - 1)
    each(images, collect_a.forward)
    moves.wait(3, 1)
    attend_weights()
    moves.start(12, 14)
    moves.wait(0)
    each(images, finish)
    each(images, close)
    if with_reduce:
        each(max(last_step - 4, 0), lambda step: reduce.tick(step + 3))
        reduce.finish()
        square_out[...] = jnp.broadcast_to(
            sum(square_sum(total[...]) for total in totals), square_out.shape
        )
    moves.wait(12, 13, 14)


def backward_layer(d_residual, mod_vec, saved, weights, terms, layer_idx, stacked):
    images, count, _ = d_residual.shape
    tokens = 4 * count
    low, full = jnp.bfloat16, jnp.float32
    w_qkv, w_up, w_out = weights
    group_width, units = w_qkv.shape[-1] // 3, w_up.shape[-1]
    shapes = [
        ((images, count, D), full),
        ((D, 3 * group_width), low),
        ((D, units), low),
        ((group_width + units, D), low),
        ((images, 6, D), full),
        ((2, D), full),
        ((1, 3 * group_width), full),
        ((1, units), full),
    ]
    scratch = [
        pltpu.SemaphoreType.DMA((4, images, 3)),
        pltpu.SemaphoreType.DMA((4, images, 3)),
        pltpu.SemaphoreType.DMA((15,)),
    ]
    near = [
        pltpu.VMEM(kept.shape[1:] if stacked else kept.shape, kept.dtype)
        for kept in tuple(saved) + tuple(weights)
    ]
    near += [pltpu.VMEM(*shape) for shape in shapes[1:4]]
    if terms:
        spots = lax.axis_size("dp") // 2
        blocks = [term.shape[1:] for term in terms]
        shapes += [(block, full) for block in blocks] + [((8, 128), full)]
        scratch += [pltpu.VMEM((spots,) + block, low) for block in blocks]
        scratch += [pltpu.VMEM((spots,) + block, low) for block in blocks]
        scratch += [pltpu.VMEM((2, spots) + block, low) for block in blocks]
        scratch += [pltpu.VMEM((2, spots) + block, low) for block in blocks]
        scratch += [
            pltpu.SemaphoreType.DMA((3, spots, 3)),
            pltpu.SemaphoreType.DMA((3, spots, 3)),
            pltpu.SemaphoreType.DMA((3, spots)),
        ]
    return pl.pallas_call(
        functools.partial(backward_kernel, layer_idx if stacked else None),
        out_shape=[jax.ShapeDtypeStruct(*shape) for shape in shapes],
        in_specs=[pl.BlockSpec(memory_space=pltpu.VMEM)] * 2
        + [pl.BlockSpec(memory_space=pl.ANY)] * (12 + len(terms)),
        out_specs=[pl.BlockSpec(memory_space=pltpu.VMEM)]
        + [pl.BlockSpec(memory_space=pl.ANY)] * 3
        + [pl.BlockSpec(memory_space=pltpu.VMEM)] * (len(shapes) - 4),
        scratch_shapes=near
        + [
            pltpu.VMEM((images, count, D), full),
            pltpu.VMEM((images, tokens, D), low),
            pltpu.VMEM((images, tokens, D), low),
            pltpu.VMEM((images, tokens, units), low),
            pltpu.VMEM((images, tokens, units), low),
            pltpu.VMEM((images, tokens, 3 * group_width), low),
        ]
        + collect_scratch(images, tokens)
        + collect_scratch(images, tokens)
        + scratch,
        compiler_params=pltpu.CompilerParams(
            collective_id=20 + layer_idx if stacked else (21 if terms else 23), has_side_effects=True, vmem_limit_bytes=ACT_VMEM
        ),
        cost_estimate=pl.CostEstimate(
            flops=60 * 10**9, bytes_accessed=25 * 2**20, transcendentals=0
        ),
        name="block_backward",
    )(d_residual, mod_vec, *saved, *weights, *terms)


def dense_nt(left_op, right_op):
    return lax.dot_general(
        left_op,
        right_op,
        (((1,), (1,)), ((), ())),
        precision=PRECISE,
        preferred_element_type=jnp.float32,
    )


def dense_tn(left_op, right_op):
    return lax.dot_general(
        left_op,
        right_op,
        (((0,), (0,)), ((), ())),
        precision=PRECISE,
        preferred_element_type=jnp.float32,
    )


def chosen(shape, rule, kind):
    row = lax.broadcasted_iota(jnp.int32, shape, 0)
    col = lax.broadcasted_iota(jnp.int32, shape, 1)
    return jnp.where(rule(row, col), 1.0, 0.0).astype(kind)


def fold(values):
    groups = values.shape[-2] // 8
    pieces = [values[..., 8 * at : 8 * at + 8, :] for at in range(groups)]
    used = groups * values.shape[-1]
    if used % 128:
        pieces.append(jnp.zeros(values.shape[:-2] + (8, 128 - used % 128), values.dtype))
    return jnp.concatenate(pieces, axis=-1)


def folded_lanes(cols, count):
    return -(-(cols // 8 * count) // 128) * 128


def unfold_all(values, cols, count):
    ordered = [
        values[tensor_at, dp_at]
        for dp_at in range(values.shape[1])
        for tensor_at in range(values.shape[0])
    ]
    return jnp.concatenate([unfold(value, cols, count) for value in ordered], axis=0)


def unfold(values, cols, count):
    pieces = [values[..., at * count : (at + 1) * count] for at in range(cols // 8)]
    return jnp.concatenate(pieces, axis=-2)


def slots_of(images):
    return -(-LAYERS * images // 16) * 16


def head_kernel(
    images,
    small_ref,
    feats_ref,
    table_ref,
    time_ref,
    second_ref,
    shift_ref,
    scale_ref,
    bias_ref,
    mod_ref,
    *rest,
):
    shards = rest[0:3]
    (
        small_all,
        feats_out,
        pre_time_out,
        hidden_out,
        pre_signal_out,
        signal_out,
        final_all,
        mod_all,
    ) = rest[3:11]
    wholes = rest[11:14]
    (
        feats_all,
        hidden_own,
        hidden_dp,
        hidden_all,
        signal_own,
        signal_dp,
        signal_all,
        final_own,
        final_dp,
        mod_part,
        mod_in,
        mod_own,
        small_dp,
    ) = rest[14:27]
    crowds = [rest[27 + 3 * index : 30 + 3 * index] for index in range(11)]
    gather_sems = rest[60:]
    dp_size = lax.axis_size("dp")
    tensor_size = lax.axis_size("tensor")
    dp_rank = lax.axis_index("dp")
    images_all = images * dp_size
    slots = mod_own.shape[0]
    greet_groups("dp", "tensor")
    gather = Gather(Line(), [shard.at[0] for shard in shards], wholes, *gather_sems)
    feats = Crowd("dp", lambda place: feats_ref, feats_all, *crowds[0])
    mod_sum = Crowd("dp", lambda place: mod_part.at[place], mod_in, *crowds[1])
    mod_spread = Crowd("tensor", lambda place: mod_own, mod_all, *crowds[2])
    small = Relay(lambda place: small_ref, small_dp, small_all, *crowds[3:5])
    hidden = Relay(lambda place: hidden_own, hidden_dp, hidden_all, *crowds[5:7])
    signal = Relay(lambda place: signal_own, signal_dp, signal_all, *crowds[7:9])
    final = Relay(lambda place: final_own.at[place], final_dp, final_all, *crowds[9:11])
    line = gather.line
    first, last = line.at == 0, line.at == line.size - 1
    feats.start()
    gather.start()
    feats.wait()
    pick = chosen(
        (images_all, 8 * dp_size),
        lambda row, col: (row // images == col // 8) & (lax.rem(row, images) == lax.rem(col, 8)),
        jnp.float32,
    )
    feats_sum = dense(pick, feats_all[...].reshape(8 * dp_size, feats_all.shape[2]))
    feats_out[...] = feats_sum
    pre_time = dense_nt(time_ref[...], feats_sum[:, 0:FREQ]) + bias_ref[:, 1:2]
    pre_time_out[...] = pre_time
    hidden_own[...] = fold(jax.nn.silu(pre_time))
    hidden.start()
    class_lanes = -(-CLASSES // 128) * 128
    labels = jnp.round(feats_sum[:, FREQ : FREQ + 1]).astype(jnp.int32)
    lane = lax.broadcasted_iota(jnp.int32, (images_all, class_lanes), 1)
    onehot = jnp.where(lane == labels, 1.0, 0.0)
    class_part = dense_nt(table_ref[:, 0:class_lanes], onehot) + bias_ref[:, 2:3]
    small.start()
    hidden.hand_on()
    for way in (UP, DOWN):
        gather.hand_on(1, way)
    gather.hand_over(1, UP)
    gather.hand_over(1, DOWN, first)
    hidden.wait()
    cols = second_ref.shape[0]
    hidden_full = unfold_all(hidden_all[...], cols, images_all)
    hidden_out[...] = hidden_full
    pre_signal = dense(second_ref[...], hidden_full) + class_part
    pre_signal_out[...] = pre_signal
    signal_own[...] = fold(jax.nn.silu(pre_signal))
    signal.start()
    small.hand_on()
    signal.hand_on()
    for way in (UP, DOWN):
        gather.hand_on(2, way)
    gather.hand_over(1, DOWN, jnp.logical_not(first))
    gather.hand_over(2, UP, last)
    gather.hand_over(2, DOWN, first)
    signal.wait()
    signal_full = unfold_all(signal_all[...], cols, images_all)
    signal_out[...] = signal_full
    mod_rows = mod_ref.shape[1]
    own_rows = pl.ds(pl.multiple_of(dp_rank * mod_rows, 8), mod_rows)
    signal_low = signal_out[own_rows, :].astype(jnp.bfloat16)
    total = None
    for layer_idx in range(LAYERS):
        pick = chosen(
            (images_all, dp_size * slots),
            lambda row, col: (
                (row // images == col // slots)
                & (lax.rem(row, images) + layer_idx * images == lax.rem(col, slots))
            ),
            jnp.bfloat16,
        )
        placed = dot_nn(signal_low, pick).astype(jnp.bfloat16)
        term = dot_tn(placed, mod_ref[layer_idx])
        total = term if total is None else total + term
    mod_part[...] = total.reshape(mod_part.shape).astype(mod_part.dtype)
    mod_sum.start()
    gather.hand_over(2, UP, jnp.logical_not(last))
    gather.hand_over(2, DOWN, jnp.logical_not(first))
    finals = jnp.concatenate(
        [
            dense(shift_ref[...], signal_full) + bias_ref[:, 3:4],
            dense(scale_ref[...], signal_full) + bias_ref[:, 4:5],
            jnp.zeros((128 - 2 * shift_ref.shape[0], images_all), jnp.float32),
        ],
        axis=0,
    )
    pick = chosen(
        (8 * dp_size, images_all),
        lambda row, col: (row // 8 == col // images) & (lax.rem(row, 8) == lax.rem(col, images)),
        jnp.float32,
    )
    final_own[...] = dense_nt(pick, finals).reshape(final_own.shape)
    final.start()
    run_ticks(gather, 3, min(4, dp_size // 2))
    mod_sum.wait()
    mod_own[...] = jnp.sum(mod_in[...].astype(jnp.float32), axis=0)
    mod_spread.start()
    final.hand_on()
    each(max(dp_size // 2 - 4, 0), lambda step: gather.tick(step + 4))
    small.wait()
    final.wait()
    mod_spread.wait()
    gather.finish()


def head_call(small, feats, table, times, second, shift, scale, bias, mod_low, shards, images):
    dp_size, tensor_size = lax.axis_size("dp"), lax.axis_size("tensor")
    images_all = images * dp_size
    cols = table.shape[0]
    slots = slots_of(images)
    folded = folded_lanes(cols, images_all)
    full, low = jnp.float32, jnp.bfloat16
    shapes = [
        ((tensor_size, dp_size) + small.shape, full),
        ((images_all, feats.shape[1]), full),
        ((cols, images_all), full),
        ((D, images_all), full),
        ((cols, images_all), full),
        ((D, images_all), full),
        ((tensor_size, dp_size, 8, 128), full),
        ((tensor_size, slots, mod_low.shape[2]), full),
    ] + [((dp_size,) + shard.shape[1:], low) for shard in shards]
    scratch = [
        pltpu.VMEM((dp_size,) + feats.shape, full),
        pltpu.VMEM((8, folded), full),
        pltpu.VMEM((dp_size, 8, folded), full),
        pltpu.VMEM((tensor_size, dp_size, 8, folded), full),
        pltpu.VMEM((8, folded), full),
        pltpu.VMEM((dp_size, 8, folded), full),
        pltpu.VMEM((tensor_size, dp_size, 8, folded), full),
        pltpu.VMEM((dp_size, 8, 128), full),
        pltpu.VMEM((dp_size, 8, 128), full),
        pltpu.VMEM((dp_size, slots, mod_low.shape[2]), low),
        pltpu.VMEM((dp_size, slots, mod_low.shape[2]), low),
        pltpu.VMEM((slots, mod_low.shape[2]), full),
        pltpu.VMEM((dp_size,) + small.shape, full),
    ]
    for count in (dp_size, dp_size) + (tensor_size, dp_size) * 4 + (tensor_size,):
        scratch += crowd_scratch(count)
    scratch += [
        pltpu.SemaphoreType.DMA((3, dp_size // 2, 3)),
        pltpu.SemaphoreType.DMA((3, dp_size // 2, 3)),
        pltpu.SemaphoreType.DMA((3,)),
    ]
    return pl.pallas_call(
        functools.partial(head_kernel, images),
        out_shape=[jax.ShapeDtypeStruct(*shape) for shape in shapes],
        in_specs=[pl.BlockSpec(memory_space=pltpu.VMEM)] * 9
        + [pl.BlockSpec(memory_space=pl.ANY)] * len(shards),
        out_specs=[pl.BlockSpec(memory_space=pltpu.VMEM)] * 8
        + [pl.BlockSpec(memory_space=pl.ANY)] * len(shards),
        scratch_shapes=scratch,
        compiler_params=pltpu.CompilerParams(
            collective_id=30, has_side_effects=True, vmem_limit_bytes=ACT_VMEM
        ),
        name="head",
    )(small, feats, table, times, second, shift, scale, bias, mod_low, *shards)


def tail_kernel(
    images,
    final_at,
    row_ref,
    mod_ref,
    weight_ref,
    second_ref,
    shift_ref,
    scale_ref,
    pre_signal_ref,
    pre_time_ref,
    feats_ref,
    hidden_ref,
    signal_ref,
    loss_ref,
    *rest,
):
    terms, others = rest[0:3], rest[3 : 2 + LAYERS]
    rest = rest[2 + LAYERS :]
    table_grad, mod_grad, scalar_sums = rest[0:3]
    totals, rest = rest[3:6], rest[6:]
    (
        row_in,
        row_mid,
        row_fin,
        mod_in,
        mod_low,
        d_mod_all,
        signal_part,
        scalar_own,
        scalar_in,
        scalar_mid,
        scalar_fin,
    ) = rest[0:11]
    signal_refs, hidden_refs = rest[11:15], rest[15:19]
    own, pair_in, way_in, way_out = rest[19:22], rest[22:25], rest[25:28], rest[28:31]
    crowds = [rest[31 + 3 * index : 34 + 3 * index] for index in range(10)]
    reduce_sems = rest[61:]
    signal_out, hidden_out = signal_refs[0], hidden_refs[0]
    dp_size = lax.axis_size("dp")
    tensor_size = lax.axis_size("tensor")
    places = dp_size * tensor_size
    dp_rank = lax.axis_index("dp")
    images_all = images * dp_size
    cols, lanes = row_ref.shape[2:]
    mod_rows = weight_ref.shape[1]
    slots = mod_low.shape[0]
    last_step = dp_size // 2
    greet_groups("tensor", "dp")
    reduce = Reduce(Line(), terms, totals, own, pair_in, way_in, way_out, *reduce_sems)
    mod_sum = Crowd("tensor", lambda place: mod_ref.at[place], mod_in, *crowds[0])
    mod_spread = Crowd("dp", lambda place: mod_low, d_mod_all, *crowds[1])
    rows = Funnel(row_ref, row_in, row_mid, row_fin, *crowds[2:4])
    signal = Funnel(*signal_refs, *crowds[4:6])
    hidden = Funnel(*hidden_refs, *crowds[6:8])
    scalars = Crowd("tensor", lambda place: scalar_own, scalar_in, *crowds[8])
    scalars_dp = Crowd("dp", lambda place: scalar_mid, scalar_fin, *crowds[9])
    mod_sum.start()
    rows.start()
    reduce.send_pair(0)
    reduce.load_own()
    mod_sum.wait()
    mod_low[...] = jnp.sum(mod_in[...], axis=0).astype(jnp.bfloat16)
    mod_spread.start()
    rows.hand_on()
    reduce.send_pair(1)
    other_squares = sum(other[0:1, 0:1] for other in others)
    reduce.wait_own()
    row_total = rows.take()
    patch_start, time_start, second_start, final_start, head_start, vector_start, layer_start = (
        table_starts()
    )
    patch_in = time_start - patch_start
    layer_at = 2 * patch_in + 1

    def put(start, values):
        table_grad[:, start : start + values.shape[1]] = values

    put(patch_start, row_total[:, 0:patch_in])
    put(head_start, row_total[:, patch_in:layer_at])
    put(layer_start, row_total[:, layer_at:final_at])
    joined = jnp.concatenate([row_fin[at] for at in range(dp_size)], axis=1)

    def final_of(piece):
        return dense(
            joined,
            chosen(
                (dp_size * lanes, images_all),
                lambda row, col: (
                    (row // lanes == col // images)
                    & (lax.rem(row, lanes) == final_at + piece * images + lax.rem(col, images))
                ),
                jnp.float32,
            ),
        )

    d_shift, d_scale = final_of(0), final_of(1)
    signal_part[...] = dense_tn(shift_ref[...], d_shift) + dense_tn(scale_ref[...], d_scale)
    mod_spread.wait()
    d_mod = d_mod_all[...].reshape(dp_size * slots, mod_low.shape[1])
    own_rows = pl.ds(pl.multiple_of(dp_rank * mod_rows, 8), mod_rows)

    def layer_pick(layer_idx, kind):
        return chosen(
            (dp_size * slots, images_all),
            lambda row, col: (
                (row // slots == col // images)
                & (lax.rem(row, slots) == layer_idx * images + lax.rem(col, images))
            ),
            kind,
        )

    for layer_idx in range(LAYERS):
        signal_part[own_rows, :] += dense(
            dot_nt(weight_ref[layer_idx], d_mod), layer_pick(layer_idx, jnp.float32)
        )
    signal_out[...] = fold(signal_part[...].reshape(places, cols, images_all)).reshape(
        signal_out.shape
    )
    signal.start()
    signal.hand_on()
    reduce.send_pair(2)
    run_ticks(reduce, 0, min(1, last_step - 1))
    signal_low = signal_ref[own_rows, :].astype(jnp.bfloat16)
    for layer_idx in range(LAYERS):
        placed = dot_nt(signal_low, layer_pick(layer_idx, jnp.bfloat16)).astype(jnp.bfloat16)
        grad = dot_nn(placed, d_mod)
        mod_grad[layer_idx] = grad
        other_squares = other_squares + square_sum(grad)
    grad = dense_nt(d_shift, signal_ref[...])
    put(final_start, grad)
    other_squares = other_squares + square_sum(grad)
    grad = dense_nt(d_scale, signal_ref[...])
    put(final_start + D, grad)
    other_squares = other_squares + square_sum(grad)
    lane = lax.broadcasted_iota(jnp.int32, row_total.shape, 1)
    other_squares = other_squares + square_sum(jnp.where(lane < final_at, row_total, 0.0))
    d_signal = unfold(signal.take(), cols, images_all)
    d_signal = d_signal * silu_slope(pre_signal_ref[...])
    d_hidden = dense_tn(second_ref[...], d_signal)
    hidden_out[...] = fold(d_hidden.reshape(places, cols, images_all)).reshape(hidden_out.shape)
    hidden.start()
    hidden.hand_on()
    each(max(last_step - 3, 0), lambda step: reduce.send_pair(step + 3))
    run_ticks(reduce, 1, min(2, last_step - 1))
    labels = jnp.round(feats_ref[:, FREQ : FREQ + 1]).astype(jnp.int32)
    class_lane = lax.broadcasted_iota(jnp.int32, (images_all, -(-CLASSES // 128) * 128), 1)
    grad = dense(d_signal, jnp.where(class_lane == labels, 1.0, 0.0))
    put(0, grad[:, 0:CLASSES])
    other_squares = other_squares + square_sum(grad)
    grad = dense_nt(d_signal, hidden_ref[...])
    put(second_start, grad)
    other_squares = other_squares + square_sum(grad)
    d_hidden = unfold(hidden.take(), cols, images_all)
    d_hidden = d_hidden * silu_slope(pre_time_ref[...])
    grad = dense(d_hidden, feats_ref[:, 0:FREQ])
    put(time_start, grad)
    other_squares = other_squares + square_sum(grad)
    vectors = [
        jnp.sum(values, axis=1, keepdims=True) for values in (d_hidden, d_signal, d_shift, d_scale)
    ]
    lane = lax.broadcasted_iota(jnp.int32, (cols, 128), 1)
    grad = sum(jnp.where(lane == at, vector, 0.0) for at, vector in enumerate(vectors))
    put(vector_start + 1, grad[:, 0:4])
    other_squares = other_squares + square_sum(grad)
    run_ticks(reduce, 2, min(3, last_step - 1))
    each(max(last_step - 4, 0), lambda step: reduce.tick(step + 3))
    reduce.finish()
    for total in totals:
        other_squares = other_squares + square_sum(total[...])
    lane = lax.broadcasted_iota(jnp.int32, scalar_own.shape, 1)
    scalar_own[...] = jnp.where(lane == 0, loss_ref[...], other_squares)
    scalars.start()
    scalars.wait()
    scalar_mid[...] = jnp.sum(scalar_in[...], axis=0)
    scalars_dp.start()
    scalars_dp.wait()
    scalar_sums[...] = jnp.sum(scalar_fin[...], axis=0)


def tail_call(
    rows, mods, mod_low, second, shift, scale, pre_signal, pre_time, feats, hidden, signal, loss,
    terms, others, images, at,
):
    dp_size, tensor_size = lax.axis_size("dp"), lax.axis_size("tensor")
    images_all = images * dp_size
    cols, lanes = rows.shape[2:]
    folded = folded_lanes(cols, images_all)
    full, low = jnp.float32, jnp.bfloat16
    spots = dp_size // 2
    blocks = [term.shape[1:] for term in terms]
    table_rows = table_starts()[-1] + LAYERS * (10 + FF // D)
    shapes = [
        ((cols, table_rows), full),
        (mod_low.shape, full),
        ((8, 128), full),
    ] + [(block, full) for block in blocks]
    scratch = [
        pltpu.VMEM((tensor_size, dp_size, cols, lanes), full),
        pltpu.VMEM((dp_size, cols, lanes), full),
        pltpu.VMEM((dp_size, cols, lanes), full),
        pltpu.VMEM(mods.shape, full),
        pltpu.VMEM(mods.shape[1:], low),
        pltpu.VMEM((dp_size,) + mods.shape[1:], low),
        pltpu.VMEM((D, images_all), full),
        pltpu.VMEM((8, 128), full),
        pltpu.VMEM((tensor_size, 8, 128), full),
        pltpu.VMEM((8, 128), full),
        pltpu.VMEM((dp_size, 8, 128), full),
    ]
    for _ in range(2):
        scratch += [
            pltpu.VMEM((dp_size, tensor_size, 8, folded), full),
            pltpu.VMEM((tensor_size, dp_size, 8, folded), full),
            pltpu.VMEM((dp_size, 8, folded), full),
            pltpu.VMEM((dp_size, 8, folded), full),
        ]
    scratch += [pltpu.VMEM((spots,) + block, low) for block in blocks]
    scratch += [pltpu.VMEM((spots,) + block, low) for block in blocks]
    scratch += [pltpu.VMEM((2, spots) + block, low) for block in blocks]
    scratch += [pltpu.VMEM((2, spots) + block, low) for block in blocks]
    for count in (tensor_size, dp_size) * 5:
        scratch += crowd_scratch(count)
    scratch += [
        pltpu.SemaphoreType.DMA((3, spots, 3)),
        pltpu.SemaphoreType.DMA((3, spots, 3)),
        pltpu.SemaphoreType.DMA((3, spots)),
    ]
    return pl.pallas_call(
        functools.partial(tail_kernel, images, at),
        out_shape=[jax.ShapeDtypeStruct(*shape) for shape in shapes],
        in_specs=[pl.BlockSpec(memory_space=pltpu.VMEM)] * 12
        + [pl.BlockSpec(memory_space=pl.ANY)] * len(terms)
        + [pl.BlockSpec(memory_space=pltpu.VMEM)] * len(others),
        out_specs=[pl.BlockSpec(memory_space=pltpu.VMEM)] * len(shapes),
        scratch_shapes=scratch,
        compiler_params=pltpu.CompilerParams(
            collective_id=31, has_side_effects=True, vmem_limit_bytes=ACT_VMEM
        ),
        name="tail",
    )(
        rows, mods, mod_low, second, shift, scale, pre_signal, pre_time, feats, hidden, signal,
        loss, *terms, *others,
    )


def adam_update(weight, first, second, grad, factor, first_fix, second_fix):
    clipped = grad * factor
    first_new = BETA_ONE * first + (1.0 - BETA_ONE) * clipped
    second_new = BETA_TWO * second + (1.0 - BETA_TWO) * clipped * clipped
    step_size = first_new / first_fix / (jnp.sqrt(second_new / second_fix) + ADAM_EPS)
    change = -LEARN_RATE * (step_size + DECAY * weight)
    master = weight + change
    return (master, first_new, second_new, master.astype(jnp.bfloat16), change)


def local(
    latents,
    target_noise,
    timesteps,
    labels,
    step_count,
    embed_table,
    layer_in,
    layer_out,
    layer_ada,
    embed_first,
    embed_second,
    input_first,
    input_second,
    output_first,
    output_second,
    mod_first,
    mod_second,
):
    tensor_size = lax.axis_size("tensor")
    tensor_rank = lax.axis_index("tensor")
    images = latents.shape[0]
    grid_side = SIDE // PATCH
    local_rows = grid_side // tensor_size
    tokens_all = grid_side * grid_side
    heads_local = HEADS // tensor_size
    group_width = heads_local * HEAD_DIM
    unit_count = FF // tensor_size
    patch_in = PATCH * PATCH * CHANNELS
    count_all = images * lax.axis_size("dp") * tokens_all * patch_in
    patch_start, time_start, second_start, final_start, head_start, vector_start, layer_start = (
        table_starts()
    )
    layer_rows = 10 + FF // D
    dp_rank = lax.axis_index("dp")
    dp_size = lax.axis_size("dp")
    place_count = dp_size * tensor_size
    images_all = images * dp_size
    table_cols = lax.reduce_precision(embed_table.T, 8, 7)
    cols = table_cols.shape[0]
    mod_rows = layer_ada.shape[1]
    mod_cols = layer_ada.shape[2]
    mod_low = layer_ada.astype(jnp.bfloat16)

    def col_block(row_start, row_count):
        return table_cols[:, row_start : row_start + row_count]

    vector_count = 5 + LAYERS * layer_rows
    small_count = 2 * patch_in + vector_count
    lanes = -(-(small_count + 2 * images) // 128) * 128
    shards_in = layer_in[:, :, 0].astype(jnp.bfloat16)
    shards = (
        shards_in[:, :, : 3 * group_width],
        shards_in[:, :, 3 * group_width :],
        layer_out[:, 0].astype(jnp.bfloat16),
    )
    second_cols = col_block(second_start, D)
    shift_cols = col_block(final_start, D)
    scale_cols = col_block(final_start + D, D)
    fused = cols % 8 == 0 and images <= 8
    if fused:
        small_send = jnp.concatenate(
            [
                col_block(patch_start, patch_in),
                col_block(head_start, patch_in + vector_count),
                jnp.zeros((cols, lanes - small_count), jnp.float32),
            ],
            axis=1,
        )
        feats_send = jnp.concatenate(
            [
                time_features(timesteps),
                jnp.broadcast_to(labels.astype(jnp.float32)[:, None], (images, 128)),
            ],
            axis=1,
        )
        feats_send = jnp.pad(feats_send, ((0, 8 - images), (0, 0)))
        outs = head_call(
            small_send,
            feats_send,
            table_cols,
            col_block(time_start, FREQ),
            second_cols,
            shift_cols,
            scale_cols,
            col_block(vector_start, 5),
            mod_low,
            shards,
            images,
        )
        small_all, feats_all, pre_time, hidden, pre_signal, signal, final_all, mod_full = outs[:8]
        wholes = outs[8:]
        small_all = small_all.transpose(1, 0, 2, 3)
        time_feats = feats_all[:, :FREQ]
        labels_all = jnp.round(feats_all[:, FREQ]).astype(jnp.int32)
        signal_low = lax.dynamic_slice_in_dim(
            signal.astype(jnp.bfloat16), dp_rank * mod_rows, mod_rows, 0
        )
        final_all = final_all.transpose(1, 0, 2, 3)[:, :, :images, : 2 * cols]
        final_own = final_all.reshape(place_count, images, 2, cols)
        final_own = final_own.transpose(2, 1, 0, 3).reshape(2, images, D)
        mod_full = mod_full[:, : LAYERS * images].reshape(tensor_size, LAYERS, images, mod_cols)
        mod_full = mod_full.transpose(1, 2, 0, 3).reshape(LAYERS, images, tensor_size * mod_cols)
    else:
        scalar_lanes = jnp.concatenate([timesteps, labels]).astype(jnp.float32)
        small_send = jnp.concatenate(
            [
                col_block(patch_start, patch_in),
                col_block(head_start, patch_in + vector_count),
                jnp.broadcast_to(scalar_lanes[None, :], (cols, 2 * images)),
                jnp.zeros((cols, lanes - small_count - 2 * images), jnp.float32),
            ],
            axis=1,
        )
        small_all = exchange(small_send, "all", False, 1)
        scalars_all = small_all[::tensor_size, 0, small_count : small_count + 2 * images].astype(
            jnp.int32
        )
        timesteps_all = scalars_all[:, :images].reshape(images_all)
        labels_all = scalars_all[:, images:].reshape(images_all)
        time_feats = time_features(timesteps_all)
        onehot = (labels_all[:, None] == jnp.arange(CLASSES, dtype=jnp.int32)[None, :]).astype(
            jnp.float32
        )
        pre_time = dense(col_block(time_start, FREQ), time_feats.T) + col_block(vector_start + 1, 1)
        hidden = exchange(jax.nn.silu(pre_time), "all", False, 2).reshape(D, images_all)
        pre_signal = (
            dense(second_cols, hidden)
            + col_block(vector_start + 2, 1)
            + dense(col_block(0, CLASSES), onehot.T)
        )
        signal = exchange(jax.nn.silu(pre_signal), "all", False, 3).reshape(D, images_all)
        final_send = jnp.concatenate(
            [
                dense(shift_cols, signal) + col_block(vector_start + 3, 1),
                dense(scale_cols, signal) + col_block(vector_start + 4, 1),
            ],
            axis=0,
        )
        final_all = exchange(final_send, "all", False, 4).reshape(place_count, 2, cols, images_all)
        final_own = lax.dynamic_slice_in_dim(final_all, dp_rank * images, images, 3)
        final_own = final_own.transpose(1, 3, 0, 2).reshape(2, images, D)
        signal_low = lax.dynamic_slice_in_dim(
            signal.astype(jnp.bfloat16), dp_rank * mod_rows, mod_rows, 0
        )
        mod_part = jnp.einsum("db,lde->ble", signal_low, mod_low, preferred_element_type=jnp.float32)
        mod_part = mod_part.reshape(dp_size, images * LAYERS, mod_cols)
        mod_local = jnp.sum(exchange(mod_part, "dp", True, 5), axis=0)
        mod_full = exchange(mod_local, "tensor", False, 6)
        mod_full = mod_full.reshape(tensor_size, images, LAYERS, mod_cols)
        mod_full = mod_full.transpose(2, 1, 0, 3).reshape(LAYERS, images, tensor_size * mod_cols)
        wholes = [lax.all_gather(shard[0], "dp") for shard in shards]
    small_rows = small_all.reshape(D, lanes).T
    patch_w = small_rows[0:patch_in]
    head_w = small_rows[patch_in : 2 * patch_in]
    vectors = small_rows[2 * patch_in : 2 * patch_in + 5]
    bias_all = small_rows[2 * patch_in + 5 : small_count]
    onehot = (labels_all[:, None] == jnp.arange(CLASSES, dtype=jnp.int32)[None, :]).astype(
        jnp.float32
    )
    final_shift, final_scale = final_own[0], final_own[1]
    pixels = patchify(latents, local_rows)
    targets = patchify(target_noise, local_rows)
    keep_coef, drop_coef = noise_levels(timesteps)
    noisy = keep_coef[:, None, None] * pixels + drop_coef[:, None, None] * targets
    residual = (
        jnp.einsum("btp,pd->btd", noisy, patch_w, precision=PRECISE)
        + vectors[0]
        + position_table(tensor_rank * local_rows, local_rows)[None]
    )
    saved_acts = []
    bias_all = bias_all.reshape(LAYERS, layer_rows, D)
    mod_vecs = mod_full.reshape(LAYERS, images, 6, D) + bias_all[:, None, 0:6]
    part_bias = lax.dynamic_slice_in_dim(
        bias_all[:, 8:10], tensor_rank * group_width, group_width, 2
    )
    qkv_bias = jnp.concatenate(
        [part_bias[:, 0], jnp.zeros((LAYERS, group_width), jnp.float32), part_bias[:, 1]], axis=1
    )
    up_bias = lax.dynamic_slice_in_dim(
        bias_all[:, 10:].reshape(LAYERS, FF), tensor_rank * unit_count, unit_count, 1
    )
    joined = fused and shards[0].shape[1] % 16 == 0 and shards[2].shape[1] % 8 == 0
    if joined:
        outs = forward_all(
            count_all,
            residual,
            mod_vecs,
            bias_all[:, 6:8],
            qkv_bias[:, None],
            up_bias[:, None],
            (final_shift[:, None], final_scale[:, None], head_w, targets),
            wholes,
            shards,
        )
        d_residual, d_head, loss_part, d_final_shift, d_final_scale = outs[:5]
        loss_part = loss_part[0, 0]
        d_final_shift, d_final_scale = d_final_shift[:, 0], d_final_scale[:, 0]
        saved_acts = [
            (mod_vecs[layer_idx], outs[5:14], outs[14:17]) for layer_idx in range(LAYERS)
        ]
    else:
        for layer_idx in range(LAYERS):
            weights = (
                wholes[0].reshape(D, 3 * group_width),
                wholes[1].reshape(D, unit_count),
                wholes[2].reshape(group_width + unit_count, D),
            )
            outs = forward_layer(
                residual,
                mod_vecs[layer_idx],
                bias_all[layer_idx, 6:8],
                qkv_bias[layer_idx : layer_idx + 1],
                up_bias[layer_idx : layer_idx + 1],
                *weights,
                shards if layer_idx + 1 < LAYERS else (),
                layer_idx,
            )
            wholes = outs[9:]
            saved_acts.append((mod_vecs[layer_idx], (residual,) + tuple(outs[1:9]), weights))
            residual = outs[0]
        final_in, final_norm_pull = jax.vjp(modulate, residual, final_shift, final_scale)
        predicted = jnp.einsum("btd,pd->btp", final_in, head_w, precision=PRECISE)
        error_all = predicted - targets
        loss_part = jnp.sum(error_all * error_all) / count_all
        d_pred = 2.0 * error_all / count_all
        d_head = jnp.einsum("btp,btd->pd", d_pred, final_in, precision=PRECISE)
        d_final = jnp.einsum("btp,pd->btd", d_pred, head_w, precision=PRECISE)
        d_residual, d_final_shift, d_final_scale = final_norm_pull(d_final)
    totals = []
    squares = []
    terms = ()
    bias_parts = []
    for layer_idx in reversed(range(LAYERS)):
        mod_vec, saved, weights = saved_acts[layer_idx]
        outs = backward_layer(
            d_residual, mod_vec, saved, weights, terms, layer_idx, joined
        )
        d_residual, d_w_qkv, d_w_up, d_w_out, d_mod_vec, d_vec, d_qkv_bias, d_up_bias = outs[:8]
        if terms:
            totals.insert(0, outs[8:11])
            squares.append(outs[11])
        terms = [
            term.reshape((dp_size, -1) + term.shape[1:]) for term in (d_w_qkv, d_w_up, d_w_out)
        ]
        bias_parts.insert(0, (d_mod_vec, d_vec, d_qkv_bias, d_up_bias))
    d_mods, d_vecs, d_qkv_rows, d_up_rows = [jnp.stack(parts) for parts in zip(*bias_parts)]
    part_rows = jnp.stack([d_qkv_rows[:, 0, :group_width], d_qkv_rows[:, 0, 2 * group_width :]], 1)
    bias_blocks = jnp.concatenate(
        [
            jnp.sum(d_mods, axis=1),
            d_vecs,
            lax.dynamic_update_slice_in_dim(
                jnp.zeros((LAYERS, 2, D), jnp.float32), part_rows, tensor_rank * group_width, 2
            ),
            lax.dynamic_update_slice_in_dim(
                jnp.zeros((LAYERS, FF), jnp.float32), d_up_rows[:, 0], tensor_rank * unit_count, 1
            ).reshape(LAYERS, FF // D, D),
        ],
        axis=1,
    ).reshape(LAYERS * layer_rows, D)
    d_patch_w = jnp.einsum("btp,btd->pd", noisy, d_residual, precision=PRECISE)
    d_patch_b = jnp.sum(d_residual, axis=(0, 1))
    row_parts = jnp.concatenate(
        [d_patch_w, d_head, d_patch_b[None], bias_blocks, d_final_shift, d_final_scale],
        axis=0,
    )
    row_count = row_parts.shape[0]
    row_lanes = -(-row_count // 128) * 128
    row_parts = jnp.pad(row_parts, ((0, row_lanes - row_count), (0, 0)))
    final_at = row_count - 2 * images
    row_send = row_parts.T.reshape(dp_size, tensor_size, cols, row_lanes)
    mod_send = d_mods.reshape(LAYERS * images, tensor_size, mod_cols)
    mod_send = mod_send.transpose(1, 0, 2)
    if fused:
        slots = slots_of(images)
        outs = tail_call(
            row_send,
            jnp.pad(mod_send, ((0, 0), (0, slots - LAYERS * images), (0, 0))),
            mod_low,
            second_cols,
            shift_cols,
            scale_cols,
            pre_signal,
            pre_time,
            feats_all,
            hidden,
            signal,
            loss_part.reshape(1, 1),
            terms,
            squares,
            images,
            final_at,
        )
        table_grad, mod_grad, scalar_sums = outs[:3]
        totals.insert(0, outs[3:])
        scalar_sums = scalar_sums[0]
    else:
        totals.insert(
            0,
            [
                lax.psum_scatter(term, "dp", scatter_dimension=0).astype(jnp.float32)
                for term in terms
            ],
        )
        row_all = exchange(row_send.reshape(place_count, cols, row_lanes), "all", True, 7)
        row_sums = jnp.sum(row_all, axis=0)
        final_sums = jnp.sum(
            row_all[:, :, final_at:row_count].reshape(dp_size, tensor_size, cols, 2, images), axis=1
        )
        final_sums = final_sums.transpose(2, 1, 0, 3).reshape(2, cols, images_all)
        d_shift_cols, d_scale_cols = final_sums[0], final_sums[1]
        d_mod_own = jnp.sum(exchange(mod_send, "tensor", True, 8), axis=0)
        d_mod_low = exchange(d_mod_own.astype(jnp.bfloat16), "dp", False, 9)
        d_mod_low = d_mod_low.reshape(dp_size, LAYERS, images, mod_cols)
        d_mod_low = d_mod_low.transpose(1, 0, 2, 3).reshape(LAYERS, images_all, mod_cols)
        d_signal_rows = jnp.einsum(
            "lbe,lde->db", d_mod_low, mod_low, preferred_element_type=jnp.float32
        )
        d_signal_part = dense(shift_cols.T, d_shift_cols) + dense(scale_cols.T, d_scale_cols)
        d_signal_part = d_signal_part + lax.dynamic_update_slice_in_dim(
            jnp.zeros((D, images_all), jnp.float32), d_signal_rows, dp_rank * mod_rows, 0
        )
        d_signal_cols = jnp.sum(
            exchange(d_signal_part.reshape(place_count, cols, images_all), "all", True, 10), axis=0
        )
        d_pre_signal = d_signal_cols * silu_slope(pre_signal)
        d_hidden_part = dense(second_cols.T, d_pre_signal)
        d_hidden_cols = jnp.sum(
            exchange(d_hidden_part.reshape(place_count, cols, images_all), "all", True, 11), axis=0
        )
        d_hidden = d_hidden_cols * silu_slope(pre_time)
        mod_grad = jnp.einsum(
            "db,lbe->lde", signal_low, d_mod_low, preferred_element_type=jnp.float32
        )
        class_grad = dense(d_pre_signal, onehot)
        time_grad = dense(d_hidden, time_feats)
        second_grad = dense(d_pre_signal, hidden.T)
        shift_grad = dense(d_shift_cols, signal.T)
        scale_grad = dense(d_scale_cols, signal.T)
        vector_sums = jnp.stack(
            [
                jnp.sum(values, axis=1)
                for values in (d_hidden, d_pre_signal, d_shift_cols, d_scale_cols)
            ],
            axis=1,
        )
        table_grad = jnp.concatenate(
            [
                class_grad,
                row_sums[:, 0:patch_in],
                time_grad,
                second_grad,
                shift_grad,
                scale_grad,
                row_sums[:, patch_in : 2 * patch_in + 1],
                vector_sums,
                row_sums[:, 2 * patch_in + 1 : final_at],
            ],
            axis=1,
        )
    input_grad = jnp.stack([jnp.concatenate(total[0:2], axis=1) for total in totals])
    input_grad = input_grad.reshape(layer_in.shape)
    output_grad = jnp.stack([total[2] for total in totals]).reshape(layer_out.shape)
    if not fused:
        local_squares = (
            jnp.sum(table_grad * table_grad)
            + jnp.sum(input_grad * input_grad)
            + jnp.sum(output_grad * output_grad)
            + jnp.sum(mod_grad * mod_grad)
        )
        scalar_send = jnp.where(
            lax.broadcasted_iota(jnp.int32, (8, 128), 1) == 0, loss_part, local_squares
        )
        scalar_sums = jnp.sum(exchange(scalar_send, "all", False, 12)[:, 0, 0:2], axis=0)
    loss_value = scalar_sums[0]
    square_total = scalar_sums[1]
    grad_norm = jnp.sqrt(square_total)
    factor = jnp.minimum(1.0, CLIP_NORM / grad_norm)
    first_fix = 1.0 - BETA_ONE ** step_count.astype(jnp.float32)
    second_fix = 1.0 - BETA_TWO ** step_count.astype(jnp.float32)
    embed_out = adam_update(
        embed_table.T, embed_first.T, embed_second.T, table_grad, factor, first_fix, second_fix
    )
    input_out = adam_update(
        layer_in, input_first, input_second, input_grad, factor, first_fix, second_fix
    )
    output_out = adam_update(
        layer_out, output_first, output_second, output_grad, factor, first_fix, second_fix
    )
    mod_out = adam_update(layer_ada, mod_first, mod_second, mod_grad, factor, first_fix, second_fix)
    return (
        (loss_value, grad_norm, embed_out[4].T, embed_out[1].T, embed_out[2].T)
        + input_out[0:4]
        + output_out[0:4]
        + mod_out[0:4]
    )


def solution(mesh):
    placed = (
        P("dp", "tensor"),
        P("dp", "tensor"),
        P("dp"),
        P("dp"),
        P(),
        P(None, ("dp", "tensor")),
        P(None, "dp", "tensor", None),
        P(None, "tensor", "dp", None),
        P(None, "dp", "tensor"),
        P(None, ("dp", "tensor")),
        P(None, ("dp", "tensor")),
        P(None, "dp", "tensor", None),
        P(None, "dp", "tensor", None),
        P(None, "tensor", "dp", None),
        P(None, "tensor", "dp", None),
        P(None, "dp", "tensor"),
        P(None, "dp", "tensor"),
    )
    return jax.shard_map(
        local,
        mesh=mesh,
        in_specs=placed,
        out_specs=(
            P(),
            P(),
            P(None, ("dp", "tensor")),
            P(None, ("dp", "tensor")),
            P(None, ("dp", "tensor")),
            P(None, "dp", "tensor", None),
            P(None, "dp", "tensor", None),
            P(None, "dp", "tensor", None),
            P(None, "dp", "tensor", None),
            P(None, "tensor", "dp", None),
            P(None, "tensor", "dp", None),
            P(None, "tensor", "dp", None),
            P(None, "tensor", "dp", None),
            P(None, "dp", "tensor"),
            P(None, "dp", "tensor"),
            P(None, "dp", "tensor"),
            P(None, "dp", "tensor"),
        ),
        check_vma=False,
    )
```

```python
import functools
import math

import jax
import jax.numpy as jnp
from jax import lax
from jax.experimental import pallas as pl
from jax.experimental.pallas import tpu as pltpu
from jax.sharding import PartitionSpec as P

D = 768
HEADS = 12
HEAD_DIM = 64
FF = 3072
CLASSES = 1001
FREQ = 256
CHANNELS = 4
PATCH = 2
SIDE = 32
LAYERS = 3


EPS_NORM = 1e-06
LEARN_RATE = 0.01
DECAY = 0.01
BETA_ONE = 0.5
BETA_TWO = 0.5
ADAM_EPS = 1e-08
CLIP_NORM = 0.25
PRECISE = lax.Precision.HIGHEST


def dense(left_op, right_op):
    return jnp.dot(left_op, right_op, precision=PRECISE, preferred_element_type=jnp.float32)


def layer_norm(values):
    center = values - jnp.mean(values, axis=-1, keepdims=True)
    return center * lax.rsqrt(jnp.mean(center * center, axis=-1, keepdims=True) + EPS_NORM)


def modulate(values, shift_vec, scale_vec):
    return layer_norm(values) * (1.0 + scale_vec[:, None, :]) + shift_vec[:, None, :]


def gelu_tanh(values):
    return jax.nn.gelu(values, approximate=True)


def silu_slope(values):
    sigmoid_val = jax.nn.sigmoid(values)
    return sigmoid_val * (1.0 + values * (1.0 - sigmoid_val))


def time_features(step_ints):
    half_width = FREQ // 2
    frequency = jnp.exp(-math.log(10000.0) * jnp.arange(half_width, dtype=jnp.float32) / half_width)
    angles = step_ints.astype(jnp.float32)[:, None] * frequency[None, :]
    return jnp.concatenate([jnp.cos(angles), jnp.sin(angles)], axis=1)


def noise_levels(step_ints):
    base_cos = math.cos(0.008 / 1.008 * math.pi / 2)
    angles = (step_ints.astype(jnp.float32) / 1000.0 + 0.008) / 1.008 * (math.pi / 2)
    signal_level = jnp.cos(angles) ** 2 / base_cos**2
    return (jnp.sqrt(signal_level), jnp.sqrt(1.0 - signal_level))


def position_table(first_row, row_count):
    grid_side = SIDE // PATCH
    quarter = D // 4
    omegas = jnp.exp(-math.log(10000.0) * jnp.arange(quarter, dtype=jnp.float32) / quarter)
    token_index = jnp.arange(row_count * grid_side, dtype=jnp.int32)
    row_angle = (first_row + token_index // grid_side).astype(jnp.float32)[:, None] * omegas[
        None, :
    ]
    col_angle = (token_index % grid_side).astype(jnp.float32)[:, None] * omegas[None, :]
    return jnp.concatenate(
        [jnp.sin(row_angle), jnp.cos(row_angle), jnp.sin(col_angle), jnp.cos(col_angle)], axis=1
    )


def patchify(flat_pixels, row_count):
    grid_side = SIDE // PATCH
    shaped = flat_pixels.reshape(flat_pixels.shape[0], row_count, PATCH, grid_side, PATCH, CHANNELS)
    return shaped.transpose(0, 1, 3, 2, 4, 5).reshape(
        flat_pixels.shape[0], row_count * grid_side, PATCH * PATCH * CHANNELS
    )


def table_starts():
    patch_in = PATCH * PATCH * CHANNELS
    patch_start = CLASSES
    time_start = patch_start + patch_in
    second_start = time_start + FREQ
    final_start = second_start + D
    head_start = final_start + 2 * D
    vector_start = head_start + patch_in
    layer_start = vector_start + 5
    return (
        patch_start,
        time_start,
        second_start,
        final_start,
        head_start,
        vector_start,
        layer_start,
    )


def group_place(group):
    if group == "all":
        width = lax.axis_size("tensor")
        place = lax.axis_index("dp") * width + lax.axis_index("tensor")
        size = lax.axis_size("dp") * width
        return place, size, lambda at: {"dp": at // width, "tensor": lax.rem(at, width)}
    return lax.axis_index(group), lax.axis_size(group), lambda at: {group: at}


def greet_group(group):
    place, size, coords = group_place(group)
    barrier = pltpu.get_barrier_semaphore()

    def greet_one(step, carry):
        peer = coords(lax.rem(place + step, size))
        pl.semaphore_signal(barrier, inc=1, device_id=peer, device_id_type=pl.DeviceIdType.MESH)
        return carry

    lax.fori_loop(1, size, greet_one, 0)
    pl.semaphore_wait(barrier, size - 1)


def greet_groups(*groups):
    barrier = pltpu.get_barrier_semaphore()
    count = 0
    for group in groups:
        place, size, coords = group_place(group)

        def greet_one(step, carry, place=place, size=size, coords=coords):
            peer = coords(lax.rem(place + step, size))
            pl.semaphore_signal(barrier, inc=1, device_id=peer, device_id_type=pl.DeviceIdType.MESH)
            return carry

        lax.fori_loop(1, size, greet_one, 0)
        count += size - 1
    pl.semaphore_wait(barrier, count)


class Crowd:
    def __init__(self, group, source_at, target, send_sems, recv_sems, local_sem):
        self.place, self.size, self.coords = group_place(group)
        self.source_at, self.target = source_at, target
        self.sends, self.recvs, self.local_sem = send_sems, recv_sems, local_sem

    def copy_to(self, step):
        there = lax.rem(self.place + step, self.size)
        return pltpu.make_async_remote_copy(
            src_ref=self.source_at(there),
            dst_ref=self.target.at[self.place],
            send_sem=self.sends.at[step],
            recv_sem=self.recvs.at[step],
            device_id=self.coords(there),
            device_id_type=pl.DeviceIdType.MESH,
        )

    def own_copy(self):
        return pltpu.make_async_copy(
            self.source_at(self.place), self.target.at[self.place], self.local_sem
        )

    def start(self):
        def begin(step, carry):
            self.copy_to(step).start()
            return carry

        lax.fori_loop(1, self.size, begin, 0)
        self.own_copy().start()

    def wait(self):
        def finish(step, carry):
            self.copy_to(step).wait()
            return carry

        self.own_copy().wait()
        lax.fori_loop(1, self.size, finish, 0)


class Relay:
    def __init__(self, source_at, middle, whole, sems_dp, sems_tensor):
        self.first = Crowd("dp", source_at, middle, *sems_dp)
        self.second = Crowd("tensor", lambda place: middle, whole, *sems_tensor)

    def start(self):
        self.first.start()

    def hand_on(self):
        self.first.wait()
        self.second.start()

    def wait(self):
        self.second.wait()


class Funnel:
    def __init__(self, source, across, middle, along, sems_tensor, sems_dp):
        self.across, self.middle, self.along = across, middle, along
        self.first = Crowd("tensor", lambda place: source.at[:, place], across, *sems_tensor)
        self.second = Crowd("dp", lambda place: middle.at[place], along, *sems_dp)

    def start(self):
        self.first.start()

    def hand_on(self):
        self.first.wait()
        self.middle[...] = jnp.sum(self.across[...], axis=0)
        self.second.start()

    def take(self):
        self.second.wait()
        return jnp.sum(self.along[...], axis=0)


def crowd_scratch(size):
    return [
        pltpu.SemaphoreType.DMA((size,)),
        pltpu.SemaphoreType.DMA((size,)),
        pltpu.SemaphoreType.DMA,
    ]


def exchange_kernel(group, spread, source, target, send_sems, recv_sems, local_sem):
    greet_group(group)
    crowd = Crowd(
        group,
        lambda place: source.at[place] if spread else source,
        target,
        send_sems,
        recv_sems,
        local_sem,
    )
    crowd.start()
    crowd.wait()


def exchange(values, group, spread, call_id):
    if group == "all":
        size = lax.axis_size("dp") * lax.axis_size("tensor")
    else:
        size = lax.axis_size(group)
    block = values.shape[1:] if spread else values.shape
    return pl.pallas_call(
        functools.partial(exchange_kernel, group, spread),
        out_shape=jax.ShapeDtypeStruct((size,) + block, values.dtype),
        in_specs=[pl.BlockSpec(memory_space=pltpu.VMEM)],
        out_specs=pl.BlockSpec(memory_space=pltpu.VMEM),
        scratch_shapes=crowd_scratch(size),
        compiler_params=pltpu.CompilerParams(
            collective_id=call_id, has_side_effects=True, vmem_limit_bytes=32 * 2**20
        ),
        name="exchange_" + group,
    )(values)


MESH = pl.DeviceIdType.MESH
ACT_VMEM = 60 * 2**20


def dot_nn(left_op, right_op):
    return jnp.dot(left_op, right_op, preferred_element_type=jnp.float32)


def dot_nt(left_op, right_op):
    return lax.dot_general(
        left_op, right_op, (((1,), (1,)), ((), ())), preferred_element_type=jnp.float32
    )


def dot_tn(left_op, right_op):
    return lax.dot_general(
        left_op, right_op, (((0,), (0,)), ((), ())), preferred_element_type=jnp.float32
    )


def square_sum(values):
    return jnp.sum(jnp.sum(values * values, axis=0, keepdims=True), axis=1, keepdims=True)


def norm_parts(values):
    center = values - jnp.mean(values, axis=-1, keepdims=True)
    rstd = lax.rsqrt(jnp.mean(center * center, axis=-1, keepdims=True) + EPS_NORM)
    return center * rstd, rstd


def greet(line):
    rank = lax.axis_index("tensor")
    half = lax.axis_size("tensor") // 2
    core_peer = {"tensor": rank + 1 - 2 * lax.rem(rank, 2)}
    chip_peer = {"tensor": lax.rem(rank + half, 2 * half)}
    barrier = pltpu.get_barrier_semaphore()
    for peer in (core_peer, chip_peer):
        pl.semaphore_signal(barrier, inc=1, device_id=peer, device_id_type=MESH)
    count = 2
    if line is not None:
        line.greet()
        count = count + line.answers()
    pl.semaphore_wait(barrier, count)


class Spread:
    def __init__(self, rows_ref, send_sems, recv_sems):
        self.rows, self.send, self.recv = rows_ref, send_sems, recv_sems
        self.rank = lax.axis_index("tensor")
        self.own_core = lax.rem(self.rank, 2)
        self.core_peer = self.rank + 1 - 2 * self.own_core
        self.chip_peer = lax.rem(self.rank + 2, 4)
        self.count = rows_ref.shape[1] // 4

    def block(self, image, owner):
        return self.rows.at[image, pl.ds(pl.multiple_of(owner * self.count, 16), self.count), :]

    def copy(self, image, owner, peer, which):
        return pltpu.make_async_remote_copy(
            src_ref=self.block(image, owner),
            dst_ref=self.block(image, owner),
            send_sem=self.send.at[image, which],
            recv_sem=self.recv.at[image, which],
            device_id={"tensor": peer},
            device_id_type=MESH,
        )

    def put(self, image, values):
        self.rows[image, pl.ds(pl.multiple_of(self.rank * self.count, 16), self.count), :] = values
        self.copy(image, self.rank, self.chip_peer, 0).start()
        self.copy(image, self.rank, self.core_peer, 1).start()

    def forward(self, image):
        self.copy(image, self.rank, self.chip_peer, 0).wait_recv()
        self.copy(image, self.chip_peer, self.core_peer, 2).start()

    def wait(self, image):
        self.copy(image, self.rank, self.core_peer, 1).wait_recv()
        self.copy(image, self.chip_peer, self.core_peer, 2).wait_recv()

    def close(self, image):
        self.copy(image, self.rank, self.chip_peer, 0).wait_send()
        self.copy(image, self.rank, self.core_peer, 1).wait_send()
        self.copy(image, self.chip_peer, self.core_peer, 2).wait_send()


class Collect:
    def __init__(self, part, near, far_out, far_in, send_sems, recv_sems):
        self.part, self.near, self.far_out, self.far_in = part, near, far_out, far_in
        self.send, self.recv = send_sems, recv_sems
        self.rank = lax.axis_index("tensor")
        self.own_core = lax.rem(self.rank, 2)
        self.own_chip = self.rank // 2
        self.core_peer = self.rank + 1 - 2 * self.own_core
        self.chip_peer = lax.rem(self.rank + 2, 4)
        self.count = part.shape[1] // 4

    def block(self, image, owner):
        return self.part.at[image, pl.ds(pl.multiple_of(owner * self.count, 16), self.count), :]

    def near_copy(self, image, far):
        chip = 1 - self.own_chip if far else self.own_chip
        return pltpu.make_async_remote_copy(
            src_ref=self.block(image, 2 * chip + 1 - self.own_core),
            dst_ref=self.near.at[image, far],
            send_sem=self.send.at[image, far],
            recv_sem=self.recv.at[image, far],
            device_id={"tensor": self.core_peer},
            device_id_type=MESH,
        )

    def far_copy(self, image):
        return pltpu.make_async_remote_copy(
            src_ref=self.far_out.at[image],
            dst_ref=self.far_in.at[image],
            send_sem=self.send.at[image, 2],
            recv_sem=self.recv.at[image, 2],
            device_id={"tensor": self.chip_peer},
            device_id_type=MESH,
        )

    def put(self, image, values):
        self.part[image] = values.astype(jnp.bfloat16)
        self.near_copy(image, 1).start()
        self.near_copy(image, 0).start()

    def load(self, image, owner):
        at = pl.ds(pl.multiple_of(owner * self.count, 16), self.count)
        return self.part[image, at, :].astype(jnp.float32)

    def forward(self, image):
        self.near_copy(image, 1).wait_recv()
        total = self.load(image, self.chip_peer) + self.near[image, 1].astype(jnp.float32)
        self.far_out[image] = total.astype(jnp.bfloat16)
        self.far_copy(image).start()

    def take(self, image):
        self.near_copy(image, 0).wait_recv()
        total = self.load(image, self.rank) + self.near[image, 0].astype(jnp.float32)
        self.far_copy(image).wait_recv()
        return total + self.far_in[image].astype(jnp.float32)

    def close(self, image):
        self.near_copy(image, 1).wait_send()
        self.near_copy(image, 0).wait_send()
        self.far_copy(image).wait_send()


def collect_scratch(images, tokens):
    count = tokens // 4
    return [
        pltpu.VMEM((images, tokens, D), jnp.bfloat16),
        pltpu.VMEM((images, 2, count, D), jnp.bfloat16),
        pltpu.VMEM((images, count, D), jnp.bfloat16),
        pltpu.VMEM((images, count, D), jnp.bfloat16),
    ]


def each(count, body):
    def step(index, carry):
        body(index)
        return carry

    lax.fori_loop(0, count, step, 0)


class Moves:
    def __init__(self, pairs, sems):
        self.copies = [
            pltpu.make_async_copy(source, target, sems.at[at])
            for at, (source, target) in enumerate(pairs)
        ]

    def start(self, *which):
        for at in which:
            self.copies[at].start()

    def wait(self, *which):
        for at in which:
            self.copies[at].wait()


class Line:
    def __init__(self):
        self.size = lax.axis_size("dp") // 2
        self.place = lax.axis_index("dp")
        self.at = self.place // 2
        self.side = lax.rem(self.place, 2)
        self.pair = self.place + 1 - 2 * self.side
        self.has_up = self.at + 1 < self.size
        self.has_down = self.at > 0

    def greet(self):
        barrier = pltpu.get_barrier_semaphore()
        pl.semaphore_signal(barrier, inc=1, device_id={"dp": self.pair}, device_id_type=MESH)

        @pl.when(self.has_up)
        def _():
            up = {"dp": self.place + 2}
            pl.semaphore_signal(barrier, inc=1, device_id=up, device_id_type=MESH)

        @pl.when(self.has_down)
        def _():
            down = {"dp": self.place - 2}
            pl.semaphore_signal(barrier, inc=1, device_id=down, device_id_type=MESH)

    def answers(self):
        return 1 + self.has_up.astype(jnp.int32) + self.has_down.astype(jnp.int32)


UP, DOWN, PAIR = 0, 1, 2


class Gather:
    def __init__(self, line, shards, wholes, sends, recvs, local_sems):
        self.line, self.shards, self.wholes = line, shards, wholes
        self.sends, self.recvs, self.local_sems = sends, recvs, local_sems

    def copy(self, part, way, step, owner, fresh=False):
        line = self.line
        there = {UP: line.place + 2, DOWN: line.place - 2, PAIR: line.pair}[way]
        return pltpu.make_async_remote_copy(
            src_ref=self.shards[part] if fresh else self.wholes[part].at[owner],
            dst_ref=self.wholes[part].at[owner],
            send_sem=self.sends.at[way, step, part],
            recv_sem=self.recvs.at[way, step, part],
            device_id={"dp": there},
            device_id_type=MESH,
        )

    def local_copy(self, part):
        return pltpu.make_async_copy(
            self.shards[part], self.wholes[part].at[self.line.place], self.local_sems.at[part]
        )

    def start(self):
        line = self.line
        parts = range(len(self.shards))

        @pl.when(line.has_up)
        def _():
            for part in parts:
                self.copy(part, UP, 0, line.place, True).start()

        @pl.when(line.has_down)
        def _():
            for part in parts:
                self.copy(part, DOWN, 0, line.place, True).start()

        for part in parts:
            self.copy(part, PAIR, line.at, line.place, True).start()
            self.local_copy(part).start()

    def came(self, way, step):
        there = -step if way == UP else step
        spot = self.line.at + there
        return self.line.place + 2 * there, spot, (spot >= 0) & (spot < self.line.size)

    def hand_on(self, step, way):
        line = self.line
        owner, _, real = self.came(way, step)
        can = line.has_up if way == UP else line.has_down

        @pl.when(real)
        def _():
            for part in range(len(self.shards)):
                self.copy(part, way, step - 1, owner).wait_recv()

            @pl.when(can)
            def _():
                for part in range(len(self.shards)):
                    self.copy(part, way, step, owner).start()

    def hand_over(self, step, way, when=True):
        owner, spot, real = self.came(way, step)

        @pl.when(real & when)
        def _():
            for part in range(len(self.shards)):
                self.copy(part, PAIR, spot, owner).start()

    def tick(self, step):
        for way in (UP, DOWN):
            self.hand_on(step, way)
            self.hand_over(step, way)

    def finish(self):
        line = self.line
        parts = range(len(self.shards))
        for part in parts:
            self.local_copy(part).wait()

        def side(spot):
            for part in parts:
                self.copy(part, PAIR, spot, 2 * spot + line.side).wait()

        each(line.size, side)

        def along(step):
            for way, there, can in ((UP, -step, line.has_up), (DOWN, step, line.has_down)):
                spot = line.at + there

                @pl.when((spot >= 0) & (spot < line.size) & can)
                def _(way=way, there=there):
                    for part in parts:
                        self.copy(part, way, step, line.place + 2 * there).wait_send()

        each(line.size, along)


class Reduce:
    def __init__(self, line, terms, totals, own, pair_in, way_in, way_out, sends, recvs, own_sems):
        self.line, self.terms, self.totals, self.own = line, terms, totals, own
        self.own_sems = own_sems
        self.pair_in, self.way_in, self.way_out = pair_in, way_in, way_out
        self.sends, self.recvs = sends, recvs

    def pair_copy(self, part, spot):
        return pltpu.make_async_remote_copy(
            src_ref=self.terms[part].at[2 * spot + 1 - self.line.side],
            dst_ref=self.pair_in[part].at[spot],
            send_sem=self.sends.at[PAIR, spot, part],
            recv_sem=self.recvs.at[PAIR, spot, part],
            device_id={"dp": self.line.pair},
            device_id_type=MESH,
        )

    def way_copy(self, part, way, spot):
        there = self.line.place + 2 if way == UP else self.line.place - 2
        return pltpu.make_async_remote_copy(
            src_ref=self.way_out[part].at[way, spot],
            dst_ref=self.way_in[part].at[way, spot],
            send_sem=self.sends.at[way, spot, part],
            recv_sem=self.recvs.at[way, spot, part],
            device_id={"dp": there},
            device_id_type=MESH,
        )

    def start(self):
        self.load_own()
        each(self.line.size, self.send_pair)

    def own_copy(self, part, spot):
        return pltpu.make_async_copy(
            self.terms[part].at[2 * spot + self.line.side],
            self.own[part].at[spot],
            self.own_sems.at[part, spot],
        )

    def load_own(self):
        def load(spot):
            for part in range(len(self.terms)):
                self.own_copy(part, spot).start()

        each(self.line.size, load)

    def wait_own(self):
        def wait(spot):
            for part in range(len(self.terms)):
                self.own_copy(part, spot).wait()

        each(self.line.size, wait)

    def send_pair(self, step):
        line = self.line
        far = line.size - 1 - step

        @pl.when(line.at + far < line.size)
        def _():
            for part in range(len(self.terms)):
                self.pair_copy(part, line.at + far).start()

        @pl.when((line.at - far >= 0) & (far > 0))
        def _():
            for part in range(len(self.terms)):
                self.pair_copy(part, line.at - far).start()

    def pair_sum(self, part, spot):
        own = self.own[part][spot].astype(jnp.float32)
        return own + self.pair_in[part][spot].astype(jnp.float32)

    def pass_on(self, way, spot, more):
        for part in range(len(self.terms)):
            self.pair_copy(part, spot).wait_recv()
            self.way_out[part][way, spot] = self.pair_sum(part, spot).astype(jnp.bfloat16)

            @pl.when(more)
            def _(part=part):
                self.way_copy(part, way, spot).wait_recv()
                self.way_out[part][way, spot] = (
                    self.pair_sum(part, spot) + self.way_in[part][way, spot].astype(jnp.float32)
                ).astype(jnp.bfloat16)

            self.way_copy(part, way, spot).start()

    def tick(self, step):
        line = self.line
        far = line.size - 1 - step

        @pl.when(line.at + far < line.size)
        def _():
            self.pass_on(UP, line.at + far, line.has_down)

        @pl.when(line.at - far >= 0)
        def _():
            self.pass_on(DOWN, line.at - far, line.has_up)

    def finish(self):
        line = self.line
        spot = line.at
        for part in range(len(self.terms)):
            self.pair_copy(part, spot).wait_recv()
            self.totals[part][...] = self.pair_sum(part, spot)
        for way, can in ((UP, line.has_down), (DOWN, line.has_up)):

            @pl.when(can)
            def _(way=way):
                for part in range(len(self.terms)):
                    self.way_copy(part, way, spot).wait_recv()
                    self.totals[part][...] += self.way_in[part][way, spot].astype(jnp.float32)

        def close(spot):
            for part in range(len(self.terms)):
                self.pair_copy(part, spot).wait_send()
            for way, passed in ((UP, spot > line.at), (DOWN, spot < line.at)):

                @pl.when(passed)
                def _(way=way):
                    for part in range(len(self.terms)):
                        self.way_copy(part, way, spot).wait_send()

        each(line.size, close)


def run_ticks(task, first, last):
    if task is not None:
        for step in range(first, last):
            task.tick(step)


def head_slice(matrix, head):
    return matrix[:, head * HEAD_DIM : (head + 1) * HEAD_DIM]


def soft_rows(queries, keys_in):
    scores = dot_nt(queries, keys_in) * (HEAD_DIM ** (-0.5))
    exponent = jnp.exp(scores - jnp.max(scores, axis=-1, keepdims=True))
    return exponent / jnp.sum(exponent, axis=-1, keepdims=True)


def forward_kernel(
    layer_idx,
    res_ref,
    mod_ref,
    vec_ref,
    qkv_bias_ref,
    up_bias_ref,
    w_qkv_far,
    w_up_far,
    w_out_far,
    *rest,
):
    with_gather = len(rest) > 31
    shards, rest = (rest[:3], rest[3:]) if with_gather else ((), rest)
    res_out, kept = rest[0], rest[1:9]
    wholes, rest = (rest[9:12], rest[12:]) if with_gather else ((), rest[9:])
    rows_a, qkv_out, mixed_out, branch_out, mid_out, rows_m, upper_out, down_out = rest[:8]
    w_qkv_ref, w_up_ref, w_out_ref = rest[8:11]
    (
        part_a,
        near_a,
        far_out_a,
        far_in_a,
        part_m,
        near_m,
        far_out_m,
        far_in_m,
        sends,
        recvs,
        move_sems,
    ) = rest[11:22]
    group_width = w_qkv_ref.shape[1] // 3
    w_attn_ref, w_down_ref = w_out_ref.at[0:group_width, :], w_out_ref.at[group_width:, :]
    far = (w_qkv_far, w_out_far, w_up_far)
    pairs = list(zip(far, (w_qkv_ref, w_out_ref, w_up_ref))) + list(zip(rest[:8], kept))
    moves = Moves(pairs, move_sems)
    moves.start(0, 1, 2)
    images = res_ref.shape[0]
    gather, last_step = None, 0
    if with_gather:
        line = Line()
        greet(line)
        own = [shard.at[layer_idx + 1] for shard in shards]
        gather = Gather(line, own, wholes, *rest[22:])
        last_step = line.size
    else:
        greet(None)
    spread_a = Spread(rows_a, sends.at[0], recvs.at[0])
    spread_m = Spread(rows_m, sends.at[1], recvs.at[1])
    collect_a = Collect(part_a, near_a, far_out_a, far_in_a, sends.at[2], recvs.at[2])
    collect_m = Collect(part_m, near_m, far_out_m, far_in_m, sends.at[3], recvs.at[3])

    def mod_row(image, piece):
        return mod_ref[image, pl.ds(piece, 1), :]

    def start_norm(image):
        normed, _ = norm_parts(res_ref[image])
        normed = normed * (1.0 + mod_row(image, 1)) + mod_row(image, 0)
        spread_a.put(image, normed.astype(jnp.bfloat16))

    def attend(image):
        spread_a.wait(image)
        rows = rows_a[image]
        projected = dot_nn(rows, w_qkv_ref[...]) + qkv_bias_ref[...]
        qkv = projected.astype(jnp.bfloat16)
        qkv_out[image] = qkv
        heads = []
        for head in range(group_width // HEAD_DIM):
            probs = soft_rows(
                head_slice(qkv[:, :group_width], head),
                head_slice(qkv[:, group_width : 2 * group_width], head),
            )
            heads.append(
                dot_nn(probs.astype(jnp.bfloat16), head_slice(qkv[:, 2 * group_width :], head))
            )
        mixed = jnp.concatenate(heads, axis=1).astype(jnp.bfloat16)
        mixed_out[image] = mixed
        collect_a.put(image, dot_nn(mixed, w_attn_ref[...]))

    def middle(image):
        branch = collect_a.take(image) + vec_ref[0:1, :]
        branch_out[image] = branch
        mid = res_ref[image] + mod_row(image, 2) * branch
        mid_out[image] = mid
        normed, _ = norm_parts(mid)
        normed = normed * (1.0 + mod_row(image, 4)) + mod_row(image, 3)
        spread_m.put(image, normed.astype(jnp.bfloat16))

    def feed(image):
        spread_m.wait(image)
        upper = dot_nn(rows_m[image], w_up_ref[...]) + up_bias_ref[...]
        upper_out[image] = upper
        collect_m.put(image, dot_nn(gelu_tanh(upper).astype(jnp.bfloat16), w_down_ref[...]))

    def finish(image):
        down = collect_m.take(image) + vec_ref[1:2, :]
        down_out[image] = down
        res_out[image] = mid_out[image] + mod_row(image, 5) * down

    def close(image):
        spread_a.close(image)
        spread_m.close(image)
        collect_a.close(image)
        collect_m.close(image)

    if with_gather:
        gather.start()
    each(images, start_norm)
    each(images, spread_a.forward)
    moves.wait(0, 1)
    each(images, attend)
    moves.start(3, 4, 5)
    run_ticks(gather, 1, min(2, last_step))
    each(images, collect_a.forward)
    each(images, middle)
    moves.start(6, 7)
    each(images, spread_m.forward)
    run_ticks(gather, 2, min(3, last_step))
    moves.wait(2)
    each(images, feed)
    moves.start(8, 9)
    run_ticks(gather, 3, min(4, last_step))
    each(images, collect_m.forward)
    each(images, finish)
    moves.start(10)
    each(images, close)
    moves.wait(*range(3, 11))
    if with_gather:
        each(max(last_step - 4, 0), lambda step: gather.tick(step + 4))
        gather.finish()


def forward_layer(
    residual, mod_vec, vec_bias, qkv_bias, up_bias, w_qkv, w_up, w_out, shards, layer_idx
):
    images, count, _ = residual.shape
    tokens = 4 * count
    low, full = jnp.bfloat16, jnp.float32
    shapes = [
        ((images, count, D), full),
        ((images, tokens, D), low),
        ((images, tokens, w_qkv.shape[1]), low),
        ((images, tokens, w_qkv.shape[1] // 3), low),
        ((images, count, D), full),
        ((images, count, D), full),
        ((images, tokens, D), low),
        ((images, tokens, w_up.shape[1]), full),
        ((images, count, D), full),
    ]
    scratch = [
        pltpu.SemaphoreType.DMA((4, images, 3)),
        pltpu.SemaphoreType.DMA((4, images, 3)),
        pltpu.SemaphoreType.DMA((11,)),
    ]
    near = [pltpu.VMEM(*shape) for shape in shapes[1:]]
    near += [pltpu.VMEM(weight.shape, low) for weight in (w_qkv, w_up, w_out)]
    if shards:
        dp_size = lax.axis_size("dp")
        shapes += [((dp_size,) + shard.shape[1:], low) for shard in shards]
        scratch += [
            pltpu.SemaphoreType.DMA((3, dp_size // 2, 3)),
            pltpu.SemaphoreType.DMA((3, dp_size // 2, 3)),
            pltpu.SemaphoreType.DMA((3,)),
        ]
    return pl.pallas_call(
        functools.partial(forward_kernel, layer_idx),
        out_shape=[jax.ShapeDtypeStruct(*shape) for shape in shapes],
        in_specs=[pl.BlockSpec(memory_space=pltpu.VMEM)] * 5
        + [pl.BlockSpec(memory_space=pl.ANY)] * (3 + len(shards)),
        out_specs=[pl.BlockSpec(memory_space=pltpu.VMEM)]
        + [pl.BlockSpec(memory_space=pl.ANY)] * (len(shapes) - 1),
        scratch_shapes=near
        + collect_scratch(images, tokens)
        + collect_scratch(images, tokens)
        + scratch,
        compiler_params=pltpu.CompilerParams(
            collective_id=16 + layer_idx, has_side_effects=True, vmem_limit_bytes=ACT_VMEM
        ),
        cost_estimate=pl.CostEstimate(
            flops=30 * 10**9, bytes_accessed=15 * 2**20, transcendentals=0
        ),
        name="block_forward",
    )(residual, mod_vec, vec_bias, qkv_bias, up_bias, w_qkv, w_up, w_out, *shards)


def flat(ref):
    value = ref[...]
    return value.reshape(-1, value.shape[-1])


def forward_all_kernel(
    count_all,
    res_ref,
    mod_ref,
    vec_ref,
    qkv_bias_ref,
    up_bias_ref,
    final_shift_ref,
    final_scale_ref,
    head_ref,
    targets_ref,
    qkv_far,
    up_far,
    out_far,
    *rest,
):
    shards, rest = rest[0:3], rest[3:]
    d_res_out, d_head_out, loss_out, d_shift_out, d_scale_out = rest[0:5]
    kept_far, whole_far = rest[5:14], rest[14:17]
    kept, rest = rest[17:26], rest[26:]
    res_all, rows_a_all, qkv_all, mixed_all, branch_all, mid_all, rows_m_all, upper_all, down_all = kept
    w_qkv_all, w_up_all, w_blocks_all, w_out_all = rest[0:4]
    part_a, near_a, far_out_a, far_in_a, part_m, near_m, far_out_m, far_in_m = rest[4:12]
    sends, recvs, keep_sems, load_sems, whole_sems, gather_sends, gather_recvs, local_sems = rest[12:]
    images = res_ref.shape[0]
    group_width = w_qkv_all.shape[-1] // 3
    line = Line()
    last_step = line.size
    loads = Moves(
        [(qkv_far, w_qkv_all.at[0]), (out_far, w_blocks_all.at[0]), (up_far, w_up_all.at[0])],
        load_sems,
    )
    loads.start(0, 1, 2)
    greet(line)
    gathers = [None]
    for layer_idx in range(1, LAYERS):
        gathers.append(
            Gather(
                line,
                [shard.at[layer_idx] for shard in shards],
                [whole.at[layer_idx] for whole in (w_qkv_all, w_up_all, w_blocks_all)],
                gather_sends.at[layer_idx],
                gather_recvs.at[layer_idx],
                local_sems.at[layer_idx],
            )
        )
    gathers.append(None)

    def join_blocks(layer_idx):
        rows = w_blocks_all.shape[2]
        for pair in range(w_blocks_all.shape[1] // 2):
            halves = [
                w_blocks_all[layer_idx, 2 * pair + side].astype(jnp.float32) for side in range(2)
            ]
            w_out_all[layer_idx, 2 * rows * pair : 2 * rows * (pair + 1), :] = jnp.concatenate(
                halves, axis=0
            ).astype(jnp.bfloat16)

    def mod_row(layer_idx, image, piece):
        return mod_ref[layer_idx, image, pl.ds(piece, 1), :]

    d_head_out[...] = jnp.zeros_like(d_head_out)
    loss_out[...] = jnp.zeros_like(loss_out)

    def final_loss(image, value):
        normed, _ = norm_parts(value)
        final_in = normed * (1.0 + final_scale_ref[image]) + final_shift_ref[image]
        error_all = dense_nt(final_in, head_ref[...]) - targets_ref[image]
        loss_out[...] += square_sum(error_all) / count_all
        d_pred = 2.0 * error_all / count_all
        d_head_out[...] += dense_tn(d_pred, final_in)
        d_value, d_shift, d_scale = norm_pull(
            value, final_scale_ref[image], dense(d_pred, head_ref[...])
        )
        d_shift_out[image] = d_shift
        d_scale_out[image] = d_scale
        d_res_out[image] = d_value

    for layer_idx in range(LAYERS):
        res, rows_a, qkv_out, mixed_out, branch_out, mid_out, rows_m, upper_out, down_out = [
            ref.at[layer_idx] for ref in kept
        ]
        w_qkv, w_up, w_out = w_qkv_all.at[layer_idx], w_up_all.at[layer_idx], w_out_all.at[layer_idx]
        w_attn, w_down = w_out.at[0:group_width, :], w_out.at[group_width:, :]
        spread_a = Spread(rows_a, sends.at[layer_idx, 0], recvs.at[layer_idx, 0])
        spread_m = Spread(rows_m, sends.at[layer_idx, 1], recvs.at[layer_idx, 1])
        collect_a = Collect(
            part_a,
            near_a.at[layer_idx],
            far_out_a.at[layer_idx],
            far_in_a.at[layer_idx],
            sends.at[layer_idx, 2],
            recvs.at[layer_idx, 2],
        )
        collect_m = Collect(
            part_m,
            near_m.at[layer_idx],
            far_out_m.at[layer_idx],
            far_in_m.at[layer_idx],
            sends.at[layer_idx, 3],
            recvs.at[layer_idx, 3],
        )
        keep = Moves(
            [(ref.at[layer_idx], far.at[layer_idx]) for ref, far in zip(kept, kept_far)],
            keep_sems.at[layer_idx],
        )
        keep_whole = Moves(
            [
                (ref.at[layer_idx], far.at[layer_idx])
                for ref, far in zip((w_qkv_all, w_up_all, w_out_all), whole_far)
            ],
            whole_sems.at[layer_idx],
        )
        gather = gathers[layer_idx + 1]

        def start_norm(image, at, values, target):
            normed, _ = norm_parts(values)
            normed = normed * (1.0 + mod_row(at, image, 1)) + mod_row(at, image, 0)
            target.put(image, normed.astype(jnp.bfloat16))

        def first_norm(image, res=res, spread_a=spread_a):
            res[image] = res_ref[image]
            start_norm(image, 0, res_ref[image], spread_a)

        def attend(image):
            spread_a.wait(image)
            projected = dot_nn(rows_a[image], flat(w_qkv)) + qkv_bias_ref[layer_idx]
            qkv = projected.astype(jnp.bfloat16)
            qkv_out[image] = qkv
            heads = []
            for head in range(group_width // HEAD_DIM):
                probs = soft_rows(
                    head_slice(qkv[:, :group_width], head),
                    head_slice(qkv[:, group_width : 2 * group_width], head),
                )
                heads.append(
                    dot_nn(probs.astype(jnp.bfloat16), head_slice(qkv[:, 2 * group_width :], head))
                )
            mixed = jnp.concatenate(heads, axis=1).astype(jnp.bfloat16)
            mixed_out[image] = mixed
            collect_a.put(image, dot_nn(mixed, w_attn[...]))

        def middle(image):
            branch = collect_a.take(image) + vec_ref[layer_idx, 0:1, :]
            branch_out[image] = branch
            mid = res[image] + mod_row(layer_idx, image, 2) * branch
            mid_out[image] = mid
            normed, _ = norm_parts(mid)
            normed = normed * (1.0 + mod_row(layer_idx, image, 4)) + mod_row(layer_idx, image, 3)
            spread_m.put(image, normed.astype(jnp.bfloat16))

        def feed(image):
            spread_m.wait(image)
            upper = dot_nn(rows_m[image], flat(w_up)) + up_bias_ref[layer_idx]
            upper_out[image] = upper
            collect_m.put(image, dot_nn(gelu_tanh(upper).astype(jnp.bfloat16), w_down[...]))

        def finish(image):
            down = collect_m.take(image) + vec_ref[layer_idx, 1:2, :]
            down_out[image] = down
            value = mid_out[image] + mod_row(layer_idx, image, 5) * down
            if layer_idx + 1 < LAYERS:
                res_all[layer_idx + 1, image] = value
                following = Spread(
                    rows_a_all.at[layer_idx + 1],
                    sends.at[layer_idx + 1, 0],
                    recvs.at[layer_idx + 1, 0],
                )
                start_norm(image, layer_idx + 1, value, following)
            else:
                final_loss(image, value)

        def close(image):
            spread_a.close(image)
            spread_m.close(image)
            collect_a.close(image)
            collect_m.close(image)

        if layer_idx == 0:
            gather.start()
            each(images, first_norm)
        if layer_idx > 0:
            run_ticks(gather, 1, min(2, last_step))
        each(images, spread_a.forward)
        if layer_idx == 0:
            loads.wait(0, 1)
            join_blocks(0)
        each(images - 1, attend)
        at = 1 if layer_idx == 0 else 2
        run_ticks(gather, at, min(at + 1, last_step))
        attend(images - 1)
        keep.start(0, 1, 2, 3)
        each(images, collect_a.forward)
        each(images - 1, middle)
        at = 2 if layer_idx == 0 else 3
        run_ticks(gather, at, min(at + 1, last_step))
        middle(images - 1)
        keep.start(4, 5)
        each(images, spread_m.forward)
        if layer_idx == 0:
            loads.wait(2)
        each(images, feed)
        keep.start(6, 7)
        if layer_idx == 0:
            run_ticks(gather, 3, min(4, last_step))
        if gather is not None and gathers[layer_idx + 2] is not None:
            gathers[layer_idx + 2].start()
        each(images, collect_m.forward)
        each(images, finish)
        keep.start(8)
        keep_whole.start(0, 1, 2)
        each(images, close)
        if gather is not None:
            each(max(last_step - 4, 0), lambda step, gather=gather: gather.tick(step + 4))
            gather.finish()
            join_blocks(layer_idx + 1)
        keep.wait(*range(9))
        keep_whole.wait(0, 1, 2)


def forward_all(
    count_all, residual, mod_vecs, vec_bias, qkv_bias, up_bias, finals, wholes, shards
):
    images, count, _ = residual.shape
    tokens = 4 * count
    low, full = jnp.bfloat16, jnp.float32
    dp_size = lax.axis_size("dp")
    qkv_width, units = wholes[0].shape[-1], wholes[1].shape[-1]
    own = (images, count, D)
    kept = [
        (own, full),
        ((images, tokens, D), low),
        ((images, tokens, qkv_width), low),
        ((images, tokens, qkv_width // 3), low),
        (own, full),
        (own, full),
        ((images, tokens, D), low),
        ((images, tokens, units), full),
        (own, full),
    ]
    kept = [((LAYERS,) + shape, kind) for shape, kind in kept]
    out_rows = wholes[2].shape[0] * wholes[2].shape[1]
    matrices = [
        ((LAYERS,) + wholes[0].shape, low),
        ((LAYERS,) + wholes[1].shape, low),
        ((LAYERS, out_rows, D), low),
    ]
    shapes = [(own, full), (finals[2].shape, full), ((1, 1), full)]
    shapes += [(finals[0].shape, full), (finals[1].shape, full)]
    shapes += kept + matrices
    collect = [
        pltpu.VMEM((images, tokens, D), low),
        pltpu.VMEM((LAYERS, images, 2, count, D), low),
        pltpu.VMEM((LAYERS, images, count, D), low),
        pltpu.VMEM((LAYERS, images, count, D), low),
    ]
    return pl.pallas_call(
        functools.partial(forward_all_kernel, count_all),
        out_shape=[jax.ShapeDtypeStruct(*shape) for shape in shapes],
        in_specs=[pl.BlockSpec(memory_space=pltpu.VMEM)] * 9
        + [pl.BlockSpec(memory_space=pl.ANY)] * 6,
        out_specs=[pl.BlockSpec(memory_space=pltpu.VMEM)] * 5
        + [pl.BlockSpec(memory_space=pl.ANY)] * (len(shapes) - 5),
        scratch_shapes=[pltpu.VMEM(*shape) for shape in kept]
        + [
            pltpu.VMEM(*matrices[0]),
            pltpu.VMEM(*matrices[1]),
            pltpu.VMEM((LAYERS,) + wholes[2].shape, low),
            pltpu.VMEM(*matrices[2]),
        ]
        + collect
        + collect
        + [
            pltpu.SemaphoreType.DMA((LAYERS, 4, images, 3)),
            pltpu.SemaphoreType.DMA((LAYERS, 4, images, 3)),
            pltpu.SemaphoreType.DMA((LAYERS, 9)),
            pltpu.SemaphoreType.DMA((3,)),
            pltpu.SemaphoreType.DMA((LAYERS, 3)),
            pltpu.SemaphoreType.DMA((LAYERS, 3, dp_size // 2, 3)),
            pltpu.SemaphoreType.DMA((LAYERS, 3, dp_size // 2, 3)),
            pltpu.SemaphoreType.DMA((LAYERS, 3)),
        ],
        compiler_params=pltpu.CompilerParams(
            collective_id=24, has_side_effects=True, vmem_limit_bytes=ACT_VMEM
        ),
        name="blocks_forward",
    )(residual, mod_vecs, vec_bias, qkv_bias, up_bias, *finals, *wholes, *shards)


def gelu_slope(values):
    root = math.sqrt(2.0 / math.pi)
    square = values * values
    tanh = jnp.tanh(root * (values + 0.044715 * values * square))
    half = 0.5 * (1.0 + tanh)
    slope = half + 0.5 * values * (1.0 - tanh * tanh) * root * (1.0 + 3.0 * 0.044715 * square)
    return values * half, slope


def norm_pull(values, scale_row, d_normed):
    normed, rstd = norm_parts(values)
    d_shift = jnp.sum(d_normed, axis=0, keepdims=True)
    d_scale = jnp.sum(d_normed * normed, axis=0, keepdims=True)
    inner = d_normed * (1.0 + scale_row)
    mean_one = jnp.mean(inner, axis=-1, keepdims=True)
    mean_two = jnp.mean(inner * normed, axis=-1, keepdims=True)
    return (inner - mean_one - normed * mean_two) * rstd, d_shift, d_scale


def backward_kernel(layer_idx, d_res_ref, mod_ref, *rest):
    kept, rest = rest[:12], rest[12:]
    if layer_idx is not None:
        kept = [ref.at[layer_idx] for ref in kept]
    with_reduce = len(rest) > 40
    terms, rest = (rest[:3], rest[3:]) if with_reduce else ((), rest)
    d_res_out, d_far, (d_mod, d_vec, d_qkv_bias, d_up_bias) = rest[0], rest[1:4], rest[4:8]
    totals, square_out = (rest[8:11], rest[11]) if with_reduce else ((), None)
    rest = rest[12:] if with_reduce else rest[8:]
    (
        res_ref,
        rows_a,
        qkv_ref,
        mixed_ref,
        branch_ref,
        mid_ref,
        rows_m,
        upper_ref,
        down_ref,
        w_qkv_ref,
        w_up_ref,
        w_out_ref,
        d_w_qkv,
        d_w_up,
        d_out,
    ) = rest[:15]
    (
        d_mid,
        d_rows_m,
        d_rows_a,
        act_low,
        d_upper,
        d_qkv,
        part_a,
        near_a,
        far_out_a,
        far_in_a,
        part_m,
        near_m,
        far_out_m,
        far_in_m,
        sends,
        recvs,
        move_sems,
    ) = rest[15:32]
    group_width = w_qkv_ref.shape[-1] // 3
    w_attn_ref, w_down_ref = w_out_ref.at[0:group_width, :], w_out_ref.at[group_width:, :]
    pairs = list(zip(kept, rest[:12])) + list(zip(rest[12:15], d_far))
    moves = Moves(pairs, move_sems)
    moves.start(8, 11, 7, 10, 6, 5, 4, 2, 9, 3, 1, 0)
    images = res_ref.shape[0]
    tokens = rows_a.shape[1]
    qkv_width = 3 * group_width
    units = w_up_ref.shape[-1]
    reduce, last_step = None, 0
    if with_reduce:
        line = Line()
        greet(line)
        own, pair_in, way_in, way_out = rest[32:35], rest[35:38], rest[38:41], rest[41:44]
        reduce = Reduce(line, terms, totals, own, pair_in, way_in, way_out, *rest[44:])
        last_step = line.size
    else:
        greet(None)
    spread_m = Spread(d_rows_m, sends.at[0], recvs.at[0])
    spread_a = Spread(d_rows_a, sends.at[1], recvs.at[1])
    collect_m = Collect(part_m, near_m, far_out_m, far_in_m, sends.at[2], recvs.at[2])
    collect_a = Collect(part_a, near_a, far_out_a, far_in_a, sends.at[3], recvs.at[3])
    d_vec[...] = jnp.zeros_like(d_vec)
    d_qkv_bias[...] = jnp.zeros_like(d_qkv_bias)
    d_up_bias[...] = jnp.zeros_like(d_up_bias)

    def mod_row(image, piece):
        return mod_ref[image, pl.ds(piece, 1), :]

    def start_down(image):
        d_res = d_res_ref[image]
        d_mod[image, pl.ds(5, 1), :] = jnp.sum(d_res * down_ref[image], axis=0, keepdims=True)
        d_down = d_res * mod_row(image, 5)
        d_vec[1:2, :] += jnp.sum(d_down, axis=0, keepdims=True)
        spread_m.put(image, d_down.astype(jnp.bfloat16))

    def feed(image):
        spread_m.wait(image)
        d_act = dot_nt(d_rows_m[image], w_down_ref[...])
        act, slope = gelu_slope(upper_ref[image])
        act_low[image] = act.astype(jnp.bfloat16)
        d_up = d_act * slope
        d_up_bias[...] += jnp.sum(d_up, axis=0, keepdims=True)
        d_up_low = d_up.astype(jnp.bfloat16)
        d_upper[image] = d_up_low
        collect_m.put(image, dot_nt(d_up_low, flat(w_up_ref)))

    def rows_of(ref, width):
        return ref[...].reshape(images * tokens, width)

    def feed_weights():
        tile = 256

        def step(index, carry):
            at = pl.ds(pl.multiple_of(index * tile, tile), tile)
            grad = dot_tn(
                act_low[:, :, at].reshape(images * tokens, tile), rows_of(d_rows_m, D)
            )
            d_out[pl.ds(pl.multiple_of(group_width + index * tile, 64), tile), :] = grad.astype(
                jnp.bfloat16
            )
            grad = dot_tn(
                rows_m[:, :, at].reshape(images * tokens, tile), rows_of(d_upper, units)
            )
            d_w_up[pl.ds(pl.multiple_of(index * tile, tile), tile), :] = grad.astype(jnp.bfloat16)
            return carry

        lax.fori_loop(0, units // tile, step, 0)

    def middle(image):
        d_value, d_shift, d_scale = norm_pull(
            mid_ref[image], mod_row(image, 4), collect_m.take(image)
        )
        d_mod[image, pl.ds(3, 1), :] = d_shift
        d_mod[image, pl.ds(4, 1), :] = d_scale
        d_value = d_res_ref[image] + d_value
        d_mid[image] = d_value
        d_mod[image, pl.ds(2, 1), :] = jnp.sum(d_value * branch_ref[image], axis=0, keepdims=True)
        d_branch = d_value * mod_row(image, 2)
        d_vec[0:1, :] += jnp.sum(d_branch, axis=0, keepdims=True)
        spread_a.put(image, d_branch.astype(jnp.bfloat16))

    def attend(image):
        spread_a.wait(image)
        d_mixed = dot_nt(d_rows_a[image], w_attn_ref[...]).astype(jnp.bfloat16)
        qkv = qkv_ref[image]
        d_queries, d_keys, d_values = [], [], []
        scale_dot = HEAD_DIM ** (-0.5)
        for head in range(group_width // HEAD_DIM):
            queries = head_slice(qkv[:, :group_width], head)
            keys_in = head_slice(qkv[:, group_width : 2 * group_width], head)
            values_in = head_slice(qkv[:, 2 * group_width :], head)
            d_head = head_slice(d_mixed, head)
            probs = soft_rows(queries, keys_in)
            d_probs = dot_nt(d_head, values_in)
            d_values.append(dot_tn(probs.astype(jnp.bfloat16), d_head))
            inner = jnp.sum(probs * d_probs, axis=-1, keepdims=True)
            d_scores = (probs * (d_probs - inner)).astype(jnp.bfloat16)
            d_queries.append(dot_nn(d_scores, keys_in) * scale_dot)
            d_keys.append(dot_tn(d_scores, queries) * scale_dot)
        joined = jnp.concatenate(d_queries + d_keys + d_values, axis=1)
        d_qkv_bias[...] += jnp.sum(joined, axis=0, keepdims=True)
        joined = joined.astype(jnp.bfloat16)
        d_qkv[image] = joined
        collect_a.put(image, dot_nt(joined, flat(w_qkv_ref)))

    def attend_weights():
        d_out[0:group_width, :] = dot_tn(
            rows_of(mixed_ref, group_width), rows_of(d_rows_a, D)
        ).astype(jnp.bfloat16)
        tile = 256

        def step(index, carry):
            at = pl.ds(pl.multiple_of(index * tile, tile), tile)
            grad = dot_tn(
                rows_a[:, :, at].reshape(images * tokens, tile), rows_of(d_qkv, qkv_width)
            )
            d_w_qkv[at, :] = grad.astype(jnp.bfloat16)
            return carry

        lax.fori_loop(0, D // tile, step, 0)

    def finish(image):
        d_value, d_shift, d_scale = norm_pull(
            res_ref[image], mod_row(image, 1), collect_a.take(image)
        )
        d_mod[image, pl.ds(0, 1), :] = d_shift
        d_mod[image, pl.ds(1, 1), :] = d_scale
        d_res_out[image] = d_mid[image] + d_value

    def close(image):
        spread_a.close(image)
        spread_m.close(image)
        collect_a.close(image)
        collect_m.close(image)

    if with_reduce:
        reduce.start()
    moves.wait(8)
    each(images, start_down)
    each(images, spread_m.forward)
    moves.wait(11, 7, 10)
    each(images, feed)
    if with_reduce:
        reduce.wait_own()
    run_ticks(reduce, 0, min(1, last_step - 1))
    each(images, collect_m.forward)
    moves.wait(6)
    feed_weights()
    moves.start(13)
    moves.wait(5, 4)
    each(images - 1, middle)
    run_ticks(reduce, 1, min(2, last_step - 1))
    middle(images - 1)
    each(images, spread_a.forward)
    moves.wait(2, 9)
    each(images - 1, attend)
    run_ticks(reduce, 2, min(3, last_step - 1))
    attend(images - 1)
    each(images, collect_a.forward)
    moves.wait(3, 1)
    attend_weights()
    moves.start(12, 14)
    moves.wait(0)
    each(images, finish)
    each(images, close)
    if with_reduce:
        each(max(last_step - 4, 0), lambda step: reduce.tick(step + 3))
        reduce.finish()
        square_out[...] = jnp.broadcast_to(
            sum(square_sum(total[...]) for total in totals), square_out.shape
        )
    moves.wait(12, 13, 14)


def backward_layer(d_residual, mod_vec, saved, weights, terms, layer_idx, stacked):
    images, count, _ = d_residual.shape
    tokens = 4 * count
    low, full = jnp.bfloat16, jnp.float32
    w_qkv, w_up, w_out = weights
    group_width, units = w_qkv.shape[-1] // 3, w_up.shape[-1]
    shapes = [
        ((images, count, D), full),
        ((D, 3 * group_width), low),
        ((D, units), low),
        ((group_width + units, D), low),
        ((images, 6, D), full),
        ((2, D), full),
        ((1, 3 * group_width), full),
        ((1, units), full),
    ]
    scratch = [
        pltpu.SemaphoreType.DMA((4, images, 3)),
        pltpu.SemaphoreType.DMA((4, images, 3)),
        pltpu.SemaphoreType.DMA((15,)),
    ]
    near = [
        pltpu.VMEM(kept.shape[1:] if stacked else kept.shape, kept.dtype)
        for kept in tuple(saved) + tuple(weights)
    ]
    near += [pltpu.VMEM(*shape) for shape in shapes[1:4]]
    if terms:
        spots = lax.axis_size("dp") // 2
        blocks = [term.shape[1:] for term in terms]
        shapes += [(block, full) for block in blocks] + [((8, 128), full)]
        scratch += [pltpu.VMEM((spots,) + block, low) for block in blocks]
        scratch += [pltpu.VMEM((spots,) + block, low) for block in blocks]
        scratch += [pltpu.VMEM((2, spots) + block, low) for block in blocks]
        scratch += [pltpu.VMEM((2, spots) + block, low) for block in blocks]
        scratch += [
            pltpu.SemaphoreType.DMA((3, spots, 3)),
            pltpu.SemaphoreType.DMA((3, spots, 3)),
            pltpu.SemaphoreType.DMA((3, spots)),
        ]
    return pl.pallas_call(
        functools.partial(backward_kernel, layer_idx if stacked else None),
        out_shape=[jax.ShapeDtypeStruct(*shape) for shape in shapes],
        in_specs=[pl.BlockSpec(memory_space=pltpu.VMEM)] * 2
        + [pl.BlockSpec(memory_space=pl.ANY)] * (12 + len(terms)),
        out_specs=[pl.BlockSpec(memory_space=pltpu.VMEM)]
        + [pl.BlockSpec(memory_space=pl.ANY)] * 3
        + [pl.BlockSpec(memory_space=pltpu.VMEM)] * (len(shapes) - 4),
        scratch_shapes=near
        + [
            pltpu.VMEM((images, count, D), full),
            pltpu.VMEM((images, tokens, D), low),
            pltpu.VMEM((images, tokens, D), low),
            pltpu.VMEM((images, tokens, units), low),
            pltpu.VMEM((images, tokens, units), low),
            pltpu.VMEM((images, tokens, 3 * group_width), low),
        ]
        + collect_scratch(images, tokens)
        + collect_scratch(images, tokens)
        + scratch,
        compiler_params=pltpu.CompilerParams(
            collective_id=20 + layer_idx if stacked else (21 if terms else 23), has_side_effects=True, vmem_limit_bytes=ACT_VMEM
        ),
        cost_estimate=pl.CostEstimate(
            flops=60 * 10**9, bytes_accessed=25 * 2**20, transcendentals=0
        ),
        name="block_backward",
    )(d_residual, mod_vec, *saved, *weights, *terms)


def dense_nt(left_op, right_op):
    return lax.dot_general(
        left_op,
        right_op,
        (((1,), (1,)), ((), ())),
        precision=PRECISE,
        preferred_element_type=jnp.float32,
    )


def dense_tn(left_op, right_op):
    return lax.dot_general(
        left_op,
        right_op,
        (((0,), (0,)), ((), ())),
        precision=PRECISE,
        preferred_element_type=jnp.float32,
    )


def chosen(shape, rule, kind):
    row = lax.broadcasted_iota(jnp.int32, shape, 0)
    col = lax.broadcasted_iota(jnp.int32, shape, 1)
    return jnp.where(rule(row, col), 1.0, 0.0).astype(kind)


def fold(values):
    groups = values.shape[-2] // 8
    pieces = [values[..., 8 * at : 8 * at + 8, :] for at in range(groups)]
    used = groups * values.shape[-1]
    if used % 128:
        pieces.append(jnp.zeros(values.shape[:-2] + (8, 128 - used % 128), values.dtype))
    return jnp.concatenate(pieces, axis=-1)


def folded_lanes(cols, count):
    return -(-(cols // 8 * count) // 128) * 128


def unfold_all(values, cols, count):
    ordered = [
        values[tensor_at, dp_at]
        for dp_at in range(values.shape[1])
        for tensor_at in range(values.shape[0])
    ]
    return jnp.concatenate([unfold(value, cols, count) for value in ordered], axis=0)


def unfold(values, cols, count):
    pieces = [values[..., at * count : (at + 1) * count] for at in range(cols // 8)]
    return jnp.concatenate(pieces, axis=-2)


def slots_of(images):
    return -(-LAYERS * images // 16) * 16


def head_kernel(
    images,
    small_ref,
    feats_ref,
    table_ref,
    time_ref,
    second_ref,
    shift_ref,
    scale_ref,
    bias_ref,
    mod_ref,
    *rest,
):
    shards = rest[0:3]
    (
        small_all,
        feats_out,
        pre_time_out,
        hidden_out,
        pre_signal_out,
        signal_out,
        final_all,
        mod_all,
    ) = rest[3:11]
    wholes = rest[11:14]
    (
        feats_all,
        hidden_own,
        hidden_dp,
        hidden_all,
        signal_own,
        signal_dp,
        signal_all,
        final_own,
        final_dp,
        mod_part,
        mod_in,
        mod_own,
        small_dp,
    ) = rest[14:27]
    crowds = [rest[27 + 3 * index : 30 + 3 * index] for index in range(11)]
    gather_sems = rest[60:]
    dp_size = lax.axis_size("dp")
    tensor_size = lax.axis_size("tensor")
    dp_rank = lax.axis_index("dp")
    images_all = images * dp_size
    slots = mod_own.shape[0]
    greet_groups("dp", "tensor")
    gather = Gather(Line(), [shard.at[0] for shard in shards], wholes, *gather_sems)
    feats = Crowd("dp", lambda place: feats_ref, feats_all, *crowds[0])
    mod_sum = Crowd("dp", lambda place: mod_part.at[place], mod_in, *crowds[1])
    mod_spread = Crowd("tensor", lambda place: mod_own, mod_all, *crowds[2])
    small = Relay(lambda place: small_ref, small_dp, small_all, *crowds[3:5])
    hidden = Relay(lambda place: hidden_own, hidden_dp, hidden_all, *crowds[5:7])
    signal = Relay(lambda place: signal_own, signal_dp, signal_all, *crowds[7:9])
    final = Relay(lambda place: final_own.at[place], final_dp, final_all, *crowds[9:11])
    line = gather.line
    first, last = line.at == 0, line.at == line.size - 1
    feats.start()
    gather.start()
    feats.wait()
    pick = chosen(
        (images_all, 8 * dp_size),
        lambda row, col: (row // images == col // 8) & (lax.rem(row, images) == lax.rem(col, 8)),
        jnp.float32,
    )
    feats_sum = dense(pick, feats_all[...].reshape(8 * dp_size, feats_all.shape[2]))
    feats_out[...] = feats_sum
    pre_time = dense_nt(time_ref[...], feats_sum[:, 0:FREQ]) + bias_ref[:, 1:2]
    pre_time_out[...] = pre_time
    hidden_own[...] = fold(jax.nn.silu(pre_time))
    hidden.start()
    class_lanes = -(-CLASSES // 128) * 128
    labels = jnp.round(feats_sum[:, FREQ : FREQ + 1]).astype(jnp.int32)
    lane = lax.broadcasted_iota(jnp.int32, (images_all, class_lanes), 1)
    onehot = jnp.where(lane == labels, 1.0, 0.0)
    class_part = dense_nt(table_ref[:, 0:class_lanes], onehot) + bias_ref[:, 2:3]
    small.start()
    hidden.hand_on()
    for way in (UP, DOWN):
        gather.hand_on(1, way)
    gather.hand_over(1, UP)
    gather.hand_over(1, DOWN, first)
    hidden.wait()
    cols = second_ref.shape[0]
    hidden_full = unfold_all(hidden_all[...], cols, images_all)
    hidden_out[...] = hidden_full
    pre_signal = dense(second_ref[...], hidden_full) + class_part
    pre_signal_out[...] = pre_signal
    signal_own[...] = fold(jax.nn.silu(pre_signal))
    signal.start()
    small.hand_on()
    signal.hand_on()
    for way in (UP, DOWN):
        gather.hand_on(2, way)
    gather.hand_over(1, DOWN, jnp.logical_not(first))
    gather.hand_over(2, UP, last)
    gather.hand_over(2, DOWN, first)
    signal.wait()
    signal_full = unfold_all(signal_all[...], cols, images_all)
    signal_out[...] = signal_full
    mod_rows = mod_ref.shape[1]
    own_rows = pl.ds(pl.multiple_of(dp_rank * mod_rows, 8), mod_rows)
    signal_low = signal_out[own_rows, :].astype(jnp.bfloat16)
    total = None
    for layer_idx in range(LAYERS):
        pick = chosen(
            (images_all, dp_size * slots),
            lambda row, col: (
                (row // images == col // slots)
                & (lax.rem(row, images) + layer_idx * images == lax.rem(col, slots))
            ),
            jnp.bfloat16,
        )
        placed = dot_nn(signal_low, pick).astype(jnp.bfloat16)
        term = dot_tn(placed, mod_ref[layer_idx])
        total = term if total is None else total + term
    mod_part[...] = total.reshape(mod_part.shape).astype(mod_part.dtype)
    mod_sum.start()
    gather.hand_over(2, UP, jnp.logical_not(last))
    gather.hand_over(2, DOWN, jnp.logical_not(first))
    finals = jnp.concatenate(
        [
            dense(shift_ref[...], signal_full) + bias_ref[:, 3:4],
            dense(scale_ref[...], signal_full) + bias_ref[:, 4:5],
            jnp.zeros((128 - 2 * shift_ref.shape[0], images_all), jnp.float32),
        ],
        axis=0,
    )
    pick = chosen(
        (8 * dp_size, images_all),
        lambda row, col: (row // 8 == col // images) & (lax.rem(row, 8) == lax.rem(col, images)),
        jnp.float32,
    )
    final_own[...] = dense_nt(pick, finals).reshape(final_own.shape)
    final.start()
    run_ticks(gather, 3, min(4, dp_size // 2))
    mod_sum.wait()
    mod_own[...] = jnp.sum(mod_in[...].astype(jnp.float32), axis=0)
    mod_spread.start()
    final.hand_on()
    each(max(dp_size // 2 - 4, 0), lambda step: gather.tick(step + 4))
    small.wait()
    final.wait()
    mod_spread.wait()
    gather.finish()


def head_call(small, feats, table, times, second, shift, scale, bias, mod_low, shards, images):
    dp_size, tensor_size = lax.axis_size("dp"), lax.axis_size("tensor")
    images_all = images * dp_size
    cols = table.shape[0]
    slots = slots_of(images)
    folded = folded_lanes(cols, images_all)
    full, low = jnp.float32, jnp.bfloat16
    shapes = [
        ((tensor_size, dp_size) + small.shape, full),
        ((images_all, feats.shape[1]), full),
        ((cols, images_all), full),
        ((D, images_all), full),
        ((cols, images_all), full),
        ((D, images_all), full),
        ((tensor_size, dp_size, 8, 128), full),
        ((tensor_size, slots, mod_low.shape[2]), full),
    ] + [((dp_size,) + shard.shape[1:], low) for shard in shards]
    scratch = [
        pltpu.VMEM((dp_size,) + feats.shape, full),
        pltpu.VMEM((8, folded), full),
        pltpu.VMEM((dp_size, 8, folded), full),
        pltpu.VMEM((tensor_size, dp_size, 8, folded), full),
        pltpu.VMEM((8, folded), full),
        pltpu.VMEM((dp_size, 8, folded), full),
        pltpu.VMEM((tensor_size, dp_size, 8, folded), full),
        pltpu.VMEM((dp_size, 8, 128), full),
        pltpu.VMEM((dp_size, 8, 128), full),
        pltpu.VMEM((dp_size, slots, mod_low.shape[2]), low),
        pltpu.VMEM((dp_size, slots, mod_low.shape[2]), low),
        pltpu.VMEM((slots, mod_low.shape[2]), full),
        pltpu.VMEM((dp_size,) + small.shape, full),
    ]
    for count in (dp_size, dp_size) + (tensor_size, dp_size) * 4 + (tensor_size,):
        scratch += crowd_scratch(count)
    scratch += [
        pltpu.SemaphoreType.DMA((3, dp_size // 2, 3)),
        pltpu.SemaphoreType.DMA((3, dp_size // 2, 3)),
        pltpu.SemaphoreType.DMA((3,)),
    ]
    return pl.pallas_call(
        functools.partial(head_kernel, images),
        out_shape=[jax.ShapeDtypeStruct(*shape) for shape in shapes],
        in_specs=[pl.BlockSpec(memory_space=pltpu.VMEM)] * 9
        + [pl.BlockSpec(memory_space=pl.ANY)] * len(shards),
        out_specs=[pl.BlockSpec(memory_space=pltpu.VMEM)] * 8
        + [pl.BlockSpec(memory_space=pl.ANY)] * len(shards),
        scratch_shapes=scratch,
        compiler_params=pltpu.CompilerParams(
            collective_id=30, has_side_effects=True, vmem_limit_bytes=ACT_VMEM
        ),
        name="head",
    )(small, feats, table, times, second, shift, scale, bias, mod_low, *shards)


def tail_kernel(
    images,
    final_at,
    row_ref,
    mod_ref,
    weight_ref,
    second_ref,
    shift_ref,
    scale_ref,
    pre_signal_ref,
    pre_time_ref,
    feats_ref,
    hidden_ref,
    signal_ref,
    loss_ref,
    *rest,
):
    terms, others = rest[0:3], rest[3 : 2 + LAYERS]
    rest = rest[2 + LAYERS :]
    table_grad, mod_grad, scalar_sums = rest[0:3]
    totals, rest = rest[3:6], rest[6:]
    (
        row_in,
        row_mid,
        row_fin,
        mod_in,
        mod_low,
        d_mod_all,
        signal_part,
        scalar_own,
        scalar_in,
        scalar_mid,
        scalar_fin,
    ) = rest[0:11]
    signal_refs, hidden_refs = rest[11:15], rest[15:19]
    own, pair_in, way_in, way_out = rest[19:22], rest[22:25], rest[25:28], rest[28:31]
    crowds = [rest[31 + 3 * index : 34 + 3 * index] for index in range(10)]
    reduce_sems = rest[61:]
    signal_out, hidden_out = signal_refs[0], hidden_refs[0]
    dp_size = lax.axis_size("dp")
    tensor_size = lax.axis_size("tensor")
    places = dp_size * tensor_size
    dp_rank = lax.axis_index("dp")
    images_all = images * dp_size
    cols, lanes = row_ref.shape[2:]
    mod_rows = weight_ref.shape[1]
    slots = mod_low.shape[0]
    last_step = dp_size // 2
    greet_groups("tensor", "dp")
    reduce = Reduce(Line(), terms, totals, own, pair_in, way_in, way_out, *reduce_sems)
    mod_sum = Crowd("tensor", lambda place: mod_ref.at[place], mod_in, *crowds[0])
    mod_spread = Crowd("dp", lambda place: mod_low, d_mod_all, *crowds[1])
    rows = Funnel(row_ref, row_in, row_mid, row_fin, *crowds[2:4])
    signal = Funnel(*signal_refs, *crowds[4:6])
    hidden = Funnel(*hidden_refs, *crowds[6:8])
    scalars = Crowd("tensor", lambda place: scalar_own, scalar_in, *crowds[8])
    scalars_dp = Crowd("dp", lambda place: scalar_mid, scalar_fin, *crowds[9])
    mod_sum.start()
    rows.start()
    reduce.send_pair(0)
    reduce.load_own()
    mod_sum.wait()
    mod_low[...] = jnp.sum(mod_in[...], axis=0).astype(jnp.bfloat16)
    mod_spread.start()
    rows.hand_on()
    reduce.send_pair(1)
    other_squares = sum(other[0:1, 0:1] for other in others)
    reduce.wait_own()
    row_total = rows.take()
    patch_start, time_start, second_start, final_start, head_start, vector_start, layer_start = (
        table_starts()
    )
    patch_in = time_start - patch_start
    layer_at = 2 * patch_in + 1

    def put(start, values):
        table_grad[:, start : start + values.shape[1]] = values

    put(patch_start, row_total[:, 0:patch_in])
    put(head_start, row_total[:, patch_in:layer_at])
    put(layer_start, row_total[:, layer_at:final_at])
    joined = jnp.concatenate([row_fin[at] for at in range(dp_size)], axis=1)

    def final_of(piece):
        return dense(
            joined,
            chosen(
                (dp_size * lanes, images_all),
                lambda row, col: (
                    (row // lanes == col // images)
                    & (lax.rem(row, lanes) == final_at + piece * images + lax.rem(col, images))
                ),
                jnp.float32,
            ),
        )

    d_shift, d_scale = final_of(0), final_of(1)
    signal_part[...] = dense_tn(shift_ref[...], d_shift) + dense_tn(scale_ref[...], d_scale)
    mod_spread.wait()
    d_mod = d_mod_all[...].reshape(dp_size * slots, mod_low.shape[1])
    own_rows = pl.ds(pl.multiple_of(dp_rank * mod_rows, 8), mod_rows)

    def layer_pick(layer_idx, kind):
        return chosen(
            (dp_size * slots, images_all),
            lambda row, col: (
                (row // slots == col // images)
                & (lax.rem(row, slots) == layer_idx * images + lax.rem(col, images))
            ),
            kind,
        )

    for layer_idx in range(LAYERS):
        signal_part[own_rows, :] += dense(
            dot_nt(weight_ref[layer_idx], d_mod), layer_pick(layer_idx, jnp.float32)
        )
    signal_out[...] = fold(signal_part[...].reshape(places, cols, images_all)).reshape(
        signal_out.shape
    )
    signal.start()
    signal.hand_on()
    reduce.send_pair(2)
    run_ticks(reduce, 0, min(1, last_step - 1))
    signal_low = signal_ref[own_rows, :].astype(jnp.bfloat16)
    for layer_idx in range(LAYERS):
        placed = dot_nt(signal_low, layer_pick(layer_idx, jnp.bfloat16)).astype(jnp.bfloat16)
        grad = dot_nn(placed, d_mod)
        mod_grad[layer_idx] = grad
        other_squares = other_squares + square_sum(grad)
    grad = dense_nt(d_shift, signal_ref[...])
    put(final_start, grad)
    other_squares = other_squares + square_sum(grad)
    grad = dense_nt(d_scale, signal_ref[...])
    put(final_start + D, grad)
    other_squares = other_squares + square_sum(grad)
    lane = lax.broadcasted_iota(jnp.int32, row_total.shape, 1)
    other_squares = other_squares + square_sum(jnp.where(lane < final_at, row_total, 0.0))
    d_signal = unfold(signal.take(), cols, images_all)
    d_signal = d_signal * silu_slope(pre_signal_ref[...])
    d_hidden = dense_tn(second_ref[...], d_signal)
    hidden_out[...] = fold(d_hidden.reshape(places, cols, images_all)).reshape(hidden_out.shape)
    hidden.start()
    hidden.hand_on()
    each(max(last_step - 3, 0), lambda step: reduce.send_pair(step + 3))
    run_ticks(reduce, 1, min(2, last_step - 1))
    labels = jnp.round(feats_ref[:, FREQ : FREQ + 1]).astype(jnp.int32)
    class_lane = lax.broadcasted_iota(jnp.int32, (images_all, -(-CLASSES // 128) * 128), 1)
    grad = dense(d_signal, jnp.where(class_lane == labels, 1.0, 0.0))
    put(0, grad[:, 0:CLASSES])
    other_squares = other_squares + square_sum(grad)
    grad = dense_nt(d_signal, hidden_ref[...])
    put(second_start, grad)
    other_squares = other_squares + square_sum(grad)
    d_hidden = unfold(hidden.take(), cols, images_all)
    d_hidden = d_hidden * silu_slope(pre_time_ref[...])
    grad = dense(d_hidden, feats_ref[:, 0:FREQ])
    put(time_start, grad)
    other_squares = other_squares + square_sum(grad)
    vectors = [
        jnp.sum(values, axis=1, keepdims=True) for values in (d_hidden, d_signal, d_shift, d_scale)
    ]
    lane = lax.broadcasted_iota(jnp.int32, (cols, 128), 1)
    grad = sum(jnp.where(lane == at, vector, 0.0) for at, vector in enumerate(vectors))
    put(vector_start + 1, grad[:, 0:4])
    other_squares = other_squares + square_sum(grad)
    run_ticks(reduce, 2, min(3, last_step - 1))
    each(max(last_step - 4, 0), lambda step: reduce.tick(step + 3))
    reduce.finish()
    for total in totals:
        other_squares = other_squares + square_sum(total[...])
    lane = lax.broadcasted_iota(jnp.int32, scalar_own.shape, 1)
    scalar_own[...] = jnp.where(lane == 0, loss_ref[...], other_squares)
    scalars.start()
    scalars.wait()
    scalar_mid[...] = jnp.sum(scalar_in[...], axis=0)
    scalars_dp.start()
    scalars_dp.wait()
    scalar_sums[...] = jnp.sum(scalar_fin[...], axis=0)


def tail_call(
    rows, mods, mod_low, second, shift, scale, pre_signal, pre_time, feats, hidden, signal, loss,
    terms, others, images, at,
):
    dp_size, tensor_size = lax.axis_size("dp"), lax.axis_size("tensor")
    images_all = images * dp_size
    cols, lanes = rows.shape[2:]
    folded = folded_lanes(cols, images_all)
    full, low = jnp.float32, jnp.bfloat16
    spots = dp_size // 2
    blocks = [term.shape[1:] for term in terms]
    table_rows = table_starts()[-1] + LAYERS * (10 + FF // D)
    shapes = [
        ((cols, table_rows), full),
        (mod_low.shape, full),
        ((8, 128), full),
    ] + [(block, full) for block in blocks]
    scratch = [
        pltpu.VMEM((tensor_size, dp_size, cols, lanes), full),
        pltpu.VMEM((dp_size, cols, lanes), full),
        pltpu.VMEM((dp_size, cols, lanes), full),
        pltpu.VMEM(mods.shape, full),
        pltpu.VMEM(mods.shape[1:], low),
        pltpu.VMEM((dp_size,) + mods.shape[1:], low),
        pltpu.VMEM((D, images_all), full),
        pltpu.VMEM((8, 128), full),
        pltpu.VMEM((tensor_size, 8, 128), full),
        pltpu.VMEM((8, 128), full),
        pltpu.VMEM((dp_size, 8, 128), full),
    ]
    for _ in range(2):
        scratch += [
            pltpu.VMEM((dp_size, tensor_size, 8, folded), full),
            pltpu.VMEM((tensor_size, dp_size, 8, folded), full),
            pltpu.VMEM((dp_size, 8, folded), full),
            pltpu.VMEM((dp_size, 8, folded), full),
        ]
    scratch += [pltpu.VMEM((spots,) + block, low) for block in blocks]
    scratch += [pltpu.VMEM((spots,) + block, low) for block in blocks]
    scratch += [pltpu.VMEM((2, spots) + block, low) for block in blocks]
    scratch += [pltpu.VMEM((2, spots) + block, low) for block in blocks]
    for count in (tensor_size, dp_size) * 5:
        scratch += crowd_scratch(count)
    scratch += [
        pltpu.SemaphoreType.DMA((3, spots, 3)),
        pltpu.SemaphoreType.DMA((3, spots, 3)),
        pltpu.SemaphoreType.DMA((3, spots)),
    ]
    return pl.pallas_call(
        functools.partial(tail_kernel, images, at),
        out_shape=[jax.ShapeDtypeStruct(*shape) for shape in shapes],
        in_specs=[pl.BlockSpec(memory_space=pltpu.VMEM)] * 12
        + [pl.BlockSpec(memory_space=pl.ANY)] * len(terms)
        + [pl.BlockSpec(memory_space=pltpu.VMEM)] * len(others),
        out_specs=[pl.BlockSpec(memory_space=pltpu.VMEM)] * len(shapes),
        scratch_shapes=scratch,
        compiler_params=pltpu.CompilerParams(
            collective_id=31, has_side_effects=True, vmem_limit_bytes=ACT_VMEM
        ),
        name="tail",
    )(
        rows, mods, mod_low, second, shift, scale, pre_signal, pre_time, feats, hidden, signal,
        loss, *terms, *others,
    )


def adam_update(weight, first, second, grad, factor, first_fix, second_fix):
    clipped = grad * factor
    first_new = BETA_ONE * first + (1.0 - BETA_ONE) * clipped
    second_new = BETA_TWO * second + (1.0 - BETA_TWO) * clipped * clipped
    step_size = first_new / first_fix / (jnp.sqrt(second_new / second_fix) + ADAM_EPS)
    change = -LEARN_RATE * (step_size + DECAY * weight)
    master = weight + change
    return (master, first_new, second_new, master.astype(jnp.bfloat16), change)


def local(
    latents,
    target_noise,
    timesteps,
    labels,
    step_count,
    embed_table,
    layer_in,
    layer_out,
    layer_ada,
    embed_first,
    embed_second,
    input_first,
    input_second,
    output_first,
    output_second,
    mod_first,
    mod_second,
):
    tensor_size = lax.axis_size("tensor")
    tensor_rank = lax.axis_index("tensor")
    images = latents.shape[0]
    grid_side = SIDE // PATCH
    local_rows = grid_side // tensor_size
    tokens_all = grid_side * grid_side
    heads_local = HEADS // tensor_size
    group_width = heads_local * HEAD_DIM
    unit_count = FF // tensor_size
    patch_in = PATCH * PATCH * CHANNELS
    count_all = images * lax.axis_size("dp") * tokens_all * patch_in
    patch_start, time_start, second_start, final_start, head_start, vector_start, layer_start = (
        table_starts()
    )
    layer_rows = 10 + FF // D
    dp_rank = lax.axis_index("dp")
    dp_size = lax.axis_size("dp")
    place_count = dp_size * tensor_size
    images_all = images * dp_size
    table_cols = lax.reduce_precision(embed_table.T, 8, 7)
    cols = table_cols.shape[0]
    mod_rows = layer_ada.shape[1]
    mod_cols = layer_ada.shape[2]
    mod_low = layer_ada.astype(jnp.bfloat16)

    def col_block(row_start, row_count):
        return table_cols[:, row_start : row_start + row_count]

    vector_count = 5 + LAYERS * layer_rows
    small_count = 2 * patch_in + vector_count
    lanes = -(-(small_count + 2 * images) // 128) * 128
    shards_in = layer_in[:, :, 0].astype(jnp.bfloat16)
    shards = (
        shards_in[:, :, : 3 * group_width],
        shards_in[:, :, 3 * group_width :],
        layer_out[:, 0].astype(jnp.bfloat16),
    )
    second_cols = col_block(second_start, D)
    shift_cols = col_block(final_start, D)
    scale_cols = col_block(final_start + D, D)
    fused = cols % 8 == 0 and images <= 8
    if fused:
        small_send = jnp.concatenate(
            [
                col_block(patch_start, patch_in),
                col_block(head_start, patch_in + vector_count),
                jnp.zeros((cols, lanes - small_count), jnp.float32),
            ],
            axis=1,
        )
        feats_send = jnp.concatenate(
            [
                time_features(timesteps),
                jnp.broadcast_to(labels.astype(jnp.float32)[:, None], (images, 128)),
            ],
            axis=1,
        )
        feats_send = jnp.pad(feats_send, ((0, 8 - images), (0, 0)))
        outs = head_call(
            small_send,
            feats_send,
            table_cols,
            col_block(time_start, FREQ),
            second_cols,
            shift_cols,
            scale_cols,
            col_block(vector_start, 5),
            mod_low,
            shards,
            images,
        )
        small_all, feats_all, pre_time, hidden, pre_signal, signal, final_all, mod_full = outs[:8]
        wholes = outs[8:]
        small_all = small_all.transpose(1, 0, 2, 3)
        time_feats = feats_all[:, :FREQ]
        labels_all = jnp.round(feats_all[:, FREQ]).astype(jnp.int32)
        signal_low = lax.dynamic_slice_in_dim(
            signal.astype(jnp.bfloat16), dp_rank * mod_rows, mod_rows, 0
        )
        final_all = final_all.transpose(1, 0, 2, 3)[:, :, :images, : 2 * cols]
        final_own = final_all.reshape(place_count, images, 2, cols)
        final_own = final_own.transpose(2, 1, 0, 3).reshape(2, images, D)
        mod_full = mod_full[:, : LAYERS * images].reshape(tensor_size, LAYERS, images, mod_cols)
        mod_full = mod_full.transpose(1, 2, 0, 3).reshape(LAYERS, images, tensor_size * mod_cols)
    else:
        scalar_lanes = jnp.concatenate([timesteps, labels]).astype(jnp.float32)
        small_send = jnp.concatenate(
            [
                col_block(patch_start, patch_in),
                col_block(head_start, patch_in + vector_count),
                jnp.broadcast_to(scalar_lanes[None, :], (cols, 2 * images)),
                jnp.zeros((cols, lanes - small_count - 2 * images), jnp.float32),
            ],
            axis=1,
        )
        small_all = exchange(small_send, "all", False, 1)
        scalars_all = small_all[::tensor_size, 0, small_count : small_count + 2 * images].astype(
            jnp.int32
        )
        timesteps_all = scalars_all[:, :images].reshape(images_all)
        labels_all = scalars_all[:, images:].reshape(images_all)
        time_feats = time_features(timesteps_all)
        onehot = (labels_all[:, None] == jnp.arange(CLASSES, dtype=jnp.int32)[None, :]).astype(
            jnp.float32
        )
        pre_time = dense(col_block(time_start, FREQ), time_feats.T) + col_block(vector_start + 1, 1)
        hidden = exchange(jax.nn.silu(pre_time), "all", False, 2).reshape(D, images_all)
        pre_signal = (
            dense(second_cols, hidden)
            + col_block(vector_start + 2, 1)
            + dense(col_block(0, CLASSES), onehot.T)
        )
        signal = exchange(jax.nn.silu(pre_signal), "all", False, 3).reshape(D, images_all)
        final_send = jnp.concatenate(
            [
                dense(shift_cols, signal) + col_block(vector_start + 3, 1),
                dense(scale_cols, signal) + col_block(vector_start + 4, 1),
            ],
            axis=0,
        )
        final_all = exchange(final_send, "all", False, 4).reshape(place_count, 2, cols, images_all)
        final_own = lax.dynamic_slice_in_dim(final_all, dp_rank * images, images, 3)
        final_own = final_own.transpose(1, 3, 0, 2).reshape(2, images, D)
        signal_low = lax.dynamic_slice_in_dim(
            signal.astype(jnp.bfloat16), dp_rank * mod_rows, mod_rows, 0
        )
        mod_part = jnp.einsum("db,lde->ble", signal_low, mod_low, preferred_element_type=jnp.float32)
        mod_part = mod_part.reshape(dp_size, images * LAYERS, mod_cols)
        mod_local = jnp.sum(exchange(mod_part, "dp", True, 5), axis=0)
        mod_full = exchange(mod_local, "tensor", False, 6)
        mod_full = mod_full.reshape(tensor_size, images, LAYERS, mod_cols)
        mod_full = mod_full.transpose(2, 1, 0, 3).reshape(LAYERS, images, tensor_size * mod_cols)
        wholes = [lax.all_gather(shard[0], "dp") for shard in shards]
    small_rows = small_all.reshape(D, lanes).T
    patch_w = small_rows[0:patch_in]
    head_w = small_rows[patch_in : 2 * patch_in]
    vectors = small_rows[2 * patch_in : 2 * patch_in + 5]
    bias_all = small_rows[2 * patch_in + 5 : small_count]
    onehot = (labels_all[:, None] == jnp.arange(CLASSES, dtype=jnp.int32)[None, :]).astype(
        jnp.float32
    )
    final_shift, final_scale = final_own[0], final_own[1]
    pixels = patchify(latents, local_rows)
    targets = patchify(target_noise, local_rows)
    keep_coef, drop_coef = noise_levels(timesteps)
    noisy = keep_coef[:, None, None] * pixels + drop_coef[:, None, None] * targets
    residual = (
        jnp.einsum("btp,pd->btd", noisy, patch_w, precision=PRECISE)
        + vectors[0]
        + position_table(tensor_rank * local_rows, local_rows)[None]
    )
    saved_acts = []
    bias_all = bias_all.reshape(LAYERS, layer_rows, D)
    mod_vecs = mod_full.reshape(LAYERS, images, 6, D) + bias_all[:, None, 0:6]
    part_bias = lax.dynamic_slice_in_dim(
        bias_all[:, 8:10], tensor_rank * group_width, group_width, 2
    )
    qkv_bias = jnp.concatenate(
        [part_bias[:, 0], jnp.zeros((LAYERS, group_width), jnp.float32), part_bias[:, 1]], axis=1
    )
    up_bias = lax.dynamic_slice_in_dim(
        bias_all[:, 10:].reshape(LAYERS, FF), tensor_rank * unit_count, unit_count, 1
    )
    joined = fused and shards[0].shape[1] % 16 == 0 and shards[2].shape[1] % 8 == 0
    if joined:
        outs = forward_all(
            count_all,
            residual,
            mod_vecs,
            bias_all[:, 6:8],
            qkv_bias[:, None],
            up_bias[:, None],
            (final_shift[:, None], final_scale[:, None], head_w, targets),
            wholes,
            shards,
        )
        d_residual, d_head, loss_part, d_final_shift, d_final_scale = outs[:5]
        loss_part = loss_part[0, 0]
        d_final_shift, d_final_scale = d_final_shift[:, 0], d_final_scale[:, 0]
        saved_acts = [
            (mod_vecs[layer_idx], outs[5:14], outs[14:17]) for layer_idx in range(LAYERS)
        ]
    else:
        for layer_idx in range(LAYERS):
            weights = (
                wholes[0].reshape(D, 3 * group_width),
                wholes[1].reshape(D, unit_count),
                wholes[2].reshape(group_width + unit_count, D),
            )
            outs = forward_layer(
                residual,
                mod_vecs[layer_idx],
                bias_all[layer_idx, 6:8],
                qkv_bias[layer_idx : layer_idx + 1],
                up_bias[layer_idx : layer_idx + 1],
                *weights,
                shards if layer_idx + 1 < LAYERS else (),
                layer_idx,
            )
            wholes = outs[9:]
            saved_acts.append((mod_vecs[layer_idx], (residual,) + tuple(outs[1:9]), weights))
            residual = outs[0]
        final_in, final_norm_pull = jax.vjp(modulate, residual, final_shift, final_scale)
        predicted = jnp.einsum("btd,pd->btp", final_in, head_w, precision=PRECISE)
        error_all = predicted - targets
        loss_part = jnp.sum(error_all * error_all) / count_all
        d_pred = 2.0 * error_all / count_all
        d_head = jnp.einsum("btp,btd->pd", d_pred, final_in, precision=PRECISE)
        d_final = jnp.einsum("btp,pd->btd", d_pred, head_w, precision=PRECISE)
        d_residual, d_final_shift, d_final_scale = final_norm_pull(d_final)
    totals = []
    squares = []
    terms = ()
    bias_parts = []
    for layer_idx in reversed(range(LAYERS)):
        mod_vec, saved, weights = saved_acts[layer_idx]
        outs = backward_layer(
            d_residual, mod_vec, saved, weights, terms, layer_idx, joined
        )
        d_residual, d_w_qkv, d_w_up, d_w_out, d_mod_vec, d_vec, d_qkv_bias, d_up_bias = outs[:8]
        if terms:
            totals.insert(0, outs[8:11])
            squares.append(outs[11])
        terms = [
            term.reshape((dp_size, -1) + term.shape[1:]) for term in (d_w_qkv, d_w_up, d_w_out)
        ]
        bias_parts.insert(0, (d_mod_vec, d_vec, d_qkv_bias, d_up_bias))
    d_mods, d_vecs, d_qkv_rows, d_up_rows = [jnp.stack(parts) for parts in zip(*bias_parts)]
    part_rows = jnp.stack([d_qkv_rows[:, 0, :group_width], d_qkv_rows[:, 0, 2 * group_width :]], 1)
    bias_blocks = jnp.concatenate(
        [
            jnp.sum(d_mods, axis=1),
            d_vecs,
            lax.dynamic_update_slice_in_dim(
                jnp.zeros((LAYERS, 2, D), jnp.float32), part_rows, tensor_rank * group_width, 2
            ),
            lax.dynamic_update_slice_in_dim(
                jnp.zeros((LAYERS, FF), jnp.float32), d_up_rows[:, 0], tensor_rank * unit_count, 1
            ).reshape(LAYERS, FF // D, D),
        ],
        axis=1,
    ).reshape(LAYERS * layer_rows, D)
    d_patch_w = jnp.einsum("btp,btd->pd", noisy, d_residual, precision=PRECISE)
    d_patch_b = jnp.sum(d_residual, axis=(0, 1))
    row_parts = jnp.concatenate(
        [d_patch_w, d_head, d_patch_b[None], bias_blocks, d_final_shift, d_final_scale],
        axis=0,
    )
    row_count = row_parts.shape[0]
    row_lanes = -(-row_count // 128) * 128
    row_parts = jnp.pad(row_parts, ((0, row_lanes - row_count), (0, 0)))
    final_at = row_count - 2 * images
    row_send = row_parts.T.reshape(dp_size, tensor_size, cols, row_lanes)
    mod_send = d_mods.reshape(LAYERS * images, tensor_size, mod_cols)
    mod_send = mod_send.transpose(1, 0, 2)
    if fused:
        slots = slots_of(images)
        outs = tail_call(
            row_send,
            jnp.pad(mod_send, ((0, 0), (0, slots - LAYERS * images), (0, 0))),
            mod_low,
            second_cols,
            shift_cols,
            scale_cols,
            pre_signal,
            pre_time,
            feats_all,
            hidden,
            signal,
            loss_part.reshape(1, 1),
            terms,
            squares,
            images,
            final_at,
        )
        table_grad, mod_grad, scalar_sums = outs[:3]
        totals.insert(0, outs[3:])
        scalar_sums = scalar_sums[0]
    else:
        totals.insert(
            0,
            [
                lax.psum_scatter(term, "dp", scatter_dimension=0).astype(jnp.float32)
                for term in terms
            ],
        )
        row_all = exchange(row_send.reshape(place_count, cols, row_lanes), "all", True, 7)
        row_sums = jnp.sum(row_all, axis=0)
        final_sums = jnp.sum(
            row_all[:, :, final_at:row_count].reshape(dp_size, tensor_size, cols, 2, images), axis=1
        )
        final_sums = final_sums.transpose(2, 1, 0, 3).reshape(2, cols, images_all)
        d_shift_cols, d_scale_cols = final_sums[0], final_sums[1]
        d_mod_own = jnp.sum(exchange(mod_send, "tensor", True, 8), axis=0)
        d_mod_low = exchange(d_mod_own.astype(jnp.bfloat16), "dp", False, 9)
        d_mod_low = d_mod_low.reshape(dp_size, LAYERS, images, mod_cols)
        d_mod_low = d_mod_low.transpose(1, 0, 2, 3).reshape(LAYERS, images_all, mod_cols)
        d_signal_rows = jnp.einsum(
            "lbe,lde->db", d_mod_low, mod_low, preferred_element_type=jnp.float32
        )
        d_signal_part = dense(shift_cols.T, d_shift_cols) + dense(scale_cols.T, d_scale_cols)
        d_signal_part = d_signal_part + lax.dynamic_update_slice_in_dim(
            jnp.zeros((D, images_all), jnp.float32), d_signal_rows, dp_rank * mod_rows, 0
        )
        d_signal_cols = jnp.sum(
            exchange(d_signal_part.reshape(place_count, cols, images_all), "all", True, 10), axis=0
        )
        d_pre_signal = d_signal_cols * silu_slope(pre_signal)
        d_hidden_part = dense(second_cols.T, d_pre_signal)
        d_hidden_cols = jnp.sum(
            exchange(d_hidden_part.reshape(place_count, cols, images_all), "all", True, 11), axis=0
        )
        d_hidden = d_hidden_cols * silu_slope(pre_time)
        mod_grad = jnp.einsum(
            "db,lbe->lde", signal_low, d_mod_low, preferred_element_type=jnp.float32
        )
        class_grad = dense(d_pre_signal, onehot)
        time_grad = dense(d_hidden, time_feats)
        second_grad = dense(d_pre_signal, hidden.T)
        shift_grad = dense(d_shift_cols, signal.T)
        scale_grad = dense(d_scale_cols, signal.T)
        vector_sums = jnp.stack(
            [
                jnp.sum(values, axis=1)
                for values in (d_hidden, d_pre_signal, d_shift_cols, d_scale_cols)
            ],
            axis=1,
        )
        table_grad = jnp.concatenate(
            [
                class_grad,
                row_sums[:, 0:patch_in],
                time_grad,
                second_grad,
                shift_grad,
                scale_grad,
                row_sums[:, patch_in : 2 * patch_in + 1],
                vector_sums,
                row_sums[:, 2 * patch_in + 1 : final_at],
            ],
            axis=1,
        )
    input_grad = jnp.stack([jnp.concatenate(total[0:2], axis=1) for total in totals])
    input_grad = input_grad.reshape(layer_in.shape)
    output_grad = jnp.stack([total[2] for total in totals]).reshape(layer_out.shape)
    if not fused:
        local_squares = (
            jnp.sum(table_grad * table_grad)
            + jnp.sum(input_grad * input_grad)
            + jnp.sum(output_grad * output_grad)
            + jnp.sum(mod_grad * mod_grad)
        )
        scalar_send = jnp.where(
            lax.broadcasted_iota(jnp.int32, (8, 128), 1) == 0, loss_part, local_squares
        )
        scalar_sums = jnp.sum(exchange(scalar_send, "all", False, 12)[:, 0, 0:2], axis=0)
    loss_value = scalar_sums[0]
    square_total = scalar_sums[1]
    grad_norm = jnp.sqrt(square_total)
    factor = jnp.minimum(1.0, CLIP_NORM / grad_norm)
    first_fix = 1.0 - BETA_ONE ** step_count.astype(jnp.float32)
    second_fix = 1.0 - BETA_TWO ** step_count.astype(jnp.float32)
    embed_out = adam_update(
        embed_table.T, embed_first.T, embed_second.T, table_grad, factor, first_fix, second_fix
    )
    input_out = adam_update(
        layer_in, input_first, input_second, input_grad, factor, first_fix, second_fix
    )
    output_out = adam_update(
        layer_out, output_first, output_second, output_grad, factor, first_fix, second_fix
    )
    mod_out = adam_update(layer_ada, mod_first, mod_second, mod_grad, factor, first_fix, second_fix)
    return (
        (loss_value, grad_norm, embed_out[4].T, embed_out[1].T, embed_out[2].T)
        + input_out[0:4]
        + output_out[0:4]
        + mod_out[0:4]
    )


def solution(mesh):
    placed = (
        P("dp", "tensor"),
        P("dp", "tensor"),
        P("dp"),
        P("dp"),
        P(),
        P(None, ("dp", "tensor")),
        P(None, "dp", "tensor", None),
        P(None, "tensor", "dp", None),
        P(None, "dp", "tensor"),
        P(None, ("dp", "tensor")),
        P(None, ("dp", "tensor")),
        P(None, "dp", "tensor", None),
        P(None, "dp", "tensor", None),
        P(None, "tensor", "dp", None),
        P(None, "tensor", "dp", None),
        P(None, "dp", "tensor"),
        P(None, "dp", "tensor"),
    )
    return jax.shard_map(
        local,
        mesh=mesh,
        in_specs=placed,
        out_specs=(
            P(),
            P(),
            P(None, ("dp", "tensor")),
            P(None, ("dp", "tensor")),
            P(None, ("dp", "tensor")),
            P(None, "dp", "tensor", None),
            P(None, "dp", "tensor", None),
            P(None, "dp", "tensor", None),
            P(None, "dp", "tensor", None),
            P(None, "tensor", "dp", None),
            P(None, "tensor", "dp", None),
            P(None, "tensor", "dp", None),
            P(None, "tensor", "dp", None),
            P(None, "dp", "tensor"),
            P(None, "dp", "tensor"),
            P(None, "dp", "tensor"),
            P(None, "dp", "tensor"),
        ),
        check_vma=False,
    )
```
